32 devices in a mesh: clip: 8 (over z, x), row: 2 (over y), col: 2 (over core).
Axes of the slice: x: 2, y: 2, z: 4, core: 2. Of those that a mesh axis runs over, the one named last changes fastest.
Arguments:
- patches: bfloat16 [2, 16, 1176, 1536], P(None, ('clip', 'col'), None, 'row'), may hold values from -20 to 20
- visible: int32 [2, 16, 118], P(None, ('clip', 'col')), may hold values from 0 to 1175, as said below
- masked: int32 [2, 16, 1058], P(None, ('clip', 'col')), may hold values from 0 to 1175
- enc_layers: float32 [2, 2, 768, 4608], P(None, 'row', ('clip', 'col')), may hold values from -0.65 to 0.65
- enc_first: float32 [2, 2, 768, 4608], P(None, 'row', ('clip', 'col')), may hold values from -0.00036621094 to 0.00036621094
- enc_second: float32 [2, 2, 768, 4608], P(None, 'row', ('clip', 'col')), may hold values from 2.7777778e-11 to 4.4444445e-10
- embed: float32 [2, 768, 768], P('row', ('clip', 'col')), may hold values from -0.15625 to 0.15625
- embed_first: float32 [2, 768, 768], P('row', ('clip', 'col')), may hold values from -0.00036621094 to 0.00036621094
- embed_second: float32 [2, 768, 768], P('row', ('clip', 'col')), may hold values from 2.7777778e-11 to 4.4444445e-10
- dec_mats: float32 [2, 384, 3456], P('row', ('clip', 'col')), may hold values from -0.65 to 0.65
- dec_first: float32 [2, 384, 3456], P('row', ('clip', 'col')), may hold values from -0.00036621094 to 0.00036621094
- dec_second: float32 [2, 384, 3456], P('row', ('clip', 'col')), may hold values from 2.7777778e-11 to 4.4444445e-10
- enc_vec: float32 [10, 768], P(None, ('clip', 'col')), may hold values from -4 to 4
- enc_vec_first: float32 [10, 768], P(None, ('clip', 'col')), may hold values from -0.0017089844 to 0.0017089844
- enc_vec_second: float32 [10, 768], P(None, ('clip', 'col')), may hold values from 1.1111111e-10 to 1.7777778e-09
- dec_vec: float32 [7, 384], P(None, ('clip', 'col')), may hold values from -4 to 4
- dec_vec_first: float32 [7, 384], P(None, ('clip', 'col')), may hold values from -0.0017089844 to 0.0017089844
- dec_vec_second: float32 [7, 384], P(None, ('clip', 'col')), may hold values from 1.1111111e-10 to 1.7777778e-09
Outputs:
- loss_sum: float32 [], replicated
- grad_norm: float32 [], replicated
- enc_layers_new: float32 [2, 2, 768, 4608], P(None, 'row', ('clip', 'col'))
- enc_first_new: float32 [2, 2, 768, 4608], P(None, 'row', ('clip', 'col'))
- enc_second_new: float32 [2, 2, 768, 4608], P(None, 'row', ('clip', 'col'))
- embed_new: float32 [2, 768, 768], P('row', ('clip', 'col'))
- embed_first_new: float32 [2, 768, 768], P('row', ('clip', 'col'))
- embed_second_new: float32 [2, 768, 768], P('row', ('clip', 'col'))
- dec_mats_new: float32 [2, 384, 3456], P('row', ('clip', 'col'))
- dec_first_new: float32 [2, 384, 3456], P('row', ('clip', 'col'))
- dec_second_new: float32 [2, 384, 3456], P('row', ('clip', 'col'))
- enc_vec_new: float32 [10, 768], P(None, ('clip', 'col'))
- enc_vec_first_new: float32 [10, 768], P(None, ('clip', 'col'))
- enc_vec_second_new: float32 [10, 768], P(None, ('clip', 'col'))
- dec_vec_new: float32 [7, 384], P(None, ('clip', 'col'))
- dec_vec_first_new: float32 [7, 384], P(None, ('clip', 'col'))
- dec_vec_second_new: float32 [7, 384], P(None, ('clip', 'col'))
The draws below stay inside these ranges and needn't reach their ends.
Inputs may be any that keep to these rules, and one draw needn't show every extreme that they name: For every micro-batch and clip, visible and masked together hold every tube number of 0 to 1175 exactly once.
All inputs are finite; a program needn't handle non-finite values.
Results may differ from the reference program's by a relative error of at most 0.011.
Values may be sent and summed in bfloat16 or wider, within the bound.
A program may use at most 256 MiB of HBM per device.

```python
import math
import jax
import jax.numpy as jnp
from jax import lax

D = 768
HEADS = 12
HEAD = 64
FF = 3072
DD = 384
DHEADS = 6
DFF = 1536
PIX = 1536
TUBES = 1176
VIS = 118
LAYERS = 2
MICRO = 2
STEP = 10
CLIPS = 16
MASKED = 1058
ENC_W = 4608
DEC_W = 3456
EMB_W = 768
ENC_VECS = 10
PARAMS = 18000000
N_ROW = 2


def tube_order(key):
    keys_all = jax.random.split(key, MICRO * CLIPS)

    def shuffle_one(sub_key):
        return jax.random.permutation(sub_key, TUBES)
    orders = jax.vmap(shuffle_one)(keys_all)
    return orders.reshape(MICRO, CLIPS, TUBES).astype(jnp.int32)


def draw_visible(key, part):
    return tube_order(key)[..., :VIS]


def draw_masked(key, part):
    return tube_order(key)[..., VIS:]


def draw_patches(key, part):
    key = jax.random.fold_in(key, 11)
    shape = (MICRO, CLIPS, TUBES, PIX)
    base = jax.random.truncated_normal(key, -4.0, 4.0, shape, jnp.float32)
    reach = 2.0
    clip_scale = 1.0 + reach * jnp.arange(CLIPS, dtype=jnp.float32) / max(CLIPS - 1, 1)
    pixel_scale = 0.6 + jnp.arange(PIX, dtype=jnp.float32) / max(PIX - 1, 1)
    return (base * clip_scale[None, :, None, None] * pixel_scale).astype(jnp.bfloat16)


def column_spread(widths, scales):
    return jnp.concatenate([jnp.full((piece_width,), scale_value, jnp.float32) for piece_width, scale_value in zip(widths, scales)])


def draw_enc_layers(key, part):
    key = jax.random.fold_in(key, 21)
    shape = (LAYERS, N_ROW, D, ENC_W)
    base = jax.random.truncated_normal(key, -4.0, 4.0, shape, jnp.float32)
    widths = (3 * D // N_ROW, D // N_ROW, FF // N_ROW, FF // N_ROW)
    scales = (D ** (-0.5), 0.5 * VIS ** 0.25 * D ** (-0.5), D ** (-0.5), FF ** (-0.5))
    return base * column_spread(widths, scales)


def draw_dec_mats(key, part):
    key = jax.random.fold_in(key, 23)
    shape = (N_ROW, DD, DEC_W)
    base = jax.random.truncated_normal(key, -4.0, 4.0, shape, jnp.float32)
    widths = (3 * DD // N_ROW, DD // N_ROW, DFF // N_ROW, DFF // N_ROW, PIX // N_ROW, D // N_ROW)
    scales = (DD ** (-0.5), 0.5 * TUBES ** 0.25 * DD ** (-0.5), DD ** (-0.5), DFF ** (-0.5), DD ** (-0.5), D ** (-0.5))
    return base * column_spread(widths, scales)


def vector_rows(gain_key, shift_key, rows_count, width, ramp_low):
    ramp = ramp_low + jnp.arange(width, dtype=jnp.float32) / max(width - 1, 1)
    jitter = jax.random.uniform(gain_key, (rows_count, width), jnp.float32, 0.8, 1.2)
    shifts = 0.2 * jax.random.truncated_normal(shift_key, -4.0, 4.0, (rows_count, width), jnp.float32)
    is_gain = (jnp.arange(rows_count) % 2 == 0)[:, None]
    return jnp.where(is_gain, ramp * jitter, shifts)


def draw_enc_vec(key, part):
    key = jax.random.fold_in(key, 31)
    gain_key, shift_key = jax.random.split(key)
    return vector_rows(gain_key, shift_key, ENC_VECS, D, 0.5)


def draw_dec_vec(key, part):
    key = jax.random.fold_in(key, 37)
    gain_key, shift_key, token_key = jax.random.split(key, 3)
    table = vector_rows(gain_key, shift_key, 7, DD, 0.5)
    token_row = jax.random.truncated_normal(token_key, -4.0, 4.0, (7, DD), jnp.float32)
    return jnp.where((jnp.arange(7) == 6)[:, None], token_row, table)


def levels(rng, extent, cuts, smallest, high):
    def one(axis_at, parts):
        draws = jax.random.uniform(jax.random.fold_in(jax.random.fold_in(rng, 6), axis_at), (parts,), jnp.float32, smallest / len(cuts), high / len(cuts))
        return jnp.repeat(jnp.exp(draws), extent[axis_at] // parts).reshape((-1,) + (1,) * (len(extent) - axis_at - 1))

    loudness = one(*cuts[0])
    for cut in cuts[1:]:
        loudness = loudness * one(*cut)
    return loudness


def scatter_about(rng, dims, spread, limit, cuts=(), kind=jnp.bfloat16):
    array = spread * jax.random.normal(rng, dims, jnp.float32)
    if cuts:
        array = array * levels(rng, dims, cuts, -0.22, 0.18)
    return jnp.clip(array, -limit, limit).astype(kind)


def setup_inputs(seed: int = 0) -> dict:
    splits = jax.random.split(jax.random.key(seed), 19)
    patches = draw_patches(jax.random.fold_in(splits[18], 71), 0)
    visible = draw_visible(jax.random.fold_in(splits[18], 71), 0)
    masked = draw_masked(jax.random.fold_in(splits[18], 71), 0)
    enc_layers = draw_enc_layers(jax.random.fold_in(splits[18], 71), 0)
    enc_first = scatter_about(splits[4], (LAYERS, N_ROW, D, ENC_W), (0.111 / PARAMS ** 0.5), 0.00036621094, ((1, 2), (2, 16)), jnp.float32)
    enc_second = jnp.clip(jnp.exp(math.log(4.4444445346236705e-10) - 2.7725887 * jax.random.uniform(splits[5], (LAYERS, N_ROW, D, ENC_W), jnp.float32) ** levels(splits[5], (LAYERS, N_ROW, D, ENC_W), ((1, 2), (2, 16)), -0.2, 0.2)), 2.777777834139794e-11, 4.4444445346236705e-10)
    embed = scatter_about(splits[6], (N_ROW, D, EMB_W), PIX ** -0.5, 0.15625, ((0, 2), (1, 16)), jnp.float32)
    embed_first = scatter_about(splits[7], (N_ROW, D, EMB_W), (0.111 / PARAMS ** 0.5), 0.00036621094, ((0, 2), (1, 16)), jnp.float32)
    embed_second = jnp.clip(jnp.exp(math.log(4.4444445346236705e-10) - 2.7725887 * jax.random.uniform(splits[8], (N_ROW, D, EMB_W), jnp.float32) ** levels(splits[8], (N_ROW, D, EMB_W), ((0, 2), (1, 16)), -0.2, 0.2)), 2.777777834139794e-11, 4.4444445346236705e-10)
    dec_mats = draw_dec_mats(jax.random.fold_in(splits[18], 71), 0)
    dec_first = scatter_about(splits[10], (N_ROW, DD, DEC_W), (0.111 / PARAMS ** 0.5), 0.00036621094, ((0, 2), (1, 16)), jnp.float32)
    dec_second = jnp.clip(jnp.exp(math.log(4.4444445346236705e-10) - 2.7725887 * jax.random.uniform(splits[11], (N_ROW, DD, DEC_W), jnp.float32) ** levels(splits[11], (N_ROW, DD, DEC_W), ((0, 2), (1, 16)), -0.2, 0.2)), 2.777777834139794e-11, 4.4444445346236705e-10)
    enc_vec = draw_enc_vec(jax.random.fold_in(splits[18], 71), 0)
    enc_vec_first = scatter_about(splits[13], (ENC_VECS, D), (0.5 / PARAMS ** 0.5), 0.0017089844, ((1, 16),), jnp.float32)
    enc_vec_second = jnp.clip(jnp.exp(math.log(1.7777778138494682e-09) - 2.7725887 * jax.random.uniform(splits[14], (ENC_VECS, D), jnp.float32) ** levels(splits[14], (ENC_VECS, D), ((1, 16),), -0.2, 0.2)), 1.1111111336559176e-10, 1.7777778138494682e-09)
    dec_vec = draw_dec_vec(jax.random.fold_in(splits[18], 71), 0)
    dec_vec_first = scatter_about(splits[16], (7, DD), (0.5 / PARAMS ** 0.5), 0.0017089844, ((1, 16),), jnp.float32)
    dec_vec_second = jnp.clip(jnp.exp(math.log(1.7777778138494682e-09) - 2.7725887 * jax.random.uniform(splits[17], (7, DD), jnp.float32) ** levels(splits[17], (7, DD), ((1, 16),), -0.2, 0.2)), 1.1111111336559176e-10, 1.7777778138494682e-09)
    return {"patches": patches, "visible": visible, "masked": masked, "enc_layers": enc_layers, "enc_first": enc_first, "enc_second": enc_second, "embed": embed, "embed_first": embed_first, "embed_second": embed_second, "dec_mats": dec_mats, "dec_first": dec_first, "dec_second": dec_second, "enc_vec": enc_vec, "enc_vec_first": enc_vec_first, "enc_vec_second": enc_vec_second, "dec_vec": dec_vec, "dec_vec_first": dec_vec_first, "dec_vec_second": dec_vec_second}


@jax.custom_vjp
def low(v):
    return lax.optimization_barrier(v.astype(jnp.bfloat16)).astype(jnp.float32)

@jax.custom_vjp
def low_back(v):
    return v

def low_keep(v):
    return (low(v), None)

def low_pass(kept, grad):
    return (grad,)

def back_keep(v):
    return (v, None)

def back_low(kept, grad):
    return (low(grad),)
low.defvjp(low_keep, low_pass)
low_back.defvjp(back_keep, back_low)
EPS_NORM = 1e-06
CLIP_MAX = 1.0
BETA_ONE = 0.9
BETA_TWO = 0.999
RATE = 0.06
VEC_RATE = 0.2
DECAY = 0.05
EPS_ADAM = 1e-08

def dot_high(left, right):
    return jnp.dot(left, right, precision=lax.Precision.HIGHEST, preferred_element_type=jnp.float32)

def position_table(index, width):
    column = jnp.arange(width)
    freq = jnp.exp(-math.log(10000.0) * (2.0 * (column // 2)) / width)
    angle = index.astype(jnp.float32)[..., None] * freq
    return jnp.where(column % 2 == 0, jnp.sin(angle), jnp.cos(angle))

def layer_norm(rows, gain_row, offset):
    average = lax.optimization_barrier(jnp.mean(rows, axis=-1, keepdims=True))
    centred = rows - average
    variance = lax.optimization_barrier(jnp.mean(centred * centred, axis=-1, keepdims=True))
    return centred * lax.rsqrt(variance + EPS_NORM) * gain_row + offset

def sum_blocks(values, blocks_t):
    block_width = blocks_t[0].shape[1]
    total = jnp.zeros((values.shape[0], blocks_t[0].shape[0]), jnp.float32)
    for block_at, block in enumerate(blocks_t):
        total = total + low(dot_high(values[:, block_at * block_width:(block_at + 1) * block_width], block.T))
    return total

def cat_blocks(values, blocks):
    return jnp.concatenate([dot_high(low_back(values), block) for block in blocks], axis=-1)

def attention(qkv_rows, heads):
    length = qkv_rows.shape[0]
    packed = qkv_rows.reshape(length, heads, 3, HEAD)
    scores = jnp.einsum('thd,shd->hts', packed[:, :, 0], packed[:, :, 1], precision=lax.Precision.HIGHEST) * HEAD ** (-0.5)
    scores = low_back(scores)
    soft_weights = jax.nn.softmax(scores, axis=-1)
    output = jnp.einsum('hts,shd->thd', low(soft_weights), packed[:, :, 2], precision=lax.Precision.HIGHEST)
    return low(low_back(output.reshape(length, heads * HEAD)))

def layer_forward(resid, weights, gains, heads):
    w_qkv, w_out, w_up, w_down = weights
    normed = low(layer_norm(resid, gains[0], gains[1]))
    qkv_rows = low(low_back(cat_blocks(normed, w_qkv)))
    resid = resid + low_back(sum_blocks(attention(qkv_rows, heads), w_out))
    normed = low(layer_norm(resid, gains[2], gains[3]))
    hidden_pre = low_back(cat_blocks(normed, w_up))
    activated = low(jax.nn.gelu(hidden_pre, approximate=False))
    return resid + low_back(sum_blocks(activated, w_down))

def cut_blocks(stacked, widths):
    pieces = []
    column_at = 0
    for piece_width in widths:
        pieces.append([stacked[..., block_at, :, column_at:column_at + piece_width] for block_at in range(N_ROW)])
        column_at += piece_width
    return pieces

def clip_loss(params, pixels, seen, hidden_idx):
    enc_pieces, embed_blocks, dec_pieces, enc_gains, dec_gains = params
    resid = low_back(sum_blocks(pixels[seen], embed_blocks)) + position_table(seen, D)
    for layer_at in range(LAYERS):
        layer_weights = [[block[layer_at] for block in piece] for piece in enc_pieces]
        resid = layer_forward(resid, layer_weights, enc_gains[4 * layer_at:4 * layer_at + 4], HEADS)
    final_rows = low(layer_norm(resid, enc_gains[4 * LAYERS], enc_gains[4 * LAYERS + 1]))
    w_qkv, w_out, w_up, w_down, w_head, w_link = dec_pieces
    decoded = low_back(sum_blocks(final_rows, w_link)) + position_table(seen, DD)
    filler = dec_gains[6] + position_table(hidden_idx, DD)
    dec_rows = layer_forward(jnp.concatenate([decoded, filler], axis=0), (w_qkv, w_out, w_up, w_down), dec_gains[0:4], DHEADS)
    tail_rows = low(layer_norm(dec_rows[VIS:], dec_gains[4], dec_gains[5]))
    predicted = low_back(cat_blocks(tail_rows, w_head))
    error = predicted - pixels[hidden_idx]
    return jnp.sum(error * error) / PIX

def total_loss(masters, pixels, seen, hidden_idx):
    enc_master, embed_master, dec_master, enc_vec_master, dec_vec_master = masters
    enc_pieces = cut_blocks(low(enc_master), (3 * D // N_ROW, D // N_ROW, FF // N_ROW, FF // N_ROW))
    embed_blocks = cut_blocks(low(embed_master), (PIX // N_ROW,))[0]
    dec_pieces = cut_blocks(low(dec_master), (3 * DD // N_ROW, DD // N_ROW, DFF // N_ROW, DFF // N_ROW, PIX // N_ROW, D // N_ROW))
    params = (enc_pieces, embed_blocks, dec_pieces, low(enc_vec_master), low(dec_vec_master))
    checked = jax.checkpoint(clip_loss)

    def add_clip(running, clip_items):
        return (running + checked(params, clip_items[0], clip_items[1], clip_items[2]), None)
    running, unused = lax.scan(add_clip, jnp.zeros((), jnp.float32), (pixels, seen, hidden_idx))
    return running

def adam_update(master, first, second, grad_clip, decay_rate, step_rate):
    first_new = BETA_ONE * first + (1.0 - BETA_ONE) * grad_clip
    second_new = BETA_TWO * second + (1.0 - BETA_TWO) * grad_clip * grad_clip
    first_hat = first_new / (1.0 - BETA_ONE ** STEP)
    second_hat = second_new / (1.0 - BETA_TWO ** STEP)
    master_new = master - step_rate * (first_hat / (jnp.sqrt(second_hat) + EPS_ADAM) + decay_rate * master)
    return (master_new, first_new, second_new)

def reference(patches, visible, masked, enc_layers, enc_first, enc_second, embed, embed_first, embed_second, dec_mats, dec_first, dec_second, enc_vec, enc_vec_first, enc_vec_second, dec_vec, dec_vec_first, dec_vec_second):
    pixels = patches.astype(jnp.float32).reshape(-1, TUBES, PIX)
    seen = visible.reshape(-1, VIS).astype(jnp.int32)
    hidden_idx = masked.reshape(-1, MASKED).astype(jnp.int32)
    masters = (enc_layers, embed, dec_mats, enc_vec, dec_vec)

    def loss_of(*weights):
        return total_loss(weights, pixels, seen, hidden_idx)
    loss_value, pullback = jax.vjp(loss_of, *masters)
    grads = pullback(jnp.ones((), jnp.float32))
    square = sum((jnp.sum(piece * piece) for piece in grads))
    grad_norm = jnp.sqrt(square)
    factor = jnp.minimum(1.0, CLIP_MAX / (grad_norm + 1e-06))
    states = ((enc_first, enc_second), (embed_first, embed_second), (dec_first, dec_second), (enc_vec_first, enc_vec_second), (dec_vec_first, dec_vec_second))
    decays = (DECAY, DECAY, DECAY, 0.0, 0.0)
    rates = (RATE, RATE, RATE, VEC_RATE, VEC_RATE)
    results = []
    for master, pair, piece, decay_rate, step_rate in zip(masters, states, grads, decays, rates):
        results.extend(adam_update(master, pair[0], pair[1], piece * factor, decay_rate, step_rate))
    return (loss_value, grad_norm, results[0], results[1], results[2], results[3], results[4], results[5], results[6], results[7], results[8], results[9], results[10], results[11], results[12], results[13], results[14])
```

```python
import math

import jax
import jax.numpy as jnp
import numpy as np
from jax import lax
from jax.experimental import pallas as pl
from jax.experimental.pallas import tpu as pltpu
from jax.sharding import PartitionSpec as P

D = 768
HEADS = 12
HEAD = 64
FF = 3072
DD = 384
DHEADS = 6
DFF = 1536
PIX = 1536
TUBES = 1176
VIS = 118
LAYERS = 2
MICRO = 2
STEP = 10
MASKED = 1058


EPS_NORM = 1e-06
CLIP_MAX = 1.0
BETA_ONE = 0.9
BETA_TWO = 0.999
RATE = 0.06
VEC_RATE = 0.2
DECAY = 0.05
EPS_ADAM = 1e-08


def times_plain(left, right):
    return jnp.dot(left, right, preferred_element_type=jnp.float32)


def times_trans(left, right):
    return lax.dot_general(
        left, right, (((1,), (1,)), ((), ())), preferred_element_type=jnp.float32
    )


def trans_times(left, right):
    return lax.dot_general(
        left, right, (((0,), (0,)), ((), ())), preferred_element_type=jnp.float32
    )


def position_table(index, width):
    column = jnp.arange(width)
    freq = jnp.exp(-math.log(10000.0) * (2.0 * (column // 2)) / width)
    angle = index.astype(jnp.float32)[..., None] * freq
    return jnp.where(column % 2 == 0, jnp.sin(angle), jnp.cos(angle))


def normalize(rows, gain_row, offset):
    average = jnp.mean(rows, axis=-1, keepdims=True)
    centred = rows - average
    inv_dev = lax.rsqrt(jnp.mean(centred * centred, axis=-1, keepdims=True) + EPS_NORM)
    scaled = centred * inv_dev
    return ((scaled * gain_row + offset).astype(jnp.bfloat16), scaled, inv_dev)


def normalize_back(grad_out, scaled, inv_dev, gain_row):
    inner = grad_out * gain_row
    grad_rows = inv_dev * (
        inner
        - jnp.mean(inner, axis=-1, keepdims=True)
        - scaled * jnp.mean(inner * scaled, axis=-1, keepdims=True)
    )
    return (grad_rows, jnp.sum(grad_out * scaled, axis=0), jnp.sum(grad_out, axis=0))


def gelu_pair(values):
    cumul = 0.5 * (1.0 + lax.erf(values * 0.7071067811865476))
    density = jnp.exp(-0.5 * values * values) * 0.3989422804014327
    return (values * cumul, cumul + values * density)


def attend(qkv_rows, clips, length, heads_here):
    packed = qkv_rows.reshape(clips, length, heads_here, 3, HEAD)

    def one_clip(clip_block):
        scores = jnp.einsum(
            "thd,shd->hts",
            clip_block[:, :, 0],
            clip_block[:, :, 1],
            preferred_element_type=jnp.float32,
        ) * HEAD ** (-0.5)
        row_max = jnp.max(scores, axis=-1, keepdims=True)
        logsum = row_max + jnp.log(jnp.sum(jnp.exp(scores - row_max), axis=-1, keepdims=True))
        soft_low = jnp.exp(scores - logsum).astype(jnp.bfloat16)
        output = jnp.einsum(
            "hts,shd->thd", soft_low, clip_block[:, :, 2], preferred_element_type=jnp.float32
        )
        return (output.astype(jnp.bfloat16).reshape(length, heads_here * HEAD), logsum)

    output, logsum = lax.map(one_clip, packed)
    return (output.reshape(clips * length, heads_here * HEAD), logsum)


def attend_back(qkv_rows, logsum, grad_att, clips, length, heads_here):
    packed = qkv_rows.reshape(clips, length, heads_here, 3, HEAD)
    grad_heads = grad_att.reshape(clips, length, heads_here, HEAD)

    def one_clip(clip_items):
        clip_block, grad_block, clip_sum = clip_items
        query_rows, key_rows, value_rows = (
            clip_block[:, :, 0],
            clip_block[:, :, 1],
            clip_block[:, :, 2],
        )
        scores = jnp.einsum(
            "thd,shd->hts", query_rows, key_rows, preferred_element_type=jnp.float32
        ) * HEAD ** (-0.5)
        soft_rows = jnp.exp(scores - clip_sum)
        grad_values = jnp.einsum(
            "hts,thd->shd",
            soft_rows.astype(jnp.bfloat16),
            grad_block,
            preferred_element_type=jnp.float32,
        )
        grad_soft = jnp.einsum(
            "thd,shd->hts", grad_block, value_rows, preferred_element_type=jnp.float32
        )
        grad_scores = soft_rows * (
            grad_soft - jnp.sum(soft_rows * grad_soft, axis=-1, keepdims=True)
        )
        grad_low = grad_scores.astype(jnp.bfloat16)
        grad_query = jnp.einsum(
            "hts,shd->thd", grad_low, key_rows, preferred_element_type=jnp.float32
        ) * HEAD ** (-0.5)
        grad_keys = jnp.einsum(
            "hts,thd->shd", grad_low, query_rows, preferred_element_type=jnp.float32
        ) * HEAD ** (-0.5)
        return jnp.stack([grad_query, grad_keys, grad_values], axis=2).reshape(
            length, heads_here * 3 * HEAD
        )

    result = lax.map(one_clip, (packed, grad_heads, logsum))
    return result.reshape(clips * length, heads_here * 3 * HEAD)


def layer_forward(resid, weights, gains, clips, length, heads_here):
    w_qkv, w_out, w_up, w_down = weights
    normed_one, scaled_one, inv_one = normalize(resid, gains[0], gains[1])
    qkv_rows = times_plain(normed_one, w_qkv).astype(jnp.bfloat16)
    attended, logsum = attend(qkv_rows, clips, length, heads_here)
    middle = resid + pair_total(times_trans(attended, w_out))
    normed_two, scaled_two, inv_two = normalize(middle, gains[2], gains[3])
    hidden_pre = times_plain(normed_two, w_up)
    activated, slope = gelu_pair(hidden_pre)
    activated = activated.astype(jnp.bfloat16)
    result = middle + pair_total(times_trans(activated, w_down))
    kept = (
        scaled_one,
        inv_one,
        normed_one,
        qkv_rows,
        logsum,
        attended,
        scaled_two,
        inv_two,
        normed_two,
        slope,
        activated,
    )
    return (result, kept)


def layer_backward(grad_resid, weights, gains, kept, clips, length, heads_here):
    w_qkv, w_out, w_up, w_down = weights
    (
        scaled_one,
        inv_one,
        normed_one,
        qkv_rows,
        logsum,
        attended,
        scaled_two,
        inv_two,
        normed_two,
        slope,
        activated,
    ) = kept
    grad_branch = grad_resid.astype(jnp.bfloat16)
    grad_down = trans_times(grad_branch, activated)
    grad_hidden = (times_plain(grad_branch, w_down) * slope).astype(jnp.bfloat16)
    grad_up = trans_times(normed_two, grad_hidden)
    grad_normed = pair_total(times_trans(grad_hidden, w_up))
    grad_rows, gain_two, shift_two = normalize_back(grad_normed, scaled_two, inv_two, gains[2])
    grad_middle = grad_resid + grad_rows
    grad_branch = grad_middle.astype(jnp.bfloat16)
    grad_out = trans_times(grad_branch, attended)
    grad_att = times_plain(grad_branch, w_out).astype(jnp.bfloat16)
    grad_qkv = attend_back(qkv_rows, logsum, grad_att, clips, length, heads_here).astype(
        jnp.bfloat16
    )
    grad_wqkv = trans_times(normed_one, grad_qkv)
    grad_normed = pair_total(times_trans(grad_qkv, w_qkv))
    grad_rows, gain_one, shift_one = normalize_back(grad_normed, scaled_one, inv_one, gains[0])
    grad_vectors = jnp.stack([gain_one, shift_one, gain_two, shift_two])
    return (
        grad_middle + grad_rows,
        jnp.concatenate([grad_wqkv, grad_out, grad_up, grad_down], axis=-1),
        grad_vectors,
    )


def split_columns(matrix_block, widths):
    pieces = []
    column_at = 0
    for piece_width in widths:
        pieces.append(matrix_block[..., column_at : column_at + piece_width])
        column_at += piece_width
    return pieces


def adam_update(master, first, second, grad_clip, decay_rate, step_rate):
    first_new = BETA_ONE * first + (1.0 - BETA_ONE) * grad_clip
    second_new = BETA_TWO * second + (1.0 - BETA_TWO) * grad_clip * grad_clip
    first_hat = first_new / (1.0 - BETA_ONE**STEP)
    second_hat = second_new / (1.0 - BETA_TWO**STEP)
    master_new = master - step_rate * (
        first_hat / (jnp.sqrt(second_hat) + EPS_ADAM) + decay_rate * master
    )
    return (master_new, first_new, second_new)


ROWS = 1200
LANES = 1280
STEP_ROWS = 240
N_STEPS = ROWS // STEP_ROWS
KEY_ROWS = 256
N_KEYS = LANES // KEY_ROWS
LOG2E = 1.4426950408889634
SCALE = HEAD ** (-0.5)
MIB = 1 << 20


def low(values):
    return values.astype(jnp.bfloat16)


def lane_ids(shape):
    return lax.broadcasted_iota(jnp.int32, shape, len(shape) - 1)


def row_ids(shape):
    return lax.broadcasted_iota(jnp.int32, shape, 0)


def norm_rows(rows):
    average = jnp.mean(rows, axis=-1, keepdims=True)
    centred = rows - average
    inv_dev = lax.rsqrt(jnp.mean(centred * centred, axis=-1, keepdims=True) + EPS_NORM)
    return centred * inv_dev, inv_dev


def norm_rows_back(grad_out, scaled, inv_dev, gain_row):
    inner = grad_out * gain_row
    return inv_dev * (
        inner
        - jnp.mean(inner, axis=-1, keepdims=True)
        - scaled * jnp.mean(inner * scaled, axis=-1, keepdims=True)
    )


def column_sum(values):
    return jnp.sum(values, axis=0, keepdims=True)


def decoder_body(
    seen_ref,
    feat_ref,
    pixel_ref,
    table_ref,
    w_ref,
    vec_ref,
    loss_ref,
    grad_ref,
    gvec_ref,
    gfeat_ref,
    z_s,
    n1_s,
    q_s,
    k_s,
    v_s,
    o_s,
    do_s,
    dx_s,
    dqkv_s,
    dqt_s,
    lse_s,
    delta_s,
    lse_t,
    delta_t,
    bias_s,
    wqkv_s,
    wo_s,
    y_s,
    gqkv_s,
    go_s,
    gup_s,
    gdn_s,
    ghd_s,
    gy_s,
    gv_s,
):
    bf, f32 = jnp.bfloat16, jnp.float32
    half = 3 * HEAD
    up0, dn0, hd0, ed0 = 768, 1536, 2304, 3072
    vec = vec_ref[...]
    gain1, shift1, gain2, shift2, gain_f, shift_f, token = [vec[i : i + 1] for i in range(7)]

    for part in range(3):
        for r in range(2):
            wqkv_s[:, part * DD + r * half : part * DD + (r + 1) * half] = w_ref[
                r, :, part * half : (part + 1) * half
            ]
    for r in range(2):
        wo_s[:, r * half : (r + 1) * half] = w_ref[r, :, 3 * half : 4 * half]
    for ref in (q_s, k_s, v_s, do_s):
        ref[ROWS:LANES, :] = jnp.zeros((LANES - ROWS, DD), bf)
    lse_s[ROWS:LANES, :] = jnp.zeros((LANES - ROWS, 128), f32)
    delta_s[ROWS:LANES, :] = jnp.zeros((LANES - ROWS, 128), f32)
    bias_s[...] = jnp.where(row_ids((LANES, 128)) < TUBES, 0.0, -1e30)
    for ref in (gqkv_s, go_s, gup_s, gdn_s, ghd_s, gy_s, gv_s):
        ref[...] = jnp.zeros(ref.shape, f32)
    for r in range(2):
        y_s[:, r * DD : (r + 1) * DD] = low(
            times_trans(feat_ref[:, r * DD : (r + 1) * DD], w_ref[r, :, ed0 : ed0 + DD])
        )
    seen = seen_ref[0:1, :]

    def tile(i):
        return pl.ds(pl.multiple_of(i * STEP_ROWS, STEP_ROWS), STEP_ROWS)

    def picks(i):
        ids = row_ids((STEP_ROWS, 128)) + i * STEP_ROWS
        hits = ids == seen
        taken = jnp.sum(hits.astype(f32), axis=-1, keepdims=True)
        valid = (row_ids((STEP_ROWS, 1)) + i * STEP_ROWS < TUBES).astype(f32)
        return hits.astype(bf), valid - taken

    @pl.loop(0, N_STEPS)
    def _(i):
        hits, hidden = picks(i)
        placed = times_plain(hits, y_s[...])
        z = placed[:, :DD] + placed[:, DD:] + table_ref[tile(i), :] + token * hidden
        z_s[tile(i), :] = z
        scaled, _ = norm_rows(z)
        n1 = low(scaled * gain1 + shift1)
        n1_s[tile(i), :] = n1
        q_s[tile(i), :] = low(times_plain(n1, wqkv_s[:, 0:DD]))
        k_s[tile(i), :] = low(times_plain(n1, wqkv_s[:, DD : 2 * DD]))
        v_s[tile(i), :] = low(times_plain(n1, wqkv_s[:, 2 * DD : 3 * DD]))

    first_half = lane_ids((1, 128)) < HEAD
    key_lanes = lane_ids((1, LANES)) < TUBES
    half_masks = [first_half, jnp.logical_not(first_half)]

    @pl.loop(0, 3)
    def _(p):
        lanes = pl.ds(pl.multiple_of(p * 128, 128), 128)

        @pl.loop(0, N_STEPS)
        def _(i):
            queries = q_s[tile(i), lanes]
            parts = []
            stat = lse_s[tile(i), :]
            for h in range(2):
                one = jnp.where(half_masks[h], queries, jnp.zeros_like(queries))
                scores = times_trans(one, k_s[:, lanes])
                scores = jnp.where(key_lanes, scores, -1e30)
                top = jnp.max(scores, axis=-1, keepdims=True) * (SCALE * LOG2E)
                weights = jnp.exp2(scores * (SCALE * LOG2E) - top)
                total = jnp.sum(weights, axis=-1, keepdims=True)
                parts.append(times_plain(low(weights), v_s[:, lanes]) / total)
                lse = top + jnp.log(total) * LOG2E
                stat = jnp.where(lane_ids((1, 128)) == 2 * p + h, lse, stat)
            lse_s[tile(i), :] = stat
            o_s[tile(i), lanes] = low(jnp.where(first_half, parts[0], parts[1]))

    lse_t[...] = lse_s[...].T

    @pl.loop(0, N_STEPS)
    def _(i):
        _, hidden = picks(i)
        attended = o_s[tile(i), :]
        x1 = z_s[tile(i), :] + times_trans(attended, wo_s[...])
        scaled2, inv2 = norm_rows(x1)
        n2 = low(scaled2 * gain2 + shift2)
        x2 = x1
        acts, slopes = [], []
        for r in range(2):
            u = times_plain(n2, w_ref[r, :, up0 : up0 + 768])
            act, slope = gelu_pair(u)
            act = low(act)
            acts.append(act)
            slopes.append(slope)
            x2 = x2 + times_trans(act, w_ref[r, :, dn0 : dn0 + 768])
        scaled_f, inv_f = norm_rows(x2)
        t = low(scaled_f * gain_f + shift_f)
        d_t = jnp.zeros((STEP_ROWS, DD), f32)
        for r in range(2):
            error = times_plain(t, w_ref[r, :, hd0 : hd0 + 768]) - pixel_ref[r, tile(i), :].astype(
                f32
            )
            error = error * hidden
            gv_s[7:8, :] += column_sum(error * error)
            d_pred = low(error * (2.0 / PIX))
            ghd_s[r] += trans_times(t, d_pred)
            d_t = d_t + times_trans(d_pred, w_ref[r, :, hd0 : hd0 + 768])
        gv_s[4:5, 0:DD] += column_sum(d_t * scaled_f)
        gv_s[5:6, 0:DD] += column_sum(d_t)
        d_x2 = norm_rows_back(d_t, scaled_f, inv_f, gain_f)
        d_low = low(d_x2)
        d_n2 = jnp.zeros((STEP_ROWS, DD), f32)
        for r in range(2):
            gdn_s[r] += trans_times(d_low, acts[r])
            d_u = low(times_plain(d_low, w_ref[r, :, dn0 : dn0 + 768]) * slopes[r])
            gup_s[r] += trans_times(n2, d_u)
            d_n2 = d_n2 + times_trans(d_u, w_ref[r, :, up0 : up0 + 768])
        gv_s[2:3, 0:DD] += column_sum(d_n2 * scaled2)
        gv_s[3:4, 0:DD] += column_sum(d_n2)
        d_x1 = d_x2 + norm_rows_back(d_n2, scaled2, inv2, gain2)
        dx_s[tile(i), :] = d_x1
        d_low = low(d_x1)
        go_s[...] += trans_times(d_low, attended)
        d_o = low(times_plain(d_low, wo_s[...]))
        do_s[tile(i), :] = d_o
        both = d_o.astype(f32) * attended.astype(f32)
        stat = jnp.zeros((STEP_ROWS, 128), f32)
        for p in range(3):
            pair = both[:, 128 * p : 128 * (p + 1)]
            for h in range(2):
                one = jnp.sum(jnp.where(half_masks[h], pair, 0.0), axis=-1, keepdims=True)
                stat = jnp.where(lane_ids((1, 128)) == 2 * p + h, one, stat)
        delta_s[tile(i), :] = stat

    delta_t[...] = delta_s[...].T

    @pl.loop(0, 3)
    def _(p):
        lanes = pl.ds(pl.multiple_of(p * 128, 128), 128)
        dqt_s[...] = jnp.zeros(dqt_s.shape, f32)

        @pl.loop(0, N_KEYS)
        def _(j):
            rows = pl.ds(pl.multiple_of(j * KEY_ROWS, KEY_ROWS), KEY_ROWS)
            keys = k_s[rows, lanes]
            values = v_s[rows, lanes]
            bias = bias_s[rows, 0:1]
            d_keys, d_values = [], []
            for h in range(2):
                key_one = jnp.where(half_masks[h], keys, jnp.zeros_like(keys))
                value_one = jnp.where(half_masks[h], values, jnp.zeros_like(values))
                lse = lse_t[pl.ds(2 * p + h, 1), :]
                delta = delta_t[pl.ds(2 * p + h, 1), :]
                scores = times_trans(key_one, q_s[:, lanes])
                soft = jnp.exp2((scores * (SCALE * LOG2E) + bias) - lse)
                d_soft = times_trans(value_one, do_s[:, lanes])
                d_scores = low(soft * (d_soft - delta))
                d_values.append(times_plain(low(soft), do_s[:, lanes]))
                d_keys.append(times_plain(d_scores, q_s[:, lanes]))
                dqt_s[...] += trans_times(key_one, d_scores)
            k_out = pl.ds(pl.multiple_of(DD + p * 128, 128), 128)
            v_out = pl.ds(pl.multiple_of(2 * DD + p * 128, 128), 128)
            dqkv_s[rows, k_out] = low(jnp.where(first_half, d_keys[0], d_keys[1]) * SCALE)
            dqkv_s[rows, v_out] = low(jnp.where(first_half, d_values[0], d_values[1]))

        dqkv_s[:, lanes] = low(dqt_s[...].T * SCALE)

    @pl.loop(0, N_STEPS)
    def _(i):
        hits, hidden = picks(i)
        d_qkv = dqkv_s[tile(i), :]
        gqkv_s[...] += trans_times(n1_s[tile(i), :], d_qkv)
        d_n1 = times_trans(d_qkv, wqkv_s[...])
        scaled1, inv1 = norm_rows(z_s[tile(i), :])
        gv_s[0:1, 0:DD] += column_sum(d_n1 * scaled1)
        gv_s[1:2, 0:DD] += column_sum(d_n1)
        d_z = dx_s[tile(i), :] + norm_rows_back(d_n1, scaled1, inv1, gain1)
        gv_s[6:7, 0:DD] += column_sum(d_z * hidden)
        gy_s[...] += trans_times(hits, low(d_z))

    d_y = low(gy_s[...])
    for r in range(2):
        grad_ref[r, :, ed0 : ed0 + DD] = low(trans_times(d_y, feat_ref[:, r * DD : (r + 1) * DD]))
        gfeat_ref[:, r * DD : (r + 1) * DD] = low(times_plain(d_y, w_ref[r, :, ed0 : ed0 + DD]))
        for part in range(3):
            grad_ref[r, :, part * half : (part + 1) * half] = low(
                gqkv_s[:, part * DD + r * half : part * DD + (r + 1) * half]
            )
        grad_ref[r, :, 3 * half : 4 * half] = low(go_s[:, r * half : (r + 1) * half])
        grad_ref[r, :, up0 : up0 + 768] = low(gup_s[r])
        grad_ref[r, :, dn0 : dn0 + 768] = low(gdn_s[r])
        grad_ref[r, :, hd0 : hd0 + 768] = low(ghd_s[r])
    gvec_ref[...] = gv_s[:, 0:DD]
    loss_ref[...] = jnp.zeros((8, 128), f32) + jnp.sum(gv_s[7:8, :]) / PIX


def run_decoder(seen, feat, pixels, table, weights, vectors):
    bf, f32 = jnp.bfloat16, jnp.float32
    vmem = pl.BlockSpec(memory_space=pltpu.VMEM)
    return pl.pallas_call(
        decoder_body,
        out_shape=(
            jax.ShapeDtypeStruct((8, 128), f32),
            jax.ShapeDtypeStruct((2, DD, 3456), bf),
            jax.ShapeDtypeStruct((8, DD), f32),
            jax.ShapeDtypeStruct((128, D), bf),
        ),
        in_specs=[vmem] * 6,
        out_specs=(vmem,) * 4,
        scratch_shapes=[
            pltpu.VMEM((ROWS, DD), f32),
            pltpu.VMEM((ROWS, DD), bf),
            pltpu.VMEM((LANES, DD), bf),
            pltpu.VMEM((LANES, DD), bf),
            pltpu.VMEM((LANES, DD), bf),
            pltpu.VMEM((ROWS, DD), bf),
            pltpu.VMEM((LANES, DD), bf),
            pltpu.VMEM((ROWS, DD), f32),
            pltpu.VMEM((LANES, 3 * DD), bf),
            pltpu.VMEM((128, LANES), f32),
            pltpu.VMEM((LANES, 128), f32),
            pltpu.VMEM((LANES, 128), f32),
            pltpu.VMEM((128, LANES), f32),
            pltpu.VMEM((128, LANES), f32),
            pltpu.VMEM((LANES, 128), f32),
            pltpu.VMEM((DD, 3 * DD), bf),
            pltpu.VMEM((DD, DD), bf),
            pltpu.VMEM((128, 2 * DD), bf),
            pltpu.VMEM((DD, 3 * DD), f32),
            pltpu.VMEM((DD, DD), f32),
            pltpu.VMEM((2, DD, 768), f32),
            pltpu.VMEM((2, DD, 768), f32),
            pltpu.VMEM((2, DD, 768), f32),
            pltpu.VMEM((128, DD), f32),
            pltpu.VMEM((8, 768), f32),
        ],
        compiler_params=pltpu.CompilerParams(vmem_limit_bytes=62 * MIB),
        cost_estimate=pl.CostEstimate(
            flops=30 * 10**9, bytes_accessed=20 * 10**6, transcendentals=20 * 10**6
        ),
        name="decoder",
    )(seen, feat, pixels, table, weights, vectors)


def swap_rows(values):
    return lax.ppermute(values, "row", [(0, 1), (1, 0)])


def pair_total(partial_value):
    mine = low(partial_value)
    return mine.astype(jnp.float32) + swap_rows(mine).astype(jnp.float32)


def head_order(matrix, heads, width):
    lead = matrix.shape[:-1]
    cut = matrix[..., :width].reshape(lead + (heads, 3, HEAD))
    cut = jnp.swapaxes(cut, -3, -2).reshape(lead + (width,))
    return jnp.concatenate([cut, matrix[..., width:]], axis=-1)


def head_order_back(matrix, heads, width):
    lead = matrix.shape[:-1]
    cut = matrix[..., :width].reshape(lead + (3, heads, HEAD))
    cut = jnp.swapaxes(cut, -3, -2).reshape(lead + (width,))
    return jnp.concatenate([cut, matrix[..., width:]], axis=-1)


def sine_table(length, width):
    column = np.arange(width)
    freq = np.exp(-math.log(10000.0) * (2.0 * (column // 2)) / width)
    angle = np.arange(length)[:, None] * freq
    table = np.where(column % 2 == 0, np.sin(angle), np.cos(angle))
    return np.pad(table, ((0, ROWS - length), (0, 0))).astype(np.float32)


def local(
    patches,
    visible,
    masked,
    enc_layers,
    enc_first,
    enc_second,
    embed,
    embed_first,
    embed_second,
    dec_mats,
    dec_first,
    dec_second,
    enc_vec,
    enc_vec_first,
    enc_vec_second,
    dec_vec,
    dec_vec_first,
    dec_vec_second,
):
    f32 = jnp.float32
    group = ("clip", "col")
    row_here = lax.axis_index("row")
    heads_here = HEADS // 2
    embed_here = lax.all_gather(low(embed), group, axis=1, tiled=True)[0]
    enc_full = [
        lax.all_gather(low(enc_layers[layer_at, 0]), group, axis=0, tiled=True)
        for layer_at in range(LAYERS)
    ]
    shard_rows = dec_mats.shape[1]
    dec_full = lax.all_gather(
        low(head_order(dec_mats[0], DHEADS // 2, 3 * DD // 2)), ("row", "clip", "col"), axis=0, tiled=True
    ).reshape(2, DD, -1)
    vectors = jnp.concatenate([enc_vec.reshape(-1), dec_vec.reshape(-1)])
    vectors = lax.all_gather(low(vectors), group, axis=0, tiled=False).astype(f32)
    cut = enc_vec.size
    enc_gains = jnp.swapaxes(vectors[:, :cut].reshape(-1, *enc_vec.shape), 0, 1).reshape(-1, D)
    dec_gains = jnp.swapaxes(vectors[:, cut:].reshape(-1, *dec_vec.shape), 0, 1).reshape(-1, DD)
    enc_widths = (3 * D // 2, D // 2, FF // 2, FF // 2)
    enc_weights = [split_columns(enc_full[layer_at], enc_widths) for layer_at in range(LAYERS)]

    pixels = patches[:, 0]
    seen = visible[:, 0]
    pick_seen = (seen[..., None] == jnp.arange(TUBES)).astype(jnp.bfloat16)
    seen_pixels = jnp.einsum(
        "cvt,ctp->cvp", pick_seen, pixels, preferred_element_type=f32
    ).astype(jnp.bfloat16)
    seen_pixels = seen_pixels.reshape(MICRO * VIS, -1)
    padded = jnp.pad(pixels, ((0, 0), (0, ROWS - TUBES), (0, 0)))
    own = lax.dynamic_index_in_dim(padded, row_here, 0, keepdims=False)
    other = swap_rows(lax.dynamic_index_in_dim(padded, 1 - row_here, 0, keepdims=False))
    pixel_pair = jnp.where(row_here == 0, jnp.stack([own, other]), jnp.stack([other, own]))

    resid = pair_total(times_trans(seen_pixels, embed_here)) + position_table(seen, D).reshape(-1, D)
    enc_kept = []
    for layer_at in range(LAYERS):
        resid, kept = layer_forward(
            resid,
            enc_weights[layer_at],
            enc_gains[4 * layer_at : 4 * layer_at + 4],
            MICRO,
            VIS,
            heads_here,
        )
        enc_kept.append(kept)
    normed_fin, scaled_fin, inv_fin = normalize(
        resid, enc_gains[4 * LAYERS], enc_gains[4 * LAYERS + 1]
    )
    feat = lax.dynamic_index_in_dim(normed_fin.reshape(MICRO, VIS, D), row_here, 0, keepdims=False)
    feat = jnp.pad(feat, ((0, 128 - VIS), (0, 0)))
    seen_here = lax.dynamic_index_in_dim(seen, row_here, 0, keepdims=True)
    seen_here = jnp.pad(seen_here, ((0, 7), (0, 128 - VIS)), constant_values=-1)
    loss_block, dec_grads, dec_grad_vec, grad_feat = run_decoder(
        seen_here, feat, pixel_pair, jnp.asarray(sine_table(TUBES, DD)), dec_full, dec_gains
    )
    loss_part = loss_block[0, 0]
    dec_total = lax.psum_scatter(
        dec_grads.reshape(-1, dec_grads.shape[-1]), ("row", "clip", "col"), scatter_dimension=0, tiled=True
    ).astype(f32)
    dec_total = head_order_back(dec_total, DHEADS // 2, 3 * DD // 2)[None]
    grad_feats = lax.all_gather(grad_feat[:VIS], "row", axis=0, tiled=True).astype(f32)
    grad_resid, gain_fin, shift_fin = normalize_back(
        grad_feats, scaled_fin, inv_fin, enc_gains[4 * LAYERS]
    )
    enc_grad_mats = [None] * LAYERS
    enc_grad_vectors = [None] * LAYERS
    for layer_at in reversed(range(LAYERS)):
        grad_resid, enc_grad_mats[layer_at], enc_grad_vectors[layer_at] = layer_backward(
            grad_resid,
            enc_weights[layer_at],
            enc_gains[4 * layer_at : 4 * layer_at + 4],
            enc_kept[layer_at],
            MICRO,
            VIS,
            heads_here,
        )
    grad_embed = trans_times(grad_resid.astype(jnp.bfloat16), seen_pixels)
    enc_total = jnp.stack(
        [
            lax.psum_scatter(low(mats), group, scatter_dimension=0, tiled=True).astype(f32)
            for mats in enc_grad_mats
        ]
    )[:, None]
    embed_total = lax.psum_scatter(low(grad_embed), group, scatter_dimension=0, tiled=True).astype(f32)[None]
    enc_grad_vec = jnp.concatenate(enc_grad_vectors + [jnp.stack([gain_fin, shift_fin])], axis=0)
    vec_grads = jnp.concatenate([0.5 * enc_grad_vec.reshape(-1), dec_grad_vec[:7].reshape(-1), loss_part[None]])
    vec_total = lax.psum(vec_grads, ("row", "clip", "col"))
    loss_total = vec_total[-1]
    shard = lax.axis_index("clip") * lax.axis_size("col") + lax.axis_index("col")
    enc_vec_total = vec_total[: (4 * LAYERS + 2) * D].reshape(-1, D)
    dec_vec_total = vec_total[(4 * LAYERS + 2) * D : -1].reshape(-1, DD)
    square_total = lax.psum(
        sum(jnp.sum(g * g) for g in (enc_total, embed_total, dec_total)), ("row", "clip", "col")
    ) + jnp.sum(enc_vec_total**2) + jnp.sum(dec_vec_total**2)
    grad_norm = jnp.sqrt(square_total)
    factor = jnp.minimum(1.0, CLIP_MAX / (grad_norm + 1e-06))
    enc_w, dec_w = enc_vec.shape[1], dec_vec.shape[1]
    total_grads = (
        enc_total,
        embed_total,
        dec_total,
        lax.dynamic_slice_in_dim(enc_vec_total, shard * enc_w, enc_w, 1),
        lax.dynamic_slice_in_dim(dec_vec_total, shard * dec_w, dec_w, 1),
    )
    masters = (enc_layers, embed, dec_mats, enc_vec, dec_vec)
    states = (
        (enc_first, enc_second),
        (embed_first, embed_second),
        (dec_first, dec_second),
        (enc_vec_first, enc_vec_second),
        (dec_vec_first, dec_vec_second),
    )
    decays = (DECAY, DECAY, DECAY, 0.0, 0.0)
    rates = (RATE, RATE, RATE, VEC_RATE, VEC_RATE)
    results = []
    for master, pair, piece_grad, decay_rate, step_rate in zip(
        masters, states, total_grads, decays, rates
    ):
        results.extend(
            adam_update(master, pair[0], pair[1], piece_grad * factor, decay_rate, step_rate)
        )
    return (loss_total, grad_norm, *results)


def solution(mesh):
    in_specs = (
        P(None, ("clip", "col"), None, "row"),
        P(None, ("clip", "col"), None),
        P(None, ("clip", "col"), None),
        P(None, "row", ("clip", "col"), None),
        P(None, "row", ("clip", "col"), None),
        P(None, "row", ("clip", "col"), None),
        P("row", ("clip", "col"), None),
        P("row", ("clip", "col"), None),
        P("row", ("clip", "col"), None),
        P("row", ("clip", "col"), None),
        P("row", ("clip", "col"), None),
        P("row", ("clip", "col"), None),
        P(None, ("clip", "col")),
        P(None, ("clip", "col")),
        P(None, ("clip", "col")),
        P(None, ("clip", "col")),
        P(None, ("clip", "col")),
        P(None, ("clip", "col")),
    )
    out_specs = (
        P(),
        P(),
        P(None, "row", ("clip", "col"), None),
        P(None, "row", ("clip", "col"), None),
        P(None, "row", ("clip", "col"), None),
        P("row", ("clip", "col"), None),
        P("row", ("clip", "col"), None),
        P("row", ("clip", "col"), None),
        P("row", ("clip", "col"), None),
        P("row", ("clip", "col"), None),
        P("row", ("clip", "col"), None),
        P(None, ("clip", "col")),
        P(None, ("clip", "col")),
        P(None, ("clip", "col")),
        P(None, ("clip", "col")),
        P(None, ("clip", "col")),
        P(None, ("clip", "col")),
    )
    return jax.shard_map(local, mesh=mesh, in_specs=in_specs, out_specs=out_specs, check_vma=False)
```

```python
import functools
import math

import jax
import jax.numpy as jnp
import numpy as np
from jax import lax
from jax.experimental import pallas as pl
from jax.experimental.pallas import tpu as pltpu
from jax.sharding import PartitionSpec as P

D = 768
HEADS = 12
HEAD = 64
FF = 3072
DD = 384
DHEADS = 6
DFF = 1536
PIX = 1536
TUBES = 1176
VIS = 118
LAYERS = 2
MICRO = 2
STEP = 10
MASKED = 1058


EPS_NORM = 1e-06
CLIP_MAX = 1.0
BETA_ONE = 0.9
BETA_TWO = 0.999
RATE = 0.06
VEC_RATE = 0.2
DECAY = 0.05
EPS_ADAM = 1e-08


def times_plain(left, right):
    return jnp.dot(left, right, preferred_element_type=jnp.float32)


def times_trans(left, right):
    return lax.dot_general(
        left, right, (((1,), (1,)), ((), ())), preferred_element_type=jnp.float32
    )


def trans_times(left, right):
    return lax.dot_general(
        left, right, (((0,), (0,)), ((), ())), preferred_element_type=jnp.float32
    )


def gelu_pair(values):
    cumul = 0.5 * (1.0 + lax.erf(values * 0.7071067811865476))
    density = jnp.exp(-0.5 * values * values) * 0.3989422804014327
    return (values * cumul, cumul + values * density)


def adam_update(master, first, second, grad_clip, decay_rate, step_rate):
    first_new = BETA_ONE * first + (1.0 - BETA_ONE) * grad_clip
    second_new = BETA_TWO * second + (1.0 - BETA_TWO) * grad_clip * grad_clip
    first_hat = first_new / (1.0 - BETA_ONE**STEP)
    second_hat = second_new / (1.0 - BETA_TWO**STEP)
    master_new = master - step_rate * (
        first_hat / (jnp.sqrt(second_hat) + EPS_ADAM) + decay_rate * master
    )
    return (master_new, first_new, second_new)


ROWS = 1200
LANES = 1280
STEP_ROWS = 240
N_STEPS = ROWS // STEP_ROWS
KEY_ROWS = 256
N_KEYS = LANES // KEY_ROWS
LOG2E = 1.4426950408889634
SCALE = HEAD ** (-0.5)
MIB = 1 << 20


def low(values):
    return values.astype(jnp.bfloat16)


def lane_ids(shape):
    return lax.broadcasted_iota(jnp.int32, shape, len(shape) - 1)


def row_ids(shape):
    return lax.broadcasted_iota(jnp.int32, shape, 0)


def norm_rows(rows):
    average = jnp.mean(rows, axis=-1, keepdims=True)
    centred = rows - average
    inv_dev = lax.rsqrt(jnp.mean(centred * centred, axis=-1, keepdims=True) + EPS_NORM)
    return centred * inv_dev, inv_dev


def norm_rows_back(grad_out, scaled, inv_dev, gain_row):
    inner = grad_out * gain_row
    return inv_dev * (
        inner
        - jnp.mean(inner, axis=-1, keepdims=True)
        - scaled * jnp.mean(inner * scaled, axis=-1, keepdims=True)
    )


def column_sum(values):
    return jnp.sum(values, axis=0, keepdims=True)


def decoder_body(
    seen_ref,
    feat_ref,
    pixel_ref,
    table_ref,
    w_ref,
    vec_ref,
    loss_ref,
    grad_ref,
    gvec_ref,
    gfeat_ref,
    z_s,
    n1_s,
    q_s,
    k_s,
    v_s,
    o_s,
    do_s,
    dx_s,
    dqkv_s,
    dqt_s,
    lse_s,
    delta_s,
    lse_t,
    delta_t,
    bias_s,
    wqkv_s,
    wo_s,
    y_s,
    gqkv_s,
    go_s,
    gup_s,
    gdn_s,
    ghd_s,
    gy_s,
    gv_s,
):
    bf, f32 = jnp.bfloat16, jnp.float32
    half = 3 * HEAD
    up0, dn0, hd0, ed0 = 768, 1536, 2304, 3072
    vec = vec_ref[...]
    gain1, shift1, gain2, shift2, gain_f, shift_f, token = [vec[i : i + 1] for i in range(7)]

    for part in range(3):
        for r in range(2):
            wqkv_s[:, part * DD + r * half : part * DD + (r + 1) * half] = w_ref[
                r, :, part * half : (part + 1) * half
            ]
    for r in range(2):
        wo_s[:, r * half : (r + 1) * half] = w_ref[r, :, 3 * half : 4 * half]
    for ref in (q_s, k_s, v_s, do_s):
        ref[ROWS:LANES, :] = jnp.zeros((LANES - ROWS, DD), bf)
    lse_s[ROWS:LANES, :] = jnp.zeros((LANES - ROWS, 128), f32)
    delta_s[ROWS:LANES, :] = jnp.zeros((LANES - ROWS, 128), f32)
    bias_s[...] = jnp.where(row_ids((LANES, 128)) < TUBES, 0.0, -1e30)
    for ref in (gqkv_s, go_s, gup_s, gdn_s, ghd_s, gy_s, gv_s):
        ref[...] = jnp.zeros(ref.shape, f32)
    for r in range(2):
        y_s[:, r * DD : (r + 1) * DD] = low(
            times_trans(feat_ref[:, r * DD : (r + 1) * DD], w_ref[r, :, ed0 : ed0 + DD])
        )
    seen = seen_ref[0:1, :]

    def tile(i):
        return pl.ds(pl.multiple_of(i * STEP_ROWS, STEP_ROWS), STEP_ROWS)

    def picks(i):
        ids = row_ids((STEP_ROWS, 128)) + i * STEP_ROWS
        hits = ids == seen
        taken = jnp.sum(hits.astype(f32), axis=-1, keepdims=True)
        valid = (row_ids((STEP_ROWS, 1)) + i * STEP_ROWS < TUBES).astype(f32)
        return hits.astype(bf), valid - taken

    @pl.loop(0, N_STEPS)
    def _(i):
        hits, hidden = picks(i)
        placed = times_plain(hits, y_s[...])
        z = placed[:, :DD] + placed[:, DD:] + table_ref[tile(i), :] + token * hidden
        z_s[tile(i), :] = z
        scaled, _ = norm_rows(z)
        n1 = low(scaled * gain1 + shift1)
        n1_s[tile(i), :] = n1
        q_s[tile(i), :] = low(times_plain(n1, wqkv_s[:, 0:DD]))
        k_s[tile(i), :] = low(times_plain(n1, wqkv_s[:, DD : 2 * DD]))
        v_s[tile(i), :] = low(times_plain(n1, wqkv_s[:, 2 * DD : 3 * DD]))

    first_half = lane_ids((1, 128)) < HEAD
    key_lanes = lane_ids((1, LANES)) < TUBES
    half_masks = [first_half, jnp.logical_not(first_half)]

    @pl.loop(0, 3)
    def _(p):
        lanes = pl.ds(pl.multiple_of(p * 128, 128), 128)

        @pl.loop(0, N_STEPS)
        def _(i):
            queries = q_s[tile(i), lanes]
            parts = []
            stat = lse_s[tile(i), :]
            for h in range(2):
                one = jnp.where(half_masks[h], queries, jnp.zeros_like(queries))
                scores = times_trans(one, k_s[:, lanes])
                scores = jnp.where(key_lanes, scores, -1e30)
                top = jnp.max(scores, axis=-1, keepdims=True) * (SCALE * LOG2E)
                weights = jnp.exp2(scores * (SCALE * LOG2E) - top)
                total = jnp.sum(weights, axis=-1, keepdims=True)
                parts.append(times_plain(low(weights), v_s[:, lanes]) / total)
                lse = top + jnp.log(total) * LOG2E
                stat = jnp.where(lane_ids((1, 128)) == 2 * p + h, lse, stat)
            lse_s[tile(i), :] = stat
            o_s[tile(i), lanes] = low(jnp.where(first_half, parts[0], parts[1]))

    lse_t[...] = lse_s[...].T

    @pl.loop(0, N_STEPS)
    def _(i):
        _, hidden = picks(i)
        attended = o_s[tile(i), :]
        x1 = z_s[tile(i), :] + times_trans(attended, wo_s[...])
        scaled2, inv2 = norm_rows(x1)
        n2 = low(scaled2 * gain2 + shift2)
        x2 = x1
        acts, slopes = [], []
        for r in range(2):
            u = times_plain(n2, w_ref[r, :, up0 : up0 + 768])
            act, slope = gelu_pair(u)
            act = low(act)
            acts.append(act)
            slopes.append(slope)
            x2 = x2 + times_trans(act, w_ref[r, :, dn0 : dn0 + 768])
        scaled_f, inv_f = norm_rows(x2)
        t = low(scaled_f * gain_f + shift_f)
        d_t = jnp.zeros((STEP_ROWS, DD), f32)
        for r in range(2):
            error = times_plain(t, w_ref[r, :, hd0 : hd0 + 768]) - pixel_ref[r, tile(i), :].astype(
                f32
            )
            error = error * hidden
            gv_s[7:8, :] += column_sum(error * error)
            d_pred = low(error * (2.0 / PIX))
            ghd_s[r] += trans_times(t, d_pred)
            d_t = d_t + times_trans(d_pred, w_ref[r, :, hd0 : hd0 + 768])
        gv_s[4:5, 0:DD] += column_sum(d_t * scaled_f)
        gv_s[5:6, 0:DD] += column_sum(d_t)
        d_x2 = norm_rows_back(d_t, scaled_f, inv_f, gain_f)
        d_low = low(d_x2)
        d_n2 = jnp.zeros((STEP_ROWS, DD), f32)
        for r in range(2):
            gdn_s[r] += trans_times(d_low, acts[r])
            d_u = low(times_plain(d_low, w_ref[r, :, dn0 : dn0 + 768]) * slopes[r])
            gup_s[r] += trans_times(n2, d_u)
            d_n2 = d_n2 + times_trans(d_u, w_ref[r, :, up0 : up0 + 768])
        gv_s[2:3, 0:DD] += column_sum(d_n2 * scaled2)
        gv_s[3:4, 0:DD] += column_sum(d_n2)
        d_x1 = d_x2 + norm_rows_back(d_n2, scaled2, inv2, gain2)
        dx_s[tile(i), :] = d_x1
        d_low = low(d_x1)
        go_s[...] += trans_times(d_low, attended)
        d_o = low(times_plain(d_low, wo_s[...]))
        do_s[tile(i), :] = d_o
        both = d_o.astype(f32) * attended.astype(f32)
        stat = jnp.zeros((STEP_ROWS, 128), f32)
        for p in range(3):
            pair = both[:, 128 * p : 128 * (p + 1)]
            for h in range(2):
                one = jnp.sum(jnp.where(half_masks[h], pair, 0.0), axis=-1, keepdims=True)
                stat = jnp.where(lane_ids((1, 128)) == 2 * p + h, one, stat)
        delta_s[tile(i), :] = stat

    delta_t[...] = delta_s[...].T

    @pl.loop(0, 3)
    def _(p):
        lanes = pl.ds(pl.multiple_of(p * 128, 128), 128)
        dqt_s[...] = jnp.zeros(dqt_s.shape, f32)

        @pl.loop(0, N_KEYS)
        def _(j):
            rows = pl.ds(pl.multiple_of(j * KEY_ROWS, KEY_ROWS), KEY_ROWS)
            keys = k_s[rows, lanes]
            values = v_s[rows, lanes]
            bias = bias_s[rows, 0:1]
            d_keys, d_values = [], []
            for h in range(2):
                key_one = jnp.where(half_masks[h], keys, jnp.zeros_like(keys))
                value_one = jnp.where(half_masks[h], values, jnp.zeros_like(values))
                lse = lse_t[pl.ds(2 * p + h, 1), :]
                delta = delta_t[pl.ds(2 * p + h, 1), :]
                scores = times_trans(key_one, q_s[:, lanes])
                soft = jnp.exp2((scores * (SCALE * LOG2E) + bias) - lse)
                d_soft = times_trans(value_one, do_s[:, lanes])
                d_scores = low(soft * (d_soft - delta))
                d_values.append(times_plain(low(soft), do_s[:, lanes]))
                d_keys.append(times_plain(d_scores, q_s[:, lanes]))
                dqt_s[...] += trans_times(key_one, d_scores)
            k_out = pl.ds(pl.multiple_of(DD + p * 128, 128), 128)
            v_out = pl.ds(pl.multiple_of(2 * DD + p * 128, 128), 128)
            dqkv_s[rows, k_out] = low(jnp.where(first_half, d_keys[0], d_keys[1]) * SCALE)
            dqkv_s[rows, v_out] = low(jnp.where(first_half, d_values[0], d_values[1]))

        dqkv_s[:, lanes] = low(dqt_s[...].T * SCALE)

    @pl.loop(0, N_STEPS)
    def _(i):
        hits, hidden = picks(i)
        d_qkv = dqkv_s[tile(i), :]
        gqkv_s[...] += trans_times(n1_s[tile(i), :], d_qkv)
        d_n1 = times_trans(d_qkv, wqkv_s[...])
        scaled1, inv1 = norm_rows(z_s[tile(i), :])
        gv_s[0:1, 0:DD] += column_sum(d_n1 * scaled1)
        gv_s[1:2, 0:DD] += column_sum(d_n1)
        d_z = dx_s[tile(i), :] + norm_rows_back(d_n1, scaled1, inv1, gain1)
        gv_s[6:7, 0:DD] += column_sum(d_z * hidden)
        gy_s[...] += trans_times(hits, low(d_z))

    d_y = low(gy_s[...])
    for r in range(2):
        grad_ref[r, :, ed0 : ed0 + DD] = low(trans_times(d_y, feat_ref[:, r * DD : (r + 1) * DD]))
        gfeat_ref[:, r * DD : (r + 1) * DD] = low(times_plain(d_y, w_ref[r, :, ed0 : ed0 + DD]))
        for part in range(3):
            grad_ref[r, :, part * half : (part + 1) * half] = low(
                gqkv_s[:, part * DD + r * half : part * DD + (r + 1) * half]
            )
        grad_ref[r, :, 3 * half : 4 * half] = low(go_s[:, r * half : (r + 1) * half])
        grad_ref[r, :, up0 : up0 + 768] = low(gup_s[r])
        grad_ref[r, :, dn0 : dn0 + 768] = low(gdn_s[r])
        grad_ref[r, :, hd0 : hd0 + 768] = low(ghd_s[r])
    gvec_ref[...] = gv_s[:, 0:DD]
    loss_ref[...] = jnp.zeros((8, 128), f32) + jnp.sum(gv_s[7:8, :]) / PIX


def run_decoder(seen, feat, pixels, table, weights, vectors):
    bf, f32 = jnp.bfloat16, jnp.float32
    vmem = pl.BlockSpec(memory_space=pltpu.VMEM)
    return pl.pallas_call(
        decoder_body,
        out_shape=(
            jax.ShapeDtypeStruct((8, 128), f32),
            jax.ShapeDtypeStruct((2, DD, 3456), bf),
            jax.ShapeDtypeStruct((8, DD), f32),
            jax.ShapeDtypeStruct((128, D), bf),
        ),
        in_specs=[vmem] * 6,
        out_specs=(vmem,) * 4,
        scratch_shapes=[
            pltpu.VMEM((ROWS, DD), f32),
            pltpu.VMEM((ROWS, DD), bf),
            pltpu.VMEM((LANES, DD), bf),
            pltpu.VMEM((LANES, DD), bf),
            pltpu.VMEM((LANES, DD), bf),
            pltpu.VMEM((ROWS, DD), bf),
            pltpu.VMEM((LANES, DD), bf),
            pltpu.VMEM((ROWS, DD), f32),
            pltpu.VMEM((LANES, 3 * DD), bf),
            pltpu.VMEM((128, LANES), f32),
            pltpu.VMEM((LANES, 128), f32),
            pltpu.VMEM((LANES, 128), f32),
            pltpu.VMEM((128, LANES), f32),
            pltpu.VMEM((128, LANES), f32),
            pltpu.VMEM((LANES, 128), f32),
            pltpu.VMEM((DD, 3 * DD), bf),
            pltpu.VMEM((DD, DD), bf),
            pltpu.VMEM((128, 2 * DD), bf),
            pltpu.VMEM((DD, 3 * DD), f32),
            pltpu.VMEM((DD, DD), f32),
            pltpu.VMEM((2, DD, 768), f32),
            pltpu.VMEM((2, DD, 768), f32),
            pltpu.VMEM((2, DD, 768), f32),
            pltpu.VMEM((128, DD), f32),
            pltpu.VMEM((8, 768), f32),
        ],
        compiler_params=pltpu.CompilerParams(vmem_limit_bytes=62 * MIB),
        cost_estimate=pl.CostEstimate(
            flops=30 * 10**9, bytes_accessed=20 * 10**6, transcendentals=20 * 10**6
        ),
        name="decoder",
    )(seen, feat, pixels, table, weights, vectors)


PAIR = 256
HALF_D = D // 2
QKV_W = 3 * D // 2
HID = FF // 2
A_COLS = QKV_W + D // 2
ENC_COLS = A_COLS + 2 * HID
UP_AT, DN_AT = A_COLS, A_COLS + HID
N_SHARDS = 16
SHARD = D // N_SHARDS
EMB_ROWS = SHARD + 16
MESH_IDS = pl.DeviceIdType.MESH
GATHERS = (
    (-1, 0, D),
    (0, 0, A_COLS),
    (0, A_COLS, 2 * HID),
    (1, 0, A_COLS),
    (1, A_COLS, 2 * HID),
)


def remote(src, dst, send_sem, recv_sem, device):
    return pltpu.make_async_remote_copy(
        src_ref=src,
        dst_ref=dst,
        send_sem=send_sem,
        recv_sem=recv_sem,
        device_id=device,
        device_id_type=MESH_IDS,
    )


class Place:
    def __init__(self):
        self.clip = lax.axis_index("clip")
        self.row = lax.axis_index("row")
        self.col = lax.axis_index("col")
        self.z = self.clip // 2
        self.x = self.clip % 2

    def z_mate(self, step):
        return (((self.z + step) % 4) * 2 + self.x, self.row, self.col)

    def x_mate(self):
        return (self.z * 2 + 1 - self.x, self.row, self.col)

    def core_mate(self):
        return (self.clip, self.row, 1 - self.col)

    def row_mate(self):
        return (self.clip, 1 - self.row, self.col)

    def mates(self, wide):
        near = [self.row_mate()]
        if wide:
            near += [self.core_mate(), self.x_mate()] + [self.z_mate(s) for s in (1, 2, 3)]
        return near


def shard_at(z, x, col):
    return (z * 2 + x) * 2 + col


def greet(mates):
    barrier = pltpu.get_barrier_semaphore()
    for mate in mates:
        pl.semaphore_signal(barrier, inc=1, device_id=mate, device_id_type=MESH_IDS)
    pl.semaphore_wait(barrier, len(mates))


class Gather:
    def __init__(self, place, mine, buffers, sems):
        self.at = place
        self.mine = mine
        self.buffers = buffers
        self.z_ss, self.z_rs, self.x_ss, self.x_rs, self.c_ss, self.c_rs = sems
        self.sent = []

    def spot(self, k, z, x, col):
        layer, start, width = GATHERS[k]
        rows = EMB_ROWS if layer < 0 else SHARD
        first = pl.multiple_of(shard_at(z, x, col) * rows, 16)
        if layer < 0:
            return self.buffers[0].at[pl.ds(first, rows), :]
        return self.buffers[1].at[layer, pl.ds(first, rows), pl.ds(start, width)]

    def own(self, k):
        layer, start, width = GATHERS[k]
        if layer < 0:
            return self.mine[0]
        return self.mine[1].at[layer, :, pl.ds(start, width)]

    def go(self, src, dst, ss, rs, device):
        copy = remote(src, dst, ss, rs, device)
        copy.start()
        self.sent.append(copy)

    def came(self, dst, ss, rs):
        remote(dst, dst, ss, rs, self.at.core_mate()).wait_recv()

    def begin(self, k):
        at = self.at
        src, dst = self.own(k), self.spot(k, at.z, at.x, at.col)
        for s in (1, 2, 3):
            self.go(src, dst, self.z_ss.at[k, s - 1], self.z_rs.at[k, s - 1], at.z_mate(s))
        self.go(src, dst, self.x_ss.at[k, 0], self.x_rs.at[k, 0], at.x_mate())
        self.go(src, dst, self.c_ss.at[k, 0], self.c_rs.at[k, 0], at.core_mate())

    def forward(self, k):
        at = self.at
        for s in (1, 2, 3):
            spot = self.spot(k, (at.z - s) % 4, at.x, at.col)
            self.came(spot, self.z_ss.at[k, s - 1], self.z_rs.at[k, s - 1])
            self.go(spot, spot, self.x_ss.at[k, s], self.x_rs.at[k, s], at.x_mate())
            self.go(spot, spot, self.c_ss.at[k, s], self.c_rs.at[k, s], at.core_mate())

    def across(self, k):
        at = self.at
        for s in range(4):
            spot = self.spot(k, (at.z - s) % 4, 1 - at.x, at.col)
            self.came(spot, self.x_ss.at[k, s], self.x_rs.at[k, s])
            self.go(spot, spot, self.c_ss.at[k, 4 + s], self.c_rs.at[k, 4 + s], at.core_mate())

    def finish(self, k):
        at = self.at
        for s in range(8):
            x = at.x if s < 4 else 1 - at.x
            spot = self.spot(k, (at.z - s % 4) % 4, x, 1 - at.col)
            self.came(spot, self.c_ss.at[k, s], self.c_rs.at[k, s])

    def drain(self):
        for copy in self.sent:
            copy.wait_send()


class Swap:
    def __init__(self, place, sent, got, send_sems, recv_sems):
        self.at, self.sent, self.got = place, sent, got
        self.ss, self.rs = send_sems, recv_sems
        self.copies = {}

    def start(self, i, value):
        self.sent[i] = low(value)
        copy = remote(
            self.sent.at[i], self.got.at[i], self.ss.at[i], self.rs.at[i], self.at.row_mate()
        )
        copy.start()
        self.copies[i] = copy

    def total(self, i):
        self.copies[i].wait_recv()
        return self.sent[i].astype(jnp.float32) + self.got[i].astype(jnp.float32)

    def drain(self):
        for copy in self.copies.values():
            copy.wait_send()


def half_lanes():
    first = lane_ids((1, 128)) < HEAD
    return [first, jnp.logical_not(first)]


def same_clip():
    a, b = row_ids((PAIR, PAIR)), lane_ids((PAIR, PAIR))
    return jnp.logical_and(a // 128 == b // 128, b % 128 < VIS)


def encoder_scores(queries, keys, allowed):
    scores = jnp.where(allowed, times_trans(queries, keys), -1e30)
    top = jnp.max(scores, axis=-1, keepdims=True) * (SCALE * LOG2E)
    weights = jnp.exp2(scores * (SCALE * LOG2E) - top)
    return weights, jnp.sum(weights, axis=-1, keepdims=True)


def encoder_attention(qkv_ref, out_ref):
    allowed = same_clip()
    halves = half_lanes()
    for p in range(3):
        q = qkv_ref[:, 128 * p : 128 * (p + 1)]
        k = qkv_ref[:, HALF_D + 128 * p : HALF_D + 128 * (p + 1)]
        v = qkv_ref[:, 2 * HALF_D + 128 * p : 2 * HALF_D + 128 * (p + 1)]
        parts = []
        for h in range(2):
            one = jnp.where(halves[h], q, jnp.zeros_like(q))
            weights, total = encoder_scores(one, k, allowed)
            parts.append(times_plain(low(weights), v) / total)
        out_ref[:, 128 * p : 128 * (p + 1)] = low(jnp.where(halves[0], parts[0], parts[1]))


def encoder_body(wide, *refs):
    f32 = jnp.float32
    if wide:
        seen_ref, pixel_ref, freq_ref, emb_in, enc_in = refs[:5]
        refs = refs[5:]
    else:
        seen_ref, pixel_ref, freq_ref, emb_full, w_s, gain_in = refs[:6]
        refs = refs[6:]
    feat_ref, x_ref, qkv_ref, o_ref, h_ref, slope_ref, px_ref = refs[:7]
    refs = refs[7:]
    if wide:
        gain_ref, dgain_ref, w_out, emb_s, w_s, embc_s = refs[:6]
        refs = refs[6:]
    sent_s, got_s, y_ss, y_rs = refs[:4]
    refs = refs[4:]
    place = Place()
    greet(place.mates(wide))
    swap = Swap(place, sent_s, got_s, y_ss, y_rs)
    if wide:
        gather = Gather(place, (emb_in, enc_in), (emb_s, w_s), refs[:6])
        keep_sem = refs[6]
        for k in (0, 1, 2):
            gather.begin(k)
        own = shard_at(place.z, place.x, place.col)
        emb_s[pl.ds(pl.multiple_of(own * EMB_ROWS, 16), EMB_ROWS), :] = emb_in[...]
        for layer in range(LAYERS):
            w_s[layer, pl.ds(pl.multiple_of(own * SHARD, 16), SHARD), :] = enc_in[layer]

    def step(name, k):
        if wide:
            getattr(gather, name)(k)

    odd = (lane_ids((1, D)) % 2).astype(f32) * (0.5 * math.pi)
    freq = freq_ref[0:1, :]
    places = []
    for m in range(MICRO):
        row = seen_ref[m : m + 1, :]
        hits = (row_ids((TUBES, 128)) == row).astype(jnp.bfloat16)
        px_ref[128 * m : 128 * (m + 1), :] = low(trans_times(hits, pixel_ref[m]))
        column = jnp.broadcast_to(row.astype(f32), (128, 128)).T[:, 0:1]
        places.append(jnp.sin(column * freq + odd))

    if wide:
        gather.forward(0)
        gather.across(0)
        gather.finish(0)
        for s in range(N_SHARDS):
            embc_s[SHARD * s : SHARD * (s + 1), :] = emb_s[EMB_ROWS * s : EMB_ROWS * s + SHARD, :]
            tail = emb_s[EMB_ROWS * s + SHARD : EMB_ROWS * (s + 1), 0:128].astype(f32)
            gain_ref[:, SHARD * s : SHARD * (s + 1)] = tail[:, 0:SHARD]
            dgain_ref[:, DD // 16 * s : DD // 16 * (s + 1)] = tail[0:8, SHARD : SHARD + DD // 16]
        emb_full, gain_in = embc_s, gain_ref
    swap.start(0, times_trans(px_ref[...], emb_full[...]))
    step("forward", 1)
    step("begin", 3)
    step("across", 1)
    x = swap.total(0) + jnp.concatenate(places, axis=0)
    for layer in range(LAYERS):
        gains = gain_in[4 * layer : 4 * layer + 4, :]
        x_ref[2 * layer] = x
        scaled, _ = norm_rows(x)
        n1 = low(scaled * gains[0:1] + gains[1:2])
        step("finish", 1 + 2 * layer)
        qkv_ref[layer] = low(times_plain(n1, w_s[layer, :, 0:QKV_W]))
        encoder_attention(qkv_ref.at[layer], o_ref.at[layer])
        swap.start(1 + 2 * layer, times_trans(o_ref[layer], w_s[layer, :, QKV_W:A_COLS]))
        step("forward", 2 + 2 * layer)
        if layer == 0:
            step("begin", 4)
        step("across", 2 + 2 * layer)
        x = x + swap.total(1 + 2 * layer)
        x_ref[2 * layer + 1] = x
        scaled, _ = norm_rows(x)
        n2 = low(scaled * gains[2:3] + gains[3:4])
        step("finish", 2 + 2 * layer)
        if wide:
            keep = pltpu.make_async_copy(w_s.at[layer], w_out.at[layer], keep_sem.at[layer])
            keep.start()
        act, slope = gelu_pair(times_plain(n2, w_s[layer, :, UP_AT:DN_AT]))
        act = low(act)
        h_ref[layer] = act
        slope_ref[layer] = slope
        swap.start(2 + 2 * layer, times_trans(act, w_s[layer, :, DN_AT:ENC_COLS]))
        if layer == 0:
            step("forward", 3)
            step("across", 3)
        x = x + swap.total(2 + 2 * layer)
    x_ref[2 * LAYERS] = x
    scaled, _ = norm_rows(x)
    gains = gain_in[4 * LAYERS : 4 * LAYERS + 2, :]
    feat = low(scaled * gains[0:1] + gains[1:2])
    feat_ref[...] = jnp.where(place.row == 0, feat[0:128], feat[128:256])
    swap.drain()
    if wide:
        gather.drain()
        for layer in range(LAYERS):
            pltpu.make_async_copy(w_s.at[layer], w_out.at[layer], keep_sem.at[layer]).wait()


def run_encoder(wide, *operands):
    bf, f32 = jnp.bfloat16, jnp.float32
    vmem = pl.BlockSpec(memory_space=pltpu.VMEM)
    dma = pltpu.SemaphoreType.DMA
    shape = jax.ShapeDtypeStruct
    n_swaps = 1 + 2 * LAYERS
    outs = [
        shape((128, D), bf),
        shape((2 * LAYERS + 1, PAIR, D), f32),
        shape((LAYERS, PAIR, QKV_W), bf),
        shape((LAYERS, PAIR, HALF_D), bf),
        shape((LAYERS, PAIR, HID), bf),
        shape((LAYERS, PAIR, HID), f32),
        shape((PAIR, D), bf),
    ]
    out_specs = [vmem] * len(outs)
    scratch = []
    if wide:
        outs += [shape((16, D), f32), shape((8, DD), f32), shape((LAYERS, D, ENC_COLS), bf)]
        out_specs += [vmem, vmem, pl.BlockSpec(memory_space=pl.ANY)]
        scratch += [
            pltpu.VMEM((N_SHARDS * EMB_ROWS, D), bf),
            pltpu.VMEM((LAYERS, D, ENC_COLS), bf),
            pltpu.VMEM((D, D), bf),
        ]
    scratch += [
        pltpu.VMEM((n_swaps, PAIR, D), bf),
        pltpu.VMEM((n_swaps, PAIR, D), bf),
        dma((n_swaps,)),
        dma((n_swaps,)),
    ]
    if wide:
        n = len(GATHERS)
        scratch += [dma((n, 3)), dma((n, 3)), dma((n, 4)), dma((n, 4)), dma((n, 8)), dma((n, 8))]
        scratch += [dma((LAYERS,))]
    return pl.pallas_call(
        functools.partial(encoder_body, wide),
        out_shape=tuple(outs),
        in_specs=[vmem] * len(operands),
        out_specs=tuple(out_specs),
        scratch_shapes=scratch,
        compiler_params=pltpu.CompilerParams(
            collective_id=1, has_side_effects=True, vmem_limit_bytes=60 * MIB
        ),
        cost_estimate=pl.CostEstimate(
            flops=10 * 10**9, bytes_accessed=60 * 10**6, transcendentals=10**6
        ),
        name="encoder",
    )(*operands)


SUMS = (
    ("dn1", HID),
    ("up1", HID),
    ("at1", A_COLS),
    ("dn0", HID),
    ("up0", HID),
    ("at0", A_COLS),
    ("emb", D),
)
SUM_AT = {name: sum(w for _, w in SUMS[:i]) for i, (name, _) in enumerate(SUMS)}
SUM_COLS = sum(w for _, w in SUMS)
BLOCKS = N_SHARDS // 2 * SHARD
QUARTER = BLOCKS // 2


class Scatter:
    def __init__(self, place, bufs, sems):
        self.at = place
        self.perm, self.flip, self.cs, self.cr, self.xs, self.xr, self.zs, self.zr, self.own = bufs
        self.c_ss, self.c_rs, self.x_ss, self.x_rs, self.z_ss, self.z_rs = sems
        self.sent = []

    def span(self, name, shift=0, width=None):
        k = [n for n, _ in SUMS].index(name)
        return k, pl.ds(SUM_AT[name] + shift, SUMS[k][1] if width is None else width)

    def go(self, src, dst, ss, rs, device):
        copy = remote(src, dst, ss, rs, device)
        copy.start()
        self.sent.append(copy)

    def turn(self, slot, left):
        at = self.at
        flip = self.flip.at[slot]
        flip[...] = left.T
        order = [
            (s, x, c) for c, x in ((1, 1), (1, 0), (0, 1), (0, 0)) for s in range(4)
        ]
        for i, (s, other_x, other_c) in enumerate(order):
            x = 1 - at.x if other_x else at.x
            c = 1 - at.col if other_c else at.col
            first = pl.multiple_of(shard_at((at.z + s) % 4, x, c) * SHARD, 16)
            self.perm[slot, SHARD * i : SHARD * (i + 1), :] = flip[pl.ds(first, SHARD), :]

    def cores(self, name, items):
        for slot, right, shift, width in items:
            _, span = self.span(name, shift, width)
            self.cs[:, span] = low(times_plain(self.perm[slot, 0:BLOCKS, :], right[...]))
        k, span = self.span(name)
        self.go(
            self.cs.at[:, span],
            self.cr.at[:, span],
            self.c_ss.at[k],
            self.c_rs.at[k],
            self.at.core_mate(),
        )

    def over_x(self, name, items):
        f32 = jnp.float32
        k, whole = self.span(name)
        spot = self.cr.at[:, whole]
        remote(spot, spot, self.c_ss.at[k], self.c_rs.at[k], self.at.core_mate()).wait_recv()
        for slot, right, shift, width in items:
            _, span = self.span(name, shift, width)
            mine = times_plain(self.perm[slot, BLOCKS : BLOCKS + QUARTER, :], right[...])
            self.xs[:, span] = low(mine + self.cr[0:QUARTER, span].astype(f32))
        self.go(
            self.xs.at[:, whole],
            self.xr.at[:, whole],
            self.x_ss.at[k],
            self.x_rs.at[k],
            self.at.x_mate(),
        )
        for slot, right, shift, width in items:
            _, span = self.span(name, shift, width)
            mine = times_plain(self.perm[slot, BLOCKS + QUARTER : 2 * BLOCKS, :], right[...])
            self.own[:, span] = mine + self.cr[QUARTER:BLOCKS, span].astype(f32)

    def along_z(self, name):
        f32 = jnp.float32
        k, span = self.span(name)
        spot = self.xr.at[:, span]
        remote(spot, spot, self.x_ss.at[k], self.x_rs.at[k], self.at.x_mate()).wait_recv()
        for s in (1, 2, 3):
            rows = slice(SHARD * s, SHARD * (s + 1))
            self.zs[s - 1, :, span] = low(self.own[rows, span] + self.xr[rows, span].astype(f32))
            self.go(
                self.zs.at[s - 1, :, span],
                self.zr.at[s - 1, :, span],
                self.z_ss.at[k, s - 1],
                self.z_rs.at[k, s - 1],
                self.at.z_mate(s),
            )
        self.own[0:SHARD, span] += self.xr[0:SHARD, span].astype(f32)

    def finish(self, name):
        k, span = self.span(name)
        total = self.own[0:SHARD, span]
        for s in (1, 2, 3):
            spot = self.zr.at[s - 1, :, span]
            remote(
                spot, spot, self.z_ss.at[k, s - 1], self.z_rs.at[k, s - 1], self.at.z_mate(s)
            ).wait_recv()
            total = total + self.zr[s - 1, :, span].astype(jnp.float32)
        return total

    def drain(self):
        for copy in self.sent:
            copy.wait_send()


def encoder_attention_back(qkv_ref, d_out, out_ref):
    allowed = same_clip()
    halves = half_lanes()
    for p in range(3):
        spans = [slice(part * HALF_D + 128 * p, part * HALF_D + 128 * (p + 1)) for part in range(3)]
        q, k, v = (qkv_ref[:, span] for span in spans)
        d_pair = d_out[:, 128 * p : 128 * (p + 1)]
        found = []
        for h in range(2):
            one = jnp.where(halves[h], q, jnp.zeros_like(q))
            weights, total = encoder_scores(one, k, allowed)
            soft = weights / total
            d_one = jnp.where(halves[h], d_pair, jnp.zeros_like(d_pair))
            d_soft = times_trans(d_one, v)
            delta = jnp.sum(soft * d_soft, axis=-1, keepdims=True)
            d_scores = low(soft * (d_soft - delta))
            found.append(
                (
                    times_plain(d_scores, k) * SCALE,
                    trans_times(d_scores, q) * SCALE,
                    trans_times(low(soft), d_pair),
                )
            )
        for part in range(3):
            out_ref[:, spans[part]] = low(jnp.where(halves[0], found[0][part], found[1][part]))


def encoder_back_body(wide, *refs):
    f32 = jnp.float32
    gfeat_ref, x_ref, qkv_ref, o_ref, h_ref, slope_ref, px_ref, gain_ref, w_ref = refs[:9]
    refs = refs[9:]
    genc_ref, gemb_ref, gvec_ref = refs[:3]
    refs = refs[3:]
    wa_s, wb_s, du_s, dqkv_s, feat_s, sent_s, got_s = refs[:7]
    load_sem, f_ss, f_rs, y_ss, y_rs = refs[7:12]
    refs = refs[12:]
    place = Place()
    greet(place.mates(wide))
    swap = Swap(place, sent_s, got_s, y_ss, y_rs)
    swapped = remote(gfeat_ref, feat_s, f_ss, f_rs, place.row_mate())
    swapped.start()
    scatter = Scatter(place, refs[:9], refs[9:15]) if wide else None

    def load(layer, part):
        if part == 0:
            src, dst = w_ref.at[layer, :, pl.ds(0, A_COLS)], wa_s
        else:
            src, dst = w_ref.at[layer, :, pl.ds(A_COLS, 2 * HID)], wb_s
        return pltpu.make_async_copy(src, dst, load_sem.at[layer, part])

    load(1, 1).start()
    load(1, 0).start()

    lefts = {}

    def factor(slot, left):
        lefts[slot] = left
        if wide:
            scatter.turn(slot, left)

    def emit(name, items):
        if wide:
            scatter.cores(name, items)
            return
        for slot, right, shift, width in items:
            value = low(trans_times(lefts[slot], right[...]))
            if name == "emb":
                gemb_ref[...] = value
                continue
            start = {"at": 0, "up": UP_AT, "dn": DN_AT}[name[:2]] + shift
            genc_ref[int(name[2]), :, start : start + width] = value

    def later(step, *args):
        if wide:
            getattr(scatter, step)(*args)

    swapped.wait_recv()
    near, far = gfeat_ref[...].astype(f32), feat_s[...].astype(f32)
    first = place.row == 0
    grad = jnp.concatenate([jnp.where(first, near, far), jnp.where(first, far, near)], axis=0)
    gvec_ref[...] = jnp.zeros(gvec_ref.shape, f32)

    def note(row, grad_out, scaled):
        gvec_ref[row : row + 1, :] = column_sum(grad_out * scaled)
        gvec_ref[row + 1 : row + 2, :] = column_sum(grad_out)

    scaled, inv = norm_rows(x_ref[2 * LAYERS])
    note(4 * LAYERS, grad, scaled)
    d_x = norm_rows_back(grad, scaled, inv, gain_ref[4 * LAYERS : 4 * LAYERS + 1, :])
    for layer in (1, 0):
        gains = gain_ref[4 * layer : 4 * layer + 4, :]
        dn, up, at = (f"{kind}{layer}" for kind in ("dn", "up", "at"))
        scaled2, inv2 = norm_rows(x_ref[2 * layer + 1])
        n2 = low(scaled2 * gains[2:3] + gains[3:4])
        d_low = low(d_x)
        factor(0, d_low)
        dn_items = [(0, h_ref.at[layer], 0, HID)]
        emit(dn, dn_items)
        load(layer, 1).wait()
        d_hidden = times_plain(d_low, wb_s[:, HID : 2 * HID])
        du_s[...] = low(d_hidden * slope_ref[layer])
        swap.start(2 * layer + 1, times_trans(du_s[...], wb_s[:, 0:HID]))
        factor(1, n2)
        up_items = [(1, du_s, 0, HID)]
        emit(up, up_items)
        later("over_x", dn, dn_items)
        later("over_x", up, up_items)
        if layer == 1:
            load(0, 1).start()
        else:
            later("along_z", "at1")
        d_n2 = swap.total(2 * layer + 1)
        note(4 * layer + 2, d_n2, scaled2)
        d_x = d_x + norm_rows_back(d_n2, scaled2, inv2, gains[2:3])
        d_low = low(d_x)
        factor(2, d_low)
        load(layer, 0).wait()
        d_att = low(times_plain(d_low, wa_s[:, QKV_W:A_COLS]))
        encoder_attention_back(qkv_ref.at[layer], d_att, dqkv_s)
        swap.start(2 * layer, times_trans(dqkv_s[...], wa_s[:, 0:QKV_W]))
        scaled1, inv1 = norm_rows(x_ref[2 * layer])
        factor(3, low(scaled1 * gains[0:1] + gains[1:2]))
        at_items = [(3, dqkv_s, 0, QKV_W), (2, o_ref.at[layer], QKV_W, HALF_D)]
        emit(at, at_items)
        if layer == 1:
            load(0, 0).start()
        later("along_z", dn)
        later("over_x", at, at_items)
        later("along_z", up)
        d_n1 = swap.total(2 * layer)
        note(4 * layer, d_n1, scaled1)
        d_x = d_x + norm_rows_back(d_n1, scaled1, inv1, gains[0:1])
    factor(0, low(d_x))
    emb_items = [(0, px_ref, 0, D)]
    emit("emb", emb_items)
    later("along_z", "at0")
    later("over_x", "emb", emb_items)
    later("along_z", "emb")
    if wide:
        for layer in (1, 0):
            genc_ref[layer, :, DN_AT:ENC_COLS] = scatter.finish(f"dn{layer}")
            genc_ref[layer, :, UP_AT:DN_AT] = scatter.finish(f"up{layer}")
            genc_ref[layer, :, 0:A_COLS] = scatter.finish(f"at{layer}")
        gemb_ref[...] = scatter.finish("emb")
        scatter.drain()
    swapped.wait_send()
    swap.drain()


def run_encoder_back(wide, *operands):
    bf, f32 = jnp.bfloat16, jnp.float32
    vmem = pl.BlockSpec(memory_space=pltpu.VMEM)
    dma = pltpu.SemaphoreType.DMA
    shape = jax.ShapeDtypeStruct
    rows, kind = (SHARD, f32) if wide else (D, bf)
    scratch = [
        pltpu.VMEM((D, A_COLS), bf),
        pltpu.VMEM((D, 2 * HID), bf),
        pltpu.VMEM((PAIR, HID), bf),
        pltpu.VMEM((PAIR, QKV_W), bf),
        pltpu.VMEM((128, D), bf),
        pltpu.VMEM((2 * LAYERS, PAIR, D), bf),
        pltpu.VMEM((2 * LAYERS, PAIR, D), bf),
        dma((LAYERS, 2)),
        dma,
        dma,
        dma((2 * LAYERS,)),
        dma((2 * LAYERS,)),
    ]
    if wide:
        n = len(SUMS)
        scratch += [
            pltpu.VMEM((4, D, PAIR), bf),
            pltpu.VMEM((4, D, PAIR), bf),
            pltpu.VMEM((BLOCKS, SUM_COLS), bf),
            pltpu.VMEM((BLOCKS, SUM_COLS), bf),
            pltpu.VMEM((QUARTER, SUM_COLS), bf),
            pltpu.VMEM((QUARTER, SUM_COLS), bf),
            pltpu.VMEM((3, SHARD, SUM_COLS), bf),
            pltpu.VMEM((3, SHARD, SUM_COLS), bf),
            pltpu.VMEM((QUARTER, SUM_COLS), f32),
            dma((n,)),
            dma((n,)),
            dma((n,)),
            dma((n,)),
            dma((n, 3)),
            dma((n, 3)),
        ]
    return pl.pallas_call(
        functools.partial(encoder_back_body, wide),
        out_shape=(
            shape((LAYERS, rows, ENC_COLS), kind),
            shape((rows, D), kind),
            shape((16, D), f32),
        ),
        in_specs=[vmem] * 8 + [pl.BlockSpec(memory_space=pl.ANY)],
        out_specs=(vmem,) * 3,
        scratch_shapes=scratch,
        compiler_params=pltpu.CompilerParams(
            collective_id=2, has_side_effects=True, vmem_limit_bytes=63 * MIB
        ),
        cost_estimate=pl.CostEstimate(
            flops=20 * 10**9, bytes_accessed=60 * 10**6, transcendentals=10**6
        ),
        name="encoder_back",
    )(*operands)


def adam_at(refs, spot, grad, decay_rate, step_rate):
    master, first, second, master_out, first_out, second_out = refs
    new = adam_update(master[spot], first[spot], second[spot], grad, decay_rate, step_rate)
    master_out[spot], first_out[spot], second_out[spot] = new


def update_body(*refs):
    f32 = jnp.float32
    loss_ref, gdec_ref, gvec_ref = refs[:3]
    grads = refs[3:6]
    states = [refs[6 + 3 * i : 9 + 3 * i] for i in range(5)]
    scalar_ref = refs[21]
    outs = [refs[22 + 3 * i : 25 + 3 * i] for i in range(5)]
    send_s, got_s, ss, rs = refs[37:]
    place = Place()
    greet(place.mates(True))
    square = jnp.zeros((1, 1), f32)
    for ref in grads:
        whole = ref[...]
        square = square + jnp.sum(whole * whole)
    lane = lane_ids((1, D))
    send_s[0, 0:16, :] = 0.5 * gvec_ref[...]
    send_s[0, 16:24, 0:DD] = gdec_ref[...]
    send_s[0, 16:24, DD:D] = jnp.zeros((8, D - DD), f32)
    send_s[0, 23:24, :] = jnp.where(lane == 0, loss_ref[0:1, 0:1], 0.0) + jnp.where(
        lane == 1, square, 0.0
    )
    copies = []
    stages = [
        [place.core_mate()],
        [place.row_mate()],
        [place.x_mate()],
        [place.z_mate(1), place.z_mate(2), place.z_mate(3)],
    ]
    at = 0
    for i, mates in enumerate(stages):
        here = []
        for mate in mates:
            copy = remote(send_s.at[i], got_s.at[at], ss.at[at], rs.at[at], mate)
            copy.start()
            here.append((copy, at))
            at += 1
        total = send_s[i]
        for copy, spot in here:
            copy.wait_recv()
            total = total + got_s[spot]
        send_s[i + 1] = total
        copies += [copy for copy, _ in here]
    total = send_s[len(stages)]
    squares = jnp.sum(total[0:23, :] * total[0:23, :]) + jnp.sum(total[23:24, 1:2])
    norm = jnp.sqrt(jnp.zeros((1, 1), f32) + squares)
    factor = jnp.minimum(1.0, CLIP_MAX / (norm + 1e-06))
    scalar_ref[...] = jnp.where(lane_ids((8, 128)) == 0, total[23:24, 0:1], norm)
    enc = states[0] + outs[0]
    blocks = SHARD // 8

    @pl.loop(0, LAYERS * blocks)
    def _(i):
        spot = (i // blocks, 0, pl.ds(pl.multiple_of(i % blocks * 8, 8), 8), slice(None))
        grad = grads[0][spot[0], spot[2], :]
        adam_at(enc, spot, grad * factor, DECAY, RATE)

    for kind, rows in ((1, SHARD), (2, DD // N_SHARDS)):
        adam_at(states[kind] + outs[kind], (0,), grads[kind][...] * factor, DECAY, RATE)
    own = shard_at(place.z, place.x, place.col)
    for kind, top, count, width in ((3, 0, 10, D), (4, 16, 7, DD)):
        share = width // N_SHARDS
        turned = pltpu.roll(total, (D - own * share) % D, 1)
        grad = turned[top : top + count, 0:share] * factor
        adam_at(states[kind] + outs[kind], (slice(None), slice(None)), grad, 0.0, VEC_RATE)
    for copy in copies:
        copy.wait_send()


def run_update(loss_block, dec_vec_grads, enc_vec_grads, grads, states):
    f32 = jnp.float32
    vmem = pl.BlockSpec(memory_space=pltpu.VMEM)
    flat = [a for triple in states for a in triple]
    dma = pltpu.SemaphoreType.DMA
    outs = (jax.ShapeDtypeStruct((8, 128), f32),) + tuple(
        jax.ShapeDtypeStruct(a.shape, f32) for a in flat
    )
    return pl.pallas_call(
        update_body,
        out_shape=outs,
        in_specs=[vmem] * (6 + len(flat)),
        out_specs=(vmem,) * len(outs),
        scratch_shapes=[
            pltpu.VMEM((5, 24, D), f32),
            pltpu.VMEM((6, 24, D), f32),
            dma((6,)),
            dma((6,)),
        ],
        compiler_params=pltpu.CompilerParams(
            collective_id=3, has_side_effects=True, vmem_limit_bytes=60 * MIB
        ),
        name="update",
    )(loss_block, dec_vec_grads, enc_vec_grads, *grads, *flat)


def head_order(matrix, heads, width):
    lead = matrix.shape[:-1]
    cut = matrix[..., :width].reshape(lead + (heads, 3, HEAD))
    cut = jnp.swapaxes(cut, -3, -2).reshape(lead + (width,))
    return jnp.concatenate([cut, matrix[..., width:]], axis=-1)


def head_order_back(matrix, heads, width):
    lead = matrix.shape[:-1]
    cut = matrix[..., :width].reshape(lead + (3, heads, HEAD))
    cut = jnp.swapaxes(cut, -3, -2).reshape(lead + (width,))
    return jnp.concatenate([cut, matrix[..., width:]], axis=-1)


def sine_table(length, width):
    column = np.arange(width)
    freq = np.exp(-math.log(10000.0) * (2.0 * (column // 2)) / width)
    angle = np.arange(length)[:, None] * freq
    table = np.where(column % 2 == 0, np.sin(angle), np.cos(angle))
    return np.pad(table, ((0, ROWS - length), (0, 0))).astype(np.float32)


def frequency_rows(width):
    column = np.arange(width)
    freq = np.exp(-math.log(10000.0) * (2.0 * (column // 2)) / width)
    return np.broadcast_to(freq.astype(np.float32), (8, width))


def gather_vectors(enc_vec, dec_vec, group):
    vectors = jnp.concatenate([enc_vec.reshape(-1), dec_vec.reshape(-1)])
    vectors = lax.all_gather(low(vectors), group, axis=0, tiled=False).astype(jnp.float32)
    cut = enc_vec.size
    enc_gains = jnp.swapaxes(vectors[:, :cut].reshape(-1, *enc_vec.shape), 0, 1).reshape(-1, D)
    dec_gains = jnp.swapaxes(vectors[:, cut:].reshape(-1, *dec_vec.shape), 0, 1).reshape(-1, DD)
    return (
        jnp.pad(enc_gains, ((0, 16 - enc_gains.shape[0]), (0, 0))),
        jnp.pad(dec_gains, ((0, 8 - dec_gains.shape[0]), (0, 0))),
    )


def update_plain(loss_part, dec_vec_grads, enc_vec_grads, grads, states):
    everyone = ("row", "clip", "col")
    n_enc, n_dec = states[3][0].shape[0], states[4][0].shape[0]
    enc_vec_total, dec_vec_total, loss_total, square = lax.psum(
        (
            0.5 * enc_vec_grads[:n_enc],
            dec_vec_grads[:n_dec],
            loss_part,
            sum(jnp.sum(g * g) for g in grads),
        ),
        everyone,
    )
    square = square + jnp.sum(enc_vec_total**2) + jnp.sum(dec_vec_total**2)
    grad_norm = jnp.sqrt(square)
    factor = jnp.minimum(1.0, CLIP_MAX / (grad_norm + 1e-06))
    shard = lax.axis_index("clip") * lax.axis_size("col") + lax.axis_index("col")
    own = []
    for total, state in ((enc_vec_total, states[3][0]), (dec_vec_total, states[4][0])):
        width = state.shape[1]
        own.append(lax.dynamic_slice_in_dim(total, shard * width, width, 1))
    decays = (DECAY, DECAY, DECAY, 0.0, 0.0)
    rates = (RATE, RATE, RATE, VEC_RATE, VEC_RATE)
    results = []
    for triple, grad, decay_rate, step_rate in zip(states, (*grads, *own), decays, rates):
        grad = grad.reshape(triple[0].shape)
        results.extend(adam_update(*triple, grad * factor, decay_rate, step_rate))
    return (loss_total, grad_norm, *results)


def local(
    patches,
    visible,
    masked,
    enc_layers,
    enc_first,
    enc_second,
    embed,
    embed_first,
    embed_second,
    dec_mats,
    dec_first,
    dec_second,
    enc_vec,
    enc_vec_first,
    enc_vec_second,
    dec_vec,
    dec_vec_first,
    dec_vec_second,
):
    f32 = jnp.float32
    group = ("clip", "col")
    everyone = ("row", "clip", "col")
    wide = lax.axis_size("clip") == 8 and lax.axis_size("col") == 2
    row_here = lax.axis_index("row")
    pixels = patches[:, 0]
    seen = visible[:, 0]
    dec_full = lax.all_gather(
        low(head_order(dec_mats[0], DHEADS // 2, 3 * DD // 2)), everyone, axis=0, tiled=True
    ).reshape(2, DD, -1)
    padded = jnp.pad(pixels, ((0, 0), (0, ROWS - TUBES), (0, 0)))
    own = lax.dynamic_index_in_dim(padded, row_here, 0, keepdims=False)
    other = lax.dynamic_index_in_dim(padded, 1 - row_here, 0, keepdims=False)
    other = lax.ppermute(other, "row", [(0, 1), (1, 0)])

    enc_here = low(head_order(enc_layers[:, 0], HEADS // 2, QKV_W))
    embed_here = low(embed[0])
    seen_rows = jnp.pad(seen, ((0, 6), (0, 128 - VIS)), constant_values=-1)
    freq = jnp.asarray(frequency_rows(D))
    if wide:
        vectors = jnp.zeros((16, D), jnp.bfloat16)
        vectors = vectors.at[: enc_vec.shape[0], : enc_vec.shape[1]].set(low(enc_vec))
        vectors = vectors.at[: dec_vec.shape[0], SHARD : SHARD + dec_vec.shape[1]].set(low(dec_vec))
        emb_in = jnp.concatenate([embed_here, vectors], axis=0)
        feat, xs, qkv, att, hid, slope, px, enc_gains, dec_gains, enc_full = run_encoder(
            True, seen_rows, pixels, freq, emb_in, enc_here
        )
    else:
        embed_full = lax.all_gather(embed_here, group, axis=0, tiled=True)
        enc_full = lax.all_gather(enc_here, group, axis=1, tiled=True)
        enc_gains, dec_gains = gather_vectors(enc_vec, dec_vec, group)
        feat, xs, qkv, att, hid, slope, px = run_encoder(
            False, seen_rows, pixels, freq, embed_full, enc_full, enc_gains
        )
    pixel_pair = jnp.where(row_here == 0, jnp.stack([own, other]), jnp.stack([other, own]))
    seen_here = lax.dynamic_index_in_dim(seen, row_here, 0, keepdims=True)
    seen_here = jnp.pad(seen_here, ((0, 7), (0, 128 - VIS)), constant_values=-1)
    loss_block, dec_grads, dec_vec_grads, grad_feat = run_decoder(
        seen_here, feat, pixel_pair, jnp.asarray(sine_table(TUBES, DD)), dec_full, dec_gains
    )
    dec_total = lax.psum_scatter(
        dec_grads.reshape(-1, dec_grads.shape[-1]), everyone, scatter_dimension=0, tiled=True
    ).astype(f32)
    enc_total, embed_total, enc_vec_grads = run_encoder_back(
        wide, grad_feat, xs, qkv, att, hid, slope, px, enc_gains, enc_full
    )
    if not wide:
        enc_total = lax.psum_scatter(enc_total, group, scatter_dimension=1, tiled=True).astype(f32)
        embed_total = lax.psum_scatter(embed_total, group, scatter_dimension=0, tiled=True)
        embed_total = embed_total.astype(f32)
    grads = (
        head_order_back(enc_total, HEADS // 2, QKV_W),
        embed_total,
        head_order_back(dec_total, DHEADS // 2, 3 * DD // 2),
    )
    states = (
        (enc_layers, enc_first, enc_second),
        (embed, embed_first, embed_second),
        (dec_mats, dec_first, dec_second),
        (enc_vec, enc_vec_first, enc_vec_second),
        (dec_vec, dec_vec_first, dec_vec_second),
    )
    if wide:
        scalars, *results = run_update(loss_block, dec_vec_grads, enc_vec_grads, grads, states)
        return (scalars[0, 0], scalars[0, 1], *results)
    return update_plain(loss_block[0, 0], dec_vec_grads, enc_vec_grads, grads, states)


def solution(mesh):
    in_specs = (
        P(None, ("clip", "col"), None, "row"),
        P(None, ("clip", "col"), None),
        P(None, ("clip", "col"), None),
        P(None, "row", ("clip", "col"), None),
        P(None, "row", ("clip", "col"), None),
        P(None, "row", ("clip", "col"), None),
        P("row", ("clip", "col"), None),
        P("row", ("clip", "col"), None),
        P("row", ("clip", "col"), None),
        P("row", ("clip", "col"), None),
        P("row", ("clip", "col"), None),
        P("row", ("clip", "col"), None),
        P(None, ("clip", "col")),
        P(None, ("clip", "col")),
        P(None, ("clip", "col")),
        P(None, ("clip", "col")),
        P(None, ("clip", "col")),
        P(None, ("clip", "col")),
    )
    out_specs = (
        P(),
        P(),
        P(None, "row", ("clip", "col"), None),
        P(None, "row", ("clip", "col"), None),
        P(None, "row", ("clip", "col"), None),
        P("row", ("clip", "col"), None),
        P("row", ("clip", "col"), None),
        P("row", ("clip", "col"), None),
        P("row", ("clip", "col"), None),
        P("row", ("clip", "col"), None),
        P("row", ("clip", "col"), None),
        P(None, ("clip", "col")),
        P(None, ("clip", "col")),
        P(None, ("clip", "col")),
        P(None, ("clip", "col")),
        P(None, ("clip", "col")),
        P(None, ("clip", "col")),
    )
    return jax.shard_map(local, mesh=mesh, in_specs=in_specs, out_specs=out_specs, check_vma=False)
```

```python
import functools
import math

import jax
import jax.numpy as jnp
import numpy as np
from jax import lax
from jax.experimental import pallas as pl
from jax.experimental.pallas import tpu as pltpu
from jax.sharding import PartitionSpec as P

D = 768
HEADS = 12
HEAD = 64
FF = 3072
DD = 384
DHEADS = 6
DFF = 1536
PIX = 1536
TUBES = 1176
VIS = 118
LAYERS = 2
MICRO = 2
STEP = 10
MASKED = 1058


EPS_NORM = 1e-06
CLIP_MAX = 1.0
BETA_ONE = 0.9
BETA_TWO = 0.999
RATE = 0.06
VEC_RATE = 0.2
DECAY = 0.05
EPS_ADAM = 1e-08


def times_plain(left, right):
    return jnp.dot(left, right, preferred_element_type=jnp.float32)


def times_trans(left, right):
    return lax.dot_general(
        left, right, (((1,), (1,)), ((), ())), preferred_element_type=jnp.float32
    )


def trans_times(left, right):
    return lax.dot_general(
        left, right, (((0,), (0,)), ((), ())), preferred_element_type=jnp.float32
    )


def gelu_pair(values):
    cumul = 0.5 * (1.0 + lax.erf(values * 0.7071067811865476))
    density = jnp.exp(-0.5 * values * values) * 0.3989422804014327
    return (values * cumul, cumul + values * density)


def adam_update(master, first, second, grad_clip, decay_rate, step_rate):
    first_new = BETA_ONE * first + (1.0 - BETA_ONE) * grad_clip
    second_new = BETA_TWO * second + (1.0 - BETA_TWO) * grad_clip * grad_clip
    first_hat = first_new / (1.0 - BETA_ONE**STEP)
    second_hat = second_new / (1.0 - BETA_TWO**STEP)
    master_new = master - step_rate * (
        first_hat / (jnp.sqrt(second_hat) + EPS_ADAM) + decay_rate * master
    )
    return (master_new, first_new, second_new)


ROWS = 1200
LANES = 1280
STEP_ROWS = 240
N_STEPS = ROWS // STEP_ROWS
KEY_ROWS = 256
N_KEYS = LANES // KEY_ROWS
LOG2E = 1.4426950408889634
SCALE = HEAD ** (-0.5)
MIB = 1 << 20


def low(values):
    return values.astype(jnp.bfloat16)


def lane_ids(shape):
    return lax.broadcasted_iota(jnp.int32, shape, len(shape) - 1)


def row_ids(shape):
    return lax.broadcasted_iota(jnp.int32, shape, 0)


def norm_rows(rows):
    average = jnp.mean(rows, axis=-1, keepdims=True)
    centred = rows - average
    inv_dev = lax.rsqrt(jnp.mean(centred * centred, axis=-1, keepdims=True) + EPS_NORM)
    return centred * inv_dev, inv_dev


def norm_rows_back(grad_out, scaled, inv_dev, gain_row):
    inner = grad_out * gain_row
    return inv_dev * (
        inner
        - jnp.mean(inner, axis=-1, keepdims=True)
        - scaled * jnp.mean(inner * scaled, axis=-1, keepdims=True)
    )


def column_sum(values):
    return jnp.sum(values, axis=0, keepdims=True)


def decoder_body(
    seen_ref,
    feat_ref,
    padded_ref,
    table_ref,
    w_ref,
    vec_ref,
    loss_ref,
    grad_ref,
    gvec_ref,
    gfeat_ref,
    z_s,
    n1_s,
    q_s,
    k_s,
    v_s,
    o_s,
    do_s,
    dx_s,
    dqkv_s,
    dqt_s,
    lse_s,
    delta_s,
    lse_t,
    delta_t,
    bias_s,
    wqkv_s,
    wo_s,
    y_s,
    gqkv_s,
    go_s,
    gup_s,
    gdn_s,
    ghd_s,
    gy_s,
    gv_s,
    pixel_ref,
    seen_s,
    near_sem,
    far_ss,
    far_rs,
):
    bf, f32 = jnp.bfloat16, jnp.float32
    place = Place()
    greet([place.row_mate()])

    def tile(i):
        return pl.ds(pl.multiple_of(i * STEP_ROWS, STEP_ROWS), STEP_ROWS)

    def near(i):
        rows = tile(i)
        return pltpu.make_async_copy(
            padded_ref.at[place.row, rows, :], pixel_ref.at[place.row, rows, :], near_sem.at[i]
        )

    def far(i, half):
        rows = tile(i)
        return remote(
            padded_ref.at[1 - place.row, rows, :],
            pixel_ref.at[half, rows, :],
            far_ss.at[i],
            far_rs.at[i],
            place.row_mate(),
        )

    @pl.loop(0, N_STEPS)
    def _(i):
        near(i).start()
        far(i, place.row).start()

    half = 3 * HEAD
    up0, dn0, hd0, ed0 = 768, 1536, 2304, 3072
    vec = vec_ref[...]
    gain1, shift1, gain2, shift2, gain_f, shift_f, token = [vec[i : i + 1] for i in range(7)]

    for part in range(3):
        for r in range(2):
            wqkv_s[:, part * DD + r * half : part * DD + (r + 1) * half] = w_ref[
                r, :, part * half : (part + 1) * half
            ]
    for r in range(2):
        wo_s[:, r * half : (r + 1) * half] = w_ref[r, :, 3 * half : 4 * half]
    for ref in (q_s, k_s, v_s, do_s):
        ref[ROWS:LANES, :] = jnp.zeros((LANES - ROWS, DD), bf)
    lse_s[ROWS:LANES, :] = jnp.zeros((LANES - ROWS, 128), f32)
    delta_s[ROWS:LANES, :] = jnp.zeros((LANES - ROWS, 128), f32)
    bias_s[...] = jnp.where(row_ids((LANES, 128)) < TUBES, 0.0, -1e30)
    for ref in (gqkv_s, go_s, gup_s, gdn_s, ghd_s, gy_s, gv_s):
        ref[...] = jnp.zeros(ref.shape, f32)
    for r in range(2):
        y_s[:, r * DD : (r + 1) * DD] = low(
            times_trans(feat_ref[:, r * DD : (r + 1) * DD], w_ref[r, :, ed0 : ed0 + DD])
        )
    seen_s[...] = jnp.full(seen_s.shape, -1, jnp.int32)
    seen_s[0:1, 0:VIS] = seen_ref[place.row]
    seen = seen_s[0:1, :]

    def picks(i):
        ids = row_ids((STEP_ROWS, 128)) + i * STEP_ROWS
        hits = ids == seen
        taken = jnp.sum(hits.astype(f32), axis=-1, keepdims=True)
        valid = (row_ids((STEP_ROWS, 1)) + i * STEP_ROWS < TUBES).astype(f32)
        return hits.astype(bf), valid - taken

    @pl.loop(0, N_STEPS)
    def _(i):
        hits, hidden = picks(i)
        placed = times_plain(hits, y_s[...])
        z = placed[:, :DD] + placed[:, DD:] + table_ref[tile(i), :] + token * hidden
        z_s[tile(i), :] = z
        scaled, _ = norm_rows(z)
        n1 = low(scaled * gain1 + shift1)
        n1_s[tile(i), :] = n1
        q_s[tile(i), :] = low(times_plain(n1, wqkv_s[:, 0:DD]))
        k_s[tile(i), :] = low(times_plain(n1, wqkv_s[:, DD : 2 * DD]))
        v_s[tile(i), :] = low(times_plain(n1, wqkv_s[:, 2 * DD : 3 * DD]))

    first_half = lane_ids((1, 128)) < HEAD
    key_lanes = lane_ids((1, LANES)) < TUBES
    half_masks = [first_half, jnp.logical_not(first_half)]

    @pl.loop(0, 3)
    def _(p):
        lanes = pl.ds(pl.multiple_of(p * 128, 128), 128)

        @pl.loop(0, N_STEPS)
        def _(i):
            queries = q_s[tile(i), lanes]
            parts = []
            stat = lse_s[tile(i), :]
            for h in range(2):
                one = jnp.where(half_masks[h], queries, jnp.zeros_like(queries))
                scores = times_trans(one, k_s[:, lanes])
                scores = jnp.where(key_lanes, scores, -1e30)
                top = jnp.max(scores, axis=-1, keepdims=True) * (SCALE * LOG2E)
                weights = jnp.exp2(scores * (SCALE * LOG2E) - top)
                total = jnp.sum(weights, axis=-1, keepdims=True)
                parts.append(times_plain(low(weights), v_s[:, lanes]) / total)
                lse = top + jnp.log(total) * LOG2E
                stat = jnp.where(lane_ids((1, 128)) == 2 * p + h, lse, stat)
            lse_s[tile(i), :] = stat
            o_s[tile(i), lanes] = low(jnp.where(first_half, parts[0], parts[1]))

    lse_t[...] = lse_s[...].T

    @pl.loop(0, N_STEPS)
    def _(i):
        _, hidden = picks(i)
        near(i).wait()
        far(i, 1 - place.row).wait_recv()
        attended = o_s[tile(i), :]
        x1 = z_s[tile(i), :] + times_trans(attended, wo_s[...])
        scaled2, inv2 = norm_rows(x1)
        n2 = low(scaled2 * gain2 + shift2)
        x2 = x1
        acts, slopes = [], []
        for r in range(2):
            u = times_plain(n2, w_ref[r, :, up0 : up0 + 768])
            act, slope = gelu_pair(u)
            act = low(act)
            acts.append(act)
            slopes.append(slope)
            x2 = x2 + times_trans(act, w_ref[r, :, dn0 : dn0 + 768])
        scaled_f, inv_f = norm_rows(x2)
        t = low(scaled_f * gain_f + shift_f)
        d_t = jnp.zeros((STEP_ROWS, DD), f32)
        for r in range(2):
            error = times_plain(t, w_ref[r, :, hd0 : hd0 + 768]) - pixel_ref[r, tile(i), :].astype(
                f32
            )
            error = error * hidden
            gv_s[7:8, :] += column_sum(error * error)
            d_pred = low(error * (2.0 / PIX))
            ghd_s[r] += trans_times(t, d_pred)
            d_t = d_t + times_trans(d_pred, w_ref[r, :, hd0 : hd0 + 768])
        gv_s[4:5, 0:DD] += column_sum(d_t * scaled_f)
        gv_s[5:6, 0:DD] += column_sum(d_t)
        d_x2 = norm_rows_back(d_t, scaled_f, inv_f, gain_f)
        d_low = low(d_x2)
        d_n2 = jnp.zeros((STEP_ROWS, DD), f32)
        for r in range(2):
            gdn_s[r] += trans_times(d_low, acts[r])
            d_u = low(times_plain(d_low, w_ref[r, :, dn0 : dn0 + 768]) * slopes[r])
            gup_s[r] += trans_times(n2, d_u)
            d_n2 = d_n2 + times_trans(d_u, w_ref[r, :, up0 : up0 + 768])
        gv_s[2:3, 0:DD] += column_sum(d_n2 * scaled2)
        gv_s[3:4, 0:DD] += column_sum(d_n2)
        d_x1 = d_x2 + norm_rows_back(d_n2, scaled2, inv2, gain2)
        dx_s[tile(i), :] = d_x1
        d_low = low(d_x1)
        go_s[...] += trans_times(d_low, attended)
        d_o = low(times_plain(d_low, wo_s[...]))
        do_s[tile(i), :] = d_o
        both = d_o.astype(f32) * attended.astype(f32)
        stat = jnp.zeros((STEP_ROWS, 128), f32)
        for p in range(3):
            pair = both[:, 128 * p : 128 * (p + 1)]
            for h in range(2):
                one = jnp.sum(jnp.where(half_masks[h], pair, 0.0), axis=-1, keepdims=True)
                stat = jnp.where(lane_ids((1, 128)) == 2 * p + h, one, stat)
        delta_s[tile(i), :] = stat

    delta_t[...] = delta_s[...].T

    @pl.loop(0, 3)
    def _(p):
        lanes = pl.ds(pl.multiple_of(p * 128, 128), 128)
        dqt_s[...] = jnp.zeros(dqt_s.shape, f32)

        @pl.loop(0, N_KEYS)
        def _(j):
            rows = pl.ds(pl.multiple_of(j * KEY_ROWS, KEY_ROWS), KEY_ROWS)
            keys = k_s[rows, lanes]
            values = v_s[rows, lanes]
            bias = bias_s[rows, 0:1]
            d_keys, d_values = [], []
            for h in range(2):
                key_one = jnp.where(half_masks[h], keys, jnp.zeros_like(keys))
                value_one = jnp.where(half_masks[h], values, jnp.zeros_like(values))
                lse = lse_t[pl.ds(2 * p + h, 1), :]
                delta = delta_t[pl.ds(2 * p + h, 1), :]
                scores = times_trans(key_one, q_s[:, lanes])
                soft = jnp.exp2((scores * (SCALE * LOG2E) + bias) - lse)
                d_soft = times_trans(value_one, do_s[:, lanes])
                d_scores = low(soft * (d_soft - delta))
                d_values.append(times_plain(low(soft), do_s[:, lanes]))
                d_keys.append(times_plain(d_scores, q_s[:, lanes]))
                dqt_s[...] += trans_times(key_one, d_scores)
            k_out = pl.ds(pl.multiple_of(DD + p * 128, 128), 128)
            v_out = pl.ds(pl.multiple_of(2 * DD + p * 128, 128), 128)
            dqkv_s[rows, k_out] = low(jnp.where(first_half, d_keys[0], d_keys[1]) * SCALE)
            dqkv_s[rows, v_out] = low(jnp.where(first_half, d_values[0], d_values[1]))

        dqkv_s[:, lanes] = low(dqt_s[...].T * SCALE)

    @pl.loop(0, N_STEPS)
    def _(i):
        hits, hidden = picks(i)
        d_qkv = dqkv_s[tile(i), :]
        gqkv_s[...] += trans_times(n1_s[tile(i), :], d_qkv)
        d_n1 = times_trans(d_qkv, wqkv_s[...])
        scaled1, inv1 = norm_rows(z_s[tile(i), :])
        gv_s[0:1, 0:DD] += column_sum(d_n1 * scaled1)
        gv_s[1:2, 0:DD] += column_sum(d_n1)
        d_z = dx_s[tile(i), :] + norm_rows_back(d_n1, scaled1, inv1, gain1)
        gv_s[6:7, 0:DD] += column_sum(d_z * hidden)
        gy_s[...] += trans_times(hits, low(d_z))

    d_y = low(gy_s[...])
    for r in range(2):
        grad_ref[r, :, ed0 : ed0 + DD] = low(trans_times(d_y, feat_ref[:, r * DD : (r + 1) * DD]))
        gfeat_ref[:, r * DD : (r + 1) * DD] = low(times_plain(d_y, w_ref[r, :, ed0 : ed0 + DD]))
        for part in range(3):
            grad_ref[r, :, part * half : (part + 1) * half] = low(
                gqkv_s[:, part * DD + r * half : part * DD + (r + 1) * half]
            )
        grad_ref[r, :, 3 * half : 4 * half] = low(go_s[:, r * half : (r + 1) * half])
        grad_ref[r, :, up0 : up0 + 768] = low(gup_s[r])
        grad_ref[r, :, dn0 : dn0 + 768] = low(gdn_s[r])
        grad_ref[r, :, hd0 : hd0 + 768] = low(ghd_s[r])
    gvec_ref[...] = gv_s[:, 0:DD]

    @pl.loop(0, N_STEPS)
    def _(i):
        far(i, place.row).wait_send()

    loss_ref[...] = jnp.zeros((8, 128), f32) + jnp.sum(gv_s[7:8, :]) / PIX


def run_decoder(seen, feat, padded, table, weights, vectors):
    bf, f32 = jnp.bfloat16, jnp.float32
    vmem = pl.BlockSpec(memory_space=pltpu.VMEM)
    return pl.pallas_call(
        decoder_body,
        out_shape=(
            jax.ShapeDtypeStruct((8, 128), f32),
            jax.ShapeDtypeStruct((2, DD, 3456), bf),
            jax.ShapeDtypeStruct((8, DD), f32),
            jax.ShapeDtypeStruct((128, D), bf),
        ),
        in_specs=[vmem, vmem, pl.BlockSpec(memory_space=pl.ANY), vmem, vmem, vmem],
        out_specs=(vmem,) * 4,
        scratch_shapes=[
            pltpu.VMEM((ROWS, DD), f32),
            pltpu.VMEM((ROWS, DD), bf),
            pltpu.VMEM((LANES, DD), bf),
            pltpu.VMEM((LANES, DD), bf),
            pltpu.VMEM((LANES, DD), bf),
            pltpu.VMEM((ROWS, DD), bf),
            pltpu.VMEM((LANES, DD), bf),
            pltpu.VMEM((ROWS, DD), f32),
            pltpu.VMEM((LANES, 3 * DD), bf),
            pltpu.VMEM((128, LANES), f32),
            pltpu.VMEM((LANES, 128), f32),
            pltpu.VMEM((LANES, 128), f32),
            pltpu.VMEM((128, LANES), f32),
            pltpu.VMEM((128, LANES), f32),
            pltpu.VMEM((LANES, 128), f32),
            pltpu.VMEM((DD, 3 * DD), bf),
            pltpu.VMEM((DD, DD), bf),
            pltpu.VMEM((128, 2 * DD), bf),
            pltpu.VMEM((DD, 3 * DD), f32),
            pltpu.VMEM((DD, DD), f32),
            pltpu.VMEM((2, DD, 768), f32),
            pltpu.VMEM((2, DD, 768), f32),
            pltpu.VMEM((2, DD, 768), f32),
            pltpu.VMEM((128, DD), f32),
            pltpu.VMEM((8, 768), f32),
            pltpu.VMEM((2, ROWS, PIX // 2), bf),
            pltpu.VMEM((8, 128), jnp.int32),
            pltpu.SemaphoreType.DMA((N_STEPS,)),
            pltpu.SemaphoreType.DMA((N_STEPS,)),
            pltpu.SemaphoreType.DMA((N_STEPS,)),
        ],
        compiler_params=pltpu.CompilerParams(
            collective_id=4, has_side_effects=True, vmem_limit_bytes=62 * MIB
        ),
        cost_estimate=pl.CostEstimate(
            flops=30 * 10**9, bytes_accessed=20 * 10**6, transcendentals=20 * 10**6
        ),
        name="decoder",
    )(seen, feat, padded, table, weights, vectors)


PAIR = 256
HALF_D = D // 2
QKV_W = 3 * D // 2
HID = FF // 2
A_COLS = QKV_W + D // 2
ENC_COLS = A_COLS + 2 * HID
UP_AT, DN_AT = A_COLS, A_COLS + HID
N_SHARDS = 16
SHARD = D // N_SHARDS
EMB_ROWS = SHARD + 16
MESH_IDS = pl.DeviceIdType.MESH
GATHERS = (
    (-1, 0, D),
    (0, 0, A_COLS),
    (0, A_COLS, 2 * HID),
    (1, 0, A_COLS),
    (1, A_COLS, 2 * HID),
)


def remote(src, dst, send_sem, recv_sem, device):
    return pltpu.make_async_remote_copy(
        src_ref=src,
        dst_ref=dst,
        send_sem=send_sem,
        recv_sem=recv_sem,
        device_id=device,
        device_id_type=MESH_IDS,
    )


class Place:
    def __init__(self):
        self.clip = lax.axis_index("clip")
        self.row = lax.axis_index("row")
        self.col = lax.axis_index("col")
        self.z = self.clip // 2
        self.x = self.clip % 2

    def z_mate(self, step):
        return (((self.z + step) % 4) * 2 + self.x, self.row, self.col)

    def x_mate(self):
        return (self.z * 2 + 1 - self.x, self.row, self.col)

    def core_mate(self):
        return (self.clip, self.row, 1 - self.col)

    def row_mate(self):
        return (self.clip, 1 - self.row, self.col)

    def mates(self, wide):
        near = [self.row_mate()]
        if wide:
            near += [self.core_mate(), self.x_mate()] + [self.z_mate(s) for s in (1, 2, 3)]
        return near


def shard_at(z, x, col):
    return (z * 2 + x) * 2 + col


def greet(mates):
    barrier = pltpu.get_barrier_semaphore()
    for mate in mates:
        pl.semaphore_signal(barrier, inc=1, device_id=mate, device_id_type=MESH_IDS)
    pl.semaphore_wait(barrier, len(mates))


class Gather:
    def __init__(self, place, mine, buffers, sems):
        self.at = place
        self.mine = mine
        self.buffers = buffers
        self.z_ss, self.z_rs, self.x_ss, self.x_rs, self.c_ss, self.c_rs = sems
        self.sent = []

    def spot(self, k, z, x, col):
        layer, start, width = GATHERS[k]
        rows = EMB_ROWS if layer < 0 else SHARD
        first = pl.multiple_of(shard_at(z, x, col) * rows, 16)
        if layer < 0:
            return self.buffers[0].at[pl.ds(first, rows), :]
        return self.buffers[1].at[layer, pl.ds(first, rows), pl.ds(start, width)]

    def own(self, k):
        layer, start, width = GATHERS[k]
        if layer < 0:
            return self.mine[0]
        return self.mine[1].at[layer, :, pl.ds(start, width)]

    def go(self, src, dst, ss, rs, device):
        copy = remote(src, dst, ss, rs, device)
        copy.start()
        self.sent.append(copy)

    def came(self, dst, ss, rs):
        remote(dst, dst, ss, rs, self.at.core_mate()).wait_recv()

    def begin(self, k):
        at = self.at
        src, dst = self.own(k), self.spot(k, at.z, at.x, at.col)
        for s in (1, 2, 3):
            self.go(src, dst, self.z_ss.at[k, s - 1], self.z_rs.at[k, s - 1], at.z_mate(s))
        self.go(src, dst, self.x_ss.at[k, 0], self.x_rs.at[k, 0], at.x_mate())
        self.go(src, dst, self.c_ss.at[k, 0], self.c_rs.at[k, 0], at.core_mate())

    def forward(self, k):
        at = self.at
        for s in (1, 2, 3):
            spot = self.spot(k, (at.z - s) % 4, at.x, at.col)
            self.came(spot, self.z_ss.at[k, s - 1], self.z_rs.at[k, s - 1])
            self.go(spot, spot, self.x_ss.at[k, s], self.x_rs.at[k, s], at.x_mate())
            self.go(spot, spot, self.c_ss.at[k, s], self.c_rs.at[k, s], at.core_mate())

    def across(self, k):
        at = self.at
        for s in range(4):
            spot = self.spot(k, (at.z - s) % 4, 1 - at.x, at.col)
            self.came(spot, self.x_ss.at[k, s], self.x_rs.at[k, s])
            self.go(spot, spot, self.c_ss.at[k, 4 + s], self.c_rs.at[k, 4 + s], at.core_mate())

    def finish(self, k):
        at = self.at
        for s in range(8):
            x = at.x if s < 4 else 1 - at.x
            spot = self.spot(k, (at.z - s % 4) % 4, x, 1 - at.col)
            self.came(spot, self.c_ss.at[k, s], self.c_rs.at[k, s])

    def drain(self):
        for copy in self.sent:
            copy.wait_send()


class Swap:
    def __init__(self, place, sent, got, send_sems, recv_sems):
        self.at, self.sent, self.got = place, sent, got
        self.ss, self.rs = send_sems, recv_sems
        self.copies = {}

    def start(self, i, value):
        self.sent[i] = low(value)
        copy = remote(
            self.sent.at[i], self.got.at[i], self.ss.at[i], self.rs.at[i], self.at.row_mate()
        )
        copy.start()
        self.copies[i] = copy

    def total(self, i):
        self.copies[i].wait_recv()
        return self.sent[i].astype(jnp.float32) + self.got[i].astype(jnp.float32)

    def drain(self):
        for copy in self.copies.values():
            copy.wait_send()


def half_lanes():
    first = lane_ids((1, 128)) < HEAD
    return [first, jnp.logical_not(first)]


def same_clip():
    a, b = row_ids((PAIR, PAIR)), lane_ids((PAIR, PAIR))
    return jnp.logical_and(a // 128 == b // 128, b % 128 < VIS)


def encoder_scores(queries, keys, allowed):
    scores = jnp.where(allowed, times_trans(queries, keys), -1e30)
    top = jnp.max(scores, axis=-1, keepdims=True) * (SCALE * LOG2E)
    weights = jnp.exp2(scores * (SCALE * LOG2E) - top)
    return weights, jnp.sum(weights, axis=-1, keepdims=True)


def encoder_attention(qkv_ref, out_ref):
    allowed = same_clip()
    halves = half_lanes()
    for p in range(3):
        q = qkv_ref[:, 128 * p : 128 * (p + 1)]
        k = qkv_ref[:, HALF_D + 128 * p : HALF_D + 128 * (p + 1)]
        v = qkv_ref[:, 2 * HALF_D + 128 * p : 2 * HALF_D + 128 * (p + 1)]
        parts = []
        for h in range(2):
            one = jnp.where(halves[h], q, jnp.zeros_like(q))
            weights, total = encoder_scores(one, k, allowed)
            parts.append(times_plain(low(weights), v) / total)
        out_ref[:, 128 * p : 128 * (p + 1)] = low(jnp.where(halves[0], parts[0], parts[1]))


def pack_heads(dst, src, heads):
    for part in range(3):
        for h in range(heads):
            at = (part * heads + h) * HEAD
            dst[:, at : at + HEAD] = low(src[:, (3 * h + part) * HEAD : (3 * h + part + 1) * HEAD])


def encoder_body(wide, *refs):
    f32 = jnp.float32
    if wide:
        seen_ref, pixel_ref, freq_ref, emb_ref, enc_ref, evec_ref, dvec_ref = refs[:7]
        refs = refs[7:]
    else:
        seen_ref, pixel_ref, freq_ref, emb_full, w_s, gain_in = refs[:6]
        refs = refs[6:]
    feat_ref, x_ref, qkv_ref, o_ref, h_ref, slope_ref, px_ref, padded_out = refs[:8]
    refs = refs[8:]
    if wide:
        gain_ref, dgain_ref, w_out, emb_s, w_s, embc_s, emb_in, enc_in, small_s = refs[:9]
        refs = refs[9:]
    sent_s, got_s, padded_s, seen_s, pad_sem, y_ss, y_rs = refs[:7]
    refs = refs[7:]
    place = Place()
    greet(place.mates(wide))
    swap = Swap(place, sent_s, got_s, y_ss, y_rs)
    if wide:
        gather = Gather(place, (emb_in, enc_in), (emb_s, w_s), refs[:6])
        keep_sem = refs[6]
        emb_in[0:SHARD, :] = low(emb_ref[0])
        small_s[...] = jnp.zeros(small_s.shape, f32)
        small_s[0:10, 0:SHARD] = evec_ref[...]
        small_s[0:7, SHARD : SHARD + DD // N_SHARDS] = dvec_ref[...]
        emb_in[SHARD:EMB_ROWS, 0:128] = low(small_s[...])
        emb_in[SHARD:EMB_ROWS, 128:D] = jnp.zeros((EMB_ROWS - SHARD, D - 128), jnp.bfloat16)
        gather.begin(0)
        for layer in range(LAYERS):
            pack_heads(enc_in.at[layer], enc_ref.at[layer, 0], HEADS // 2)
            enc_in[layer, :, QKV_W:] = low(enc_ref[layer, 0, :, QKV_W:])
            if layer == 0:
                gather.begin(1)
                gather.begin(2)
        own = shard_at(place.z, place.x, place.col)
        emb_s[pl.ds(pl.multiple_of(own * EMB_ROWS, 16), EMB_ROWS), :] = emb_in[...]
        for layer in range(LAYERS):
            w_s[layer, pl.ds(pl.multiple_of(own * SHARD, 16), SHARD), :] = enc_in[layer]

    def step(name, k):
        if wide:
            getattr(gather, name)(k)

    odd = (lane_ids((1, D)) % 2).astype(f32) * (0.5 * math.pi)
    freq = freq_ref[0:1, :]
    places = []
    seen_s[...] = jnp.full(seen_s.shape, -1, jnp.int32)
    whole = TUBES // 16 * 16
    for m in range(MICRO):
        seen_s[m : m + 1, 0:VIS] = seen_ref[m]
        row = seen_s[m : m + 1, :]
        hits = (row_ids((TUBES, 128)) == row).astype(jnp.bfloat16)
        px_ref[128 * m : 128 * (m + 1), :] = low(trans_times(hits, pixel_ref[m, 0]))
        column = jnp.broadcast_to(row.astype(f32), (128, 128)).T[:, 0:1]
        places.append(jnp.sin(column * freq + odd))
        padded_s[m, 0:whole, :] = pixel_ref[m, 0, 0:whole, :]
        rest = pixel_ref[m, 0, whole:TUBES, :].astype(f32)
        rest = jnp.concatenate([rest, jnp.zeros((ROWS - TUBES, D), f32)], axis=0)
        padded_s[m, whole:ROWS, :] = low(rest)
    pad_copy = pltpu.make_async_copy(padded_s, padded_out, pad_sem)
    pad_copy.start()

    if wide:
        gather.forward(0)
        gather.across(0)
        gather.finish(0)
        for s in range(N_SHARDS):
            embc_s[SHARD * s : SHARD * (s + 1), :] = emb_s[EMB_ROWS * s : EMB_ROWS * s + SHARD, :]
            tail = emb_s[EMB_ROWS * s + SHARD : EMB_ROWS * (s + 1), 0:128].astype(f32)
            gain_ref[:, SHARD * s : SHARD * (s + 1)] = tail[:, 0:SHARD]
            dgain_ref[:, DD // 16 * s : DD // 16 * (s + 1)] = tail[0:8, SHARD : SHARD + DD // 16]
        emb_full, gain_in = embc_s, gain_ref
    swap.start(0, times_trans(px_ref[...], emb_full[...]))
    step("forward", 1)
    step("begin", 3)
    step("across", 1)
    x = swap.total(0) + jnp.concatenate(places, axis=0)
    for layer in range(LAYERS):
        gains = gain_in[4 * layer : 4 * layer + 4, :]
        x_ref[2 * layer] = x
        scaled, _ = norm_rows(x)
        n1 = low(scaled * gains[0:1] + gains[1:2])
        step("finish", 1 + 2 * layer)
        qkv_ref[layer] = low(times_plain(n1, w_s[layer, :, 0:QKV_W]))
        encoder_attention(qkv_ref.at[layer], o_ref.at[layer])
        swap.start(1 + 2 * layer, times_trans(o_ref[layer], w_s[layer, :, QKV_W:A_COLS]))
        step("forward", 2 + 2 * layer)
        if layer == 0:
            step("begin", 4)
        step("across", 2 + 2 * layer)
        x = x + swap.total(1 + 2 * layer)
        x_ref[2 * layer + 1] = x
        scaled, _ = norm_rows(x)
        n2 = low(scaled * gains[2:3] + gains[3:4])
        step("finish", 2 + 2 * layer)
        if wide:
            keep = pltpu.make_async_copy(w_s.at[layer], w_out.at[layer], keep_sem.at[layer])
            keep.start()
        act, slope = gelu_pair(times_plain(n2, w_s[layer, :, UP_AT:DN_AT]))
        act = low(act)
        h_ref[layer] = act
        slope_ref[layer] = slope
        swap.start(2 + 2 * layer, times_trans(act, w_s[layer, :, DN_AT:ENC_COLS]))
        if layer == 0:
            step("forward", 3)
            step("across", 3)
        x = x + swap.total(2 + 2 * layer)
    x_ref[2 * LAYERS] = x
    scaled, _ = norm_rows(x)
    gains = gain_in[4 * LAYERS : 4 * LAYERS + 2, :]
    feat = low(scaled * gains[0:1] + gains[1:2])
    feat_ref[...] = jnp.where(place.row == 0, feat[0:128], feat[128:256])
    swap.drain()
    pad_copy.wait()
    if wide:
        gather.drain()
        for layer in range(LAYERS):
            pltpu.make_async_copy(w_s.at[layer], w_out.at[layer], keep_sem.at[layer]).wait()


def run_encoder(wide, *operands):
    bf, f32 = jnp.bfloat16, jnp.float32
    vmem = pl.BlockSpec(memory_space=pltpu.VMEM)
    dma = pltpu.SemaphoreType.DMA
    shape = jax.ShapeDtypeStruct
    n_swaps = 1 + 2 * LAYERS
    outs = [
        shape((128, D), bf),
        shape((2 * LAYERS + 1, PAIR, D), f32),
        shape((LAYERS, PAIR, QKV_W), bf),
        shape((LAYERS, PAIR, HALF_D), bf),
        shape((LAYERS, PAIR, HID), bf),
        shape((LAYERS, PAIR, HID), f32),
        shape((PAIR, D), bf),
        shape((MICRO, ROWS, D), bf),
    ]
    out_specs = [vmem] * (len(outs) - 1) + [pl.BlockSpec(memory_space=pl.ANY)]
    scratch = []
    if wide:
        outs += [shape((16, D), f32), shape((8, DD), f32), shape((LAYERS, D, ENC_COLS), bf)]
        out_specs += [vmem, vmem, pl.BlockSpec(memory_space=pl.ANY)]
        scratch += [
            pltpu.VMEM((N_SHARDS * EMB_ROWS, D), bf),
            pltpu.VMEM((LAYERS, D, ENC_COLS), bf),
            pltpu.VMEM((D, D), bf),
            pltpu.VMEM((EMB_ROWS, D), bf),
            pltpu.VMEM((LAYERS, SHARD, ENC_COLS), bf),
            pltpu.VMEM((16, 128), f32),
        ]
    scratch += [
        pltpu.VMEM((n_swaps, PAIR, D), bf),
        pltpu.VMEM((n_swaps, PAIR, D), bf),
        pltpu.VMEM((MICRO, ROWS, D), bf),
        pltpu.VMEM((8, 128), jnp.int32),
        dma,
        dma((n_swaps,)),
        dma((n_swaps,)),
    ]
    if wide:
        n = len(GATHERS)
        scratch += [dma((n, 3)), dma((n, 3)), dma((n, 4)), dma((n, 4)), dma((n, 8)), dma((n, 8))]
        scratch += [dma((LAYERS,))]
    return pl.pallas_call(
        functools.partial(encoder_body, wide),
        out_shape=tuple(outs),
        in_specs=[vmem] * len(operands),
        out_specs=tuple(out_specs),
        scratch_shapes=scratch,
        compiler_params=pltpu.CompilerParams(
            collective_id=1, has_side_effects=True, vmem_limit_bytes=60 * MIB
        ),
        cost_estimate=pl.CostEstimate(
            flops=10 * 10**9, bytes_accessed=60 * 10**6, transcendentals=10**6
        ),
        name="encoder",
    )(*operands)


SUMS = (
    ("dn1", HID),
    ("up1", HID),
    ("at1", A_COLS),
    ("dn0", HID),
    ("up0", HID),
    ("at0", A_COLS),
    ("emb", D),
)
SUM_AT = {name: sum(w for _, w in SUMS[:i]) for i, (name, _) in enumerate(SUMS)}
SUM_COLS = sum(w for _, w in SUMS)
BLOCKS = N_SHARDS // 2 * SHARD
QUARTER = BLOCKS // 2


class Scatter:
    def __init__(self, place, bufs, sems):
        self.at = place
        self.perm, self.flip, self.cs, self.cr, self.xs, self.xr, self.zs, self.zr, self.own = bufs
        self.c_ss, self.c_rs, self.x_ss, self.x_rs, self.z_ss, self.z_rs = sems
        self.sent = []

    def span(self, name, shift=0, width=None):
        k = [n for n, _ in SUMS].index(name)
        return k, pl.ds(SUM_AT[name] + shift, SUMS[k][1] if width is None else width)

    def go(self, src, dst, ss, rs, device):
        copy = remote(src, dst, ss, rs, device)
        copy.start()
        self.sent.append(copy)

    def turn(self, slot, left):
        at = self.at
        flip = self.flip.at[slot]
        flip[...] = left.T
        order = [
            (s, x, c) for c, x in ((1, 1), (1, 0), (0, 1), (0, 0)) for s in range(4)
        ]
        for i, (s, other_x, other_c) in enumerate(order):
            x = 1 - at.x if other_x else at.x
            c = 1 - at.col if other_c else at.col
            first = pl.multiple_of(shard_at((at.z + s) % 4, x, c) * SHARD, 16)
            self.perm[slot, SHARD * i : SHARD * (i + 1), :] = flip[pl.ds(first, SHARD), :]

    def cores(self, name, items):
        for slot, right, shift, width in items:
            _, span = self.span(name, shift, width)
            self.cs[:, span] = low(times_plain(self.perm[slot, 0:BLOCKS, :], right[...]))
        k, span = self.span(name)
        self.go(
            self.cs.at[:, span],
            self.cr.at[:, span],
            self.c_ss.at[k],
            self.c_rs.at[k],
            self.at.core_mate(),
        )

    def over_x(self, name, items):
        f32 = jnp.float32
        k, whole = self.span(name)
        spot = self.cr.at[:, whole]
        remote(spot, spot, self.c_ss.at[k], self.c_rs.at[k], self.at.core_mate()).wait_recv()
        for slot, right, shift, width in items:
            _, span = self.span(name, shift, width)
            mine = times_plain(self.perm[slot, BLOCKS : BLOCKS + QUARTER, :], right[...])
            self.xs[:, span] = low(mine + self.cr[0:QUARTER, span].astype(f32))
        self.go(
            self.xs.at[:, whole],
            self.xr.at[:, whole],
            self.x_ss.at[k],
            self.x_rs.at[k],
            self.at.x_mate(),
        )
        for slot, right, shift, width in items:
            _, span = self.span(name, shift, width)
            mine = times_plain(self.perm[slot, BLOCKS + QUARTER : 2 * BLOCKS, :], right[...])
            self.own[:, span] = mine + self.cr[QUARTER:BLOCKS, span].astype(f32)

    def along_z(self, name):
        f32 = jnp.float32
        k, span = self.span(name)
        spot = self.xr.at[:, span]
        remote(spot, spot, self.x_ss.at[k], self.x_rs.at[k], self.at.x_mate()).wait_recv()
        for s in (1, 2, 3):
            rows = slice(SHARD * s, SHARD * (s + 1))
            self.zs[s - 1, :, span] = low(self.own[rows, span] + self.xr[rows, span].astype(f32))
            self.go(
                self.zs.at[s - 1, :, span],
                self.zr.at[s - 1, :, span],
                self.z_ss.at[k, s - 1],
                self.z_rs.at[k, s - 1],
                self.at.z_mate(s),
            )
        self.own[0:SHARD, span] += self.xr[0:SHARD, span].astype(f32)

    def finish(self, name):
        k, span = self.span(name)
        total = self.own[0:SHARD, span]
        for s in (1, 2, 3):
            spot = self.zr.at[s - 1, :, span]
            remote(
                spot, spot, self.z_ss.at[k, s - 1], self.z_rs.at[k, s - 1], self.at.z_mate(s)
            ).wait_recv()
            total = total + self.zr[s - 1, :, span].astype(jnp.float32)
        return total

    def drain(self):
        for copy in self.sent:
            copy.wait_send()


def encoder_attention_back(qkv_ref, d_out, out_ref):
    allowed = same_clip()
    halves = half_lanes()
    for p in range(3):
        spans = [slice(part * HALF_D + 128 * p, part * HALF_D + 128 * (p + 1)) for part in range(3)]
        q, k, v = (qkv_ref[:, span] for span in spans)
        d_pair = d_out[:, 128 * p : 128 * (p + 1)]
        found = []
        for h in range(2):
            one = jnp.where(halves[h], q, jnp.zeros_like(q))
            weights, total = encoder_scores(one, k, allowed)
            soft = weights / total
            d_one = jnp.where(halves[h], d_pair, jnp.zeros_like(d_pair))
            d_soft = times_trans(d_one, v)
            delta = jnp.sum(soft * d_soft, axis=-1, keepdims=True)
            d_scores = low(soft * (d_soft - delta))
            found.append(
                (
                    times_plain(d_scores, k) * SCALE,
                    trans_times(d_scores, q) * SCALE,
                    trans_times(low(soft), d_pair),
                )
            )
        for part in range(3):
            out_ref[:, spans[part]] = low(jnp.where(halves[0], found[0][part], found[1][part]))


def encoder_back_body(wide, *refs):
    f32 = jnp.float32
    gfeat_ref, x_ref, qkv_ref, o_ref, h_ref, slope_ref, px_ref, gain_ref, w_ref = refs[:9]
    refs = refs[9:]
    genc_ref, gemb_ref, gvec_ref = refs[:3]
    refs = refs[3:]
    wa_s, wb_s, du_s, dqkv_s, feat_s, sent_s, got_s = refs[:7]
    load_sem, f_ss, f_rs, y_ss, y_rs = refs[7:12]
    refs = refs[12:]
    place = Place()
    greet(place.mates(wide))
    swap = Swap(place, sent_s, got_s, y_ss, y_rs)
    swapped = remote(gfeat_ref, feat_s, f_ss, f_rs, place.row_mate())
    swapped.start()
    scatter = Scatter(place, refs[:9], refs[9:15]) if wide else None

    def load(layer, part):
        if part == 0:
            src, dst = w_ref.at[layer, :, pl.ds(0, A_COLS)], wa_s
        else:
            src, dst = w_ref.at[layer, :, pl.ds(A_COLS, 2 * HID)], wb_s
        return pltpu.make_async_copy(src, dst, load_sem.at[layer, part])

    load(1, 1).start()
    load(1, 0).start()

    lefts = {}

    def factor(slot, left):
        lefts[slot] = left
        if wide:
            scatter.turn(slot, left)

    def emit(name, items):
        if wide:
            scatter.cores(name, items)
            return
        for slot, right, shift, width in items:
            value = low(trans_times(lefts[slot], right[...]))
            if name == "emb":
                gemb_ref[...] = value
                continue
            start = {"at": 0, "up": UP_AT, "dn": DN_AT}[name[:2]] + shift
            genc_ref[int(name[2]), :, start : start + width] = value

    def later(step, *args):
        if wide:
            getattr(scatter, step)(*args)

    swapped.wait_recv()
    near, far = gfeat_ref[...].astype(f32), feat_s[...].astype(f32)
    first = place.row == 0
    grad = jnp.concatenate([jnp.where(first, near, far), jnp.where(first, far, near)], axis=0)
    gvec_ref[...] = jnp.zeros(gvec_ref.shape, f32)

    def note(row, grad_out, scaled):
        gvec_ref[row : row + 1, :] = column_sum(grad_out * scaled)
        gvec_ref[row + 1 : row + 2, :] = column_sum(grad_out)

    scaled, inv = norm_rows(x_ref[2 * LAYERS])
    note(4 * LAYERS, grad, scaled)
    d_x = norm_rows_back(grad, scaled, inv, gain_ref[4 * LAYERS : 4 * LAYERS + 1, :])
    for layer in (1, 0):
        gains = gain_ref[4 * layer : 4 * layer + 4, :]
        dn, up, at = (f"{kind}{layer}" for kind in ("dn", "up", "at"))
        scaled2, inv2 = norm_rows(x_ref[2 * layer + 1])
        n2 = low(scaled2 * gains[2:3] + gains[3:4])
        d_low = low(d_x)
        factor(0, d_low)
        dn_items = [(0, h_ref.at[layer], 0, HID)]
        emit(dn, dn_items)
        load(layer, 1).wait()
        d_hidden = times_plain(d_low, wb_s[:, HID : 2 * HID])
        du_s[...] = low(d_hidden * slope_ref[layer])
        swap.start(2 * layer + 1, times_trans(du_s[...], wb_s[:, 0:HID]))
        factor(1, n2)
        up_items = [(1, du_s, 0, HID)]
        emit(up, up_items)
        later("over_x", dn, dn_items)
        later("over_x", up, up_items)
        if layer == 1:
            load(0, 1).start()
        else:
            later("along_z", "at1")
        d_n2 = swap.total(2 * layer + 1)
        note(4 * layer + 2, d_n2, scaled2)
        d_x = d_x + norm_rows_back(d_n2, scaled2, inv2, gains[2:3])
        d_low = low(d_x)
        factor(2, d_low)
        load(layer, 0).wait()
        d_att = low(times_plain(d_low, wa_s[:, QKV_W:A_COLS]))
        encoder_attention_back(qkv_ref.at[layer], d_att, dqkv_s)
        swap.start(2 * layer, times_trans(dqkv_s[...], wa_s[:, 0:QKV_W]))
        scaled1, inv1 = norm_rows(x_ref[2 * layer])
        factor(3, low(scaled1 * gains[0:1] + gains[1:2]))
        at_items = [(3, dqkv_s, 0, QKV_W), (2, o_ref.at[layer], QKV_W, HALF_D)]
        emit(at, at_items)
        if layer == 1:
            load(0, 0).start()
        later("along_z", dn)
        later("over_x", at, at_items)
        later("along_z", up)
        d_n1 = swap.total(2 * layer)
        note(4 * layer, d_n1, scaled1)
        d_x = d_x + norm_rows_back(d_n1, scaled1, inv1, gains[0:1])
    factor(0, low(d_x))
    emb_items = [(0, px_ref, 0, D)]
    emit("emb", emb_items)
    later("along_z", "at0")
    later("over_x", "emb", emb_items)
    later("along_z", "emb")
    if wide:
        for layer in (1, 0):
            genc_ref[layer, :, DN_AT:ENC_COLS] = scatter.finish(f"dn{layer}")
            genc_ref[layer, :, UP_AT:DN_AT] = scatter.finish(f"up{layer}")
            genc_ref[layer, :, 0:A_COLS] = scatter.finish(f"at{layer}")
        gemb_ref[...] = scatter.finish("emb")
        scatter.drain()
    swapped.wait_send()
    swap.drain()


def run_encoder_back(wide, *operands):
    bf, f32 = jnp.bfloat16, jnp.float32
    vmem = pl.BlockSpec(memory_space=pltpu.VMEM)
    dma = pltpu.SemaphoreType.DMA
    shape = jax.ShapeDtypeStruct
    rows, kind = (SHARD, f32) if wide else (D, bf)
    scratch = [
        pltpu.VMEM((D, A_COLS), bf),
        pltpu.VMEM((D, 2 * HID), bf),
        pltpu.VMEM((PAIR, HID), bf),
        pltpu.VMEM((PAIR, QKV_W), bf),
        pltpu.VMEM((128, D), bf),
        pltpu.VMEM((2 * LAYERS, PAIR, D), bf),
        pltpu.VMEM((2 * LAYERS, PAIR, D), bf),
        dma((LAYERS, 2)),
        dma,
        dma,
        dma((2 * LAYERS,)),
        dma((2 * LAYERS,)),
    ]
    if wide:
        n = len(SUMS)
        scratch += [
            pltpu.VMEM((4, D, PAIR), bf),
            pltpu.VMEM((4, D, PAIR), bf),
            pltpu.VMEM((BLOCKS, SUM_COLS), bf),
            pltpu.VMEM((BLOCKS, SUM_COLS), bf),
            pltpu.VMEM((QUARTER, SUM_COLS), bf),
            pltpu.VMEM((QUARTER, SUM_COLS), bf),
            pltpu.VMEM((3, SHARD, SUM_COLS), bf),
            pltpu.VMEM((3, SHARD, SUM_COLS), bf),
            pltpu.VMEM((QUARTER, SUM_COLS), f32),
            dma((n,)),
            dma((n,)),
            dma((n,)),
            dma((n,)),
            dma((n, 3)),
            dma((n, 3)),
        ]
    return pl.pallas_call(
        functools.partial(encoder_back_body, wide),
        out_shape=(
            shape((LAYERS, rows, ENC_COLS), kind),
            shape((rows, D), kind),
            shape((16, D), f32),
        ),
        in_specs=[vmem] * 8 + [pl.BlockSpec(memory_space=pl.ANY)],
        out_specs=(vmem,) * 3,
        scratch_shapes=scratch,
        compiler_params=pltpu.CompilerParams(
            collective_id=2, has_side_effects=True, vmem_limit_bytes=63 * MIB
        ),
        cost_estimate=pl.CostEstimate(
            flops=20 * 10**9, bytes_accessed=60 * 10**6, transcendentals=10**6
        ),
        name="encoder_back",
    )(*operands)


def adam_at(refs, spot, grad, decay_rate, step_rate):
    master, first, second, master_out, first_out, second_out = refs
    new = adam_update(master[spot], first[spot], second[spot], grad, decay_rate, step_rate)
    master_out[spot], first_out[spot], second_out[spot] = new


def norm_body(loss_ref, gdec_ref, gvec_ref, genc_ref, gemb_ref, gmat_ref, total_ref, *refs):
    f32 = jnp.float32
    send_s, got_s, ss, rs = refs
    place = Place()
    greet(place.mates(True))
    square = jnp.zeros((1, 1), f32)
    for ref in (genc_ref, gemb_ref, gmat_ref):
        whole = ref[...]
        square = square + jnp.sum(whole * whole)
    lane = lane_ids((1, D))
    send_s[0, 0:16, :] = 0.5 * gvec_ref[...]
    send_s[0, 16:24, 0:DD] = gdec_ref[...]
    send_s[0, 16:24, DD:D] = jnp.zeros((8, D - DD), f32)
    send_s[0, 23:24, :] = jnp.where(lane == 0, loss_ref[0:1, 0:1], 0.0) + jnp.where(
        lane == 1, square, 0.0
    )
    copies = []
    stages = [
        [place.core_mate()],
        [place.row_mate()],
        [place.x_mate()],
        [place.z_mate(1), place.z_mate(2), place.z_mate(3)],
    ]
    at = 0
    for i, mates in enumerate(stages):
        here = []
        for mate in mates:
            copy = remote(send_s.at[i], got_s.at[at], ss.at[at], rs.at[at], mate)
            copy.start()
            here.append((copy, at))
            at += 1
        total = send_s[i]
        for copy, spot in here:
            copy.wait_recv()
            total = total + got_s[spot]
        send_s[i + 1] = total
        copies += [copy for copy, _ in here]
    total_ref[...] = send_s[len(stages)]
    for copy in copies:
        copy.wait_send()


def run_norm(*operands):
    f32 = jnp.float32
    vmem = pl.BlockSpec(memory_space=pltpu.VMEM)
    dma = pltpu.SemaphoreType.DMA
    return pl.pallas_call(
        norm_body,
        out_shape=jax.ShapeDtypeStruct((24, D), f32),
        in_specs=[vmem] * len(operands),
        out_specs=vmem,
        scratch_shapes=[
            pltpu.VMEM((5, 24, D), f32),
            pltpu.VMEM((6, 24, D), f32),
            dma((6,)),
            dma((6,)),
        ],
        compiler_params=pltpu.CompilerParams(
            collective_id=3, has_side_effects=True, vmem_limit_bytes=60 * MIB
        ),
        name="norm",
    )(*operands)


def head_pieces(rows, heads):
    pieces = []
    for h in range(heads):
        for part in range(3):
            at = (part * heads + h) * HEAD
            pieces.append(rows[:, at : at + HEAD])
    pieces.append(rows[:, 3 * heads * HEAD :])
    return jnp.concatenate(pieces, axis=-1)


def update_body(*refs):
    f32 = jnp.float32
    total_ref = refs[0]
    grads = refs[1:4]
    states = [refs[4 + 3 * i : 7 + 3 * i] for i in range(5)]
    loss_ref, norm_ref = refs[19:21]
    outs = [refs[21 + 3 * i : 24 + 3 * i] for i in range(5)]
    total = total_ref[...]
    squares = jnp.sum(total[0:23, :] * total[0:23, :]) + jnp.sum(total[23:24, 1:2])
    norm = jnp.sqrt(jnp.zeros((1, 1), f32) + squares)
    factor = jnp.minimum(1.0, CLIP_MAX / (norm + 1e-06))
    loss_ref[0, 0] = jnp.sum(total[23:24, 0:1])
    norm_ref[0, 0] = jnp.sum(norm)
    blocks = SHARD // 8

    @pl.loop(0, LAYERS * blocks)
    def _(i):
        rows = pl.ds(pl.multiple_of(i % blocks * 8, 8), 8)
        grad = head_pieces(grads[0][i // blocks, rows, :], HEADS // 2)
        spot = (i // blocks, 0, rows, slice(None))
        adam_at(states[0] + outs[0], spot, grad * factor, DECAY, RATE)

    adam_at(states[1] + outs[1], (0,), grads[1][...] * factor, DECAY, RATE)
    grad = head_pieces(grads[2][...], DHEADS // 2)
    adam_at(states[2] + outs[2], (0,), grad * factor, DECAY, RATE)
    place = Place()
    own = shard_at(place.z, place.x, place.col)
    for kind, top, count, width in ((3, 0, 10, D), (4, 16, 7, DD)):
        share = width // N_SHARDS
        turned = pltpu.roll(total, (D - own * share) % D, 1)
        grad = turned[top : top + count, 0:share] * factor
        adam_at(states[kind] + outs[kind], (slice(None), slice(None)), grad, 0.0, VEC_RATE)


def run_update(total, grads, states):
    f32 = jnp.float32
    vmem = pl.BlockSpec(memory_space=pltpu.VMEM)
    smem = pl.BlockSpec(memory_space=pltpu.SMEM)
    flat = [a for triple in states for a in triple]
    scalar = jax.ShapeDtypeStruct((1, 1), f32)
    outs = (scalar, scalar) + tuple(jax.ShapeDtypeStruct(a.shape, f32) for a in flat)
    return pl.pallas_call(
        update_body,
        out_shape=outs,
        in_specs=[vmem] * (4 + len(flat)),
        out_specs=(smem, smem) + (vmem,) * len(flat),
        compiler_params=pltpu.CompilerParams(vmem_limit_bytes=60 * MIB),
        name="update",
    )(total, *grads, *flat)


def head_order(matrix, heads, width):
    lead = matrix.shape[:-1]
    cut = matrix[..., :width].reshape(lead + (heads, 3, HEAD))
    cut = jnp.swapaxes(cut, -3, -2).reshape(lead + (width,))
    return jnp.concatenate([cut, matrix[..., width:]], axis=-1)


def head_order_back(matrix, heads, width):
    lead = matrix.shape[:-1]
    cut = matrix[..., :width].reshape(lead + (3, heads, HEAD))
    cut = jnp.swapaxes(cut, -3, -2).reshape(lead + (width,))
    return jnp.concatenate([cut, matrix[..., width:]], axis=-1)


def sine_table(length, width):
    column = np.arange(width)
    freq = np.exp(-math.log(10000.0) * (2.0 * (column // 2)) / width)
    angle = np.arange(length)[:, None] * freq
    table = np.where(column % 2 == 0, np.sin(angle), np.cos(angle))
    return np.pad(table, ((0, ROWS - length), (0, 0))).astype(np.float32)


def frequency_rows(width):
    column = np.arange(width)
    freq = np.exp(-math.log(10000.0) * (2.0 * (column // 2)) / width)
    return np.broadcast_to(freq.astype(np.float32), (8, width))


def gather_vectors(enc_vec, dec_vec, group):
    vectors = jnp.concatenate([enc_vec.reshape(-1), dec_vec.reshape(-1)])
    vectors = lax.all_gather(low(vectors), group, axis=0, tiled=False).astype(jnp.float32)
    cut = enc_vec.size
    enc_gains = jnp.swapaxes(vectors[:, :cut].reshape(-1, *enc_vec.shape), 0, 1).reshape(-1, D)
    dec_gains = jnp.swapaxes(vectors[:, cut:].reshape(-1, *dec_vec.shape), 0, 1).reshape(-1, DD)
    return (
        jnp.pad(enc_gains, ((0, 16 - enc_gains.shape[0]), (0, 0))),
        jnp.pad(dec_gains, ((0, 8 - dec_gains.shape[0]), (0, 0))),
    )


def update_plain(loss_part, dec_vec_grads, enc_vec_grads, grads, states):
    everyone = ("row", "clip", "col")
    n_enc, n_dec = states[3][0].shape[0], states[4][0].shape[0]
    enc_vec_total, dec_vec_total, loss_total, square = lax.psum(
        (
            0.5 * enc_vec_grads[:n_enc],
            dec_vec_grads[:n_dec],
            loss_part,
            sum(jnp.sum(g * g) for g in grads),
        ),
        everyone,
    )
    square = square + jnp.sum(enc_vec_total**2) + jnp.sum(dec_vec_total**2)
    grad_norm = jnp.sqrt(square)
    factor = jnp.minimum(1.0, CLIP_MAX / (grad_norm + 1e-06))
    shard = lax.axis_index("clip") * lax.axis_size("col") + lax.axis_index("col")
    own = []
    for total, state in ((enc_vec_total, states[3][0]), (dec_vec_total, states[4][0])):
        width = state.shape[1]
        own.append(lax.dynamic_slice_in_dim(total, shard * width, width, 1))
    decays = (DECAY, DECAY, DECAY, 0.0, 0.0)
    rates = (RATE, RATE, RATE, VEC_RATE, VEC_RATE)
    results = []
    for triple, grad, decay_rate, step_rate in zip(states, (*grads, *own), decays, rates):
        grad = grad.reshape(triple[0].shape)
        results.extend(adam_update(*triple, grad * factor, decay_rate, step_rate))
    return (loss_total, grad_norm, *results)


def local(
    patches,
    visible,
    masked,
    enc_layers,
    enc_first,
    enc_second,
    embed,
    embed_first,
    embed_second,
    dec_mats,
    dec_first,
    dec_second,
    enc_vec,
    enc_vec_first,
    enc_vec_second,
    dec_vec,
    dec_vec_first,
    dec_vec_second,
):
    f32 = jnp.float32
    group = ("clip", "col")
    everyone = ("row", "clip", "col")
    wide = lax.axis_size("clip") == 8 and lax.axis_size("col") == 2
    dec_full = lax.all_gather(
        low(head_order(dec_mats[0], DHEADS // 2, 3 * DD // 2)), everyone, axis=0, tiled=True
    ).reshape(2, DD, -1)
    freq = jnp.asarray(frequency_rows(D))
    if wide:
        feat, xs, qkv, att, hid, slope, px, padded, enc_gains, dec_gains, enc_full = run_encoder(
            True, visible, patches, freq, embed, enc_layers, enc_vec, dec_vec
        )
    else:
        embed_full = lax.all_gather(low(embed[0]), group, axis=0, tiled=True)
        enc_here = low(head_order(enc_layers[:, 0], HEADS // 2, QKV_W))
        enc_full = lax.all_gather(enc_here, group, axis=1, tiled=True)
        enc_gains, dec_gains = gather_vectors(enc_vec, dec_vec, group)
        feat, xs, qkv, att, hid, slope, px, padded = run_encoder(
            False, visible, patches, freq, embed_full, enc_full, enc_gains
        )
    loss_block, dec_grads, dec_vec_grads, grad_feat = run_decoder(
        visible, feat, padded, jnp.asarray(sine_table(TUBES, DD)), dec_full, dec_gains
    )
    dec_total = lax.psum_scatter(
        dec_grads.reshape(-1, dec_grads.shape[-1]), everyone, scatter_dimension=0, tiled=True
    ).astype(f32)
    enc_total, embed_total, enc_vec_grads = run_encoder_back(
        wide, grad_feat, xs, qkv, att, hid, slope, px, enc_gains, enc_full
    )
    if not wide:
        enc_total = lax.psum_scatter(enc_total, group, scatter_dimension=1, tiled=True).astype(f32)
        embed_total = lax.psum_scatter(embed_total, group, scatter_dimension=0, tiled=True)
        embed_total = embed_total.astype(f32)
    states = (
        (enc_layers, enc_first, enc_second),
        (embed, embed_first, embed_second),
        (dec_mats, dec_first, dec_second),
        (enc_vec, enc_vec_first, enc_vec_second),
        (dec_vec, dec_vec_first, dec_vec_second),
    )
    if wide:
        grads = (enc_total, embed_total, dec_total)
        total = run_norm(loss_block, dec_vec_grads, enc_vec_grads, *grads)
        loss_total, grad_norm, *results = run_update(total, grads, states)
        return (loss_total[0, 0], grad_norm[0, 0], *results)
    grads = (
        head_order_back(enc_total, HEADS // 2, QKV_W),
        embed_total,
        head_order_back(dec_total, DHEADS // 2, 3 * DD // 2),
    )
    return update_plain(loss_block[0, 0], dec_vec_grads, enc_vec_grads, grads, states)


def solution(mesh):
    in_specs = (
        P(None, ("clip", "col"), None, "row"),
        P(None, ("clip", "col"), None),
        P(None, ("clip", "col"), None),
        P(None, "row", ("clip", "col"), None),
        P(None, "row", ("clip", "col"), None),
        P(None, "row", ("clip", "col"), None),
        P("row", ("clip", "col"), None),
        P("row", ("clip", "col"), None),
        P("row", ("clip", "col"), None),
        P("row", ("clip", "col"), None),
        P("row", ("clip", "col"), None),
        P("row", ("clip", "col"), None),
        P(None, ("clip", "col")),
        P(None, ("clip", "col")),
        P(None, ("clip", "col")),
        P(None, ("clip", "col")),
        P(None, ("clip", "col")),
        P(None, ("clip", "col")),
    )
    out_specs = (
        P(),
        P(),
        P(None, "row", ("clip", "col"), None),
        P(None, "row", ("clip", "col"), None),
        P(None, "row", ("clip", "col"), None),
        P("row", ("clip", "col"), None),
        P("row", ("clip", "col"), None),
        P("row", ("clip", "col"), None),
        P("row", ("clip", "col"), None),
        P("row", ("clip", "col"), None),
        P("row", ("clip", "col"), None),
        P(None, ("clip", "col")),
        P(None, ("clip", "col")),
        P(None, ("clip", "col")),
        P(None, ("clip", "col")),
        P(None, ("clip", "col")),
        P(None, ("clip", "col")),
    )
    return jax.shard_map(local, mesh=mesh, in_specs=in_specs, out_specs=out_specs, check_vma=False)
```

```python
import functools
import math

import jax
import jax.numpy as jnp
import numpy as np
from jax import lax
from jax.experimental import pallas as pl
from jax.experimental.pallas import tpu as pltpu
from jax.sharding import PartitionSpec as P

D = 768
HEADS = 12
HEAD = 64
FF = 3072
DD = 384
DHEADS = 6
DFF = 1536
PIX = 1536
TUBES = 1176
VIS = 118
LAYERS = 2
MICRO = 2
STEP = 10
MASKED = 1058


EPS_NORM = 1e-06
CLIP_MAX = 1.0
BETA_ONE = 0.9
BETA_TWO = 0.999
RATE = 0.06
VEC_RATE = 0.2
DECAY = 0.05
EPS_ADAM = 1e-08


def times_plain(left, right):
    return jnp.dot(left, right, preferred_element_type=jnp.float32)


def times_trans(left, right):
    return lax.dot_general(
        left, right, (((1,), (1,)), ((), ())), preferred_element_type=jnp.float32
    )


def trans_times(left, right):
    return lax.dot_general(
        left, right, (((0,), (0,)), ((), ())), preferred_element_type=jnp.float32
    )


def gelu_pair(values):
    cumul = 0.5 * (1.0 + lax.erf(values * 0.7071067811865476))
    density = jnp.exp(-0.5 * values * values) * 0.3989422804014327
    return (values * cumul, cumul + values * density)


def adam_update(master, first, second, grad_clip, decay_rate, step_rate):
    first_new = BETA_ONE * first + (1.0 - BETA_ONE) * grad_clip
    second_new = BETA_TWO * second + (1.0 - BETA_TWO) * grad_clip * grad_clip
    first_hat = first_new / (1.0 - BETA_ONE**STEP)
    second_hat = second_new / (1.0 - BETA_TWO**STEP)
    master_new = master - step_rate * (
        first_hat / (jnp.sqrt(second_hat) + EPS_ADAM) + decay_rate * master
    )
    return (master_new, first_new, second_new)


LOG2E = 1.4426950408889634
SCALE = HEAD ** (-0.5)
MIB = 1 << 20
MESH_IDS = pl.DeviceIdType.MESH
N_SHARDS = 16
SHARD = D // N_SHARDS
PART_ONE = 1024
PART_TWO = 2560
ONE_HALF, TWO_HALF = PART_ONE // 2, PART_TWO // 2
ED_AT = 3 * DD // 2
UP_TWO, DN_TWO, HD_TWO = 256, 1024, 1792


def low(values):
    return values.astype(jnp.bfloat16)


def lane_ids(shape):
    return lax.broadcasted_iota(jnp.int32, shape, len(shape) - 1)


def row_ids(shape):
    return lax.broadcasted_iota(jnp.int32, shape, 0)


def remote(src, dst, send_sem, recv_sem, device):
    return pltpu.make_async_remote_copy(
        src_ref=src,
        dst_ref=dst,
        send_sem=send_sem,
        recv_sem=recv_sem,
        device_id=device,
        device_id_type=MESH_IDS,
    )


class Place:
    def __init__(self):
        self.clip = lax.axis_index("clip")
        self.row = lax.axis_index("row")
        self.col = lax.axis_index("col")
        self.z = self.clip // 2
        self.x = self.clip % 2

    def z_mate(self, step):
        return (((self.z + step) % 4) * 2 + self.x, self.row, self.col)

    def x_mate(self):
        return (self.z * 2 + 1 - self.x, self.row, self.col)

    def core_mate(self):
        return (self.clip, self.row, 1 - self.col)

    def row_mate(self):
        return (self.clip, 1 - self.row, self.col)

    def mates(self, wide):
        near = [self.row_mate()]
        if wide:
            near += [self.core_mate(), self.x_mate()] + [self.z_mate(s) for s in (1, 2, 3)]
        return near


def shard_at(z, x, col):
    return (z * 2 + x) * 2 + col


def greet(mates):
    barrier = pltpu.get_barrier_semaphore()
    for mate in mates:
        pl.semaphore_signal(barrier, inc=1, device_id=mate, device_id_type=MESH_IDS)
    pl.semaphore_wait(barrier, len(mates))


class Mail:
    def __init__(self):
        self.sent = []

    def go(self, src, dst, ss, rs, device, only=None):
        copy = remote(src, dst, ss, rs, device)
        if only is None:
            copy.start()
        else:
            pl.when(only)(copy.start)
        self.sent.append((copy, only))

    def came(self, dst, ss, rs, device):
        remote(dst, dst, ss, rs, device).wait_recv()

    def drain(self):
        for copy, only in self.sent:
            if only is None:
                copy.wait_send()
            else:
                pl.when(only)(copy.wait_send)
        self.sent = []


class Gather(Mail):
    def __init__(self, place, own, spot, sems):
        super().__init__()
        self.at, self.own, self.spot = place, own, spot
        self.z_ss, self.z_rs, self.x_ss, self.x_rs, self.c_ss, self.c_rs = sems

    def begin(self, k):
        at = self.at
        src, dst = self.own(k), self.spot(k, at.z, at.x, at.col)
        for s, only in ((2, None), (1, at.z != 3), (3, at.z != 0)):
            ss, rs = self.z_ss.at[k, s - 1], self.z_rs.at[k, s - 1]
            self.go(src, dst, ss, rs, at.z_mate(s), only)
        self.go(src, dst, self.x_ss.at[k, 0], self.x_rs.at[k, 0], at.x_mate())
        self.go(src, dst, self.c_ss.at[k, 0], self.c_rs.at[k, 0], at.core_mate())

    def forward(self, k):
        at = self.at
        for s in (2, 1, 3):
            spot = self.spot(k, (at.z - s) % 4, at.x, at.col)
            self.came(spot, self.z_ss.at[k, s - 1], self.z_rs.at[k, s - 1], at.z_mate(s))
            if s == 2:
                for step, only in ((3, at.z == 1), (1, at.z == 2)):
                    slot = (2 + step) % 4 - 1
                    ss, rs = self.z_ss.at[k, 3], self.z_rs.at[k, slot]
                    self.go(spot, spot, ss, rs, at.z_mate(step), only)
            self.go(spot, spot, self.x_ss.at[k, s], self.x_rs.at[k, s], at.x_mate())
            self.go(spot, spot, self.c_ss.at[k, s], self.c_rs.at[k, s], at.core_mate())

    def across(self, k):
        at = self.at
        for s in (0, 2, 1, 3):
            spot = self.spot(k, (at.z - s) % 4, 1 - at.x, at.col)
            self.came(spot, self.x_ss.at[k, s], self.x_rs.at[k, s], at.x_mate())
            self.go(spot, spot, self.c_ss.at[k, 4 + s], self.c_rs.at[k, 4 + s], at.core_mate())

    def finish(self, k):
        at = self.at
        for s in range(8):
            x = at.x if s < 4 else 1 - at.x
            spot = self.spot(k, (at.z - s % 4) % 4, x, 1 - at.col)
            self.came(spot, self.c_ss.at[k, s], self.c_rs.at[k, s], at.core_mate())


class LineSum(Mail):
    def __init__(self, place, own, sent, got, ss, rs, rows, into):
        super().__init__()
        self.at, self.own, self.out, self.got, self.ss, self.rs = place, own, sent, got, ss, rs
        self.rows, self.into = rows, into
        self.middle = jnp.logical_or(place.z == 1, place.z == 2)

    def block(self, s):
        return self.own[self.rows * s : self.rows * (s + 1), :]

    def begin(self):
        at = self.at
        self.into[...] = self.block(0)
        for s, end, step in ((1, 3, 3), (3, 0, 1)):
            self.out[s - 1] = low(self.block(s))
            src = self.out.at[s - 1]
            dst = self.got.at[s - 1]
            inner = at.z != end
            self.go(src, dst, self.ss.at[s - 1], self.rs.at[s - 1], at.z_mate(s), inner)
            other = self.got.at[3]
            self.go(src, other, self.ss.at[3], self.rs.at[3], at.z_mate(step), at.z == end)
        outer = jnp.logical_not(self.middle)

        @pl.when(outer)
        def _():
            self.out[1] = low(self.block(2))

        self.go(
            self.out.at[1], self.got.at[1], self.ss.at[1], self.rs.at[1], at.z_mate(2), outer
        )

    def relay(self):
        at = self.at

        @pl.when(self.middle)
        def _():
            self.came(self.got.at[3], self.ss.at[3], self.rs.at[3], at.z_mate(1))
            self.out[1] = low(self.block(2) + self.got[3].astype(jnp.float32))

        self.go(
            self.out.at[1], self.got.at[1], self.ss.at[1], self.rs.at[1], at.z_mate(2), self.middle
        )

    def finish(self):
        at = self.at

        def add(s):
            self.came(self.got.at[s - 1], self.ss.at[s - 1], self.rs.at[s - 1], at.z_mate(s))
            self.into[...] += self.got[s - 1].astype(jnp.float32)

        add(2)
        pl.when(at.z != 0)(lambda: add(1))
        pl.when(at.z != 3)(lambda: add(3))


class Swap:
    def __init__(self, place, sent, got, send_sems, recv_sems):
        self.at, self.sent, self.got = place, sent, got
        self.ss, self.rs = send_sems, recv_sems
        self.copies = {}

    def start(self, i, value):
        self.sent[i] = low(value)
        copy = remote(
            self.sent.at[i], self.got.at[i], self.ss.at[i], self.rs.at[i], self.at.row_mate()
        )
        copy.start()
        self.copies[i] = copy

    def total(self, i):
        self.copies[i].wait_recv()
        return self.sent[i].astype(jnp.float32) + self.got[i].astype(jnp.float32)

    def drain(self):
        for copy in self.copies.values():
            copy.wait_send()


ROWS = 1200
LANES = 1280
STEP_ROWS = 240
N_STEPS = ROWS // STEP_ROWS
KEY_ROWS = 256
N_KEYS = LANES // KEY_ROWS


def norm_rows(rows):
    average = jnp.mean(rows, axis=-1, keepdims=True)
    centred = rows - average
    inv_dev = lax.rsqrt(jnp.mean(centred * centred, axis=-1, keepdims=True) + EPS_NORM)
    return centred * inv_dev, inv_dev


def norm_rows_back(grad_out, scaled, inv_dev, gain_row):
    inner = grad_out * gain_row
    return inv_dev * (
        inner
        - jnp.mean(inner, axis=-1, keepdims=True)
        - scaled * jnp.mean(inner * scaled, axis=-1, keepdims=True)
    )


def column_sum(values):
    return jnp.sum(values, axis=0, keepdims=True)


def decoder_body(wide, *refs):
    bf, f32 = jnp.bfloat16, jnp.float32
    seen_ref, feat_ref, padded_ref, table_ref, one_ref, two_in, vec_ref = refs[:7]
    loss_ref, gone_ref, gtwo_ref, gvec_ref, gfeat_ref = refs[7:12]
    z_s, n1_s, q_s, k_s, v_s, o_s, do_s, dx_s, dqkv_s, dqt_s, lse_s, delta_s = refs[12:24]
    lse_t, delta_t, bias_s, wqkv_s, wo_s, y_s, gqkv_s, go_s, gup_s, gdn_s, ghd_s = refs[24:35]
    gy_s, gv_s, pixel_ref, seen_s, near_sem, far_ss, far_rs = refs[35:42]
    if wide:
        two_s, g_s, cr_s, xs_s, xr_s, c_ss, c_rs, x_ss, x_rs = refs[42:51]
    else:
        two_s, g_s = two_in, gtwo_ref
    place = Place()
    greet(place.mates(wide))

    def chip_rows(s, x):
        return pl.ds(pl.multiple_of(((place.z + s) % 4 * 2 + x) * SHARD, 16), SHARD)

    own_lanes = pl.ds(pl.multiple_of(place.col * TWO_HALF, 128), TWO_HALF)
    other_lanes = pl.ds(pl.multiple_of((1 - place.col) * TWO_HALF, 128), TWO_HALF)
    if wide:

        def spot(k, z, x, col):
            rows = pl.ds(pl.multiple_of((z * 2 + x) * SHARD, 16), SHARD)
            return two_s.at[:, rows, pl.ds(pl.multiple_of(col * TWO_HALF, 128), TWO_HALF)]

        gather = Gather(place, lambda k: two_in, spot, refs[51:57])
        gather.begin(0)
        two_s[:, chip_rows(0, place.x), own_lanes] = two_in[...]

    def tile(i):
        return pl.ds(pl.multiple_of(i * STEP_ROWS, STEP_ROWS), STEP_ROWS)

    def near(i):
        rows = tile(i)
        return pltpu.make_async_copy(
            padded_ref.at[place.row, rows, :], pixel_ref.at[place.row, rows, :], near_sem.at[i]
        )

    def far(i, half):
        rows = tile(i)
        return remote(
            padded_ref.at[1 - place.row, rows, :],
            pixel_ref.at[half, rows, :],
            far_ss.at[i],
            far_rs.at[i],
            place.row_mate(),
        )

    @pl.loop(0, N_STEPS)
    def _(i):
        near(i).start()
        far(i, place.row).start()

    half = 3 * HEAD
    up0, dn0, hd0, ed0 = UP_TWO, DN_TWO, HD_TWO, ED_AT
    vec = vec_ref[...]
    gain1, shift1, gain2, shift2, gain_f, shift_f, token = [vec[i : i + 1] for i in range(7)]

    for part in range(3):
        for r in range(2):
            wqkv_s[:, part * DD + r * half : part * DD + (r + 1) * half] = one_ref[
                r, :, part * half : (part + 1) * half
            ]
    for ref in (q_s, k_s, v_s, do_s):
        ref[ROWS:LANES, :] = jnp.zeros((LANES - ROWS, DD), bf)
    lse_s[ROWS:LANES, :] = jnp.zeros((LANES - ROWS, 128), f32)
    delta_s[ROWS:LANES, :] = jnp.zeros((LANES - ROWS, 128), f32)
    bias_s[...] = jnp.where(row_ids((LANES, 128)) < TUBES, 0.0, -1e30)
    for ref in (gqkv_s, go_s, gup_s, gdn_s, ghd_s, gy_s, gv_s):
        ref[...] = jnp.zeros(ref.shape, f32)
    for r in range(2):
        y_s[:, r * DD : (r + 1) * DD] = low(
            times_trans(feat_ref[:, r * DD : (r + 1) * DD], one_ref[r, :, ed0 : ed0 + DD])
        )
    seen_s[...] = jnp.full(seen_s.shape, -1, jnp.int32)
    seen_s[0:1, 0:VIS] = seen_ref[place.row]
    seen = seen_s[0:1, :]

    def picks(i):
        ids = row_ids((STEP_ROWS, 128)) + i * STEP_ROWS
        hits = ids == seen
        taken = jnp.sum(hits.astype(f32), axis=-1, keepdims=True)
        valid = (row_ids((STEP_ROWS, 1)) + i * STEP_ROWS < TUBES).astype(f32)
        return hits.astype(bf), valid - taken

    @pl.loop(0, N_STEPS)
    def _(i):
        hits, hidden = picks(i)
        placed = times_plain(hits, y_s[...])
        z = placed[:, :DD] + placed[:, DD:] + table_ref[tile(i), :] + token * hidden
        z_s[tile(i), :] = z
        scaled, _ = norm_rows(z)
        n1 = low(scaled * gain1 + shift1)
        n1_s[tile(i), :] = n1
        q_s[tile(i), :] = low(times_plain(n1, wqkv_s[:, 0:DD]))
        k_s[tile(i), :] = low(times_plain(n1, wqkv_s[:, DD : 2 * DD]))
        v_s[tile(i), :] = low(times_plain(n1, wqkv_s[:, 2 * DD : 3 * DD]))

    first_half = lane_ids((1, 128)) < HEAD
    key_lanes = lane_ids((1, LANES)) < TUBES
    half_masks = [first_half, jnp.logical_not(first_half)]

    if wide:
        gather.forward(0)
    for p in range(3):
        lanes = slice(128 * p, 128 * (p + 1))

        @pl.loop(0, N_STEPS)
        def _(i):
            queries = q_s[tile(i), lanes]
            parts = []
            stat = lse_s[tile(i), :]
            for h in range(2):
                one = jnp.where(half_masks[h], queries, jnp.zeros_like(queries))
                scores = times_trans(one, k_s[:, lanes])
                scores = jnp.where(key_lanes, scores, -1e30)
                top = jnp.max(scores, axis=-1, keepdims=True) * (SCALE * LOG2E)
                weights = jnp.exp2(scores * (SCALE * LOG2E) - top)
                total = jnp.sum(weights, axis=-1, keepdims=True)
                parts.append(times_plain(low(weights), v_s[:, lanes]) / total)
                lse = top + jnp.log(total) * LOG2E
                stat = jnp.where(lane_ids((1, 128)) == 2 * p + h, lse, stat)
            lse_s[tile(i), :] = stat
            o_s[tile(i), lanes] = low(jnp.where(first_half, parts[0], parts[1]))

        if wide and p < 2:
            (gather.across, gather.finish)[p](0)

    for r in range(2):
        wo_s[:, r * half : (r + 1) * half] = two_s[r, :, 0:half]
    lse_t[...] = lse_s[...].T

    @pl.loop(0, N_STEPS)
    def _(i):
        _, hidden = picks(i)
        near(i).wait()
        far(i, 1 - place.row).wait_recv()
        attended = o_s[tile(i), :]
        x1 = z_s[tile(i), :] + times_trans(attended, wo_s[...])
        scaled2, inv2 = norm_rows(x1)
        n2 = low(scaled2 * gain2 + shift2)
        x2 = x1
        acts, slopes = [], []
        for r in range(2):
            u = times_plain(n2, two_s[r, :, up0 : up0 + 768])
            act, slope = gelu_pair(u)
            act = low(act)
            acts.append(act)
            slopes.append(slope)
            x2 = x2 + times_trans(act, two_s[r, :, dn0 : dn0 + 768])
        scaled_f, inv_f = norm_rows(x2)
        t = low(scaled_f * gain_f + shift_f)
        d_t = jnp.zeros((STEP_ROWS, DD), f32)
        for r in range(2):
            error = times_plain(t, two_s[r, :, hd0 : hd0 + 768]) - pixel_ref[r, tile(i), :].astype(
                f32
            )
            error = error * hidden
            gv_s[7:8, :] += column_sum(error * error)
            d_pred = low(error * (2.0 / PIX))
            ghd_s[r] += trans_times(t, d_pred)
            d_t = d_t + times_trans(d_pred, two_s[r, :, hd0 : hd0 + 768])
        gv_s[4:5, 0:DD] += column_sum(d_t * scaled_f)
        gv_s[5:6, 0:DD] += column_sum(d_t)
        d_x2 = norm_rows_back(d_t, scaled_f, inv_f, gain_f)
        d_low = low(d_x2)
        d_n2 = jnp.zeros((STEP_ROWS, DD), f32)
        for r in range(2):
            gdn_s[r] += trans_times(d_low, acts[r])
            d_u = low(times_plain(d_low, two_s[r, :, dn0 : dn0 + 768]) * slopes[r])
            gup_s[r] += trans_times(n2, d_u)
            d_n2 = d_n2 + times_trans(d_u, two_s[r, :, up0 : up0 + 768])
        gv_s[2:3, 0:DD] += column_sum(d_n2 * scaled2)
        gv_s[3:4, 0:DD] += column_sum(d_n2)
        d_x1 = d_x2 + norm_rows_back(d_n2, scaled2, inv2, gain2)
        dx_s[tile(i), :] = d_x1
        d_low = low(d_x1)
        go_s[...] += trans_times(d_low, attended)
        d_o = low(times_plain(d_low, wo_s[...]))
        do_s[tile(i), :] = d_o
        both = d_o.astype(f32) * attended.astype(f32)
        stat = jnp.zeros((STEP_ROWS, 128), f32)
        for p in range(3):
            pair = both[:, 128 * p : 128 * (p + 1)]
            for h in range(2):
                one = jnp.sum(jnp.where(half_masks[h], pair, 0.0), axis=-1, keepdims=True)
                stat = jnp.where(lane_ids((1, 128)) == 2 * p + h, one, stat)
        delta_s[tile(i), :] = stat

    for r in range(2):
        g_s[r, :, 0:half] = low(go_s[:, r * half : (r + 1) * half])
        g_s[r, :, half:up0] = jnp.zeros((DD, up0 - half), bf)
        g_s[r, :, up0 : up0 + 768] = low(gup_s[r])
        g_s[r, :, dn0 : dn0 + 768] = low(gdn_s[r])
        g_s[r, :, hd0 : hd0 + 768] = low(ghd_s[r])
    if wide:
        to_core = remote(g_s.at[:, :, other_lanes], cr_s, c_ss, c_rs, place.core_mate())
        to_core.start()
        to_x = remote(xs_s, xr_s, x_ss, x_rs, place.x_mate())
    delta_t[...] = delta_s[...].T

    for p in range(3):
        lanes = slice(128 * p, 128 * (p + 1))
        dqt_s[...] = jnp.zeros(dqt_s.shape, f32)

        @pl.loop(0, N_KEYS)
        def _(j):
            rows = pl.ds(pl.multiple_of(j * KEY_ROWS, KEY_ROWS), KEY_ROWS)
            keys = k_s[rows, lanes]
            values = v_s[rows, lanes]
            bias = bias_s[rows, 0:1]
            d_keys, d_values = [], []
            for h in range(2):
                key_one = jnp.where(half_masks[h], keys, jnp.zeros_like(keys))
                value_one = jnp.where(half_masks[h], values, jnp.zeros_like(values))
                lse = lse_t[2 * p + h : 2 * p + h + 1, :]
                delta = delta_t[2 * p + h : 2 * p + h + 1, :]
                scores = times_trans(key_one, q_s[:, lanes])
                soft = jnp.exp2((scores * (SCALE * LOG2E) + bias) - lse)
                d_soft = times_trans(value_one, do_s[:, lanes])
                d_scores = low(soft * (d_soft - delta))
                d_values.append(times_plain(low(soft), do_s[:, lanes]))
                d_keys.append(times_plain(d_scores, q_s[:, lanes]))
                dqt_s[...] += trans_times(key_one, d_scores)
            k_out = slice(DD + 128 * p, DD + 128 * (p + 1))
            v_out = slice(2 * DD + 128 * p, 2 * DD + 128 * (p + 1))
            dqkv_s[rows, k_out] = low(jnp.where(first_half, d_keys[0], d_keys[1]) * SCALE)
            dqkv_s[rows, v_out] = low(jnp.where(first_half, d_values[0], d_values[1]))

        dqkv_s[:, lanes] = low(dqt_s[...].T * SCALE)
        if wide and p == 0:
            to_core.wait_recv()
            for s in range(4):
                rows = chip_rows(s, 1 - place.x)
                xs_s[s] = low(g_s[:, rows, own_lanes].astype(f32) + cr_s[:, rows, :].astype(f32))
            to_x.start()

    @pl.loop(0, N_STEPS)
    def _(i):
        hits, hidden = picks(i)
        d_qkv = dqkv_s[tile(i), :]
        gqkv_s[...] += trans_times(n1_s[tile(i), :], d_qkv)
        d_n1 = times_trans(d_qkv, wqkv_s[...])
        scaled1, inv1 = norm_rows(z_s[tile(i), :])
        gv_s[0:1, 0:DD] += column_sum(d_n1 * scaled1)
        gv_s[1:2, 0:DD] += column_sum(d_n1)
        d_z = dx_s[tile(i), :] + norm_rows_back(d_n1, scaled1, inv1, gain1)
        gv_s[6:7, 0:DD] += column_sum(d_z * hidden)
        gy_s[...] += trans_times(hits, low(d_z))

    d_y = low(gy_s[...])
    for r in range(2):
        gone_ref[r, :, ed0 : ed0 + DD] = low(trans_times(d_y, feat_ref[:, r * DD : (r + 1) * DD]))
        gone_ref[r, :, ed0 + DD : PART_ONE] = jnp.zeros((DD, PART_ONE - ed0 - DD), bf)
        gfeat_ref[:, r * DD : (r + 1) * DD] = low(times_plain(d_y, one_ref[r, :, ed0 : ed0 + DD]))
        for part in range(3):
            gone_ref[r, :, part * half : (part + 1) * half] = low(
                gqkv_s[:, part * DD + r * half : part * DD + (r + 1) * half]
            )
    if wide:
        to_x.wait_recv()
        for s in range(4):
            rows = chip_rows(s, place.x)
            total = g_s[:, rows, own_lanes].astype(f32) + cr_s[:, rows, :].astype(f32)
            total = total + xr_s[s].astype(f32)
            for r in range(2):
                at = (2 * s + r) * SHARD
                gtwo_ref[at : at + SHARD, :] = total[r]
        to_core.wait_send()
        to_x.wait_send()
        gather.drain()
    gvec_ref[...] = gv_s[:, 0:DD]

    @pl.loop(0, N_STEPS)
    def _(i):
        far(i, place.row).wait_send()

    loss_ref[...] = jnp.zeros((8, 128), f32) + jnp.sum(gv_s[7:8, :]) / PIX


def run_decoder(wide, *operands):
    bf, f32 = jnp.bfloat16, jnp.float32
    vmem = pl.BlockSpec(memory_space=pltpu.VMEM)
    dma = pltpu.SemaphoreType.DMA
    if wide:
        two = jax.ShapeDtypeStruct((8 * SHARD, TWO_HALF), f32)
    else:
        two = jax.ShapeDtypeStruct((2, DD, PART_TWO), bf)
    scratch = [
        pltpu.VMEM((ROWS, DD), f32),
        pltpu.VMEM((ROWS, DD), bf),
        pltpu.VMEM((LANES, DD), bf),
        pltpu.VMEM((LANES, DD), bf),
        pltpu.VMEM((LANES, DD), bf),
        pltpu.VMEM((ROWS, DD), bf),
        pltpu.VMEM((LANES, DD), bf),
        pltpu.VMEM((ROWS, DD), f32),
        pltpu.VMEM((LANES, 3 * DD), bf),
        pltpu.VMEM((128, LANES), f32),
        pltpu.VMEM((LANES, 128), f32),
        pltpu.VMEM((LANES, 128), f32),
        pltpu.VMEM((128, LANES), f32),
        pltpu.VMEM((128, LANES), f32),
        pltpu.VMEM((LANES, 128), f32),
        pltpu.VMEM((DD, 3 * DD), bf),
        pltpu.VMEM((DD, DD), bf),
        pltpu.VMEM((128, 2 * DD), bf),
        pltpu.VMEM((DD, 3 * DD), f32),
        pltpu.VMEM((DD, DD), f32),
        pltpu.VMEM((2, DD, 768), f32),
        pltpu.VMEM((2, DD, 768), f32),
        pltpu.VMEM((2, DD, 768), f32),
        pltpu.VMEM((128, DD), f32),
        pltpu.VMEM((8, 768), f32),
        pltpu.VMEM((2, ROWS, PIX // 2), bf),
        pltpu.VMEM((8, 128), jnp.int32),
        dma((N_STEPS,)),
        dma((N_STEPS,)),
        dma((N_STEPS,)),
    ]
    if wide:
        scratch += [
            pltpu.VMEM((2, DD, PART_TWO), bf),
            pltpu.VMEM((2, DD, PART_TWO), bf),
            pltpu.VMEM((2, DD, TWO_HALF), bf),
            pltpu.VMEM((4, 2, SHARD, TWO_HALF), bf),
            pltpu.VMEM((4, 2, SHARD, TWO_HALF), bf),
            dma,
            dma,
            dma,
            dma,
        ]
        scratch += [dma((1, 4)), dma((1, 3)), dma((1, 4)), dma((1, 4)), dma((1, 8)), dma((1, 8))]
    return pl.pallas_call(
        functools.partial(decoder_body, wide),
        out_shape=(
            jax.ShapeDtypeStruct((8, 128), f32),
            jax.ShapeDtypeStruct((2, DD, PART_ONE), bf),
            two,
            jax.ShapeDtypeStruct((8, DD), f32),
            jax.ShapeDtypeStruct((128, D), bf),
        ),
        in_specs=[vmem, vmem, pl.BlockSpec(memory_space=pl.ANY), vmem, vmem, vmem, vmem],
        out_specs=(vmem,) * 5,
        scratch_shapes=scratch,
        compiler_params=pltpu.CompilerParams(
            collective_id=4, has_side_effects=True, vmem_limit_bytes=63 * MIB
        ),
        cost_estimate=pl.CostEstimate(
            flops=30 * 10**9, bytes_accessed=20 * 10**6, transcendentals=20 * 10**6
        ),
        name="decoder",
    )(*operands)


PAIR = 256
HALF_D = D // 2
QKV_W = 3 * D // 2
HID = FF // 2
A_COLS = QKV_W + D // 2
ENC_COLS = A_COLS + 2 * HID
UP_AT, DN_AT = A_COLS, A_COLS + HID
EMB_ROWS = SHARD + 16
GATHERS = (
    (-1, 0, D),
    (0, 0, A_COLS),
    (0, A_COLS, 2 * HID),
    (1, 0, A_COLS),
    (1, A_COLS, 2 * HID),
    (-2, 0, PART_ONE),
)
PART_ONE_AT = len(GATHERS) - 1


def half_lanes():
    first = lane_ids((1, 128)) < HEAD
    return [first, jnp.logical_not(first)]


def same_clip():
    a, b = row_ids((PAIR, PAIR)), lane_ids((PAIR, PAIR))
    return jnp.logical_and(a // 128 == b // 128, b % 128 < VIS)


def encoder_scores(queries, keys, allowed):
    scores = jnp.where(allowed, times_trans(queries, keys), -1e30)
    top = jnp.max(scores, axis=-1, keepdims=True) * (SCALE * LOG2E)
    weights = jnp.exp2(scores * (SCALE * LOG2E) - top)
    return weights, jnp.sum(weights, axis=-1, keepdims=True)


def encoder_attention(qkv_ref, out_ref):
    allowed = same_clip()
    halves = half_lanes()
    for p in range(3):
        q = qkv_ref[:, 128 * p : 128 * (p + 1)]
        k = qkv_ref[:, HALF_D + 128 * p : HALF_D + 128 * (p + 1)]
        v = qkv_ref[:, 2 * HALF_D + 128 * p : 2 * HALF_D + 128 * (p + 1)]
        parts = []
        for h in range(2):
            one = jnp.where(halves[h], q, jnp.zeros_like(q))
            weights, total = encoder_scores(one, k, allowed)
            parts.append(times_plain(low(weights), v) / total)
        out_ref[:, 128 * p : 128 * (p + 1)] = low(jnp.where(halves[0], parts[0], parts[1]))


def pack_heads(dst, src, heads):
    for part in range(3):
        for h in range(heads):
            at = (part * heads + h) * HEAD
            dst[:, at : at + HEAD] = low(src[:, (3 * h + part) * HEAD : (3 * h + part + 1) * HEAD])


def encoder_body(wide, *refs):
    f32 = jnp.float32
    if wide:
        seen_ref, pixel_ref, freq_ref, emb_ref, enc_ref, dec_ref, evec_ref, dvec_ref = refs[:8]
        refs = refs[8:]
    else:
        seen_ref, pixel_ref, freq_ref, emb_full, w_s, gain_in = refs[:6]
        refs = refs[6:]
    feat_ref, x_ref, qkv_ref, o_ref, h_ref, slope_ref, px_ref, padded_out = refs[:8]
    refs = refs[8:]
    if wide:
        gain_ref, dgain_ref, w_out, one_out, two_out = refs[:5]
        emb_s, w_s, embc_s, emb_in, enc_in, small_s, one_s, two_s, block_s = refs[5:14]
        refs = refs[14:]
    sent_s, got_s, padded_s, seen_s, pad_sem, y_ss, y_rs = refs[:7]
    refs = refs[7:]
    place = Place()
    greet(place.mates(wide))
    swap = Swap(place, sent_s, got_s, y_ss, y_rs)
    if wide:

        def own_part(k):
            layer, start, width = GATHERS[k]
            if layer == -1:
                return emb_in
            if layer == -2:
                return spot(k, place.z, place.x, place.col)
            return enc_in.at[layer, :, pl.ds(start, width)]

        def spot(k, z, x, col):
            layer, start, width = GATHERS[k]
            if layer == -2:
                rows = pl.ds(pl.multiple_of((z * 2 + x) * SHARD, 16), SHARD)
                return one_s.at[:, rows, pl.ds(pl.multiple_of(col * ONE_HALF, 128), ONE_HALF)]
            rows = EMB_ROWS if layer < 0 else SHARD
            first = pl.multiple_of(shard_at(z, x, col) * rows, 16)
            if layer == -1:
                return emb_s.at[pl.ds(first, rows), :]
            return w_s.at[layer, pl.ds(first, rows), pl.ds(start, width)]

        gather = Gather(place, own_part, spot, refs[:6])
        keep_sem, block_ss, block_rs, seed_ss, seed_rs = refs[6:11]
        emb_in[0:SHARD, :] = low(emb_ref[0])
        small_s[...] = jnp.zeros(small_s.shape, f32)
        small_s[0:10, 0:SHARD] = evec_ref[...]
        small_s[0:7, SHARD : SHARD + DD // N_SHARDS] = dvec_ref[...]
        emb_in[SHARD:EMB_ROWS, 0:128] = low(small_s[...])
        emb_in[SHARD:EMB_ROWS, 128:D] = jnp.zeros((EMB_ROWS - SHARD, D - 128), jnp.bfloat16)
        gather.begin(0)
        for layer in range(LAYERS):
            pack_heads(enc_in.at[layer], enc_ref.at[layer, 0], HEADS // 2)
            enc_in[layer, :, QKV_W:] = low(enc_ref[layer, 0, :, QKV_W:])
            if layer == 0:
                gather.begin(1)
                gather.begin(2)
        own = shard_at(place.z, place.x, place.col)
        emb_s[pl.ds(pl.multiple_of(own * EMB_ROWS, 16), EMB_ROWS), :] = emb_in[...]
        for layer in range(LAYERS):
            w_s[layer, pl.ds(pl.multiple_of(own * SHARD, 16), SHARD), :] = enc_in[layer]
        mine = pl.ds(pl.multiple_of(place.col * (SHARD // 2), 8), SHARD // 2)
        block_s[mine, :] = jnp.zeros((SHARD // 2, PART_ONE + PART_TWO), f32)
        shard = dec_ref[0]
        heads = DHEADS // 2
        for part in range(3):
            for h in range(heads):
                at = (3 * h + part) * HEAD
                to = (part * heads + h) * HEAD
                block_s[mine, to : to + HEAD] = shard[:, at : at + HEAD]
        block_s[mine, ED_AT : ED_AT + DD] = shard[:, 3072:3456]
        block_s[mine, PART_ONE : PART_ONE + 192] = shard[:, ED_AT:768]
        block_s[mine, PART_ONE + UP_TWO : PART_ONE + PART_TWO] = shard[:, 768:3072]
        spread = remote(
            block_s.at[mine, :], block_s.at[mine, :], block_ss, block_rs, place.core_mate()
        )
        spread.start()
        theirs = pl.ds(pl.multiple_of((1 - place.col) * (SHARD // 2), 8), SHARD // 2)
        half_one = spot(PART_ONE_AT, place.z, place.x, place.col)
        seeds = [
            remote(part.at[place.row], part.at[place.row], ss, rs, place.row_mate())
            for part, ss, rs in (
                (half_one, seed_ss.at[0], seed_rs.at[0]),
                (two_s, seed_ss.at[1], seed_rs.at[1]),
            )
        ]
        seeds_back = [
            remote(part.at[1 - place.row], part.at[1 - place.row], ss, rs, place.row_mate())
            for part, ss, rs in (
                (half_one, seed_ss.at[0], seed_rs.at[0]),
                (two_s, seed_ss.at[1], seed_rs.at[1]),
            )
        ]

    def step(name, k):
        if wide:
            getattr(gather, name)(k)

    odd = (lane_ids((1, D)) % 2).astype(f32) * (0.5 * math.pi)
    freq = freq_ref[0:1, :]
    places = []
    seen_s[...] = jnp.full(seen_s.shape, -1, jnp.int32)
    whole = TUBES // 16 * 16
    for m in range(MICRO):
        seen_s[m : m + 1, 0:VIS] = seen_ref[m]
        row = seen_s[m : m + 1, :]
        hits = (row_ids((TUBES, 128)) == row).astype(jnp.bfloat16)
        px_ref[128 * m : 128 * (m + 1), :] = low(trans_times(hits, pixel_ref[m, 0]))
        column = jnp.broadcast_to(row.astype(f32), (128, 128)).T[:, 0:1]
        places.append(jnp.sin(column * freq + odd))
        padded_s[m, 0:whole, :] = pixel_ref[m, 0, 0:whole, :]
        rest = pixel_ref[m, 0, whole:TUBES, :].astype(f32)
        rest = jnp.concatenate([rest, jnp.zeros((ROWS - TUBES, D), f32)], axis=0)
        padded_s[m, whole:ROWS, :] = low(rest)
    pad_copy = pltpu.make_async_copy(padded_s, padded_out, pad_sem)
    pad_copy.start()

    if wide:
        gather.forward(0)
        gather.across(0)
        gather.finish(0)
        for s in range(N_SHARDS):
            embc_s[SHARD * s : SHARD * (s + 1), :] = emb_s[EMB_ROWS * s : EMB_ROWS * s + SHARD, :]
            tail = emb_s[EMB_ROWS * s + SHARD : EMB_ROWS * (s + 1), 0:128].astype(f32)
            gain_ref[:, SHARD * s : SHARD * (s + 1)] = tail[:, 0:SHARD]
            dgain_ref[:, DD // 16 * s : DD // 16 * (s + 1)] = tail[0:8, SHARD : SHARD + DD // 16]
        emb_full, gain_in = embc_s, gain_ref
    swap.start(0, times_trans(px_ref[...], emb_full[...]))
    if wide:
        other_rows = block_s.at[theirs, :]
        remote(other_rows, other_rows, block_ss, block_rs, place.core_mate()).wait_recv()
        lanes = pl.ds(pl.multiple_of(place.col * ONE_HALF, 128), ONE_HALF)
        half_one.at[place.row][...] = low(block_s[:, lanes])
        lanes = pl.ds(pl.multiple_of(PART_ONE + place.col * TWO_HALF, 128), TWO_HALF)
        two_s[place.row] = low(block_s[:, lanes])
        for copy in seeds:
            copy.start()
    step("forward", 1)
    step("begin", 3)
    step("across", 1)
    x = swap.total(0) + jnp.concatenate(places, axis=0)
    for layer in range(LAYERS):
        gains = gain_in[4 * layer : 4 * layer + 4, :]
        x_ref[2 * layer] = x
        scaled, _ = norm_rows(x)
        n1 = low(scaled * gains[0:1] + gains[1:2])
        step("finish", 1 + 2 * layer)
        qkv_ref[layer] = low(times_plain(n1, w_s[layer, :, 0:QKV_W]))
        encoder_attention(qkv_ref.at[layer], o_ref.at[layer])
        swap.start(1 + 2 * layer, times_trans(o_ref[layer], w_s[layer, :, QKV_W:A_COLS]))
        step("forward", 2 + 2 * layer)
        if layer == 0:
            step("begin", 4)
            if wide:
                for copy in seeds_back:
                    copy.wait_recv()
            step("begin", PART_ONE_AT)
        step("across", 2 + 2 * layer)
        x = x + swap.total(1 + 2 * layer)
        x_ref[2 * layer + 1] = x
        scaled, _ = norm_rows(x)
        n2 = low(scaled * gains[2:3] + gains[3:4])
        step("finish", 2 + 2 * layer)
        if wide:
            keep = pltpu.make_async_copy(w_s.at[layer], w_out.at[layer], keep_sem.at[layer])
            keep.start()
        act, slope = gelu_pair(times_plain(n2, w_s[layer, :, UP_AT:DN_AT]))
        act = low(act)
        h_ref[layer] = act
        slope_ref[layer] = slope
        swap.start(2 + 2 * layer, times_trans(act, w_s[layer, :, DN_AT:ENC_COLS]))
        ahead = 3 if layer == 0 else PART_ONE_AT
        step("forward", ahead)
        step("across", ahead)
        x = x + swap.total(2 + 2 * layer)
    x_ref[2 * LAYERS] = x
    scaled, _ = norm_rows(x)
    gains = gain_in[4 * LAYERS : 4 * LAYERS + 2, :]
    feat = low(scaled * gains[0:1] + gains[1:2])
    feat_ref[...] = jnp.where(place.row == 0, feat[0:128], feat[128:256])
    swap.drain()
    pad_copy.wait()
    if wide:
        two_out[...] = two_s[...]
        gather.finish(PART_ONE_AT)
        one_copy = pltpu.make_async_copy(one_s, one_out, keep_sem.at[LAYERS])
        one_copy.start()
        spread.wait_send()
        for copy in seeds:
            copy.wait_send()
        gather.drain()
        one_copy.wait()
        for layer in range(LAYERS):
            pltpu.make_async_copy(w_s.at[layer], w_out.at[layer], keep_sem.at[layer]).wait()


def run_encoder(wide, *operands):
    bf, f32 = jnp.bfloat16, jnp.float32
    vmem = pl.BlockSpec(memory_space=pltpu.VMEM)
    dma = pltpu.SemaphoreType.DMA
    shape = jax.ShapeDtypeStruct
    n_swaps = 1 + 2 * LAYERS
    outs = [
        shape((128, D), bf),
        shape((2 * LAYERS + 1, PAIR, D), f32),
        shape((LAYERS, PAIR, QKV_W), bf),
        shape((LAYERS, PAIR, HALF_D), bf),
        shape((LAYERS, PAIR, HID), bf),
        shape((LAYERS, PAIR, HID), f32),
        shape((PAIR, D), bf),
        shape((MICRO, ROWS, D), bf),
    ]
    out_specs = [vmem] * (len(outs) - 1) + [pl.BlockSpec(memory_space=pl.ANY)]
    scratch = []
    if wide:
        anywhere = pl.BlockSpec(memory_space=pl.ANY)
        outs += [
            shape((16, D), f32),
            shape((8, DD), f32),
            shape((LAYERS, D, ENC_COLS), bf),
            shape((2, DD, PART_ONE), bf),
            shape((2, SHARD, TWO_HALF), bf),
        ]
        out_specs += [vmem, vmem, anywhere, anywhere, vmem]
        scratch += [
            pltpu.VMEM((N_SHARDS * EMB_ROWS, D), bf),
            pltpu.VMEM((LAYERS, D, ENC_COLS), bf),
            pltpu.VMEM((D, D), bf),
            pltpu.VMEM((EMB_ROWS, D), bf),
            pltpu.VMEM((LAYERS, SHARD, ENC_COLS), bf),
            pltpu.VMEM((16, 128), f32),
            pltpu.VMEM((2, DD, PART_ONE), bf),
            pltpu.VMEM((2, SHARD, TWO_HALF), bf),
            pltpu.VMEM((SHARD, PART_ONE + PART_TWO), f32),
        ]
    scratch += [
        pltpu.VMEM((n_swaps, PAIR, D), bf),
        pltpu.VMEM((n_swaps, PAIR, D), bf),
        pltpu.VMEM((MICRO, ROWS, D), bf),
        pltpu.VMEM((8, 128), jnp.int32),
        dma,
        dma((n_swaps,)),
        dma((n_swaps,)),
    ]
    if wide:
        n = len(GATHERS)
        scratch += [dma((n, 4)), dma((n, 3)), dma((n, 4)), dma((n, 4)), dma((n, 8)), dma((n, 8))]
        scratch += [dma((LAYERS + 1,)), dma, dma, dma((2,)), dma((2,))]
    return pl.pallas_call(
        functools.partial(encoder_body, wide),
        out_shape=tuple(outs),
        in_specs=[vmem] * len(operands),
        out_specs=tuple(out_specs),
        scratch_shapes=scratch,
        compiler_params=pltpu.CompilerParams(
            collective_id=1, has_side_effects=True, vmem_limit_bytes=60 * MIB
        ),
        cost_estimate=pl.CostEstimate(
            flops=10 * 10**9, bytes_accessed=60 * 10**6, transcendentals=10**6
        ),
        name="encoder",
    )(*operands)


SUMS = (
    ("dn1", HID),
    ("up1", HID),
    ("at1", A_COLS),
    ("dn0", HID),
    ("up0", HID),
    ("at0", A_COLS),
    ("emb", D),
)
SUM_AT = {name: sum(w for _, w in SUMS[:i]) for i, (name, _) in enumerate(SUMS)}
SUM_COLS = sum(w for _, w in SUMS)
BLOCKS = N_SHARDS // 2 * SHARD
QUARTER = BLOCKS // 2


class Scatter(Mail):
    def __init__(self, place, bufs, sems, into):
        super().__init__()
        self.at, self.into = place, into
        self.perm, self.flip, self.cs, self.cr, self.xs, self.xr, self.zs, self.zr, self.own = bufs
        self.c_ss, self.c_rs, self.x_ss, self.x_rs, self.z_ss, self.z_rs = sems
        self.last = {}
        self.lines = {}

    def span(self, name, shift=0, width=None):
        k = [n for n, _ in SUMS].index(name)
        return k, pl.ds(SUM_AT[name] + shift, SUMS[k][1] if width is None else width)

    def post(self, src, dst, ss, rs, device, key):
        copy = remote(src, dst, ss, rs, device)
        copy.start()
        self.last[key] = copy

    def free(self, key):
        if key in self.last:
            self.last.pop(key).wait_send()

    def turn(self, slot, left):
        at = self.at
        flip = self.flip.at[slot % 2]
        flip[...] = left.T
        order = [
            (s, x, c) for c, x in ((1, 1), (1, 0), (0, 1), (0, 0)) for s in range(4)
        ]
        for i, (s, other_x, other_c) in enumerate(order):
            x = 1 - at.x if other_x else at.x
            c = 1 - at.col if other_c else at.col
            first = pl.multiple_of(shard_at((at.z + s) % 4, x, c) * SHARD, 16)
            self.perm[slot, SHARD * i : SHARD * (i + 1), :] = flip[pl.ds(first, SHARD), :]

    def cores(self, name, items):
        k, span = self.span(name)
        slot_at, width = k % 2, SUMS[k][1]
        self.free(("core", slot_at))
        for slot, right, shift, wide in items:
            self.cs[slot_at, :, shift : shift + wide] = low(
                times_plain(self.perm[slot, 0:BLOCKS, :], right[...])
            )
        self.post(
            self.cs.at[slot_at, :, pl.ds(0, width)],
            self.cr.at[:, span],
            self.c_ss.at[k],
            self.c_rs.at[k],
            self.at.core_mate(),
            ("core", slot_at),
        )

    def over_x(self, name, items):
        f32 = jnp.float32
        k, whole = self.span(name)
        slot_at, width = k % 3, SUMS[k][1]
        self.free(("x", slot_at))
        self.came(self.cr.at[:, whole], self.c_ss.at[k], self.c_rs.at[k], self.at.core_mate())
        for slot, right, shift, wide in items:
            _, span = self.span(name, shift, wide)
            mine = times_plain(self.perm[slot, BLOCKS : BLOCKS + QUARTER, :], right[...])
            self.xs[slot_at, :, shift : shift + wide] = low(
                mine + self.cr[0:QUARTER, span].astype(f32)
            )
        self.post(
            self.xs.at[slot_at, :, pl.ds(0, width)],
            self.xr.at[:, whole],
            self.x_ss.at[k],
            self.x_rs.at[k],
            self.at.x_mate(),
            ("x", slot_at),
        )
        for slot, right, shift, wide in items:
            _, span = self.span(name, shift, wide)
            mine = times_plain(self.perm[slot, BLOCKS + QUARTER : 2 * BLOCKS, :], right[...])
            self.own[k % 4, :, shift : shift + wide] = mine + self.cr[QUARTER:BLOCKS, span].astype(f32)

    def along_z(self, name):
        k, span = self.span(name)
        self.came(self.xr.at[:, span], self.x_ss.at[k], self.x_rs.at[k], self.at.x_mate())
        own = self.own.at[k % 4, :, pl.ds(0, SUMS[k][1])]
        own[...] += self.xr[:, span].astype(jnp.float32)
        line = LineSum(
            self.at,
            own,
            self.zs.at[:, :, span],
            self.zr.at[:, :, span],
            self.z_ss.at[k],
            self.z_rs.at[k],
            SHARD,
            self.into(name),
        )
        line.begin()
        self.lines[name] = line

    def relay(self, name):
        self.lines[name].relay()

    def finish(self, name):
        self.lines[name].finish()

    def drain(self):
        for copy in self.last.values():
            copy.wait_send()
        for line in self.lines.values():
            line.drain()


class DecoderScatter(Mail):
    def __init__(self, place, one, two, out, bufs, sems):
        super().__init__()
        self.at, self.one, self.two, self.out = place, one, two, out
        self.cr, self.xs, self.xr, self.own, self.zs1, self.zr1, self.zs2, self.zr2 = bufs[:8]
        self.fin, self.ys, self.yr, self.whole, self.part = bufs[8:]
        (
            self.c_ss, self.c_rs, self.x_ss, self.x_rs, self.z1_ss, self.z1_rs,
            self.z2_ss, self.z2_rs, self.y_ss, self.y_rs, self.f_ss, self.f_rs,
        ) = sems
        self.lanes = pl.ds(pl.multiple_of(place.col * ONE_HALF, 128), ONE_HALF)

    def rows(self, s, x):
        return pl.ds(pl.multiple_of(((self.at.z + s) % 4 * 2 + x) * SHARD, 16), SHARD)

    def begin(self):
        at = self.at
        others = pl.ds(pl.multiple_of((1 - at.col) * ONE_HALF, 128), ONE_HALF)
        src = self.one.at[:, :, others]
        self.go(src, self.cr, self.c_ss, self.c_rs, at.core_mate())
        self.line_two = LineSum(
            at, self.two, self.zs2, self.zr2, self.z2_ss, self.z2_rs, 2 * SHARD,
            self.fin.at[:, pl.ds(ONE_HALF, TWO_HALF)],
        )
        self.line_two.begin()

    def sums(self, s, x):
        rows = self.rows(s, x)
        f32 = jnp.float32
        return self.one[:, rows, self.lanes].astype(f32) + self.cr[:, rows, :].astype(f32)

    def over_x(self):
        at = self.at
        self.came(self.cr, self.c_ss, self.c_rs, at.core_mate())
        for s in range(4):
            self.xs[s] = low(self.sums(s, 1 - at.x))
        self.go(self.xs, self.xr, self.x_ss, self.x_rs, at.x_mate())

    def along_z(self):
        at = self.at
        self.came(self.xr, self.x_ss, self.x_rs, at.x_mate())
        for s in range(4):
            total = self.sums(s, at.x) + self.xr[s].astype(jnp.float32)
            for r in range(2):
                first = (2 * s + r) * SHARD
                self.own[first : first + SHARD, :] = total[r]
        self.line_one = LineSum(
            at, self.own, self.zs1, self.zr1, self.z1_ss, self.z1_rs, 2 * SHARD,
            self.fin.at[:, pl.ds(0, ONE_HALF)],
        )
        self.line_one.begin()

    def over_rows(self):
        at = self.at
        self.line_one.finish()
        self.line_two.finish()
        rows = pl.ds(pl.multiple_of((1 - at.row) * SHARD, 8), SHARD)
        self.ys[...] = low(self.fin[rows, :])
        self.go(self.ys, self.yr, self.y_ss, self.y_rs, at.row_mate())

    def to_cores(self):
        at = self.at
        self.came(self.yr, self.y_ss, self.y_rs, at.row_mate())
        rows = pl.ds(pl.multiple_of(at.row * SHARD, 8), SHARD)
        self.whole[...] = self.fin[rows, :] + self.yr[...].astype(jnp.float32)
        theirs = pl.ds(pl.multiple_of((1 - at.col) * (SHARD // 2), 8), SHARD // 2)
        self.go(self.whole.at[theirs, :], self.part, self.f_ss, self.f_rs, at.core_mate())

    def finish(self):
        at = self.at
        width = ONE_HALF + TWO_HALF
        mine = pl.ds(pl.multiple_of(at.col * (SHARD // 2), 8), SHARD // 2)
        self.out[:, pl.ds(pl.multiple_of(at.col * width, 128), width)] = self.whole[mine, :]
        self.came(self.part, self.f_ss, self.f_rs, at.core_mate())
        self.out[:, pl.ds(pl.multiple_of((1 - at.col) * width, 128), width)] = self.part[...]

    def drain(self):
        super().drain()
        self.line_one.drain()
        self.line_two.drain()


def encoder_attention_back(qkv_ref, d_out, out_ref):
    allowed = same_clip()
    halves = half_lanes()
    for p in range(3):
        spans = [slice(part * HALF_D + 128 * p, part * HALF_D + 128 * (p + 1)) for part in range(3)]
        q, k, v = (qkv_ref[:, span] for span in spans)
        d_pair = d_out[:, 128 * p : 128 * (p + 1)]
        found = []
        for h in range(2):
            one = jnp.where(halves[h], q, jnp.zeros_like(q))
            weights, total = encoder_scores(one, k, allowed)
            soft = weights / total
            d_one = jnp.where(halves[h], d_pair, jnp.zeros_like(d_pair))
            d_soft = times_trans(d_one, v)
            delta = jnp.sum(soft * d_soft, axis=-1, keepdims=True)
            d_scores = low(soft * (d_soft - delta))
            found.append(
                (
                    times_plain(d_scores, k) * SCALE,
                    trans_times(d_scores, q) * SCALE,
                    trans_times(low(soft), d_pair),
                )
            )
        for part in range(3):
            out_ref[:, spans[part]] = low(jnp.where(halves[0], found[0][part], found[1][part]))


def encoder_back_body(wide, *refs):
    f32 = jnp.float32
    gfeat_ref, x_ref, qkv_ref, o_ref, h_ref, slope_ref, px_ref, gain_ref, w_ref = refs[:9]
    refs = refs[9:]
    if wide:
        one_ref, two_ref = refs[:2]
        refs = refs[2:]
    genc_ref, gemb_ref, gvec_ref = refs[:3]
    refs = refs[3:]
    if wide:
        gdec_ref = refs[0]
        refs = refs[1:]
    wa_s, wb_s, du_s, dqkv_s, feat_s, sent_s, got_s, h_s, slope_s = refs[:9]
    load_sem, f_ss, f_rs, y_ss, y_rs = refs[9:14]
    refs = refs[14:]
    place = Place()
    greet(place.mates(wide))
    swap = Swap(place, sent_s, got_s, y_ss, y_rs)
    swapped = remote(gfeat_ref, feat_s, f_ss, f_rs, place.row_mate())
    swapped.start()

    def into(name):
        if name == "emb":
            return gemb_ref
        start, width = {"at": (0, A_COLS), "up": (UP_AT, HID), "dn": (DN_AT, HID)}[name[:2]]
        return genc_ref.at[int(name[2]), :, pl.ds(start, width)]

    scatter = Scatter(place, refs[:9], refs[9:15], into) if wide else None
    dec = DecoderScatter(place, one_ref, two_ref, gdec_ref, refs[15:28], refs[28:40]) if wide else None

    def load(layer, part):
        src, dst = (
            (w_ref.at[layer, :, pl.ds(0, A_COLS)], wa_s),
            (w_ref.at[layer, :, pl.ds(A_COLS, 2 * HID)], wb_s),
            (h_ref.at[layer], h_s),
            (slope_ref.at[layer], slope_s),
        )[part]
        return pltpu.make_async_copy(src, dst, load_sem.at[layer, part])

    load(1, 2).start()
    load(1, 3).start()
    load(1, 1).start()
    load(1, 0).start()

    lefts = {}

    def factor(slot, left):
        lefts[slot] = left
        if wide:
            scatter.turn(slot, left)

    def emit(name, items):
        if wide:
            scatter.cores(name, items)
            return
        for slot, right, shift, width in items:
            value = low(trans_times(lefts[slot], right[...]))
            if name == "emb":
                gemb_ref[...] = value
                continue
            start = {"at": 0, "up": UP_AT, "dn": DN_AT}[name[:2]] + shift
            genc_ref[int(name[2]), :, start : start + width] = value

    def later(step, *args):
        if wide:
            getattr(scatter, step)(*args)

    def dec_step(step):
        if wide:
            getattr(dec, step)()

    dec_step("begin")
    swapped.wait_recv()
    near, far = gfeat_ref[...].astype(f32), feat_s[...].astype(f32)
    first = place.row == 0
    grad = jnp.concatenate([jnp.where(first, near, far), jnp.where(first, far, near)], axis=0)
    gvec_ref[...] = jnp.zeros(gvec_ref.shape, f32)

    def note(row, grad_out, scaled):
        gvec_ref[row : row + 1, :] = column_sum(grad_out * scaled)
        gvec_ref[row + 1 : row + 2, :] = column_sum(grad_out)

    scaled, inv = norm_rows(x_ref[2 * LAYERS])
    note(4 * LAYERS, grad, scaled)
    d_x = norm_rows_back(grad, scaled, inv, gain_ref[4 * LAYERS : 4 * LAYERS + 1, :])
    for layer in (1, 0):
        gains = gain_ref[4 * layer : 4 * layer + 4, :]
        dn, up, at = (f"{kind}{layer}" for kind in ("dn", "up", "at"))
        scaled2, inv2 = norm_rows(x_ref[2 * layer + 1])
        n2 = low(scaled2 * gains[2:3] + gains[3:4])
        d_low = low(d_x)
        factor(0, d_low)
        dn_items = [(0, h_s, 0, HID)]
        load(layer, 2).wait()
        emit(dn, dn_items)
        load(layer, 3).wait()
        load(layer, 1).wait()
        d_hidden = times_plain(d_low, wb_s[:, HID : 2 * HID])
        du_s[...] = low(d_hidden * slope_s[...])
        swap.start(2 * layer + 1, times_trans(du_s[...], wb_s[:, 0:HID]))
        factor(1, n2)
        up_items = [(1, du_s, 0, HID)]
        emit(up, up_items)
        later("over_x", dn, dn_items)
        later("over_x", up, up_items)
        if layer == 1:
            load(0, 2).start()
            load(0, 3).start()
            load(0, 1).start()
            dec_step("over_x")
            if wide:
                dec.line_two.relay()
        else:
            later("along_z", "at1")
            later("relay", "up1")
        d_n2 = swap.total(2 * layer + 1)
        note(4 * layer + 2, d_n2, scaled2)
        d_x = d_x + norm_rows_back(d_n2, scaled2, inv2, gains[2:3])
        d_low = low(d_x)
        factor(2, d_low)
        load(layer, 0).wait()
        d_att = low(times_plain(d_low, wa_s[:, QKV_W:A_COLS]))
        encoder_attention_back(qkv_ref.at[layer], d_att, dqkv_s)
        swap.start(2 * layer, times_trans(dqkv_s[...], wa_s[:, 0:QKV_W]))
        scaled1, inv1 = norm_rows(x_ref[2 * layer])
        factor(3, low(scaled1 * gains[0:1] + gains[1:2]))
        at_items = [(3, dqkv_s, 0, QKV_W), (2, o_ref.at[layer], QKV_W, HALF_D)]
        emit(at, at_items)
        if layer == 1:
            load(0, 0).start()
            dec_step("along_z")
        else:
            later("relay", "at1")
        later("along_z", dn)
        later("over_x", at, at_items)
        later("along_z", up)
        later("relay", dn)
        if layer == 1:
            if wide:
                dec.line_one.relay()
        d_n1 = swap.total(2 * layer)
        note(4 * layer, d_n1, scaled1)
        d_x = d_x + norm_rows_back(d_n1, scaled1, inv1, gains[0:1])
    factor(0, low(d_x))
    emb_items = [(0, px_ref, 0, D)]
    emit("emb", emb_items)
    later("relay", "up0")
    later("over_x", "emb", emb_items)
    dec_step("over_rows")
    later("along_z", "at0")
    dec_step("to_cores")
    later("along_z", "emb")
    later("relay", "at0")
    later("relay", "emb")
    if wide:
        dec.finish()
        for name, _ in SUMS:
            scatter.finish(name)
        scatter.drain()
        dec.drain()
    swapped.wait_send()
    swap.drain()


def run_encoder_back(wide, *operands):
    bf, f32 = jnp.bfloat16, jnp.float32
    vmem = pl.BlockSpec(memory_space=pltpu.VMEM)
    dma = pltpu.SemaphoreType.DMA
    shape = jax.ShapeDtypeStruct
    rows, kind = (SHARD, f32) if wide else (D, bf)
    scratch = [
        pltpu.VMEM((D, A_COLS), bf),
        pltpu.VMEM((D, 2 * HID), bf),
        pltpu.VMEM((PAIR, HID), bf),
        pltpu.VMEM((PAIR, QKV_W), bf),
        pltpu.VMEM((128, D), bf),
        pltpu.VMEM((2 * LAYERS, PAIR, D), bf),
        pltpu.VMEM((2 * LAYERS, PAIR, D), bf),
        pltpu.VMEM((PAIR, HID), bf),
        pltpu.VMEM((PAIR, HID), f32),
        dma((LAYERS, 4)),
        dma,
        dma,
        dma((2 * LAYERS,)),
        dma((2 * LAYERS,)),
    ]
    outs = [
        shape((LAYERS, rows, ENC_COLS), kind),
        shape((rows, D), kind),
        shape((16, D), f32),
    ]
    anywhere = pl.BlockSpec(memory_space=pl.ANY)
    in_specs = [vmem] * 4 + [anywhere] * 2 + [vmem] * 2 + [anywhere]
    if wide:
        outs.append(shape((SHARD // 2, PART_ONE + PART_TWO), f32))
        in_specs += [vmem, vmem]
        n = len(SUMS)
        both = ONE_HALF + TWO_HALF
        scratch += [
            pltpu.VMEM((4, D, PAIR), bf),
            pltpu.VMEM((2, D, PAIR), bf),
            pltpu.VMEM((2, BLOCKS, HID), bf),
            pltpu.VMEM((BLOCKS, SUM_COLS), bf),
            pltpu.VMEM((3, QUARTER, HID), bf),
            pltpu.VMEM((QUARTER, SUM_COLS), bf),
            pltpu.VMEM((3, SHARD, SUM_COLS), bf),
            pltpu.VMEM((4, SHARD, SUM_COLS), bf),
            pltpu.VMEM((4, QUARTER, HID), f32),
            dma((n,)),
            dma((n,)),
            dma((n,)),
            dma((n,)),
            dma((n, 4)),
            dma((n, 4)),
            pltpu.VMEM((2, DD, ONE_HALF), bf),
            pltpu.VMEM((4, 2, SHARD, ONE_HALF), bf),
            pltpu.VMEM((4, 2, SHARD, ONE_HALF), bf),
            pltpu.VMEM((8 * SHARD, ONE_HALF), f32),
            pltpu.VMEM((3, 2 * SHARD, ONE_HALF), bf),
            pltpu.VMEM((4, 2 * SHARD, ONE_HALF), bf),
            pltpu.VMEM((3, 2 * SHARD, TWO_HALF), bf),
            pltpu.VMEM((4, 2 * SHARD, TWO_HALF), bf),
            pltpu.VMEM((2 * SHARD, both), f32),
            pltpu.VMEM((SHARD, both), bf),
            pltpu.VMEM((SHARD, both), bf),
            pltpu.VMEM((SHARD, both), f32),
            pltpu.VMEM((SHARD // 2, both), f32),
            dma,
            dma,
            dma,
            dma,
            dma((4,)),
            dma((4,)),
            dma((4,)),
            dma((4,)),
            dma,
            dma,
            dma,
            dma,
        ]
    return pl.pallas_call(
        functools.partial(encoder_back_body, wide),
        out_shape=tuple(outs),
        in_specs=in_specs,
        out_specs=(vmem,) * len(outs),
        scratch_shapes=scratch,
        compiler_params=pltpu.CompilerParams(
            collective_id=2, has_side_effects=True, vmem_limit_bytes=63 * MIB
        ),
        cost_estimate=pl.CostEstimate(
            flops=20 * 10**9, bytes_accessed=60 * 10**6, transcendentals=10**6
        ),
        name="encoder_back",
    )(*operands)


def adam_at(refs, spot, grad, decay_rate, step_rate):
    master, first, second, master_out, first_out, second_out = refs
    new = adam_update(master[spot], first[spot], second[spot], grad, decay_rate, step_rate)
    master_out[spot], first_out[spot], second_out[spot] = new


def norm_body(loss_ref, gdec_ref, gvec_ref, genc_ref, gemb_ref, gmat_ref, total_ref, *refs):
    f32 = jnp.float32
    send_s, got_s, ss, rs = refs
    place = Place()
    greet(place.mates(True))
    square = jnp.zeros((1, 1), f32)
    for ref in (genc_ref, gemb_ref, gmat_ref):
        whole = ref[...]
        square = square + jnp.sum(whole * whole)
    lane = lane_ids((1, D))
    send_s[0, 0:16, :] = 0.5 * gvec_ref[...]
    send_s[0, 16:24, 0:DD] = gdec_ref[...]
    send_s[0, 16:24, DD:D] = jnp.zeros((8, D - DD), f32)
    send_s[0, 23:24, :] = jnp.where(lane == 0, loss_ref[0:1, 0:1], 0.0) + jnp.where(
        lane == 1, square, 0.0
    )
    copies = []
    stages = [
        [place.core_mate()],
        [place.row_mate()],
        [place.x_mate()],
        [place.z_mate(1), place.z_mate(2), place.z_mate(3)],
    ]
    at = 0
    for i, mates in enumerate(stages):
        here = []
        for mate in mates:
            copy = remote(send_s.at[i], got_s.at[at], ss.at[at], rs.at[at], mate)
            copy.start()
            here.append((copy, at))
            at += 1
        total = send_s[i]
        for copy, spot in here:
            copy.wait_recv()
            total = total + got_s[spot]
        send_s[i + 1] = total
        copies += [copy for copy, _ in here]
    total_ref[...] = send_s[len(stages)]
    for copy in copies:
        copy.wait_send()


def run_norm(*operands):
    f32 = jnp.float32
    vmem = pl.BlockSpec(memory_space=pltpu.VMEM)
    dma = pltpu.SemaphoreType.DMA
    return pl.pallas_call(
        norm_body,
        out_shape=jax.ShapeDtypeStruct((24, D), f32),
        in_specs=[vmem] * len(operands),
        out_specs=vmem,
        scratch_shapes=[
            pltpu.VMEM((5, 24, D), f32),
            pltpu.VMEM((6, 24, D), f32),
            dma((6,)),
            dma((6,)),
        ],
        compiler_params=pltpu.CompilerParams(
            collective_id=3, has_side_effects=True, vmem_limit_bytes=60 * MIB
        ),
        name="norm",
    )(*operands)


def head_pieces(rows, heads):
    pieces = []
    for h in range(heads):
        for part in range(3):
            at = (part * heads + h) * HEAD
            pieces.append(rows[:, at : at + HEAD])
    pieces.append(rows[:, 3 * heads * HEAD :])
    return jnp.concatenate(pieces, axis=-1)


def update_body(*refs):
    f32 = jnp.float32
    total_ref = refs[0]
    grads = refs[1:4]
    states = [refs[4 + 3 * i : 7 + 3 * i] for i in range(5)]
    loss_ref, norm_ref = refs[19:21]
    outs = [refs[21 + 3 * i : 24 + 3 * i] for i in range(5)]
    total = total_ref[...]
    squares = jnp.sum(total[0:23, :] * total[0:23, :]) + jnp.sum(total[23:24, 1:2])
    norm = jnp.sqrt(jnp.zeros((1, 1), f32) + squares)
    factor = jnp.minimum(1.0, CLIP_MAX / (norm + 1e-06))
    loss_ref[0, 0] = jnp.sum(total[23:24, 0:1])
    norm_ref[0, 0] = jnp.sum(norm)
    blocks = SHARD // 8

    @pl.loop(0, LAYERS * blocks)
    def _(i):
        rows = pl.ds(pl.multiple_of(i % blocks * 8, 8), 8)
        grad = head_pieces(grads[0][i // blocks, rows, :], HEADS // 2)
        spot = (i // blocks, 0, rows, slice(None))
        adam_at(states[0] + outs[0], spot, grad * factor, DECAY, RATE)

    adam_at(states[1] + outs[1], (0,), grads[1][...] * factor, DECAY, RATE)
    both = ONE_HALF + TWO_HALF
    grad = grads[2][...]
    one = jnp.concatenate([grad[:, 0:ONE_HALF], grad[:, both : both + ONE_HALF]], axis=-1)
    two = jnp.concatenate([grad[:, ONE_HALF:both], grad[:, both + ONE_HALF :]], axis=-1)
    pieces = [one[:, 0:ED_AT], two[:, 0:192], two[:, UP_TWO:], one[:, ED_AT : ED_AT + DD]]
    grad = head_pieces(jnp.concatenate(pieces, axis=-1), DHEADS // 2)
    adam_at(states[2] + outs[2], (0,), grad * factor, DECAY, RATE)
    place = Place()
    own = shard_at(place.z, place.x, place.col)
    for kind, top, count, width in ((3, 0, 10, D), (4, 16, 7, DD)):
        share = width // N_SHARDS
        turned = pltpu.roll(total, (D - own * share) % D, 1)
        grad = turned[top : top + count, 0:share] * factor
        adam_at(states[kind] + outs[kind], (slice(None), slice(None)), grad, 0.0, VEC_RATE)


def run_update(total, grads, states):
    f32 = jnp.float32
    vmem = pl.BlockSpec(memory_space=pltpu.VMEM)
    smem = pl.BlockSpec(memory_space=pltpu.SMEM)
    flat = [a for triple in states for a in triple]
    scalar = jax.ShapeDtypeStruct((1, 1), f32)
    outs = (scalar, scalar) + tuple(jax.ShapeDtypeStruct(a.shape, f32) for a in flat)
    return pl.pallas_call(
        update_body,
        out_shape=outs,
        in_specs=[vmem] * (4 + len(flat)),
        out_specs=(smem, smem) + (vmem,) * len(flat),
        compiler_params=pltpu.CompilerParams(vmem_limit_bytes=60 * MIB),
        name="update",
    )(total, *grads, *flat)


def head_order(matrix, heads, width):
    lead = matrix.shape[:-1]
    cut = matrix[..., :width].reshape(lead + (heads, 3, HEAD))
    cut = jnp.swapaxes(cut, -3, -2).reshape(lead + (width,))
    return jnp.concatenate([cut, matrix[..., width:]], axis=-1)


def head_order_back(matrix, heads, width):
    lead = matrix.shape[:-1]
    cut = matrix[..., :width].reshape(lead + (3, heads, HEAD))
    cut = jnp.swapaxes(cut, -3, -2).reshape(lead + (width,))
    return jnp.concatenate([cut, matrix[..., width:]], axis=-1)


def sine_table(length, width):
    column = np.arange(width)
    freq = np.exp(-math.log(10000.0) * (2.0 * (column // 2)) / width)
    angle = np.arange(length)[:, None] * freq
    table = np.where(column % 2 == 0, np.sin(angle), np.cos(angle))
    return np.pad(table, ((0, ROWS - length), (0, 0))).astype(np.float32)


def frequency_rows(width):
    column = np.arange(width)
    freq = np.exp(-math.log(10000.0) * (2.0 * (column // 2)) / width)
    return np.broadcast_to(freq.astype(np.float32), (8, width))


def split_parts(matrices):
    gap = [(0, 0)] * (matrices.ndim - 1)
    one = jnp.concatenate([matrices[..., :ED_AT], matrices[..., 3072:]], axis=-1)
    one = jnp.pad(one, gap + [(0, PART_ONE - one.shape[-1])])
    out = jnp.pad(matrices[..., ED_AT:768], gap + [(0, UP_TWO - 192)])
    return one, jnp.concatenate([out, matrices[..., 768:3072]], axis=-1)


def join_parts(one, two):
    return jnp.concatenate(
        [one[..., :ED_AT], two[..., :192], two[..., UP_TWO:], one[..., ED_AT : ED_AT + DD]], axis=-1
    )


def gather_vectors(enc_vec, dec_vec, group):
    vectors = jnp.concatenate([enc_vec.reshape(-1), dec_vec.reshape(-1)])
    vectors = lax.all_gather(low(vectors), group, axis=0, tiled=False).astype(jnp.float32)
    cut = enc_vec.size
    enc_gains = jnp.swapaxes(vectors[:, :cut].reshape(-1, *enc_vec.shape), 0, 1).reshape(-1, D)
    dec_gains = jnp.swapaxes(vectors[:, cut:].reshape(-1, *dec_vec.shape), 0, 1).reshape(-1, DD)
    return (
        jnp.pad(enc_gains, ((0, 16 - enc_gains.shape[0]), (0, 0))),
        jnp.pad(dec_gains, ((0, 8 - dec_gains.shape[0]), (0, 0))),
    )


def update_plain(loss_part, dec_vec_grads, enc_vec_grads, grads, states):
    everyone = ("row", "clip", "col")
    n_enc, n_dec = states[3][0].shape[0], states[4][0].shape[0]
    enc_vec_total, dec_vec_total, loss_total, square = lax.psum(
        (
            0.5 * enc_vec_grads[:n_enc],
            dec_vec_grads[:n_dec],
            loss_part,
            sum(jnp.sum(g * g) for g in grads),
        ),
        everyone,
    )
    square = square + jnp.sum(enc_vec_total**2) + jnp.sum(dec_vec_total**2)
    grad_norm = jnp.sqrt(square)
    factor = jnp.minimum(1.0, CLIP_MAX / (grad_norm + 1e-06))
    shard = lax.axis_index("clip") * lax.axis_size("col") + lax.axis_index("col")
    own = []
    for total, state in ((enc_vec_total, states[3][0]), (dec_vec_total, states[4][0])):
        width = state.shape[1]
        own.append(lax.dynamic_slice_in_dim(total, shard * width, width, 1))
    decays = (DECAY, DECAY, DECAY, 0.0, 0.0)
    rates = (RATE, RATE, RATE, VEC_RATE, VEC_RATE)
    results = []
    for triple, grad, decay_rate, step_rate in zip(states, (*grads, *own), decays, rates):
        grad = grad.reshape(triple[0].shape)
        results.extend(adam_update(*triple, grad * factor, decay_rate, step_rate))
    return (loss_total, grad_norm, *results)


def local(
    patches,
    visible,
    masked,
    enc_layers,
    enc_first,
    enc_second,
    embed,
    embed_first,
    embed_second,
    dec_mats,
    dec_first,
    dec_second,
    enc_vec,
    enc_vec_first,
    enc_vec_second,
    dec_vec,
    dec_vec_first,
    dec_vec_second,
):
    f32 = jnp.float32
    group = ("clip", "col")
    everyone = ("row", "clip", "col")
    wide = lax.axis_size("clip") == 8 and lax.axis_size("col") == 2
    freq = jnp.asarray(frequency_rows(D))
    table = jnp.asarray(sine_table(TUBES, DD))
    if wide:
        feat, xs, qkv, att, hid, slope, px, padded, enc_gains, dec_gains, enc_full, one, two = (
            run_encoder(True, visible, patches, freq, embed, enc_layers, dec_mats, enc_vec, dec_vec)
        )
    else:
        embed_full = lax.all_gather(low(embed[0]), group, axis=0, tiled=True)
        enc_here = low(head_order(enc_layers[:, 0], HEADS // 2, QKV_W))
        enc_full = lax.all_gather(enc_here, group, axis=1, tiled=True)
        dec_here = low(head_order(dec_mats[0], DHEADS // 2, ED_AT))
        dec_full = lax.all_gather(dec_here, everyone, axis=0, tiled=True).reshape(2, DD, -1)
        enc_gains, dec_gains = gather_vectors(enc_vec, dec_vec, group)
        feat, xs, qkv, att, hid, slope, px, padded = run_encoder(
            False, visible, patches, freq, embed_full, enc_full, enc_gains
        )
        one, two = split_parts(dec_full)
    loss_block, grad_one, grad_two, dec_vec_grads, grad_feat = run_decoder(
        wide, visible, feat, padded, table, one, two, dec_gains
    )
    kept = (grad_feat, xs, qkv, att, hid, slope, px, enc_gains, enc_full)
    states = (
        (enc_layers, enc_first, enc_second),
        (embed, embed_first, embed_second),
        (dec_mats, dec_first, dec_second),
        (enc_vec, enc_vec_first, enc_vec_second),
        (dec_vec, dec_vec_first, dec_vec_second),
    )
    if wide:
        *grads, enc_vec_grads, dec_total = run_encoder_back(True, *kept, grad_one, grad_two)
        grads.append(dec_total)
        total = run_norm(loss_block, dec_vec_grads, enc_vec_grads, *grads)
        loss_total, grad_norm, *results = run_update(total, grads, states)
        return (loss_total[0, 0], grad_norm[0, 0], *results)
    dec_grads = join_parts(grad_one, grad_two)
    dec_total = lax.psum_scatter(
        dec_grads.reshape(-1, dec_grads.shape[-1]), everyone, scatter_dimension=0, tiled=True
    ).astype(f32)
    enc_total, embed_total, enc_vec_grads = run_encoder_back(False, *kept)
    enc_total = lax.psum_scatter(enc_total, group, scatter_dimension=1, tiled=True).astype(f32)
    embed_total = lax.psum_scatter(embed_total, group, scatter_dimension=0, tiled=True).astype(f32)
    grads = (
        head_order_back(enc_total, HEADS // 2, QKV_W),
        embed_total,
        head_order_back(dec_total, DHEADS // 2, ED_AT),
    )
    return update_plain(loss_block[0, 0], dec_vec_grads, enc_vec_grads, grads, states)


def solution(mesh):
    in_specs = (
        P(None, ("clip", "col"), None, "row"),
        P(None, ("clip", "col"), None),
        P(None, ("clip", "col"), None),
        P(None, "row", ("clip", "col"), None),
        P(None, "row", ("clip", "col"), None),
        P(None, "row", ("clip", "col"), None),
        P("row", ("clip", "col"), None),
        P("row", ("clip", "col"), None),
        P("row", ("clip", "col"), None),
        P("row", ("clip", "col"), None),
        P("row", ("clip", "col"), None),
        P("row", ("clip", "col"), None),
        P(None, ("clip", "col")),
        P(None, ("clip", "col")),
        P(None, ("clip", "col")),
        P(None, ("clip", "col")),
        P(None, ("clip", "col")),
        P(None, ("clip", "col")),
    )
    out_specs = (
        P(),
        P(),
        P(None, "row", ("clip", "col"), None),
        P(None, "row", ("clip", "col"), None),
        P(None, "row", ("clip", "col"), None),
        P("row", ("clip", "col"), None),
        P("row", ("clip", "col"), None),
        P("row", ("clip", "col"), None),
        P("row", ("clip", "col"), None),
        P("row", ("clip", "col"), None),
        P("row", ("clip", "col"), None),
        P(None, ("clip", "col")),
        P(None, ("clip", "col")),
        P(None, ("clip", "col")),
        P(None, ("clip", "col")),
        P(None, ("clip", "col")),
        P(None, ("clip", "col")),
    )
    return jax.shard_map(local, mesh=mesh, in_specs=in_specs, out_specs=out_specs, check_vma=False)
```

```python
import functools
import math

import jax
import jax.numpy as jnp
import numpy as np
from jax import lax
from jax.experimental import pallas as pl
from jax.experimental.pallas import tpu as pltpu
from jax.sharding import PartitionSpec as P

D = 768
HEADS = 12
HEAD = 64
FF = 3072
DD = 384
DHEADS = 6
DFF = 1536
PIX = 1536
TUBES = 1176
VIS = 118
LAYERS = 2
MICRO = 2
STEP = 10
MASKED = 1058


EPS_NORM = 1e-06
CLIP_MAX = 1.0
BETA_ONE = 0.9
BETA_TWO = 0.999
RATE = 0.06
VEC_RATE = 0.2
DECAY = 0.05
EPS_ADAM = 1e-08


def times_plain(left, right):
    return jnp.dot(left, right, preferred_element_type=jnp.float32)


def times_trans(left, right):
    return lax.dot_general(
        left, right, (((1,), (1,)), ((), ())), preferred_element_type=jnp.float32
    )


def trans_times(left, right):
    return lax.dot_general(
        left, right, (((0,), (0,)), ((), ())), preferred_element_type=jnp.float32
    )


def gelu_pair(values):
    cumul = 0.5 * (1.0 + lax.erf(values * 0.7071067811865476))
    density = jnp.exp(-0.5 * values * values) * 0.3989422804014327
    return (values * cumul, cumul + values * density)


def adam_update(master, first, second, grad_clip, decay_rate, step_rate):
    first_new = BETA_ONE * first + (1.0 - BETA_ONE) * grad_clip
    second_new = BETA_TWO * second + (1.0 - BETA_TWO) * grad_clip * grad_clip
    first_hat = first_new / (1.0 - BETA_ONE**STEP)
    second_hat = second_new / (1.0 - BETA_TWO**STEP)
    master_new = master - step_rate * (
        first_hat / (jnp.sqrt(second_hat) + EPS_ADAM) + decay_rate * master
    )
    return (master_new, first_new, second_new)


LOG2E = 1.4426950408889634
SCALE = HEAD ** (-0.5)
MIB = 1 << 20
MESH_IDS = pl.DeviceIdType.MESH
N_SHARDS = 16
SHARD = D // N_SHARDS
PART_ONE = 1024
PART_TWO = 2560
ONE_HALF, TWO_HALF = PART_ONE // 2, PART_TWO // 2
ED_AT = 3 * DD // 2
UP_TWO, DN_TWO, HD_TWO = 256, 1024, 1792


def low(values):
    return values.astype(jnp.bfloat16)


def lane_ids(shape):
    return lax.broadcasted_iota(jnp.int32, shape, len(shape) - 1)


def row_ids(shape):
    return lax.broadcasted_iota(jnp.int32, shape, 0)


def remote(src, dst, send_sem, recv_sem, device):
    return pltpu.make_async_remote_copy(
        src_ref=src,
        dst_ref=dst,
        send_sem=send_sem,
        recv_sem=recv_sem,
        device_id=device,
        device_id_type=MESH_IDS,
    )


class Place:
    def __init__(self):
        self.clip = lax.axis_index("clip")
        self.row = lax.axis_index("row")
        self.col = lax.axis_index("col")
        self.z = self.clip // 2
        self.x = self.clip % 2

    def z_mate(self, step):
        return (((self.z + step) % 4) * 2 + self.x, self.row, self.col)

    def x_mate(self):
        return (self.z * 2 + 1 - self.x, self.row, self.col)

    def core_mate(self):
        return (self.clip, self.row, 1 - self.col)

    def row_mate(self):
        return (self.clip, 1 - self.row, self.col)

    def mates(self, wide):
        near = [self.row_mate()]
        if wide:
            near += [self.core_mate(), self.x_mate()] + [self.z_mate(s) for s in (1, 2, 3)]
        return near

    def cube(self):
        found = []
        for i in range(1, 8):
            x = 1 - self.x if i & 1 else self.x
            row = 1 - self.row if i & 2 else self.row
            col = 1 - self.col if i & 4 else self.col
            found.append((self.z * 2 + x, row, col))
        return found


def shard_at(z, x, col):
    return (z * 2 + x) * 2 + col


def greet(mates):
    barrier = pltpu.get_barrier_semaphore()
    for mate in mates:
        pl.semaphore_signal(barrier, inc=1, device_id=mate, device_id_type=MESH_IDS)
    pl.semaphore_wait(barrier, len(mates))


class Mail:
    def __init__(self):
        self.sent = []

    def go(self, src, dst, ss, rs, device, only=None):
        copy = remote(src, dst, ss, rs, device)
        if only is None:
            copy.start()
        else:
            pl.when(only)(copy.start)
        self.sent.append((copy, only))

    def came(self, dst, ss, rs, device):
        remote(dst, dst, ss, rs, device).wait_recv()

    def drain(self):
        for copy, only in self.sent:
            if only is None:
                copy.wait_send()
            else:
                pl.when(only)(copy.wait_send)
        self.sent = []


class Gather(Mail):
    def __init__(self, place, own, spot, sems, over_x_first=None):
        super().__init__()
        self.at, self.own, self.spot, self.turned = place, own, spot, over_x_first
        self.z_ss, self.z_rs, self.x_ss, self.x_rs, self.c_ss, self.c_rs = sems

    def line(self, k, src, dst):
        for s, only in ((2, None), (1, self.at.z != 3), (3, self.at.z != 0)):
            ss, rs = self.z_ss.at[k, s - 1], self.z_rs.at[k, s - 1]
            self.go(src, dst, ss, rs, self.at.z_mate(s), only)

    def landed(self, k, s, spot):
        at = self.at
        self.came(spot, self.z_ss.at[k, s - 1], self.z_rs.at[k, s - 1], at.z_mate(s))
        if s == 2:
            for step, only in ((3, at.z == 1), (1, at.z == 2)):
                slot = (2 + step) % 4 - 1
                ss, rs = self.z_ss.at[k, 3], self.z_rs.at[k, slot]
                self.go(spot, spot, ss, rs, at.z_mate(step), only)

    def to_core(self, k, slot, spot):
        self.go(spot, spot, self.c_ss.at[k, slot], self.c_rs.at[k, slot], self.at.core_mate())

    def begin(self, k):
        at = self.at
        src, dst = self.own(k), self.spot(k, at.z, at.x, at.col)
        if k == self.turned:
            self.go(src, dst, self.x_ss.at[k, 0], self.x_rs.at[k, 0], at.x_mate())
        self.line(k, src, dst)
        if k != self.turned:
            self.go(src, dst, self.x_ss.at[k, 0], self.x_rs.at[k, 0], at.x_mate())
        self.go(src, dst, self.c_ss.at[k, 0], self.c_rs.at[k, 0], at.core_mate())

    def begin_turned(self, extra):
        at, k = self.at, self.turned
        spot = self.spot(k, at.z, 1 - at.x, at.col)
        self.came(spot, self.x_ss.at[k, 0], self.x_rs.at[k, 0], at.x_mate())
        self.line(extra, spot, spot)
        self.to_core(k, 4, spot)

    def forward_turned(self, extra):
        at, k = self.at, self.turned
        for s in (2, 1, 3):
            for line, x, slot in ((k, at.x, s), (extra, 1 - at.x, 4 + s)):
                spot = self.spot(k, (at.z - s) % 4, x, at.col)
                self.landed(line, s, spot)
                self.to_core(k, slot, spot)

    def forward(self, k):
        for s in (2, 1, 3):
            self.one("forward", s, k)

    def across(self, k):
        for s in (0, 2, 1, 3):
            self.one("across", s, k)

    def one(self, step, s, k=0):
        at = self.at
        if step == "across":
            spot = self.spot(k, (at.z - s) % 4, 1 - at.x, at.col)
            self.came(spot, self.x_ss.at[k, s], self.x_rs.at[k, s], at.x_mate())
            self.to_core(k, 4 + s, spot)
            return
        spot = self.spot(k, (at.z - s) % 4, at.x, at.col)
        self.landed(k, s, spot)
        self.go(spot, spot, self.x_ss.at[k, s], self.x_rs.at[k, s], at.x_mate())
        self.to_core(k, s, spot)

    def finish(self, k):
        at = self.at
        for s in range(8):
            x = at.x if s < 4 else 1 - at.x
            spot = self.spot(k, (at.z - s % 4) % 4, x, 1 - at.col)
            self.came(spot, self.c_ss.at[k, s], self.c_rs.at[k, s], at.core_mate())


class LineSum(Mail):
    def __init__(self, place, own, sent, got, ss, rs, rows, into):
        super().__init__()
        self.at, self.own, self.out, self.got, self.ss, self.rs = place, own, sent, got, ss, rs
        self.rows, self.into = rows, into
        self.middle = jnp.logical_or(place.z == 1, place.z == 2)

    def block(self, s):
        return self.own[self.rows * s : self.rows * (s + 1), :]

    def begin(self):
        at = self.at
        self.into[...] = self.block(0)
        for s, end, step in ((1, 3, 3), (3, 0, 1)):
            self.out[s - 1] = low(self.block(s))
            src = self.out.at[s - 1]
            dst = self.got.at[s - 1]
            inner = at.z != end
            self.go(src, dst, self.ss.at[s - 1], self.rs.at[s - 1], at.z_mate(s), inner)
            other = self.got.at[3]
            self.go(src, other, self.ss.at[3], self.rs.at[3], at.z_mate(step), at.z == end)
        outer = jnp.logical_not(self.middle)

        @pl.when(outer)
        def _():
            self.out[1] = low(self.block(2))

        self.go(
            self.out.at[1], self.got.at[1], self.ss.at[1], self.rs.at[1], at.z_mate(2), outer
        )

    def relay(self):
        at = self.at

        @pl.when(self.middle)
        def _():
            self.came(self.got.at[3], self.ss.at[3], self.rs.at[3], at.z_mate(1))
            self.out[1] = low(self.block(2) + self.got[3].astype(jnp.float32))

        self.go(
            self.out.at[1], self.got.at[1], self.ss.at[1], self.rs.at[1], at.z_mate(2), self.middle
        )

    def finish(self):
        at = self.at

        def add(s):
            self.came(self.got.at[s - 1], self.ss.at[s - 1], self.rs.at[s - 1], at.z_mate(s))
            self.into[...] += self.got[s - 1].astype(jnp.float32)

        add(2)
        pl.when(at.z != 0)(lambda: add(1))
        pl.when(at.z != 3)(lambda: add(3))


class Swap:
    def __init__(self, place, sent, got, send_sems, recv_sems):
        self.at, self.sent, self.got = place, sent, got
        self.ss, self.rs = send_sems, recv_sems
        self.copies = {}

    def start(self, i, value):
        slot = i % self.sent.shape[0]
        for j in [j for j in self.copies if j % self.sent.shape[0] == slot]:
            self.copies.pop(j).wait_send()
        self.sent[slot] = low(value)
        copy = remote(
            self.sent.at[slot], self.got.at[i], self.ss.at[i], self.rs.at[i], self.at.row_mate()
        )
        copy.start()
        self.copies[i] = copy

    def total(self, i):
        self.copies[i].wait_recv()
        sent = self.sent[i % self.sent.shape[0]]
        return sent.astype(jnp.float32) + self.got[i].astype(jnp.float32)

    def drain(self):
        for copy in self.copies.values():
            copy.wait_send()


ROWS = 1216
LANES = 1280
STEP_ROWS = 608
N_STEPS = ROWS // STEP_ROWS
KEY_ROWS = 640


def norm_rows(rows):
    average = jnp.mean(rows, axis=-1, keepdims=True)
    centred = rows - average
    inv_dev = lax.rsqrt(jnp.mean(centred * centred, axis=-1, keepdims=True) + EPS_NORM)
    return centred * inv_dev, inv_dev


def norm_rows_back(grad_out, scaled, inv_dev, gain_row):
    inner = grad_out * gain_row
    return inv_dev * (
        inner
        - jnp.mean(inner, axis=-1, keepdims=True)
        - scaled * jnp.mean(inner * scaled, axis=-1, keepdims=True)
    )


def column_sum(values):
    return jnp.sum(values, axis=0, keepdims=True)


def decoder_body(wide, *refs):
    bf, f32 = jnp.bfloat16, jnp.float32
    seen_ref, feat_ref, padded_ref, table_ref, one_ref, two_in, vec_ref = refs[:7]
    loss_ref, gone_ref, gtwo_ref, gvec_ref, gfeat_ref = refs[7:12]
    z_s, n1_s, q_s, k_s, v_s, o_s, do_s, dx_s, dqkv_s, dqt_s, lse_s, delta_s = refs[12:24]
    lse_t, delta_t, wqkv_s, wo_s, y_s, gqkv_s, go_s, gup_s, gdn_s, ghd_s = refs[24:34]
    gy_s, gv_s, pixel_ref, seen_s, near_sem, far_ss, far_rs = refs[34:41]
    if wide:
        two_s, cr_s, xs_s, xr_s, c_ss, c_rs, x_ss, x_rs = refs[41:49]
        g_s = two_s
    else:
        two_s, g_s = two_in, gtwo_ref
    place = Place()
    greet(place.mates(wide))

    def chip_rows(s, x):
        return pl.ds(pl.multiple_of(((place.z + s) % 4 * 2 + x) * SHARD, 16), SHARD)

    own_lanes = pl.ds(pl.multiple_of(place.col * TWO_HALF, 128), TWO_HALF)
    other_lanes = pl.ds(pl.multiple_of((1 - place.col) * TWO_HALF, 128), TWO_HALF)
    if wide:

        def spot(k, z, x, col):
            rows = pl.ds(pl.multiple_of((z * 2 + x) * SHARD, 16), SHARD)
            return two_s.at[:, rows, pl.ds(pl.multiple_of(col * TWO_HALF, 128), TWO_HALF)]

        gather = Gather(place, lambda k: two_in, spot, refs[49:55])
        gather.begin(0)
        two_s[:, chip_rows(0, place.x), own_lanes] = two_in[...]

    def tile(i):
        return pl.ds(pl.multiple_of(i * STEP_ROWS, STEP_ROWS), STEP_ROWS)

    def near(i):
        rows = tile(i)
        return pltpu.make_async_copy(
            padded_ref.at[place.row, rows, :], pixel_ref.at[place.row, rows, :], near_sem.at[i]
        )

    def far(i, half):
        rows = tile(i)
        return remote(
            padded_ref.at[1 - place.row, rows, :],
            pixel_ref.at[half, rows, :],
            far_ss.at[i],
            far_rs.at[i],
            place.row_mate(),
        )

    @pl.loop(0, N_STEPS)
    def _(i):
        near(i).start()
        far(i, place.row).start()

    half = 3 * HEAD
    up0, dn0, hd0, ed0 = UP_TWO, DN_TWO, HD_TWO, ED_AT
    vec = vec_ref[...]
    gain1, shift1, gain2, shift2, gain_f, shift_f, token = [vec[i : i + 1] for i in range(7)]

    for part in range(3):
        for r in range(2):
            wqkv_s[:, part * DD + r * half : part * DD + (r + 1) * half] = one_ref[
                r, :, part * half : (part + 1) * half
            ]
    for ref in (q_s, k_s, v_s, do_s):
        ref[ROWS:LANES, :] = jnp.zeros((LANES - ROWS, DD), bf)
    delta_s[ROWS:LANES, :] = jnp.zeros((LANES - ROWS, 128), f32)
    for ref in (gqkv_s, go_s, gup_s, gdn_s, ghd_s, gy_s, gv_s):
        ref[...] = jnp.zeros(ref.shape, f32)
    for r in range(2):
        y_s[:, r * DD : (r + 1) * DD] = low(
            times_trans(feat_ref[:, r * DD : (r + 1) * DD], one_ref[r, :, ed0 : ed0 + DD])
        )
    seen_s[...] = jnp.full(seen_s.shape, -1, jnp.int32)
    seen_s[0:1, 0:VIS] = seen_ref[place.row]
    seen = seen_s[0:1, :]

    def picks(i):
        ids = row_ids((STEP_ROWS, 128)) + i * STEP_ROWS
        hits = ids == seen
        taken = jnp.sum(hits.astype(f32), axis=-1, keepdims=True)
        valid = (row_ids((STEP_ROWS, 1)) + i * STEP_ROWS < TUBES).astype(f32)
        return hits.astype(bf), valid - taken

    @pl.loop(0, N_STEPS)
    def _(i):
        hits, hidden = picks(i)
        placed = times_plain(hits, y_s[...])
        z = placed[:, :DD] + placed[:, DD:] + table_ref[tile(i), :] + token * hidden
        z_s[tile(i), :] = z
        scaled, _ = norm_rows(z)
        n1 = low(scaled * gain1 + shift1)
        n1_s[tile(i), :] = n1
        q_s[tile(i), :] = low(times_plain(n1, wqkv_s[:, 0:DD]))
        k_s[tile(i), :] = low(times_plain(n1, wqkv_s[:, DD : 2 * DD]))
        v_s[tile(i), :] = low(times_plain(n1, wqkv_s[:, 2 * DD : 3 * DD]))

    first_half = lane_ids((1, 128)) < HEAD
    half_masks = [first_half, jnp.logical_not(first_half)]
    last_keys = lane_ids((1, 128)) < TUBES - (LANES - 128)
    ones = jnp.ones((LANES, 128), bf)
    lse_s[...] = jnp.zeros(lse_s.shape, f32)
    for p in range(3):
        lanes = slice(128 * p, 128 * (p + 1))

        @pl.loop(0, N_STEPS)
        def _(i):
            queries = q_s[tile(i), lanes]
            parts = []
            stat = lse_s[tile(i), :]
            for h in range(2):
                one = jnp.where(half_masks[h], queries, jnp.zeros_like(queries))
                scores = times_trans(one, k_s[:, lanes])
                tail = jnp.where(last_keys, scores[:, LANES - 128 :], -1e30)
                scores = jnp.concatenate([scores[:, : LANES - 128], tail], axis=-1)
                top = jnp.max(scores, axis=-1, keepdims=True) * (SCALE * LOG2E)
                weights = low(jnp.exp2(scores * (SCALE * LOG2E) - top))
                both = times_plain(weights, jnp.concatenate([v_s[:, lanes], ones], axis=-1))
                total = both[:, 128:129]
                parts.append(both[:, 0:128] / total)
                lse = top + jnp.log(total) * LOG2E
                stat = jnp.where(lane_ids((1, 128)) == 2 * p + h, lse, stat)
            lse_s[tile(i), :] = stat
            o_s[tile(i), lanes] = low(jnp.where(first_half, parts[0], parts[1]))

        if wide:
            for step in ((("forward", 2), ("forward", 1)), (("forward", 3), ("across", 0)), ())[p]:
                gather.one(*step)
    if wide:
        for s in (2, 1, 3):
            gather.one("across", s)
        gather.finish(0)
    for r in range(2):
        wo_s[:, r * half : (r + 1) * half] = two_s[r, :, 0:half]
    lse_t[...] = lse_s[...].T

    @pl.loop(0, N_STEPS)
    def _(i):
        _, hidden = picks(i)
        near(i).wait()
        far(i, 1 - place.row).wait_recv()
        attended = o_s[tile(i), :]
        x1 = z_s[tile(i), :] + times_trans(attended, wo_s[...])
        scaled2, inv2 = norm_rows(x1)
        n2 = low(scaled2 * gain2 + shift2)
        x2 = x1
        acts, slopes = [], []
        for r in range(2):
            u = times_plain(n2, two_s[r, :, up0 : up0 + 768])
            act, slope = gelu_pair(u)
            act = low(act)
            acts.append(act)
            slopes.append(slope)
            x2 = x2 + times_trans(act, two_s[r, :, dn0 : dn0 + 768])
        scaled_f, inv_f = norm_rows(x2)
        t = low(scaled_f * gain_f + shift_f)
        d_t = jnp.zeros((STEP_ROWS, DD), f32)
        for r in range(2):
            error = times_plain(t, two_s[r, :, hd0 : hd0 + 768]) - pixel_ref[r, tile(i), :].astype(
                f32
            )
            error = error * hidden
            gv_s[7:8, :] += column_sum(error * error)
            d_pred = low(error * (2.0 / PIX))
            ghd_s[r] += trans_times(t, d_pred)
            d_t = d_t + times_trans(d_pred, two_s[r, :, hd0 : hd0 + 768])
        gv_s[4:5, 0:DD] += column_sum(d_t * scaled_f)
        gv_s[5:6, 0:DD] += column_sum(d_t)
        d_x2 = norm_rows_back(d_t, scaled_f, inv_f, gain_f)
        d_low = low(d_x2)
        d_n2 = jnp.zeros((STEP_ROWS, DD), f32)
        for r in range(2):
            gdn_s[r] += trans_times(d_low, acts[r])
            d_u = low(times_plain(d_low, two_s[r, :, dn0 : dn0 + 768]) * slopes[r])
            gup_s[r] += trans_times(n2, d_u)
            d_n2 = d_n2 + times_trans(d_u, two_s[r, :, up0 : up0 + 768])
        gv_s[2:3, 0:DD] += column_sum(d_n2 * scaled2)
        gv_s[3:4, 0:DD] += column_sum(d_n2)
        d_x1 = d_x2 + norm_rows_back(d_n2, scaled2, inv2, gain2)
        dx_s[tile(i), :] = d_x1
        d_low = low(d_x1)
        go_s[...] += trans_times(d_low, attended)
        d_o = low(times_plain(d_low, wo_s[...]))
        do_s[tile(i), :] = d_o
        both = d_o.astype(f32) * attended.astype(f32)
        stat = jnp.zeros((STEP_ROWS, 128), f32)
        for p in range(3):
            pair = both[:, 128 * p : 128 * (p + 1)]
            for h in range(2):
                one = jnp.sum(jnp.where(half_masks[h], pair, 0.0), axis=-1, keepdims=True)
                stat = jnp.where(lane_ids((1, 128)) == 2 * p + h, one, stat)
        delta_s[tile(i), :] = stat

    if wide:
        gather.drain()
    for r in range(2):
        g_s[r, :, 0:half] = low(go_s[:, r * half : (r + 1) * half])
        g_s[r, :, half:up0] = jnp.zeros((DD, up0 - half), bf)
        g_s[r, :, up0 : up0 + 768] = low(gup_s[r])
        g_s[r, :, dn0 : dn0 + 768] = low(gdn_s[r])
        g_s[r, :, hd0 : hd0 + 768] = low(ghd_s[r])
    if wide:
        to_core = remote(g_s.at[:, :, other_lanes], cr_s, c_ss, c_rs, place.core_mate())
        to_core.start()
        to_x = remote(xs_s, xr_s, x_ss, x_rs, place.x_mate())
    delta_t[...] = delta_s[...].T

    for p in range(3):
        lanes = slice(128 * p, 128 * (p + 1))
        dqt_s[...] = jnp.zeros(dqt_s.shape, f32)

        @pl.loop(0, LANES // KEY_ROWS)
        def _(j):
            rows = pl.ds(pl.multiple_of(j * KEY_ROWS, KEY_ROWS), KEY_ROWS)
            keys, values = k_s[rows, lanes], v_s[rows, lanes]
            bias = jnp.where(row_ids((KEY_ROWS, 1)) + j * KEY_ROWS < TUBES, 0.0, -1e30)
            d_keys, d_values = [], []
            for h in range(2):
                key_one = jnp.where(half_masks[h], keys, jnp.zeros_like(keys))
                value_one = jnp.where(half_masks[h], values, jnp.zeros_like(values))
                lse = lse_t[2 * p + h : 2 * p + h + 1, :]
                delta = delta_t[2 * p + h : 2 * p + h + 1, :]
                scores = times_trans(key_one, q_s[:, lanes])
                soft = jnp.exp2((scores * (SCALE * LOG2E) + bias) - lse)
                d_soft = times_trans(value_one, do_s[:, lanes])
                d_scores = low(soft * (d_soft - delta))
                d_values.append(times_plain(low(soft), do_s[:, lanes]))
                d_keys.append(times_plain(d_scores, q_s[:, lanes]))
                dqt_s[...] += trans_times(key_one, d_scores)
            k_out = slice(DD + 128 * p, DD + 128 * (p + 1))
            v_out = slice(2 * DD + 128 * p, 2 * DD + 128 * (p + 1))
            dqkv_s[rows, k_out] = low(jnp.where(first_half, d_keys[0], d_keys[1]) * SCALE)
            dqkv_s[rows, v_out] = low(jnp.where(first_half, d_values[0], d_values[1]))

        dqkv_s[:, lanes] = low(dqt_s[...].T * SCALE)
        if wide and p == 0:
            to_core.wait_recv()
            for s in range(4):
                rows = chip_rows(s, 1 - place.x)
                xs_s[s] = low(g_s[:, rows, own_lanes].astype(f32) + cr_s[:, rows, :].astype(f32))
            to_x.start()

    @pl.loop(0, N_STEPS)
    def _(i):
        hits, hidden = picks(i)
        d_qkv = dqkv_s[tile(i), :]
        gqkv_s[...] += trans_times(n1_s[tile(i), :], d_qkv)
        d_n1 = times_trans(d_qkv, wqkv_s[...])
        scaled1, inv1 = norm_rows(z_s[tile(i), :])
        gv_s[0:1, 0:DD] += column_sum(d_n1 * scaled1)
        gv_s[1:2, 0:DD] += column_sum(d_n1)
        d_z = dx_s[tile(i), :] + norm_rows_back(d_n1, scaled1, inv1, gain1)
        gv_s[6:7, 0:DD] += column_sum(d_z * hidden)
        gy_s[...] += trans_times(hits, low(d_z))

    d_y = low(gy_s[...])
    for r in range(2):
        gone_ref[r, :, ed0 : ed0 + DD] = low(trans_times(d_y, feat_ref[:, r * DD : (r + 1) * DD]))
        gone_ref[r, :, ed0 + DD : PART_ONE] = jnp.zeros((DD, PART_ONE - ed0 - DD), bf)
        gfeat_ref[:, r * DD : (r + 1) * DD] = low(times_plain(d_y, one_ref[r, :, ed0 : ed0 + DD]))
        for part in range(3):
            gone_ref[r, :, part * half : (part + 1) * half] = low(
                gqkv_s[:, part * DD + r * half : part * DD + (r + 1) * half]
            )
    if wide:
        to_x.wait_recv()
        for s in range(4):
            rows = chip_rows(s, place.x)
            total = g_s[:, rows, own_lanes].astype(f32) + cr_s[:, rows, :].astype(f32)
            total = total + xr_s[s].astype(f32)
            for r in range(2):
                at = (2 * s + r) * SHARD
                gtwo_ref[at : at + SHARD, :] = total[r]
        to_core.wait_send()
        to_x.wait_send()
    gvec_ref[...] = gv_s[:, 0:DD]

    @pl.loop(0, N_STEPS)
    def _(i):
        far(i, place.row).wait_send()

    loss_ref[...] = jnp.zeros((8, 128), f32) + jnp.sum(gv_s[7:8, :]) / PIX


def run_decoder(wide, *operands):
    bf, f32 = jnp.bfloat16, jnp.float32
    vmem = pl.BlockSpec(memory_space=pltpu.VMEM)
    dma = pltpu.SemaphoreType.DMA
    if wide:
        two = jax.ShapeDtypeStruct((8 * SHARD, TWO_HALF), f32)
    else:
        two = jax.ShapeDtypeStruct((2, DD, PART_TWO), bf)
    scratch = [
        pltpu.VMEM((ROWS, DD), f32),
        pltpu.VMEM((ROWS, DD), bf),
        pltpu.VMEM((LANES, DD), bf),
        pltpu.VMEM((LANES, DD), bf),
        pltpu.VMEM((LANES, DD), bf),
        pltpu.VMEM((ROWS, DD), bf),
        pltpu.VMEM((LANES, DD), bf),
        pltpu.VMEM((ROWS, DD), f32),
        pltpu.VMEM((LANES, 3 * DD), bf),
        pltpu.VMEM((128, LANES), f32),
        pltpu.VMEM((LANES, 128), f32),
        pltpu.VMEM((LANES, 128), f32),
        pltpu.VMEM((128, LANES), f32),
        pltpu.VMEM((128, LANES), f32),
        pltpu.VMEM((DD, 3 * DD), bf),
        pltpu.VMEM((DD, DD), bf),
        pltpu.VMEM((128, 2 * DD), bf),
        pltpu.VMEM((DD, 3 * DD), f32),
        pltpu.VMEM((DD, DD), f32),
        pltpu.VMEM((2, DD, 768), f32),
        pltpu.VMEM((2, DD, 768), f32),
        pltpu.VMEM((2, DD, 768), f32),
        pltpu.VMEM((128, DD), f32),
        pltpu.VMEM((8, 768), f32),
        pltpu.VMEM((2, ROWS, PIX // 2), bf),
        pltpu.VMEM((8, 128), jnp.int32),
        dma((N_STEPS,)),
        dma((N_STEPS,)),
        dma((N_STEPS,)),
    ]
    if wide:
        scratch += [
            pltpu.VMEM((2, DD, PART_TWO), bf),
            pltpu.VMEM((2, DD, TWO_HALF), bf),
            pltpu.VMEM((4, 2, SHARD, TWO_HALF), bf),
            pltpu.VMEM((4, 2, SHARD, TWO_HALF), bf),
            dma,
            dma,
            dma,
            dma,
        ]
        scratch += [dma((1, 4)), dma((1, 3)), dma((1, 4)), dma((1, 4)), dma((1, 8)), dma((1, 8))]
    return pl.pallas_call(
        functools.partial(decoder_body, wide),
        out_shape=(
            jax.ShapeDtypeStruct((8, 128), f32),
            jax.ShapeDtypeStruct((2, DD, PART_ONE), bf),
            two,
            jax.ShapeDtypeStruct((8, DD), f32),
            jax.ShapeDtypeStruct((128, D), bf),
        ),
        in_specs=[vmem, vmem, pl.BlockSpec(memory_space=pl.ANY), vmem, vmem, vmem, vmem],
        out_specs=(vmem,) * 5,
        scratch_shapes=scratch,
        compiler_params=pltpu.CompilerParams(
            collective_id=4, has_side_effects=True, vmem_limit_bytes=63 * MIB
        ),
        cost_estimate=pl.CostEstimate(
            flops=30 * 10**9, bytes_accessed=20 * 10**6, transcendentals=20 * 10**6
        ),
        name="decoder",
    )(*operands)


PAIR = 256
HALF_D = D // 2
QKV_W = 3 * D // 2
HID = FF // 2
A_COLS = QKV_W + D // 2
ENC_COLS = A_COLS + 2 * HID
UP_AT, DN_AT = A_COLS, A_COLS + HID
EMB_ROWS = SHARD + 16
GATHERS = (
    (-1, 0, D),
    (0, 0, A_COLS),
    (0, A_COLS, 2 * HID),
    (1, 0, A_COLS),
    (1, A_COLS, 2 * HID),
    (-2, 0, PART_ONE),
)
PART_ONE_AT = len(GATHERS) - 1


def half_lanes():
    first = lane_ids((1, 128)) < HEAD
    return [first, jnp.logical_not(first)]


def same_clip():
    a, b = row_ids((PAIR, PAIR)), lane_ids((PAIR, PAIR))
    return jnp.logical_and(a // 128 == b // 128, b % 128 < VIS)


def encoder_scores(queries, keys, allowed):
    scores = jnp.where(allowed, times_trans(queries, keys), -1e30)
    top = jnp.max(scores, axis=-1, keepdims=True) * (SCALE * LOG2E)
    weights = jnp.exp2(scores * (SCALE * LOG2E) - top)
    return weights, jnp.sum(weights, axis=-1, keepdims=True)


def encoder_attention(qkv_ref, out_ref):
    allowed = same_clip()
    halves = half_lanes()
    for p in range(3):
        q = qkv_ref[:, 128 * p : 128 * (p + 1)]
        k = qkv_ref[:, HALF_D + 128 * p : HALF_D + 128 * (p + 1)]
        v = qkv_ref[:, 2 * HALF_D + 128 * p : 2 * HALF_D + 128 * (p + 1)]
        parts = []
        for h in range(2):
            one = jnp.where(halves[h], q, jnp.zeros_like(q))
            weights, total = encoder_scores(one, k, allowed)
            parts.append(times_plain(low(weights), v) / total)
        out_ref[:, 128 * p : 128 * (p + 1)] = low(jnp.where(halves[0], parts[0], parts[1]))


def pack_heads(dst, src, heads):
    for part in range(3):
        for h in range(heads):
            at = (part * heads + h) * HEAD
            dst[:, at : at + HEAD] = low(src[:, (3 * h + part) * HEAD : (3 * h + part + 1) * HEAD])


def encoder_body(wide, *refs):
    f32 = jnp.float32
    if wide:
        seen_ref, pixel_ref, freq_ref, emb_ref, enc_ref, dec_ref, evec_ref, dvec_ref = refs[:8]
        refs = refs[8:]
    else:
        seen_ref, pixel_ref, freq_ref, emb_full, w_s, gain_in = refs[:6]
        refs = refs[6:]
    feat_ref, x_ref, qkv_ref, o_ref, h_ref, slope_ref, px_ref, padded_out = refs[:8]
    refs = refs[8:]
    if wide:
        gain_ref, dgain_ref, w_out, one_out, two_out = refs[:5]
        emb_s, w_s, embc_s, emb_in, enc_in, small_s, one_s, two_s, block_s = refs[5:14]
        refs = refs[14:]
    sent_s, got_s, padded_s, seen_s, pad_sem, y_ss, y_rs = refs[:7]
    refs = refs[7:]
    place = Place()
    greet(place.mates(wide))
    swap = Swap(place, sent_s, got_s, y_ss, y_rs)
    if wide:

        def own_part(k):
            layer, start, width = GATHERS[k]
            if layer == -1:
                return emb_in
            if layer == -2:
                return spot(k, place.z, place.x, place.col)
            return enc_in.at[layer, :, pl.ds(start, width)]

        def spot(k, z, x, col):
            layer, start, width = GATHERS[k]
            if layer == -2:
                rows = pl.ds(pl.multiple_of((z * 2 + x) * SHARD, 16), SHARD)
                return one_s.at[:, rows, pl.ds(pl.multiple_of(col * ONE_HALF, 128), ONE_HALF)]
            rows = EMB_ROWS if layer < 0 else SHARD
            first = pl.multiple_of(shard_at(z, x, col) * rows, 16)
            if layer == -1:
                return emb_s.at[pl.ds(first, rows), :]
            return w_s.at[layer, pl.ds(first, rows), pl.ds(start, width)]

        gather = Gather(place, own_part, spot, refs[:6], over_x_first=3)
        extra = len(GATHERS)
        keep_sem, block_ss, block_rs, seed_ss, seed_rs = refs[6:11]
        emb_in[0:SHARD, :] = low(emb_ref[0])
        small_s[...] = jnp.zeros(small_s.shape, f32)
        small_s[0:10, 0:SHARD] = evec_ref[...]
        small_s[0:7, SHARD : SHARD + DD // N_SHARDS] = dvec_ref[...]
        emb_in[SHARD:EMB_ROWS, 0:128] = low(small_s[...])
        emb_in[SHARD:EMB_ROWS, 128:D] = jnp.zeros((EMB_ROWS - SHARD, D - 128), jnp.bfloat16)
        gather.begin(0)
        for layer in range(LAYERS):
            pack_heads(enc_in.at[layer], enc_ref.at[layer, 0], HEADS // 2)
            enc_in[layer, :, QKV_W:] = low(enc_ref[layer, 0, :, QKV_W:])
            if layer == 0:
                gather.begin(1)
                gather.begin(2)
        own = shard_at(place.z, place.x, place.col)
        emb_s[pl.ds(pl.multiple_of(own * EMB_ROWS, 16), EMB_ROWS), :] = emb_in[...]
        for layer in range(LAYERS):
            w_s[layer, pl.ds(pl.multiple_of(own * SHARD, 16), SHARD), :] = enc_in[layer]
        mine = pl.ds(pl.multiple_of(place.col * (SHARD // 2), 8), SHARD // 2)
        block_s[mine, :] = jnp.zeros((SHARD // 2, PART_ONE + PART_TWO), f32)
        shard = dec_ref[0]
        heads = DHEADS // 2
        for part in range(3):
            for h in range(heads):
                at = (3 * h + part) * HEAD
                to = (part * heads + h) * HEAD
                block_s[mine, to : to + HEAD] = shard[:, at : at + HEAD]
        block_s[mine, ED_AT : ED_AT + DD] = shard[:, 3072:3456]
        block_s[mine, PART_ONE : PART_ONE + 192] = shard[:, ED_AT:768]
        block_s[mine, PART_ONE + UP_TWO : PART_ONE + PART_TWO] = shard[:, 768:3072]
        spread = remote(
            block_s.at[mine, :], block_s.at[mine, :], block_ss, block_rs, place.core_mate()
        )
        spread.start()
        theirs = pl.ds(pl.multiple_of((1 - place.col) * (SHARD // 2), 8), SHARD // 2)
        half_one = spot(PART_ONE_AT, place.z, place.x, place.col)
        seeds = [
            remote(part.at[place.row], part.at[place.row], ss, rs, place.row_mate())
            for part, ss, rs in (
                (half_one, seed_ss.at[0], seed_rs.at[0]),
                (two_s, seed_ss.at[1], seed_rs.at[1]),
            )
        ]
        seeds_back = [
            remote(part.at[1 - place.row], part.at[1 - place.row], ss, rs, place.row_mate())
            for part, ss, rs in (
                (half_one, seed_ss.at[0], seed_rs.at[0]),
                (two_s, seed_ss.at[1], seed_rs.at[1]),
            )
        ]

    def step(name, k):
        if wide:
            getattr(gather, name)(k)

    odd = (lane_ids((1, D)) % 2).astype(f32) * (0.5 * math.pi)
    freq = freq_ref[0:1, :]
    places = []
    seen_s[...] = jnp.full(seen_s.shape, -1, jnp.int32)
    whole = TUBES // 16 * 16
    for m in range(MICRO):
        seen_s[m : m + 1, 0:VIS] = seen_ref[m]
        row = seen_s[m : m + 1, :]
        hits = (row_ids((TUBES, 128)) == row).astype(jnp.bfloat16)
        px_ref[128 * m : 128 * (m + 1), :] = low(trans_times(hits, pixel_ref[m, 0]))
        column = jnp.broadcast_to(row.astype(f32), (128, 128)).T[:, 0:1]
        places.append(jnp.sin(column * freq + odd))
        padded_s[m, 0:whole, :] = pixel_ref[m, 0, 0:whole, :]
        rest = pixel_ref[m, 0, whole:TUBES, :].astype(f32)
        rest = jnp.concatenate([rest, jnp.zeros((ROWS - TUBES, D), f32)], axis=0)
        padded_s[m, whole:ROWS, :] = low(rest)
    pad_copy = pltpu.make_async_copy(padded_s, padded_out, pad_sem)
    pad_copy.start()

    if wide:
        gather.forward(0)
        gather.across(0)
        gather.finish(0)
        for s in range(N_SHARDS):
            embc_s[SHARD * s : SHARD * (s + 1), :] = emb_s[EMB_ROWS * s : EMB_ROWS * s + SHARD, :]
            tail = emb_s[EMB_ROWS * s + SHARD : EMB_ROWS * (s + 1), 0:128].astype(f32)
            gain_ref[:, SHARD * s : SHARD * (s + 1)] = tail[:, 0:SHARD]
            dgain_ref[:, DD // 16 * s : DD // 16 * (s + 1)] = tail[0:8, SHARD : SHARD + DD // 16]
        emb_full, gain_in = embc_s, gain_ref
    swap.start(0, times_trans(px_ref[...], emb_full[...]))
    if wide:
        other_rows = block_s.at[theirs, :]
        remote(other_rows, other_rows, block_ss, block_rs, place.core_mate()).wait_recv()
        lanes = pl.ds(pl.multiple_of(place.col * ONE_HALF, 128), ONE_HALF)
        half_one.at[place.row][...] = low(block_s[:, lanes])
        lanes = pl.ds(pl.multiple_of(PART_ONE + place.col * TWO_HALF, 128), TWO_HALF)
        two_s[place.row] = low(block_s[:, lanes])
        for copy in seeds:
            copy.start()
    step("forward", 1)
    step("begin", 3)
    step("across", 1)
    x = swap.total(0) + jnp.concatenate(places, axis=0)
    for layer in range(LAYERS):
        gains = gain_in[4 * layer : 4 * layer + 4, :]
        x_ref[2 * layer] = x
        scaled, _ = norm_rows(x)
        n1 = low(scaled * gains[0:1] + gains[1:2])
        step("finish", 1 + 2 * layer)
        qkv_ref[layer] = low(times_plain(n1, w_s[layer, :, 0:QKV_W]))
        encoder_attention(qkv_ref.at[layer], o_ref.at[layer])
        swap.start(1 + 2 * layer, times_trans(o_ref[layer], w_s[layer, :, QKV_W:A_COLS]))
        step("forward", 2 + 2 * layer)
        if layer == 0:
            if wide:
                gather.begin_turned(extra)
            step("begin", 4)
            if wide:
                for copy in seeds_back:
                    copy.wait_recv()
            step("begin", PART_ONE_AT)
        step("across", 2 + 2 * layer)
        x = x + swap.total(1 + 2 * layer)
        x_ref[2 * layer + 1] = x
        scaled, _ = norm_rows(x)
        n2 = low(scaled * gains[2:3] + gains[3:4])
        step("finish", 2 + 2 * layer)
        if wide:
            keep = pltpu.make_async_copy(w_s.at[layer], w_out.at[layer], keep_sem.at[layer])
            keep.start()
        act, slope = gelu_pair(times_plain(n2, w_s[layer, :, UP_AT:DN_AT]))
        act = low(act)
        h_ref[layer] = act
        slope_ref[layer] = slope
        swap.start(2 + 2 * layer, times_trans(act, w_s[layer, :, DN_AT:ENC_COLS]))
        if wide and layer == 0:
            gather.forward_turned(extra)
        else:
            step("forward", PART_ONE_AT)
            step("across", PART_ONE_AT)
        x = x + swap.total(2 + 2 * layer)
    x_ref[2 * LAYERS] = x
    scaled, _ = norm_rows(x)
    gains = gain_in[4 * LAYERS : 4 * LAYERS + 2, :]
    feat = low(scaled * gains[0:1] + gains[1:2])
    feat_ref[...] = jnp.where(place.row == 0, feat[0:128], feat[128:256])
    swap.drain()
    pad_copy.wait()
    if wide:
        two_out[...] = two_s[...]
        gather.finish(PART_ONE_AT)
        one_copy = pltpu.make_async_copy(one_s, one_out, keep_sem.at[LAYERS])
        one_copy.start()
        spread.wait_send()
        for copy in seeds:
            copy.wait_send()
        gather.drain()
        one_copy.wait()
        for layer in range(LAYERS):
            pltpu.make_async_copy(w_s.at[layer], w_out.at[layer], keep_sem.at[layer]).wait()


def run_encoder(wide, *operands):
    bf, f32 = jnp.bfloat16, jnp.float32
    vmem = pl.BlockSpec(memory_space=pltpu.VMEM)
    dma = pltpu.SemaphoreType.DMA
    shape = jax.ShapeDtypeStruct
    n_swaps = 1 + 2 * LAYERS
    outs = [
        shape((128, D), bf),
        shape((2 * LAYERS + 1, PAIR, D), f32),
        shape((LAYERS, PAIR, QKV_W), bf),
        shape((LAYERS, PAIR, HALF_D), bf),
        shape((LAYERS, PAIR, HID), bf),
        shape((LAYERS, PAIR, HID), f32),
        shape((PAIR, D), bf),
        shape((MICRO, ROWS, D), bf),
    ]
    out_specs = [vmem] * (len(outs) - 1) + [pl.BlockSpec(memory_space=pl.ANY)]
    scratch = []
    if wide:
        anywhere = pl.BlockSpec(memory_space=pl.ANY)
        outs += [
            shape((16, D), f32),
            shape((8, DD), f32),
            shape((LAYERS, D, ENC_COLS), bf),
            shape((2, DD, PART_ONE), bf),
            shape((2, SHARD, TWO_HALF), bf),
        ]
        out_specs += [vmem, vmem, anywhere, anywhere, vmem]
        scratch += [
            pltpu.VMEM((N_SHARDS * EMB_ROWS, D), bf),
            pltpu.VMEM((LAYERS, D, ENC_COLS), bf),
            pltpu.VMEM((D, D), bf),
            pltpu.VMEM((EMB_ROWS, D), bf),
            pltpu.VMEM((LAYERS, SHARD, ENC_COLS), bf),
            pltpu.VMEM((16, 128), f32),
            pltpu.VMEM((2, DD, PART_ONE), bf),
            pltpu.VMEM((2, SHARD, TWO_HALF), bf),
            pltpu.VMEM((SHARD, PART_ONE + PART_TWO), f32),
        ]
    scratch += [
        pltpu.VMEM((n_swaps, PAIR, D), bf),
        pltpu.VMEM((n_swaps, PAIR, D), bf),
        pltpu.VMEM((MICRO, ROWS, D), bf),
        pltpu.VMEM((8, 128), jnp.int32),
        dma,
        dma((n_swaps,)),
        dma((n_swaps,)),
    ]
    if wide:
        n = len(GATHERS)
        scratch += [dma((n + 1, 4)), dma((n + 1, 3)), dma((n, 4)), dma((n, 4)), dma((n, 8)), dma((n, 8))]
        scratch += [dma((LAYERS + 1,)), dma, dma, dma((2,)), dma((2,))]
    return pl.pallas_call(
        functools.partial(encoder_body, wide),
        out_shape=tuple(outs),
        in_specs=[vmem] * len(operands),
        out_specs=tuple(out_specs),
        scratch_shapes=scratch,
        compiler_params=pltpu.CompilerParams(
            collective_id=1, has_side_effects=True, vmem_limit_bytes=60 * MIB
        ),
        cost_estimate=pl.CostEstimate(
            flops=10 * 10**9, bytes_accessed=60 * 10**6, transcendentals=10**6
        ),
        name="encoder",
    )(*operands)


SUMS = (
    ("dn1", HID),
    ("up1", HID),
    ("at1", A_COLS),
    ("dn0", HID),
    ("up0", HID),
    ("at0", A_COLS),
    ("emb", D),
)
SUM_AT = {name: sum(w for _, w in SUMS[:i]) for i, (name, _) in enumerate(SUMS)}
SUM_COLS = sum(w for _, w in SUMS)
BLOCKS = N_SHARDS // 2 * SHARD
QUARTER = BLOCKS // 2


class Scatter(Mail):
    def __init__(self, place, bufs, sems, into):
        super().__init__()
        self.at, self.into = place, into
        self.perm, self.flip, self.cs, self.cr, self.xs, self.xr, self.zs, self.zr, self.own = bufs
        self.c_ss, self.c_rs, self.x_ss, self.x_rs, self.z_ss, self.z_rs = sems
        self.last = {}
        self.lines = {}

    def span(self, name, shift=0, width=None):
        k = [n for n, _ in SUMS].index(name)
        return k, pl.ds(SUM_AT[name] + shift, SUMS[k][1] if width is None else width)

    def post(self, src, dst, ss, rs, device, key):
        copy = remote(src, dst, ss, rs, device)
        copy.start()
        self.last[key] = copy

    def free(self, key):
        if key in self.last:
            self.last.pop(key).wait_send()

    def turn(self, slot, left):
        at = self.at
        flip = self.flip.at[slot % 2]
        flip[...] = left.T
        order = [
            (s, x, c) for c, x in ((1, 1), (1, 0), (0, 1), (0, 0)) for s in range(4)
        ]
        for i, (s, other_x, other_c) in enumerate(order):
            x = 1 - at.x if other_x else at.x
            c = 1 - at.col if other_c else at.col
            first = pl.multiple_of(shard_at((at.z + s) % 4, x, c) * SHARD, 16)
            self.perm[slot, SHARD * i : SHARD * (i + 1), :] = flip[pl.ds(first, SHARD), :]

    def cores(self, name, items):
        k, span = self.span(name)
        slot_at, width = k % 2, SUMS[k][1]
        self.free(("core", slot_at))
        for slot, right, shift, wide in items:
            self.cs[slot_at, :, shift : shift + wide] = low(
                times_plain(self.perm[slot, 0:BLOCKS, :], right[...])
            )
        self.post(
            self.cs.at[slot_at, :, pl.ds(0, width)],
            self.cr.at[:, span],
            self.c_ss.at[k],
            self.c_rs.at[k],
            self.at.core_mate(),
            ("core", slot_at),
        )

    def over_x(self, name, items):
        f32 = jnp.float32
        k, whole = self.span(name)
        slot_at, width = k % 3, SUMS[k][1]
        self.free(("x", slot_at))
        self.came(self.cr.at[:, whole], self.c_ss.at[k], self.c_rs.at[k], self.at.core_mate())
        for slot, right, shift, wide in items:
            _, span = self.span(name, shift, wide)
            mine = times_plain(self.perm[slot, BLOCKS : BLOCKS + QUARTER, :], right[...])
            self.xs[slot_at, :, shift : shift + wide] = low(
                mine + self.cr[0:QUARTER, span].astype(f32)
            )
        self.post(
            self.xs.at[slot_at, :, pl.ds(0, width)],
            self.xr.at[:, whole],
            self.x_ss.at[k],
            self.x_rs.at[k],
            self.at.x_mate(),
            ("x", slot_at),
        )
        for slot, right, shift, wide in items:
            _, span = self.span(name, shift, wide)
            mine = times_plain(self.perm[slot, BLOCKS + QUARTER : 2 * BLOCKS, :], right[...])
            self.own[k % 4, :, shift : shift + wide] = mine + self.cr[QUARTER:BLOCKS, span].astype(f32)

    def along_z(self, name):
        k, span = self.span(name)
        self.came(self.xr.at[:, span], self.x_ss.at[k], self.x_rs.at[k], self.at.x_mate())
        own = self.own.at[k % 4, :, pl.ds(0, SUMS[k][1])]
        own[...] += self.xr[:, span].astype(jnp.float32)
        line = LineSum(
            self.at,
            own,
            self.zs.at[:, :, span],
            self.zr.at[:, :, span],
            self.z_ss.at[k],
            self.z_rs.at[k],
            SHARD,
            self.into(name),
        )
        line.begin()
        self.lines[name] = line

    def relay(self, name):
        self.lines[name].relay()

    def finish(self, name):
        self.lines[name].finish()

    def drain(self):
        for copy in self.last.values():
            copy.wait_send()
        for line in self.lines.values():
            line.drain()


class DecoderScatter(Mail):
    def __init__(self, place, one, two, out, bufs, sems):
        super().__init__()
        self.at, self.one, self.two, self.out = place, one, two, out
        self.cr, self.xs, self.xr, self.own, self.zs1, self.zr1, self.zs2, self.zr2 = bufs[:8]
        self.fin, self.ys, self.yr, self.whole, self.part = bufs[8:]
        (
            self.c_ss, self.c_rs, self.x_ss, self.x_rs, self.z1_ss, self.z1_rs,
            self.z2_ss, self.z2_rs, self.y_ss, self.y_rs, self.f_ss, self.f_rs,
        ) = sems
        self.lanes = pl.ds(pl.multiple_of(place.col * ONE_HALF, 128), ONE_HALF)

    def rows(self, s, x):
        return pl.ds(pl.multiple_of(((self.at.z + s) % 4 * 2 + x) * SHARD, 16), SHARD)

    def begin(self):
        at = self.at
        others = pl.ds(pl.multiple_of((1 - at.col) * ONE_HALF, 128), ONE_HALF)
        src = self.one.at[:, :, others]
        self.go(src, self.cr, self.c_ss, self.c_rs, at.core_mate())
        self.line_two = LineSum(
            at, self.two, self.zs2, self.zr2, self.z2_ss, self.z2_rs, 2 * SHARD,
            self.fin.at[:, pl.ds(ONE_HALF, TWO_HALF)],
        )
        self.line_two.begin()

    def sums(self, s, x):
        rows = self.rows(s, x)
        f32 = jnp.float32
        return self.one[:, rows, self.lanes].astype(f32) + self.cr[:, rows, :].astype(f32)

    def over_x(self):
        at = self.at
        self.came(self.cr, self.c_ss, self.c_rs, at.core_mate())
        for s in range(4):
            self.xs[s] = low(self.sums(s, 1 - at.x))
        self.go(self.xs, self.xr, self.x_ss, self.x_rs, at.x_mate())

    def along_z(self):
        at = self.at
        self.came(self.xr, self.x_ss, self.x_rs, at.x_mate())
        for s in range(4):
            total = self.sums(s, at.x) + self.xr[s].astype(jnp.float32)
            for r in range(2):
                first = (2 * s + r) * SHARD
                self.own[first : first + SHARD, :] = total[r]
        self.line_one = LineSum(
            at, self.own, self.zs1, self.zr1, self.z1_ss, self.z1_rs, 2 * SHARD,
            self.fin.at[:, pl.ds(0, ONE_HALF)],
        )
        self.line_one.begin()

    def over_rows(self):
        at = self.at
        self.line_one.finish()
        self.line_two.finish()
        rows = pl.ds(pl.multiple_of((1 - at.row) * SHARD, 8), SHARD)
        self.ys[...] = low(self.fin[rows, :])
        self.go(self.ys, self.yr, self.y_ss, self.y_rs, at.row_mate())

    def to_cores(self):
        at = self.at
        self.came(self.yr, self.y_ss, self.y_rs, at.row_mate())
        rows = pl.ds(pl.multiple_of(at.row * SHARD, 8), SHARD)
        self.whole[...] = self.fin[rows, :] + self.yr[...].astype(jnp.float32)
        theirs = pl.ds(pl.multiple_of((1 - at.col) * (SHARD // 2), 8), SHARD // 2)
        self.go(self.whole.at[theirs, :], self.part, self.f_ss, self.f_rs, at.core_mate())

    def finish(self):
        at = self.at
        width = ONE_HALF + TWO_HALF
        mine = pl.ds(pl.multiple_of(at.col * (SHARD // 2), 8), SHARD // 2)
        self.out[:, pl.ds(pl.multiple_of(at.col * width, 128), width)] = self.whole[mine, :]
        self.came(self.part, self.f_ss, self.f_rs, at.core_mate())
        self.out[:, pl.ds(pl.multiple_of((1 - at.col) * width, 128), width)] = self.part[...]

    def drain(self):
        super().drain()
        self.line_one.drain()
        self.line_two.drain()


class Everyone(Mail):
    def __init__(self, place, bufs, sems):
        super().__init__()
        self.at = place
        self.send, self.got, self.one, self.ones = bufs
        self.ss, self.rs, self.o_ss, self.o_rs = sems
        self.waits = []

    def first(self, enc, dec):
        self.send[0, 0:16, :] = enc
        self.send[0, 16:24, 0:DD] = dec
        self.send[0, 16:24, DD:D] = jnp.zeros((8, D - DD), jnp.float32)
        self.post(0)

    def post(self, i):
        at = self.at
        mates = ([at.core_mate()], [at.row_mate()], [at.x_mate()], [at.z_mate(s) for s in (1, 2, 3)])
        for j, mate in enumerate(mates[i]):
            self.go(
                self.send.at[i], self.got.at[i + j], self.ss.at[i + j], self.rs.at[i + j], mate
            )
        self.waits.append([(i + j, mate) for j, mate in enumerate(mates[i])])

    def stage(self, i):
        total = self.send[i - 1]
        for slot, mate in self.waits[i - 1]:
            self.came(self.got.at[slot], self.ss.at[slot], self.rs.at[slot], mate)
            total = total + self.got[slot]
        self.send[i] = total
        if i < 4:
            self.post(i)

    def total(self):
        return self.send[4]

    def number(self, value):
        at = self.at
        groups = (at.cube(), [at.z_mate(s) for s in (1, 2, 3)])
        total = jnp.zeros((8, 128), jnp.float32) + value
        first = 0
        for i, mates in enumerate(groups):
            self.one[i] = total
            for j, mate in enumerate(mates):
                slot = first + j
                self.go(
                    self.one.at[i], self.ones.at[slot], self.o_ss.at[slot], self.o_rs.at[slot], mate
                )
            for j, mate in enumerate(mates):
                slot = first + j
                self.came(self.ones.at[slot], self.o_ss.at[slot], self.o_rs.at[slot], mate)
                total = total + self.ones[slot]
            first += len(mates)
        return total[0:1, 0:1]


def encoder_attention_back(qkv_ref, d_out, out_ref):
    allowed = same_clip()
    halves = half_lanes()
    for p in range(3):
        spans = [slice(part * HALF_D + 128 * p, part * HALF_D + 128 * (p + 1)) for part in range(3)]
        q, k, v = (qkv_ref[:, span] for span in spans)
        d_pair = d_out[:, 128 * p : 128 * (p + 1)]
        found = []
        for h in range(2):
            one = jnp.where(halves[h], q, jnp.zeros_like(q))
            weights, total = encoder_scores(one, k, allowed)
            soft = weights / total
            d_one = jnp.where(halves[h], d_pair, jnp.zeros_like(d_pair))
            d_soft = times_trans(d_one, v)
            delta = jnp.sum(soft * d_soft, axis=-1, keepdims=True)
            d_scores = low(soft * (d_soft - delta))
            found.append(
                (
                    times_plain(d_scores, k) * SCALE,
                    trans_times(d_scores, q) * SCALE,
                    trans_times(low(soft), d_pair),
                )
            )
        for part in range(3):
            out_ref[:, spans[part]] = low(jnp.where(halves[0], found[0][part], found[1][part]))


def encoder_back_body(wide, *refs):
    f32 = jnp.float32
    gfeat_ref, x_ref, qkv_ref, o_ref, h_ref, slope_ref, px_ref, gain_ref, w_ref = refs[:9]
    refs = refs[9:]
    if wide:
        one_ref, two_ref, loss_ref, dvec_ref = refs[:4]
        refs = refs[4:]
    genc_ref, gemb_ref, gvec_ref = refs[:3]
    refs = refs[3:]
    if wide:
        gdec_ref, total_ref = refs[:2]
        refs = refs[2:]
    wa_s, wb_s, du_s, dqkv_s, feat_s, sent_s, got_s, h_s, slope_s = refs[:9]
    load_sem, f_ss, f_rs, y_ss, y_rs = refs[9:14]
    refs = refs[14:]
    place = Place()
    greet(place.mates(wide) + (place.cube()[2:3] + place.cube()[4:] if wide else []))
    swap = Swap(place, sent_s, got_s, y_ss, y_rs)
    swapped = remote(gfeat_ref, feat_s, f_ss, f_rs, place.row_mate())
    swapped.start()

    def into(name):
        if name == "emb":
            return gemb_ref
        start, width = {"at": (0, A_COLS), "up": (UP_AT, HID), "dn": (DN_AT, HID)}[name[:2]]
        return genc_ref.at[int(name[2]), :, pl.ds(start, width)]

    scatter = Scatter(place, refs[:9], refs[9:15], into) if wide else None
    dec = DecoderScatter(place, one_ref, two_ref, gdec_ref, refs[15:28], refs[28:40]) if wide else None
    everyone = Everyone(place, refs[40:44], refs[44:48]) if wide else None

    def load(layer, part):
        src, dst = (
            (w_ref.at[layer, :, pl.ds(0, A_COLS)], wa_s),
            (w_ref.at[layer, :, pl.ds(A_COLS, 2 * HID)], wb_s),
            (h_ref.at[layer], h_s),
            (slope_ref.at[layer], slope_s),
        )[part]
        return pltpu.make_async_copy(src, dst, load_sem.at[layer, part])

    load(1, 2).start()
    load(1, 3).start()
    load(1, 1).start()
    load(1, 0).start()

    lefts = {}

    def factor(slot, left):
        lefts[slot] = left
        if wide:
            scatter.turn(slot, left)

    def emit(name, items):
        if wide:
            scatter.cores(name, items)
            return
        for slot, right, shift, width in items:
            value = low(trans_times(lefts[slot], right[...]))
            if name == "emb":
                gemb_ref[...] = value
                continue
            start = {"at": 0, "up": UP_AT, "dn": DN_AT}[name[:2]] + shift
            genc_ref[int(name[2]), :, start : start + width] = value

    def later(step, *args):
        if wide:
            getattr(scatter, step)(*args)

    def dec_step(step):
        if wide:
            getattr(dec, step)()

    dec_step("begin")
    swapped.wait_recv()
    dec_step("over_x")
    near, far = gfeat_ref[...].astype(f32), feat_s[...].astype(f32)
    first = place.row == 0
    grad = jnp.concatenate([jnp.where(first, near, far), jnp.where(first, far, near)], axis=0)
    gvec_ref[...] = jnp.zeros(gvec_ref.shape, f32)

    def note(row, grad_out, scaled):
        gvec_ref[row : row + 1, :] = column_sum(grad_out * scaled)
        gvec_ref[row + 1 : row + 2, :] = column_sum(grad_out)

    scaled, inv = norm_rows(x_ref[2 * LAYERS])
    note(4 * LAYERS, grad, scaled)
    d_x = norm_rows_back(grad, scaled, inv, gain_ref[4 * LAYERS : 4 * LAYERS + 1, :])
    for layer in (1, 0):
        gains = gain_ref[4 * layer : 4 * layer + 4, :]
        dn, up, at = (f"{kind}{layer}" for kind in ("dn", "up", "at"))
        scaled2, inv2 = norm_rows(x_ref[2 * layer + 1])
        n2 = low(scaled2 * gains[2:3] + gains[3:4])
        d_low = low(d_x)
        factor(0, d_low)
        dn_items = [(0, h_s, 0, HID)]
        load(layer, 2).wait()
        emit(dn, dn_items)
        load(layer, 3).wait()
        load(layer, 1).wait()
        d_hidden = times_plain(d_low, wb_s[:, HID : 2 * HID])
        du_s[...] = low(d_hidden * slope_s[...])
        swap.start(2 * layer + 1, times_trans(du_s[...], wb_s[:, 0:HID]))
        factor(1, n2)
        up_items = [(1, du_s, 0, HID)]
        emit(up, up_items)
        later("over_x", dn, dn_items)
        later("over_x", up, up_items)
        if layer == 1:
            load(0, 2).start()
            load(0, 3).start()
            load(0, 1).start()
            if wide:
                dec.line_two.relay()
        else:
            later("along_z", "at1")
            later("relay", "up1")
        d_n2 = swap.total(2 * layer + 1)
        note(4 * layer + 2, d_n2, scaled2)
        d_x = d_x + norm_rows_back(d_n2, scaled2, inv2, gains[2:3])
        d_low = low(d_x)
        factor(2, d_low)
        load(layer, 0).wait()
        d_att = low(times_plain(d_low, wa_s[:, QKV_W:A_COLS]))
        encoder_attention_back(qkv_ref.at[layer], d_att, dqkv_s)
        swap.start(2 * layer, times_trans(dqkv_s[...], wa_s[:, 0:QKV_W]))
        scaled1, inv1 = norm_rows(x_ref[2 * layer])
        factor(3, low(scaled1 * gains[0:1] + gains[1:2]))
        at_items = [(3, dqkv_s, 0, QKV_W), (2, o_ref.at[layer], QKV_W, HALF_D)]
        emit(at, at_items)
        if layer == 1:
            load(0, 0).start()
            dec_step("along_z")
        else:
            later("relay", "at1")
        later("along_z", dn)
        later("over_x", at, at_items)
        later("along_z", up)
        later("relay", dn)
        if layer == 1:
            if wide:
                dec.line_one.relay()
        d_n1 = swap.total(2 * layer)
        note(4 * layer, d_n1, scaled1)
        d_x = d_x + norm_rows_back(d_n1, scaled1, inv1, gains[0:1])
    factor(0, low(d_x))
    emb_items = [(0, px_ref, 0, D)]
    emit("emb", emb_items)
    later("relay", "up0")
    later("over_x", "emb", emb_items)
    if wide:
        lane = lane_ids((1, DD))
        dvec = jnp.where(row_ids((8, 1)) < 7, dvec_ref[...], 0.0)
        loss = jnp.where(lane == 0, loss_ref[0:1, 0:1], 0.0)
        dvec = dvec + jnp.where(row_ids((8, 1)) == 7, loss, 0.0)
        everyone.first(0.5 * gvec_ref[...], dvec)
        dec.over_rows()
        everyone.stage(1)
        scatter.along_z("at0")
        everyone.stage(2)
        dec.to_cores()
        scatter.along_z("emb")
        everyone.stage(3)
        scatter.relay("at0")
        dec.finish()
        scatter.relay("emb")
        everyone.stage(4)
        square = jnp.zeros((1, 1), f32)
        for name, _ in SUMS:
            scatter.finish(name)
            whole = into(name)[...]
            square = square + jnp.sum(whole * whole)
        square = square + jnp.sum(gdec_ref[...] * gdec_ref[...])
        square = everyone.number(square)
        total_ref[...] = everyone.total()
        total_ref[23:24, 0:128] += jnp.where(lane_ids((1, 128)) == 1, square, 0.0)
        scatter.drain()
        dec.drain()
        everyone.drain()
    swapped.wait_send()
    swap.drain()


def run_encoder_back(wide, *operands):
    bf, f32 = jnp.bfloat16, jnp.float32
    vmem = pl.BlockSpec(memory_space=pltpu.VMEM)
    dma = pltpu.SemaphoreType.DMA
    shape = jax.ShapeDtypeStruct
    rows, kind = (SHARD, f32) if wide else (D, bf)
    scratch = [
        pltpu.VMEM((D, A_COLS), bf),
        pltpu.VMEM((D, 2 * HID), bf),
        pltpu.VMEM((PAIR, HID), bf),
        pltpu.VMEM((PAIR, QKV_W), bf),
        pltpu.VMEM((128, D), bf),
        pltpu.VMEM((2, PAIR, D), bf),
        pltpu.VMEM((2 * LAYERS, PAIR, D), bf),
        pltpu.VMEM((PAIR, HID), bf),
        pltpu.VMEM((PAIR, HID), f32),
        dma((LAYERS, 4)),
        dma,
        dma,
        dma((2 * LAYERS,)),
        dma((2 * LAYERS,)),
    ]
    outs = [
        shape((LAYERS, rows, ENC_COLS), kind),
        shape((rows, D), kind),
        shape((16, D), f32),
    ]
    anywhere = pl.BlockSpec(memory_space=pl.ANY)
    in_specs = [vmem] * 4 + [anywhere] * 2 + [vmem] * 2 + [anywhere]
    if wide:
        outs += [shape((SHARD // 2, PART_ONE + PART_TWO), f32), shape((24, D), f32)]
        in_specs += [vmem] * 4
        n = len(SUMS)
        both = ONE_HALF + TWO_HALF
        scratch += [
            pltpu.VMEM((4, D, PAIR), bf),
            pltpu.VMEM((2, D, PAIR), bf),
            pltpu.VMEM((2, BLOCKS, HID), bf),
            pltpu.VMEM((BLOCKS, SUM_COLS), bf),
            pltpu.VMEM((3, QUARTER, HID), bf),
            pltpu.VMEM((QUARTER, SUM_COLS), bf),
            pltpu.VMEM((3, SHARD, SUM_COLS), bf),
            pltpu.VMEM((4, SHARD, SUM_COLS), bf),
            pltpu.VMEM((4, QUARTER, HID), f32),
            dma((n,)),
            dma((n,)),
            dma((n,)),
            dma((n,)),
            dma((n, 4)),
            dma((n, 4)),
            pltpu.VMEM((2, DD, ONE_HALF), bf),
            pltpu.VMEM((4, 2, SHARD, ONE_HALF), bf),
            pltpu.VMEM((4, 2, SHARD, ONE_HALF), bf),
            pltpu.VMEM((8 * SHARD, ONE_HALF), f32),
            pltpu.VMEM((3, 2 * SHARD, ONE_HALF), bf),
            pltpu.VMEM((4, 2 * SHARD, ONE_HALF), bf),
            pltpu.VMEM((3, 2 * SHARD, TWO_HALF), bf),
            pltpu.VMEM((4, 2 * SHARD, TWO_HALF), bf),
            pltpu.VMEM((2 * SHARD, both), f32),
            pltpu.VMEM((SHARD, both), bf),
            pltpu.VMEM((SHARD, both), bf),
            pltpu.VMEM((SHARD, both), f32),
            pltpu.VMEM((SHARD // 2, both), f32),
            dma,
            dma,
            dma,
            dma,
            dma((4,)),
            dma((4,)),
            dma((4,)),
            dma((4,)),
            dma,
            dma,
            dma,
            dma,
            pltpu.VMEM((5, 24, D), f32),
            pltpu.VMEM((6, 24, D), f32),
            pltpu.VMEM((2, 8, 128), f32),
            pltpu.VMEM((10, 8, 128), f32),
            dma((6,)),
            dma((6,)),
            dma((10,)),
            dma((10,)),
        ]
    return pl.pallas_call(
        functools.partial(encoder_back_body, wide),
        out_shape=tuple(outs),
        in_specs=in_specs,
        out_specs=(vmem,) * len(outs),
        scratch_shapes=scratch,
        compiler_params=pltpu.CompilerParams(
            collective_id=2, has_side_effects=True, vmem_limit_bytes=63 * MIB
        ),
        cost_estimate=pl.CostEstimate(
            flops=20 * 10**9, bytes_accessed=60 * 10**6, transcendentals=10**6
        ),
        name="encoder_back",
    )(*operands)


def adam_at(refs, spot, grad, decay_rate, step_rate):
    master, first, second, master_out, first_out, second_out = refs
    new = adam_update(master[spot], first[spot], second[spot], grad, decay_rate, step_rate)
    master_out[spot], first_out[spot], second_out[spot] = new


def head_pieces(rows, heads):
    pieces = []
    for h in range(heads):
        for part in range(3):
            at = (part * heads + h) * HEAD
            pieces.append(rows[:, at : at + HEAD])
    pieces.append(rows[:, 3 * heads * HEAD :])
    return jnp.concatenate(pieces, axis=-1)


def update_body(*refs):
    f32 = jnp.float32
    total_ref = refs[0]
    grads = refs[1:4]
    states = [refs[4 + 3 * i : 7 + 3 * i] for i in range(5)]
    loss_ref, norm_ref = refs[19:21]
    outs = [refs[21 + 3 * i : 24 + 3 * i] for i in range(5)]
    total = total_ref[...]
    squares = jnp.sum(total[0:23, :] * total[0:23, :]) + jnp.sum(total[23:24, 1:2])
    norm = jnp.sqrt(jnp.zeros((1, 1), f32) + squares)
    factor = jnp.minimum(1.0, CLIP_MAX / (norm + 1e-06))
    loss_ref[0, 0] = jnp.sum(total[23:24, 0:1])
    norm_ref[0, 0] = jnp.sum(norm)
    blocks = SHARD // 8

    @pl.loop(0, LAYERS * blocks)
    def _(i):
        rows = pl.ds(pl.multiple_of(i % blocks * 8, 8), 8)
        grad = head_pieces(grads[0][i // blocks, rows, :], HEADS // 2)
        spot = (i // blocks, 0, rows, slice(None))
        adam_at(states[0] + outs[0], spot, grad * factor, DECAY, RATE)

    adam_at(states[1] + outs[1], (0,), grads[1][...] * factor, DECAY, RATE)
    both = ONE_HALF + TWO_HALF
    grad = grads[2][...]
    one = jnp.concatenate([grad[:, 0:ONE_HALF], grad[:, both : both + ONE_HALF]], axis=-1)
    two = jnp.concatenate([grad[:, ONE_HALF:both], grad[:, both + ONE_HALF :]], axis=-1)
    pieces = [one[:, 0:ED_AT], two[:, 0:192], two[:, UP_TWO:], one[:, ED_AT : ED_AT + DD]]
    grad = head_pieces(jnp.concatenate(pieces, axis=-1), DHEADS // 2)
    adam_at(states[2] + outs[2], (0,), grad * factor, DECAY, RATE)
    place = Place()
    own = shard_at(place.z, place.x, place.col)
    for kind, top, count, width in ((3, 0, 10, D), (4, 16, 7, DD)):
        share = width // N_SHARDS
        turned = pltpu.roll(total, (D - own * share) % D, 1)
        grad = turned[top : top + count, 0:share] * factor
        adam_at(states[kind] + outs[kind], (slice(None), slice(None)), grad, 0.0, VEC_RATE)


def run_update(total, grads, states):
    f32 = jnp.float32
    vmem = pl.BlockSpec(memory_space=pltpu.VMEM)
    smem = pl.BlockSpec(memory_space=pltpu.SMEM)
    flat = [a for triple in states for a in triple]
    scalar = jax.ShapeDtypeStruct((1, 1), f32)
    outs = (scalar, scalar) + tuple(jax.ShapeDtypeStruct(a.shape, f32) for a in flat)
    return pl.pallas_call(
        update_body,
        out_shape=outs,
        in_specs=[vmem] * (4 + len(flat)),
        out_specs=(smem, smem) + (vmem,) * len(flat),
        compiler_params=pltpu.CompilerParams(vmem_limit_bytes=60 * MIB),
        name="update",
    )(total, *grads, *flat)


def head_order(matrix, heads, width):
    lead = matrix.shape[:-1]
    cut = matrix[..., :width].reshape(lead + (heads, 3, HEAD))
    cut = jnp.swapaxes(cut, -3, -2).reshape(lead + (width,))
    return jnp.concatenate([cut, matrix[..., width:]], axis=-1)


def head_order_back(matrix, heads, width):
    lead = matrix.shape[:-1]
    cut = matrix[..., :width].reshape(lead + (3, heads, HEAD))
    cut = jnp.swapaxes(cut, -3, -2).reshape(lead + (width,))
    return jnp.concatenate([cut, matrix[..., width:]], axis=-1)


def sine_table(length, width):
    column = np.arange(width)
    freq = np.exp(-math.log(10000.0) * (2.0 * (column // 2)) / width)
    angle = np.arange(length)[:, None] * freq
    table = np.where(column % 2 == 0, np.sin(angle), np.cos(angle))
    return np.pad(table, ((0, ROWS - length), (0, 0))).astype(np.float32)


def frequency_rows(width):
    column = np.arange(width)
    freq = np.exp(-math.log(10000.0) * (2.0 * (column // 2)) / width)
    return np.broadcast_to(freq.astype(np.float32), (8, width))


def split_parts(matrices):
    gap = [(0, 0)] * (matrices.ndim - 1)
    one = jnp.concatenate([matrices[..., :ED_AT], matrices[..., 3072:]], axis=-1)
    one = jnp.pad(one, gap + [(0, PART_ONE - one.shape[-1])])
    out = jnp.pad(matrices[..., ED_AT:768], gap + [(0, UP_TWO - 192)])
    return one, jnp.concatenate([out, matrices[..., 768:3072]], axis=-1)


def join_parts(one, two):
    return jnp.concatenate(
        [one[..., :ED_AT], two[..., :192], two[..., UP_TWO:], one[..., ED_AT : ED_AT + DD]], axis=-1
    )


def gather_vectors(enc_vec, dec_vec, group):
    vectors = jnp.concatenate([enc_vec.reshape(-1), dec_vec.reshape(-1)])
    vectors = lax.all_gather(low(vectors), group, axis=0, tiled=False).astype(jnp.float32)
    cut = enc_vec.size
    enc_gains = jnp.swapaxes(vectors[:, :cut].reshape(-1, *enc_vec.shape), 0, 1).reshape(-1, D)
    dec_gains = jnp.swapaxes(vectors[:, cut:].reshape(-1, *dec_vec.shape), 0, 1).reshape(-1, DD)
    return (
        jnp.pad(enc_gains, ((0, 16 - enc_gains.shape[0]), (0, 0))),
        jnp.pad(dec_gains, ((0, 8 - dec_gains.shape[0]), (0, 0))),
    )


def update_plain(loss_part, dec_vec_grads, enc_vec_grads, grads, states):
    everyone = ("row", "clip", "col")
    n_enc, n_dec = states[3][0].shape[0], states[4][0].shape[0]
    enc_vec_total, dec_vec_total, loss_total, square = lax.psum(
        (
            0.5 * enc_vec_grads[:n_enc],
            dec_vec_grads[:n_dec],
            loss_part,
            sum(jnp.sum(g * g) for g in grads),
        ),
        everyone,
    )
    square = square + jnp.sum(enc_vec_total**2) + jnp.sum(dec_vec_total**2)
    grad_norm = jnp.sqrt(square)
    factor = jnp.minimum(1.0, CLIP_MAX / (grad_norm + 1e-06))
    shard = lax.axis_index("clip") * lax.axis_size("col") + lax.axis_index("col")
    own = []
    for total, state in ((enc_vec_total, states[3][0]), (dec_vec_total, states[4][0])):
        width = state.shape[1]
        own.append(lax.dynamic_slice_in_dim(total, shard * width, width, 1))
    decays = (DECAY, DECAY, DECAY, 0.0, 0.0)
    rates = (RATE, RATE, RATE, VEC_RATE, VEC_RATE)
    results = []
    for triple, grad, decay_rate, step_rate in zip(states, (*grads, *own), decays, rates):
        grad = grad.reshape(triple[0].shape)
        results.extend(adam_update(*triple, grad * factor, decay_rate, step_rate))
    return (loss_total, grad_norm, *results)


def local(
    patches,
    visible,
    masked,
    enc_layers,
    enc_first,
    enc_second,
    embed,
    embed_first,
    embed_second,
    dec_mats,
    dec_first,
    dec_second,
    enc_vec,
    enc_vec_first,
    enc_vec_second,
    dec_vec,
    dec_vec_first,
    dec_vec_second,
):
    f32 = jnp.float32
    group = ("clip", "col")
    everyone = ("row", "clip", "col")
    wide = lax.axis_size("clip") == 8 and lax.axis_size("col") == 2
    freq = jnp.asarray(frequency_rows(D))
    table = jnp.asarray(sine_table(TUBES, DD))
    if wide:
        feat, xs, qkv, att, hid, slope, px, padded, enc_gains, dec_gains, enc_full, one, two = (
            run_encoder(True, visible, patches, freq, embed, enc_layers, dec_mats, enc_vec, dec_vec)
        )
    else:
        embed_full = lax.all_gather(low(embed[0]), group, axis=0, tiled=True)
        enc_here = low(head_order(enc_layers[:, 0], HEADS // 2, QKV_W))
        enc_full = lax.all_gather(enc_here, group, axis=1, tiled=True)
        dec_here = low(head_order(dec_mats[0], DHEADS // 2, ED_AT))
        dec_full = lax.all_gather(dec_here, everyone, axis=0, tiled=True).reshape(2, DD, -1)
        enc_gains, dec_gains = gather_vectors(enc_vec, dec_vec, group)
        feat, xs, qkv, att, hid, slope, px, padded = run_encoder(
            False, visible, patches, freq, embed_full, enc_full, enc_gains
        )
        one, two = split_parts(dec_full)
    loss_block, grad_one, grad_two, dec_vec_grads, grad_feat = run_decoder(
        wide, visible, feat, padded, table, one, two, dec_gains
    )
    kept = (grad_feat, xs, qkv, att, hid, slope, px, enc_gains, enc_full)
    states = (
        (enc_layers, enc_first, enc_second),
        (embed, embed_first, embed_second),
        (dec_mats, dec_first, dec_second),
        (enc_vec, enc_vec_first, enc_vec_second),
        (dec_vec, dec_vec_first, dec_vec_second),
    )
    if wide:
        enc_total, embed_total, _, dec_total, total = run_encoder_back(
            True, *kept, grad_one, grad_two, loss_block, dec_vec_grads
        )
        grads = (enc_total, embed_total, dec_total)
        loss_total, grad_norm, *results = run_update(total, grads, states)
        return (loss_total[0, 0], grad_norm[0, 0], *results)
    dec_grads = join_parts(grad_one, grad_two)
    dec_total = lax.psum_scatter(
        dec_grads.reshape(-1, dec_grads.shape[-1]), everyone, scatter_dimension=0, tiled=True
    ).astype(f32)
    enc_total, embed_total, enc_vec_grads = run_encoder_back(False, *kept)
    enc_total = lax.psum_scatter(enc_total, group, scatter_dimension=1, tiled=True).astype(f32)
    embed_total = lax.psum_scatter(embed_total, group, scatter_dimension=0, tiled=True).astype(f32)
    grads = (
        head_order_back(enc_total, HEADS // 2, QKV_W),
        embed_total,
        head_order_back(dec_total, DHEADS // 2, ED_AT),
    )
    return update_plain(loss_block[0, 0], dec_vec_grads, enc_vec_grads, grads, states)


def solution(mesh):
    in_specs = (
        P(None, ("clip", "col"), None, "row"),
        P(None, ("clip", "col"), None),
        P(None, ("clip", "col"), None),
        P(None, "row", ("clip", "col"), None),
        P(None, "row", ("clip", "col"), None),
        P(None, "row", ("clip", "col"), None),
        P("row", ("clip", "col"), None),
        P("row", ("clip", "col"), None),
        P("row", ("clip", "col"), None),
        P("row", ("clip", "col"), None),
        P("row", ("clip", "col"), None),
        P("row", ("clip", "col"), None),
        P(None, ("clip", "col")),
        P(None, ("clip", "col")),
        P(None, ("clip", "col")),
        P(None, ("clip", "col")),
        P(None, ("clip", "col")),
        P(None, ("clip", "col")),
    )
    out_specs = (
        P(),
        P(),
        P(None, "row", ("clip", "col"), None),
        P(None, "row", ("clip", "col"), None),
        P(None, "row", ("clip", "col"), None),
        P("row", ("clip", "col"), None),
        P("row", ("clip", "col"), None),
        P("row", ("clip", "col"), None),
        P("row", ("clip", "col"), None),
        P("row", ("clip", "col"), None),
        P("row", ("clip", "col"), None),
        P(None, ("clip", "col")),
        P(None, ("clip", "col")),
        P(None, ("clip", "col")),
        P(None, ("clip", "col")),
        P(None, ("clip", "col")),
        P(None, ("clip", "col")),
    )
    return jax.shard_map(local, mesh=mesh, in_specs=in_specs, out_specs=out_specs, check_vma=False)
```

```python
import functools
import math

import jax
import jax.numpy as jnp
import numpy as np
from jax import lax
from jax.experimental import pallas as pl
from jax.experimental.pallas import tpu as pltpu
from jax.sharding import PartitionSpec as P

D = 768
HEADS = 12
HEAD = 64
FF = 3072
DD = 384
DHEADS = 6
DFF = 1536
PIX = 1536
TUBES = 1176
VIS = 118
LAYERS = 2
MICRO = 2
STEP = 10
MASKED = 1058


EPS_NORM = 1e-06
CLIP_MAX = 1.0
BETA_ONE = 0.9
BETA_TWO = 0.999
RATE = 0.06
VEC_RATE = 0.2
DECAY = 0.05
EPS_ADAM = 1e-08


def times_plain(left, right):
    return jnp.dot(left, right, preferred_element_type=jnp.float32)


def times_trans(left, right):
    return lax.dot_general(
        left, right, (((1,), (1,)), ((), ())), preferred_element_type=jnp.float32
    )


def trans_times(left, right):
    return lax.dot_general(
        left, right, (((0,), (0,)), ((), ())), preferred_element_type=jnp.float32
    )


def gelu_pair(values):
    cumul = 0.5 * (1.0 + lax.erf(values * 0.7071067811865476))
    density = jnp.exp(-0.5 * values * values) * 0.3989422804014327
    return (values * cumul, cumul + values * density)


def adam_update(master, first, second, grad_clip, decay_rate, step_rate):
    first_new = BETA_ONE * first + (1.0 - BETA_ONE) * grad_clip
    second_new = BETA_TWO * second + (1.0 - BETA_TWO) * grad_clip * grad_clip
    first_hat = first_new / (1.0 - BETA_ONE**STEP)
    second_hat = second_new / (1.0 - BETA_TWO**STEP)
    master_new = master - step_rate * (
        first_hat / (jnp.sqrt(second_hat) + EPS_ADAM) + decay_rate * master
    )
    return (master_new, first_new, second_new)


LOG2E = 1.4426950408889634
SCALE = HEAD ** (-0.5)
MIB = 1 << 20
MESH_IDS = pl.DeviceIdType.MESH
N_SHARDS = 16
SHARD = D // N_SHARDS
PART_ONE = 1024
PART_TWO = 2560
ONE_HALF, TWO_HALF = PART_ONE // 2, PART_TWO // 2
ED_AT = 3 * DD // 2
UP_TWO, DN_TWO, HD_TWO = 256, 1024, 1792


def low(values):
    return values.astype(jnp.bfloat16)


def lane_ids(shape):
    return lax.broadcasted_iota(jnp.int32, shape, len(shape) - 1)


def row_ids(shape):
    return lax.broadcasted_iota(jnp.int32, shape, 0)


def remote(src, dst, send_sem, recv_sem, device):
    return pltpu.make_async_remote_copy(
        src_ref=src,
        dst_ref=dst,
        send_sem=send_sem,
        recv_sem=recv_sem,
        device_id=device,
        device_id_type=MESH_IDS,
    )


class Place:
    def __init__(self):
        self.clip = lax.axis_index("clip")
        self.row = lax.axis_index("row")
        self.col = lax.axis_index("col")
        self.z = self.clip // 2
        self.x = self.clip % 2

    def z_mate(self, step):
        return (((self.z + step) % 4) * 2 + self.x, self.row, self.col)

    def x_mate(self):
        return (self.z * 2 + 1 - self.x, self.row, self.col)

    def core_mate(self):
        return (self.clip, self.row, 1 - self.col)

    def row_mate(self):
        return (self.clip, 1 - self.row, self.col)

    def mates(self, wide):
        near = [self.row_mate()]
        if wide:
            near += [self.core_mate(), self.x_mate()] + [self.z_mate(s) for s in (1, 2, 3)]
        return near

    def cube(self):
        found = []
        for i in range(1, 8):
            x = 1 - self.x if i & 1 else self.x
            row = 1 - self.row if i & 2 else self.row
            col = 1 - self.col if i & 4 else self.col
            found.append((self.z * 2 + x, row, col))
        return found


def shard_at(z, x, col):
    return (z * 2 + x) * 2 + col


def greet(mates):
    barrier = pltpu.get_barrier_semaphore()
    for mate in mates:
        pl.semaphore_signal(barrier, inc=1, device_id=mate, device_id_type=MESH_IDS)
    pl.semaphore_wait(barrier, len(mates))


class Mail:
    def __init__(self):
        self.sent = []

    def go(self, src, dst, ss, rs, device, only=None):
        copy = remote(src, dst, ss, rs, device)
        if only is None:
            copy.start()
        else:
            pl.when(only)(copy.start)
        self.sent.append((copy, only))

    def came(self, dst, ss, rs, device):
        remote(dst, dst, ss, rs, device).wait_recv()

    def drain(self):
        for copy, only in self.sent:
            if only is None:
                copy.wait_send()
            else:
                pl.when(only)(copy.wait_send)
        self.sent = []


class Gather(Mail):
    def __init__(self, place, own, spot, sems, over_x_first=None):
        super().__init__()
        self.at, self.own, self.spot, self.turned = place, own, spot, over_x_first
        self.z_ss, self.z_rs, self.x_ss, self.x_rs, self.c_ss, self.c_rs = sems

    def line(self, k, src, dst):
        for s, only in ((2, None), (1, self.at.z != 3), (3, self.at.z != 0)):
            ss, rs = self.z_ss.at[k, s - 1], self.z_rs.at[k, s - 1]
            self.go(src, dst, ss, rs, self.at.z_mate(s), only)

    def landed(self, k, s, spot):
        at = self.at
        self.came(spot, self.z_ss.at[k, s - 1], self.z_rs.at[k, s - 1], at.z_mate(s))
        if s == 2:
            for step, only in ((3, at.z == 1), (1, at.z == 2)):
                slot = (2 + step) % 4 - 1
                ss, rs = self.z_ss.at[k, 3], self.z_rs.at[k, slot]
                self.go(spot, spot, ss, rs, at.z_mate(step), only)

    def to_core(self, k, slot, spot):
        self.go(spot, spot, self.c_ss.at[k, slot], self.c_rs.at[k, slot], self.at.core_mate())

    def begin(self, k):
        at = self.at
        src, dst = self.own(k), self.spot(k, at.z, at.x, at.col)
        if k == self.turned:
            self.go(src, dst, self.x_ss.at[k, 0], self.x_rs.at[k, 0], at.x_mate())
        self.line(k, src, dst)
        if k != self.turned:
            self.go(src, dst, self.x_ss.at[k, 0], self.x_rs.at[k, 0], at.x_mate())
        self.go(src, dst, self.c_ss.at[k, 0], self.c_rs.at[k, 0], at.core_mate())

    def begin_lined(self, blocks):
        at = self.at
        for s in (0, 2, 1, 3):
            z = (at.z - s) % 4
            spot = self.spot(0, z, at.x, at.col)
            self.go(blocks.at[z], spot, self.x_ss.at[0, s], self.x_rs.at[0, s], at.x_mate())
            self.go(blocks.at[z], spot, self.c_ss.at[0, s], self.c_rs.at[0, s], at.core_mate())

    def begin_turned(self, extra):
        at, k = self.at, self.turned
        spot = self.spot(k, at.z, 1 - at.x, at.col)
        self.came(spot, self.x_ss.at[k, 0], self.x_rs.at[k, 0], at.x_mate())
        self.line(extra, spot, spot)
        self.to_core(k, 4, spot)

    def forward_turned(self, extra):
        at, k = self.at, self.turned
        for s in (2, 1, 3):
            for line, x, slot in ((k, at.x, s), (extra, 1 - at.x, 4 + s)):
                spot = self.spot(k, (at.z - s) % 4, x, at.col)
                self.landed(line, s, spot)
                self.to_core(k, slot, spot)

    def forward(self, k):
        for s in (2, 1, 3):
            self.one("forward", s, k)

    def across(self, k):
        for s in (0, 2, 1, 3):
            self.one("across", s, k)

    def one(self, step, s, k=0):
        at = self.at
        if step == "across":
            spot = self.spot(k, (at.z - s) % 4, 1 - at.x, at.col)
            self.came(spot, self.x_ss.at[k, s], self.x_rs.at[k, s], at.x_mate())
            self.to_core(k, 4 + s, spot)
            return
        spot = self.spot(k, (at.z - s) % 4, at.x, at.col)
        self.landed(k, s, spot)
        self.go(spot, spot, self.x_ss.at[k, s], self.x_rs.at[k, s], at.x_mate())
        self.to_core(k, s, spot)

    def finish(self, k):
        at = self.at
        for s in range(8):
            x = at.x if s < 4 else 1 - at.x
            spot = self.spot(k, (at.z - s % 4) % 4, x, 1 - at.col)
            self.came(spot, self.c_ss.at[k, s], self.c_rs.at[k, s], at.core_mate())


class LineSum(Mail):
    def __init__(self, place, own, sent, got, ss, rs, rows, into):
        super().__init__()
        self.at, self.own, self.out, self.got, self.ss, self.rs = place, own, sent, got, ss, rs
        self.rows, self.into = rows, into
        self.middle = jnp.logical_or(place.z == 1, place.z == 2)

    def block(self, s):
        return self.own[self.rows * s : self.rows * (s + 1), :]

    def begin(self):
        at = self.at
        self.into[...] = self.block(0)
        for s, end, step in ((1, 3, 3), (3, 0, 1)):
            self.out[s - 1] = low(self.block(s))
            src = self.out.at[s - 1]
            dst = self.got.at[s - 1]
            inner = at.z != end
            self.go(src, dst, self.ss.at[s - 1], self.rs.at[s - 1], at.z_mate(s), inner)
            other = self.got.at[3]
            self.go(src, other, self.ss.at[3], self.rs.at[3], at.z_mate(step), at.z == end)
        outer = jnp.logical_not(self.middle)

        @pl.when(outer)
        def _():
            self.out[1] = low(self.block(2))

        self.go(
            self.out.at[1], self.got.at[1], self.ss.at[1], self.rs.at[1], at.z_mate(2), outer
        )

    def relay(self):
        at = self.at

        @pl.when(self.middle)
        def _():
            self.came(self.got.at[3], self.ss.at[3], self.rs.at[3], at.z_mate(1))
            self.out[1] = low(self.block(2) + self.got[3].astype(jnp.float32))

        self.go(
            self.out.at[1], self.got.at[1], self.ss.at[1], self.rs.at[1], at.z_mate(2), self.middle
        )

    def finish(self):
        at = self.at

        def add(s):
            self.came(self.got.at[s - 1], self.ss.at[s - 1], self.rs.at[s - 1], at.z_mate(s))
            self.into[...] += self.got[s - 1].astype(jnp.float32)

        add(2)
        pl.when(at.z != 0)(lambda: add(1))
        pl.when(at.z != 3)(lambda: add(3))


class Swap:
    def __init__(self, place, sent, got, send_sems, recv_sems):
        self.at, self.sent, self.got = place, sent, got
        self.ss, self.rs = send_sems, recv_sems
        self.copies = {}

    def start(self, i, value):
        slot = i % self.sent.shape[0]
        for j in [j for j in self.copies if j % self.sent.shape[0] == slot]:
            self.copies.pop(j).wait_send()
        self.sent[slot] = low(value)
        copy = remote(
            self.sent.at[slot], self.got.at[i], self.ss.at[i], self.rs.at[i], self.at.row_mate()
        )
        copy.start()
        self.copies[i] = copy

    def total(self, i):
        self.copies[i].wait_recv()
        sent = self.sent[i % self.sent.shape[0]]
        return sent.astype(jnp.float32) + self.got[i].astype(jnp.float32)

    def drain(self):
        for copy in self.copies.values():
            copy.wait_send()


ROWS = 1216
LANES = 1280
STEP_ROWS = 608
N_STEPS = ROWS // STEP_ROWS
KEY_ROWS = 640


def norm_rows(rows):
    average = jnp.mean(rows, axis=-1, keepdims=True)
    centred = rows - average
    inv_dev = lax.rsqrt(jnp.mean(centred * centred, axis=-1, keepdims=True) + EPS_NORM)
    return centred * inv_dev, inv_dev


def norm_rows_back(grad_out, scaled, inv_dev, gain_row):
    inner = grad_out * gain_row
    return inv_dev * (
        inner
        - jnp.mean(inner, axis=-1, keepdims=True)
        - scaled * jnp.mean(inner * scaled, axis=-1, keepdims=True)
    )


def column_sum(values):
    return jnp.sum(values, axis=0, keepdims=True)


def decoder_body(wide, *refs):
    bf, f32 = jnp.bfloat16, jnp.float32
    seen_ref, feat_ref, padded_ref, table_ref, one_ref, two_in, vec_ref = refs[:7]
    loss_ref, gone_ref, gtwo_ref, gvec_ref, gfeat_ref = refs[7:12]
    z_s, n1_s, q_s, k_s, v_s, o_s, do_s, dx_s, dqkv_s, dqt_s, lse_s, delta_s = refs[12:24]
    lse_t, delta_t, wqkv_s, wo_s, y_s, gqkv_s, go_s, gup_s, gdn_s, ghd_s = refs[24:34]
    gy_s, gv_s, pixel_ref, seen_s, near_sem, far_ss, far_rs = refs[34:41]
    if wide:
        two_s, cr_s, xs_s, xr_s, c_ss, c_rs, x_ss, x_rs = refs[41:49]
        g_s = two_s
    else:
        two_s, g_s = two_in, gtwo_ref
    place = Place()
    greet(place.mates(wide))

    def chip_rows(s, x):
        return pl.ds(pl.multiple_of(((place.z + s) % 4 * 2 + x) * SHARD, 16), SHARD)

    own_lanes = pl.ds(pl.multiple_of(place.col * TWO_HALF, 128), TWO_HALF)
    other_lanes = pl.ds(pl.multiple_of((1 - place.col) * TWO_HALF, 128), TWO_HALF)
    if wide:

        def spot(k, z, x, col):
            rows = pl.ds(pl.multiple_of((z * 2 + x) * SHARD, 16), SHARD)
            return two_s.at[:, rows, pl.ds(pl.multiple_of(col * TWO_HALF, 128), TWO_HALF)]

        gather = Gather(place, lambda k: two_in, spot, refs[49:55])
        gather.begin_lined(two_in)
        for step in range(4):
            two_s[:, chip_rows(step, place.x), own_lanes] = two_in[(place.z + step) % 4]

    def tile(i):
        return pl.ds(pl.multiple_of(i * STEP_ROWS, STEP_ROWS), STEP_ROWS)

    def near(i):
        rows = tile(i)
        return pltpu.make_async_copy(
            padded_ref.at[place.row, rows, :], pixel_ref.at[place.row, rows, :], near_sem.at[i]
        )

    def far(i, half):
        rows = tile(i)
        return remote(
            padded_ref.at[1 - place.row, rows, :],
            pixel_ref.at[half, rows, :],
            far_ss.at[i],
            far_rs.at[i],
            place.row_mate(),
        )

    @pl.loop(0, N_STEPS)
    def _(i):
        near(i).start()
        far(i, place.row).start()

    half = 3 * HEAD
    up0, dn0, hd0, ed0 = UP_TWO, DN_TWO, HD_TWO, ED_AT
    vec = vec_ref[...]
    gain1, shift1, gain2, shift2, gain_f, shift_f, token = [vec[i : i + 1] for i in range(7)]

    for part in range(3):
        for r in range(2):
            wqkv_s[:, part * DD + r * half : part * DD + (r + 1) * half] = one_ref[
                r, :, part * half : (part + 1) * half
            ]
    for ref in (q_s, k_s, v_s, do_s):
        ref[ROWS:LANES, :] = jnp.zeros((LANES - ROWS, DD), bf)
    delta_s[ROWS:LANES, :] = jnp.zeros((LANES - ROWS, 128), f32)
    for ref in (gqkv_s, go_s, gup_s, gdn_s, ghd_s, gy_s, gv_s):
        ref[...] = jnp.zeros(ref.shape, f32)
    for r in range(2):
        y_s[:, r * DD : (r + 1) * DD] = low(
            times_trans(feat_ref[:, r * DD : (r + 1) * DD], one_ref[r, :, ed0 : ed0 + DD])
        )
    seen_s[...] = jnp.full(seen_s.shape, -1, jnp.int32)
    seen_s[0:1, 0:VIS] = seen_ref[place.row]
    seen = seen_s[0:1, :]

    def picks(i):
        ids = row_ids((STEP_ROWS, 128)) + i * STEP_ROWS
        hits = ids == seen
        taken = jnp.sum(hits.astype(f32), axis=-1, keepdims=True)
        valid = (row_ids((STEP_ROWS, 1)) + i * STEP_ROWS < TUBES).astype(f32)
        return hits.astype(bf), valid - taken

    @pl.loop(0, N_STEPS)
    def _(i):
        hits, hidden = picks(i)
        placed = times_plain(hits, y_s[...])
        z = placed[:, :DD] + placed[:, DD:] + table_ref[tile(i), :] + token * hidden
        z_s[tile(i), :] = z
        scaled, _ = norm_rows(z)
        n1 = low(scaled * gain1 + shift1)
        n1_s[tile(i), :] = n1
        q_s[tile(i), :] = low(times_plain(n1, wqkv_s[:, 0:DD]))
        k_s[tile(i), :] = low(times_plain(n1, wqkv_s[:, DD : 2 * DD]))
        v_s[tile(i), :] = low(times_plain(n1, wqkv_s[:, 2 * DD : 3 * DD]))

    first_half = lane_ids((1, 128)) < HEAD
    half_masks = [first_half, jnp.logical_not(first_half)]
    last_keys = lane_ids((1, 128)) < TUBES - (LANES - 128)
    ones = jnp.ones((LANES, 128), bf)
    lse_s[...] = jnp.zeros(lse_s.shape, f32)
    for p in range(3):
        lanes = slice(128 * p, 128 * (p + 1))

        @pl.loop(0, N_STEPS)
        def _(i):
            queries = q_s[tile(i), lanes]
            parts = []
            stat = lse_s[tile(i), :]
            for h in range(2):
                one = jnp.where(half_masks[h], queries, jnp.zeros_like(queries))
                scores = times_trans(one, k_s[:, lanes])
                tail = jnp.where(last_keys, scores[:, LANES - 128 :], -1e30)
                scores = jnp.concatenate([scores[:, : LANES - 128], tail], axis=-1)
                top = jnp.max(scores, axis=-1, keepdims=True) * (SCALE * LOG2E)
                weights = low(jnp.exp2(scores * (SCALE * LOG2E) - top))
                both = times_plain(weights, jnp.concatenate([v_s[:, lanes], ones], axis=-1))
                total = both[:, 128:129]
                parts.append(both[:, 0:128] / total)
                lse = top + jnp.log(total) * LOG2E
                stat = jnp.where(lane_ids((1, 128)) == 2 * p + h, lse, stat)
            lse_s[tile(i), :] = stat
            o_s[tile(i), lanes] = low(jnp.where(first_half, parts[0], parts[1]))

        if wide:
            for step in ((0,), (2,), (1, 3))[p]:
                gather.one("across", step)
    if wide:
        gather.finish(0)
    for r in range(2):
        wo_s[:, r * half : (r + 1) * half] = two_s[r, :, 0:half]
    lse_t[...] = lse_s[...].T

    @pl.loop(0, N_STEPS)
    def _(i):
        _, hidden = picks(i)
        near(i).wait()
        far(i, 1 - place.row).wait_recv()
        attended = o_s[tile(i), :]
        x1 = z_s[tile(i), :] + times_trans(attended, wo_s[...])
        scaled2, inv2 = norm_rows(x1)
        n2 = low(scaled2 * gain2 + shift2)
        x2 = x1
        acts, slopes, d_preds, d_us = [], [], [], []
        for r in range(2):
            u = times_plain(n2, two_s[r, :, up0 : up0 + 768])
            act, slope = gelu_pair(u)
            act = low(act)
            acts.append(act)
            slopes.append(slope)
            x2 = x2 + times_trans(act, two_s[r, :, dn0 : dn0 + 768])
        scaled_f, inv_f = norm_rows(x2)
        t = low(scaled_f * gain_f + shift_f)
        d_t = jnp.zeros((STEP_ROWS, DD), f32)
        for r in range(2):
            error = times_plain(t, two_s[r, :, hd0 : hd0 + 768]) - pixel_ref[r, tile(i), :].astype(
                f32
            )
            error = error * hidden
            gv_s[7:8, :] += column_sum(error * error)
            d_pred = low(error * (2.0 / PIX))
            d_preds.append(d_pred)
            d_t = d_t + times_trans(d_pred, two_s[r, :, hd0 : hd0 + 768])
        ghd_s[...] += trans_times(t, jnp.concatenate(d_preds, axis=-1))
        gv_s[4:5, 0:DD] += column_sum(d_t * scaled_f)
        gv_s[5:6, 0:DD] += column_sum(d_t)
        d_x2 = norm_rows_back(d_t, scaled_f, inv_f, gain_f)
        d_low = low(d_x2)
        d_n2 = jnp.zeros((STEP_ROWS, DD), f32)
        for r in range(2):
            d_u = low(times_plain(d_low, two_s[r, :, dn0 : dn0 + 768]) * slopes[r])
            d_us.append(d_u)
            d_n2 = d_n2 + times_trans(d_u, two_s[r, :, up0 : up0 + 768])
        gdn_s[...] += trans_times(d_low, jnp.concatenate(acts, axis=-1))
        gup_s[...] += trans_times(n2, jnp.concatenate(d_us, axis=-1))
        gv_s[2:3, 0:DD] += column_sum(d_n2 * scaled2)
        gv_s[3:4, 0:DD] += column_sum(d_n2)
        d_x1 = d_x2 + norm_rows_back(d_n2, scaled2, inv2, gain2)
        dx_s[tile(i), :] = d_x1
        d_low = low(d_x1)
        go_s[...] += trans_times(d_low, attended)
        d_o = low(times_plain(d_low, wo_s[...]))
        do_s[tile(i), :] = d_o
        both = d_o.astype(f32) * attended.astype(f32)
        stat = jnp.zeros((STEP_ROWS, 128), f32)
        for p in range(3):
            pair = both[:, 128 * p : 128 * (p + 1)]
            for h in range(2):
                one = jnp.sum(jnp.where(half_masks[h], pair, 0.0), axis=-1, keepdims=True)
                stat = jnp.where(lane_ids((1, 128)) == 2 * p + h, one, stat)
        delta_s[tile(i), :] = stat

    if wide:
        gather.drain()
    for r in range(2):
        g_s[r, :, 0:half] = low(go_s[:, r * half : (r + 1) * half])
        g_s[r, :, half:up0] = jnp.zeros((DD, up0 - half), bf)
        g_s[r, :, up0 : up0 + 768] = low(gup_s[:, r * 768 : (r + 1) * 768])
        g_s[r, :, dn0 : dn0 + 768] = low(gdn_s[:, r * 768 : (r + 1) * 768])
        g_s[r, :, hd0 : hd0 + 768] = low(ghd_s[:, r * 768 : (r + 1) * 768])
    if wide:
        to_core = remote(g_s.at[:, :, other_lanes], cr_s, c_ss, c_rs, place.core_mate())
        to_core.start()
        to_x = remote(xs_s, xr_s, x_ss, x_rs, place.x_mate())
    delta_t[...] = delta_s[...].T

    for p in range(3):
        lanes = slice(128 * p, 128 * (p + 1))
        dqt_s[...] = jnp.zeros(dqt_s.shape, f32)

        @pl.loop(0, LANES // KEY_ROWS)
        def _(j):
            rows = pl.ds(pl.multiple_of(j * KEY_ROWS, KEY_ROWS), KEY_ROWS)
            keys, values = k_s[rows, lanes], v_s[rows, lanes]
            bias = jnp.where(row_ids((KEY_ROWS, 1)) + j * KEY_ROWS < TUBES, 0.0, -1e30)
            d_keys, d_values = [], []
            for h in range(2):
                key_one = jnp.where(half_masks[h], keys, jnp.zeros_like(keys))
                value_one = jnp.where(half_masks[h], values, jnp.zeros_like(values))
                lse = lse_t[2 * p + h : 2 * p + h + 1, :]
                delta = delta_t[2 * p + h : 2 * p + h + 1, :]
                scores = times_trans(key_one, q_s[:, lanes])
                soft = jnp.exp2((scores * (SCALE * LOG2E) + bias) - lse)
                d_soft = times_trans(value_one, do_s[:, lanes])
                d_scores = low(soft * (d_soft - delta))
                d_values.append(times_plain(low(soft), do_s[:, lanes]))
                d_keys.append(times_plain(d_scores, q_s[:, lanes]))
                dqt_s[...] += trans_times(key_one, d_scores)
            k_out = slice(DD + 128 * p, DD + 128 * (p + 1))
            v_out = slice(2 * DD + 128 * p, 2 * DD + 128 * (p + 1))
            dqkv_s[rows, k_out] = low(jnp.where(first_half, d_keys[0], d_keys[1]) * SCALE)
            dqkv_s[rows, v_out] = low(jnp.where(first_half, d_values[0], d_values[1]))

        dqkv_s[:, lanes] = low(dqt_s[...].T * SCALE)
        if wide and p == 0:
            to_core.wait_recv()
            for s in range(4):
                rows = chip_rows(s, 1 - place.x)
                xs_s[s] = low(g_s[:, rows, own_lanes].astype(f32) + cr_s[:, rows, :].astype(f32))
            to_x.start()

    @pl.loop(0, N_STEPS)
    def _(i):
        hits, hidden = picks(i)
        d_qkv = dqkv_s[tile(i), :]
        gqkv_s[...] += trans_times(n1_s[tile(i), :], d_qkv)
        d_n1 = times_trans(d_qkv, wqkv_s[...])
        scaled1, inv1 = norm_rows(z_s[tile(i), :])
        gv_s[0:1, 0:DD] += column_sum(d_n1 * scaled1)
        gv_s[1:2, 0:DD] += column_sum(d_n1)
        d_z = dx_s[tile(i), :] + norm_rows_back(d_n1, scaled1, inv1, gain1)
        gv_s[6:7, 0:DD] += column_sum(d_z * hidden)
        gy_s[...] += trans_times(hits, low(d_z))

    d_y = low(gy_s[...])
    for r in range(2):
        gone_ref[r, :, ed0 : ed0 + DD] = low(trans_times(d_y, feat_ref[:, r * DD : (r + 1) * DD]))
        gone_ref[r, :, ed0 + DD : PART_ONE] = jnp.zeros((DD, PART_ONE - ed0 - DD), bf)
        gfeat_ref[:, r * DD : (r + 1) * DD] = low(times_plain(d_y, one_ref[r, :, ed0 : ed0 + DD]))
        for part in range(3):
            gone_ref[r, :, part * half : (part + 1) * half] = low(
                gqkv_s[:, part * DD + r * half : part * DD + (r + 1) * half]
            )
    if wide:
        to_x.wait_recv()
        for s in range(4):
            rows = chip_rows(s, place.x)
            total = g_s[:, rows, own_lanes].astype(f32) + cr_s[:, rows, :].astype(f32)
            total = total + xr_s[s].astype(f32)
            for r in range(2):
                at = (2 * s + r) * SHARD
                gtwo_ref[at : at + SHARD, :] = total[r]
        to_core.wait_send()
        to_x.wait_send()
    gvec_ref[...] = gv_s[:, 0:DD]

    @pl.loop(0, N_STEPS)
    def _(i):
        far(i, place.row).wait_send()

    loss_ref[...] = jnp.zeros((8, 128), f32) + jnp.sum(gv_s[7:8, :]) / PIX


def run_decoder(wide, *operands):
    bf, f32 = jnp.bfloat16, jnp.float32
    vmem = pl.BlockSpec(memory_space=pltpu.VMEM)
    dma = pltpu.SemaphoreType.DMA
    if wide:
        two = jax.ShapeDtypeStruct((8 * SHARD, TWO_HALF), f32)
    else:
        two = jax.ShapeDtypeStruct((2, DD, PART_TWO), bf)
    scratch = [
        pltpu.VMEM((ROWS, DD), f32),
        pltpu.VMEM((ROWS, DD), bf),
        pltpu.VMEM((LANES, DD), bf),
        pltpu.VMEM((LANES, DD), bf),
        pltpu.VMEM((LANES, DD), bf),
        pltpu.VMEM((ROWS, DD), bf),
        pltpu.VMEM((LANES, DD), bf),
        pltpu.VMEM((ROWS, DD), f32),
        pltpu.VMEM((LANES, 3 * DD), bf),
        pltpu.VMEM((128, LANES), f32),
        pltpu.VMEM((LANES, 128), f32),
        pltpu.VMEM((LANES, 128), f32),
        pltpu.VMEM((128, LANES), f32),
        pltpu.VMEM((128, LANES), f32),
        pltpu.VMEM((DD, 3 * DD), bf),
        pltpu.VMEM((DD, DD), bf),
        pltpu.VMEM((128, 2 * DD), bf),
        pltpu.VMEM((DD, 3 * DD), f32),
        pltpu.VMEM((DD, DD), f32),
        pltpu.VMEM((DD, DFF), f32),
        pltpu.VMEM((DD, DFF), f32),
        pltpu.VMEM((DD, DFF), f32),
        pltpu.VMEM((128, DD), f32),
        pltpu.VMEM((8, 768), f32),
        pltpu.VMEM((2, ROWS, PIX // 2), bf),
        pltpu.VMEM((8, 128), jnp.int32),
        dma((N_STEPS,)),
        dma((N_STEPS,)),
        dma((N_STEPS,)),
    ]
    if wide:
        scratch += [
            pltpu.VMEM((2, DD, PART_TWO), bf),
            pltpu.VMEM((2, DD, TWO_HALF), bf),
            pltpu.VMEM((4, 2, SHARD, TWO_HALF), bf),
            pltpu.VMEM((4, 2, SHARD, TWO_HALF), bf),
            dma,
            dma,
            dma,
            dma,
        ]
        scratch += [dma((1, 4)), dma((1, 3)), dma((1, 4)), dma((1, 4)), dma((1, 8)), dma((1, 8))]
    return pl.pallas_call(
        functools.partial(decoder_body, wide),
        out_shape=(
            jax.ShapeDtypeStruct((8, 128), f32),
            jax.ShapeDtypeStruct((2, DD, PART_ONE), bf),
            two,
            jax.ShapeDtypeStruct((8, DD), f32),
            jax.ShapeDtypeStruct((128, D), bf),
        ),
        in_specs=[vmem, vmem, pl.BlockSpec(memory_space=pl.ANY), vmem, vmem, vmem, vmem],
        out_specs=(vmem,) * 5,
        scratch_shapes=scratch,
        compiler_params=pltpu.CompilerParams(
            collective_id=4, has_side_effects=True, vmem_limit_bytes=63 * MIB
        ),
        cost_estimate=pl.CostEstimate(
            flops=30 * 10**9, bytes_accessed=20 * 10**6, transcendentals=20 * 10**6
        ),
        name="decoder",
    )(*operands)


PAIR = 256
HALF_D = D // 2
QKV_W = 3 * D // 2
HID = FF // 2
A_COLS = QKV_W + D // 2
ENC_COLS = A_COLS + 2 * HID
UP_AT, DN_AT = A_COLS, A_COLS + HID
EMB_ROWS = SHARD + 16
GATHERS = (
    (-1, 0, D),
    (0, 0, A_COLS),
    (0, UP_AT, HID),
    (0, DN_AT, HID),
    (1, 0, A_COLS),
    (1, UP_AT, HID),
    (1, DN_AT, HID),
    (-2, 0, PART_ONE),
)
PART_ONE_AT = len(GATHERS) - 1


def half_lanes():
    first = lane_ids((1, 128)) < HEAD
    return [first, jnp.logical_not(first)]


def same_clip():
    a, b = row_ids((PAIR, PAIR)), lane_ids((PAIR, PAIR))
    return jnp.logical_and(a // 128 == b // 128, b % 128 < VIS)


def encoder_scores(queries, keys, allowed):
    scores = jnp.where(allowed, times_trans(queries, keys), -1e30)
    top = jnp.max(scores, axis=-1, keepdims=True) * (SCALE * LOG2E)
    weights = jnp.exp2(scores * (SCALE * LOG2E) - top)
    return weights, jnp.sum(weights, axis=-1, keepdims=True)


def encoder_attention(qkv_ref, out_ref):
    allowed = same_clip()
    halves = half_lanes()
    for p in range(3):
        q = qkv_ref[:, 128 * p : 128 * (p + 1)]
        k = qkv_ref[:, HALF_D + 128 * p : HALF_D + 128 * (p + 1)]
        v = qkv_ref[:, 2 * HALF_D + 128 * p : 2 * HALF_D + 128 * (p + 1)]
        parts = []
        for h in range(2):
            one = jnp.where(halves[h], q, jnp.zeros_like(q))
            weights, total = encoder_scores(one, k, allowed)
            parts.append(times_plain(low(weights), v) / total)
        out_ref[:, 128 * p : 128 * (p + 1)] = low(jnp.where(halves[0], parts[0], parts[1]))


def pack_heads(dst, src, heads):
    for part in range(3):
        for h in range(heads):
            at = (part * heads + h) * HEAD
            dst[:, at : at + HEAD] = low(src[:, (3 * h + part) * HEAD : (3 * h + part + 1) * HEAD])


def encoder_body(wide, *refs):
    f32 = jnp.float32
    if wide:
        seen_ref, pixel_ref, freq_ref, emb_ref, enc_ref, dec_ref, evec_ref, dvec_ref = refs[:8]
        refs = refs[8:]
    else:
        seen_ref, pixel_ref, freq_ref, emb_full, w_s, gain_in = refs[:6]
        refs = refs[6:]
    feat_ref, *kept_out = refs[:7]
    padded_out = refs[7]
    refs = refs[8:]
    if wide:
        gain_ref, dgain_ref, w_out, one_out, two_out = refs[:5]
        emb_s, w_s, embc_s, emb_in, enc_in, small_s, one_s, two_s, block_s = refs[5:14]
        refs = refs[14:]
    sent_s, got_s, padded_s, seen_s, pad_sem, y_ss, y_rs = refs[:7]
    kept = refs[7:13]
    kept_sem = refs[13]
    refs = refs[14:]
    x_ref, qkv_ref, o_ref, h_ref, slope_ref, px_ref = kept
    leaving = []

    def leave(src, at=None):
        i = [ref is src for ref in kept].index(True)
        dst = kept_out[i]
        if at is not None:
            src, dst = src.at[at], dst.at[at]
        copy = pltpu.make_async_copy(src, dst, kept_sem.at[len(leaving)])
        copy.start()
        leaving.append(copy)

    place = Place()
    greet(place.mates(wide))
    swap = Swap(place, sent_s, got_s, y_ss, y_rs)
    if wide:

        def own_part(k):
            layer, start, width = GATHERS[k]
            if layer == -1:
                return emb_in
            if layer == -2:
                return spot(k, place.z, place.x, place.col)
            return enc_in.at[layer, :, pl.ds(start, width)]

        def spot(k, z, x, col):
            layer, start, width = GATHERS[k]
            if layer == -2:
                rows = pl.ds(pl.multiple_of((z * 2 + x) * SHARD, 16), SHARD)
                return one_s.at[:, rows, pl.ds(pl.multiple_of(col * ONE_HALF, 128), ONE_HALF)]
            rows = EMB_ROWS if layer < 0 else SHARD
            first = pl.multiple_of(shard_at(z, x, col) * rows, 16)
            if layer == -1:
                return emb_s.at[pl.ds(first, rows), :]
            return w_s.at[layer, pl.ds(first, rows), pl.ds(start, width)]

        gather = Gather(place, own_part, spot, refs[:6], over_x_first=4)
        extra = len(GATHERS)
        keep_sem, block_ss, block_rs, seed_ss, seed_rs = refs[6:11]
        emb_in[0:SHARD, :] = low(emb_ref[0])
        small_s[...] = jnp.zeros(small_s.shape, f32)
        small_s[0:10, 0:SHARD] = evec_ref[...]
        small_s[0:7, SHARD : SHARD + DD // N_SHARDS] = dvec_ref[...]
        emb_in[SHARD:EMB_ROWS, 0:128] = low(small_s[...])
        emb_in[SHARD:EMB_ROWS, 128:D] = jnp.zeros((EMB_ROWS - SHARD, D - 128), jnp.bfloat16)
        gather.begin(0)
        for layer in range(LAYERS):
            pack_heads(enc_in.at[layer], enc_ref.at[layer, 0], HEADS // 2)
            enc_in[layer, :, QKV_W:] = low(enc_ref[layer, 0, :, QKV_W:])
            if layer == 0:
                gather.begin(1)
                gather.begin(2)
                gather.begin(3)
        own = shard_at(place.z, place.x, place.col)
        emb_s[pl.ds(pl.multiple_of(own * EMB_ROWS, 16), EMB_ROWS), :] = emb_in[...]
        for layer in range(LAYERS):
            w_s[layer, pl.ds(pl.multiple_of(own * SHARD, 16), SHARD), :] = enc_in[layer]
        mine = pl.ds(pl.multiple_of(place.col * (SHARD // 2), 8), SHARD // 2)
        block_s[mine, :] = jnp.zeros((SHARD // 2, PART_ONE + PART_TWO), f32)
        shard = dec_ref[0]
        heads = DHEADS // 2
        for part in range(3):
            for h in range(heads):
                at = (3 * h + part) * HEAD
                to = (part * heads + h) * HEAD
                block_s[mine, to : to + HEAD] = shard[:, at : at + HEAD]
        block_s[mine, ED_AT : ED_AT + DD] = shard[:, 3072:3456]
        block_s[mine, PART_ONE : PART_ONE + 192] = shard[:, ED_AT:768]
        block_s[mine, PART_ONE + UP_TWO : PART_ONE + PART_TWO] = shard[:, 768:3072]
        spread = remote(
            block_s.at[mine, :], block_s.at[mine, :], block_ss, block_rs, place.core_mate()
        )
        spread.start()
        theirs = pl.ds(pl.multiple_of((1 - place.col) * (SHARD // 2), 8), SHARD // 2)
        half_one = spot(PART_ONE_AT, place.z, place.x, place.col)
        half_two = two_s.at[place.z]
        seeds = [
            remote(part.at[place.row], part.at[place.row], ss, rs, place.row_mate())
            for part, ss, rs in (
                (half_one, seed_ss.at[0], seed_rs.at[0]),
                (half_two, seed_ss.at[1], seed_rs.at[1]),
            )
        ]
        seeds_back = [
            remote(part.at[1 - place.row], part.at[1 - place.row], ss, rs, place.row_mate())
            for part, ss, rs in (
                (half_one, seed_ss.at[0], seed_rs.at[0]),
                (half_two, seed_ss.at[1], seed_rs.at[1]),
            )
        ]

    def step(name, k):
        if wide:
            getattr(gather, name)(k)

    odd = (lane_ids((1, D)) % 2).astype(f32) * (0.5 * math.pi)
    freq = freq_ref[0:1, :]
    places = []
    seen_s[...] = jnp.full(seen_s.shape, -1, jnp.int32)
    whole = TUBES // 16 * 16
    for m in range(MICRO):
        seen_s[m : m + 1, 0:VIS] = seen_ref[m]
        row = seen_s[m : m + 1, :]
        hits = (row_ids((TUBES, 128)) == row).astype(jnp.bfloat16)
        px_ref[128 * m : 128 * (m + 1), :] = low(trans_times(hits, pixel_ref[m, 0]))
        column = jnp.broadcast_to(row.astype(f32), (128, 128)).T[:, 0:1]
        places.append(jnp.sin(column * freq + odd))
        padded_s[m, 0:whole, :] = pixel_ref[m, 0, 0:whole, :]
        rest = pixel_ref[m, 0, whole:TUBES, :].astype(f32)
        rest = jnp.concatenate([rest, jnp.zeros((ROWS - TUBES, D), f32)], axis=0)
        padded_s[m, whole:ROWS, :] = low(rest)
    pad_copy = pltpu.make_async_copy(padded_s, padded_out, pad_sem)
    pad_copy.start()
    leave(px_ref)

    if wide:
        gather.forward(0)
        gather.forward(1)
        gather.begin(4)
        gather.across(0)
        gather.finish(0)
        for s in range(N_SHARDS):
            embc_s[SHARD * s : SHARD * (s + 1), :] = emb_s[EMB_ROWS * s : EMB_ROWS * s + SHARD, :]
            tail = emb_s[EMB_ROWS * s + SHARD : EMB_ROWS * (s + 1), 0:128].astype(f32)
            gain_ref[:, SHARD * s : SHARD * (s + 1)] = tail[:, 0:SHARD]
            dgain_ref[:, DD // 16 * s : DD // 16 * (s + 1)] = tail[0:8, SHARD : SHARD + DD // 16]
        emb_full, gain_in = embc_s, gain_ref
    swap.start(0, times_trans(px_ref[...], emb_full[...]))
    if wide:
        other_rows = block_s.at[theirs, :]
        remote(other_rows, other_rows, block_ss, block_rs, place.core_mate()).wait_recv()
        lanes = pl.ds(pl.multiple_of(place.col * ONE_HALF, 128), ONE_HALF)
        half_one.at[place.row][...] = low(block_s[:, lanes])
        lanes = pl.ds(pl.multiple_of(PART_ONE + place.col * TWO_HALF, 128), TWO_HALF)
        half_two.at[place.row][...] = low(block_s[:, lanes])
        for copy in seeds:
            copy.start()
    step("forward", 2)
    step("across", 1)
    x = swap.total(0) + jnp.concatenate(places, axis=0)
    for layer in range(LAYERS):
        gains = gain_in[4 * layer : 4 * layer + 4, :]
        x_ref[2 * layer] = x
        leave(x_ref, 2 * layer)
        scaled, _ = norm_rows(x)
        n1 = low(scaled * gains[0:1] + gains[1:2])
        first = 1 + 3 * layer
        step("finish", first)
        qkv_ref[layer] = low(times_plain(n1, w_s[layer, :, 0:QKV_W]))
        encoder_attention(qkv_ref.at[layer], o_ref.at[layer])
        if wide and layer == 1:
            gather.forward(6)
        swap.start(1 + 2 * layer, times_trans(o_ref[layer], w_s[layer, :, QKV_W:A_COLS]))
        if wide and layer == 0:
            gather.begin_turned(extra)
            gather.begin(5)
            gather.forward(3)
        elif wide:
            gather.forward(PART_ONE_AT)
            gather.line(extra + 1, half_two, half_two)
        step("across", first + 1)
        x = x + swap.total(1 + 2 * layer)
        x_ref[2 * layer + 1] = x
        leave(x_ref, 2 * layer + 1)
        leave(qkv_ref, layer)
        leave(o_ref, layer)
        scaled, _ = norm_rows(x)
        n2 = low(scaled * gains[2:3] + gains[3:4])
        step("finish", first + 1)
        act, slope = gelu_pair(times_plain(n2, w_s[layer, :, UP_AT:DN_AT]))
        act = low(act)
        h_ref[layer] = act
        slope_ref[layer] = slope
        leave(h_ref, layer)
        leave(slope_ref, layer)
        if layer == 0:
            step("begin", 6)
        step("across", first + 2)
        step("finish", first + 2)
        swap.start(2 + 2 * layer, times_trans(act, w_s[layer, :, DN_AT:ENC_COLS]))
        if wide:
            keep = pltpu.make_async_copy(w_s.at[layer], w_out.at[layer], keep_sem.at[layer])
            keep.start()
        if wide and layer == 0:
            gather.forward_turned(extra)
            for copy in seeds_back:
                copy.wait_recv()
            gather.begin(PART_ONE_AT)
            gather.forward(5)
        elif wide:
            gather.across(PART_ONE_AT)
        x = x + swap.total(2 + 2 * layer)
    x_ref[2 * LAYERS] = x
    leave(x_ref, 2 * LAYERS)
    scaled, _ = norm_rows(x)
    gains = gain_in[4 * LAYERS : 4 * LAYERS + 2, :]
    feat = low(scaled * gains[0:1] + gains[1:2])
    feat_ref[...] = jnp.where(place.row == 0, feat[0:128], feat[128:256])
    swap.drain()
    pad_copy.wait()
    for copy in leaving:
        copy.wait()
    if wide:
        gather.finish(PART_ONE_AT)
        for s in (2, 1, 3):
            gather.landed(extra + 1, s, two_s.at[(place.z - s) % 4])
        one_copy = pltpu.make_async_copy(one_s, one_out, keep_sem.at[LAYERS])
        one_copy.start()
        two_copy = pltpu.make_async_copy(two_s, two_out, keep_sem.at[LAYERS + 1])
        two_copy.start()
        spread.wait_send()
        for copy in seeds:
            copy.wait_send()
        gather.drain()
        one_copy.wait()
        two_copy.wait()
        for layer in range(LAYERS):
            pltpu.make_async_copy(w_s.at[layer], w_out.at[layer], keep_sem.at[layer]).wait()


def run_encoder(wide, *operands):
    bf, f32 = jnp.bfloat16, jnp.float32
    vmem = pl.BlockSpec(memory_space=pltpu.VMEM)
    dma = pltpu.SemaphoreType.DMA
    shape = jax.ShapeDtypeStruct
    n_swaps = 1 + 2 * LAYERS
    outs = [
        shape((128, D), bf),
        shape((2 * LAYERS + 1, PAIR, D), f32),
        shape((LAYERS, PAIR, QKV_W), bf),
        shape((LAYERS, PAIR, HALF_D), bf),
        shape((LAYERS, PAIR, HID), bf),
        shape((LAYERS, PAIR, HID), f32),
        shape((PAIR, D), bf),
        shape((MICRO, ROWS, D), bf),
    ]
    out_specs = [vmem] + [pl.BlockSpec(memory_space=pl.ANY)] * (len(outs) - 1)
    kept = [pltpu.VMEM(out.shape, out.dtype) for out in outs[1:7]]
    scratch = []
    if wide:
        anywhere = pl.BlockSpec(memory_space=pl.ANY)
        outs += [
            shape((16, D), f32),
            shape((8, DD), f32),
            shape((LAYERS, D, ENC_COLS), bf),
            shape((2, DD, PART_ONE), bf),
            shape((4, 2, SHARD, TWO_HALF), bf),
        ]
        out_specs += [vmem, vmem, anywhere, anywhere, anywhere]
        scratch += [
            pltpu.VMEM((N_SHARDS * EMB_ROWS, D), bf),
            pltpu.VMEM((LAYERS, D, ENC_COLS), bf),
            pltpu.VMEM((D, D), bf),
            pltpu.VMEM((EMB_ROWS, D), bf),
            pltpu.VMEM((LAYERS, SHARD, ENC_COLS), bf),
            pltpu.VMEM((16, 128), f32),
            pltpu.VMEM((2, DD, PART_ONE), bf),
            pltpu.VMEM((4, 2, SHARD, TWO_HALF), bf),
            pltpu.VMEM((SHARD, PART_ONE + PART_TWO), f32),
        ]
    scratch += [
        pltpu.VMEM((n_swaps, PAIR, D), bf),
        pltpu.VMEM((n_swaps, PAIR, D), bf),
        pltpu.VMEM((MICRO, ROWS, D), bf),
        pltpu.VMEM((8, 128), jnp.int32),
        dma,
        dma((n_swaps,)),
        dma((n_swaps,)),
        *kept,
        dma((2 + 6 * LAYERS,)),
    ]
    if wide:
        n = len(GATHERS)
        scratch += [dma((n + 2, 4)), dma((n + 2, 3)), dma((n, 4)), dma((n, 4)), dma((n, 8)), dma((n, 8))]
        scratch += [dma((LAYERS + 2,)), dma, dma, dma((2,)), dma((2,))]
    return pl.pallas_call(
        functools.partial(encoder_body, wide),
        out_shape=tuple(outs),
        in_specs=[vmem] * len(operands),
        out_specs=tuple(out_specs),
        scratch_shapes=scratch,
        compiler_params=pltpu.CompilerParams(
            collective_id=1, has_side_effects=True, vmem_limit_bytes=60 * MIB
        ),
        cost_estimate=pl.CostEstimate(
            flops=10 * 10**9, bytes_accessed=60 * 10**6, transcendentals=10**6
        ),
        name="encoder",
    )(*operands)


SUMS = (
    ("dn1", HID),
    ("up1", HID),
    ("at1", A_COLS),
    ("dn0", HID),
    ("up0", HID),
    ("at0", A_COLS),
    ("emb", D),
)
SUM_AT = {name: sum(w for _, w in SUMS[:i]) for i, (name, _) in enumerate(SUMS)}
SUM_COLS = sum(w for _, w in SUMS)
BLOCKS = N_SHARDS // 2 * SHARD
QUARTER = BLOCKS // 2


class Scatter(Mail):
    def __init__(self, place, bufs, sems, into):
        super().__init__()
        self.at, self.into = place, into
        self.perm, self.flip, self.cs, self.cr, self.xs, self.xr, self.zs, self.zr, self.own = bufs
        self.c_ss, self.c_rs, self.x_ss, self.x_rs, self.z_ss, self.z_rs = sems
        self.last = {}
        self.lines = {}

    def span(self, name, shift=0, width=None):
        k = [n for n, _ in SUMS].index(name)
        return k, pl.ds(SUM_AT[name] + shift, SUMS[k][1] if width is None else width)

    def post(self, src, dst, ss, rs, device, key):
        copy = remote(src, dst, ss, rs, device)
        copy.start()
        self.last[key] = copy

    def free(self, key):
        if key in self.last:
            self.last.pop(key).wait_send()

    def turn(self, slot, left):
        at = self.at
        flip = self.flip.at[slot % 2]
        flip[...] = left.T
        order = [
            (s, x, c) for c, x in ((1, 1), (1, 0), (0, 1), (0, 0)) for s in range(4)
        ]
        for i, (s, other_x, other_c) in enumerate(order):
            x = 1 - at.x if other_x else at.x
            c = 1 - at.col if other_c else at.col
            first = pl.multiple_of(shard_at((at.z + s) % 4, x, c) * SHARD, 16)
            self.perm[slot, SHARD * i : SHARD * (i + 1), :] = flip[pl.ds(first, SHARD), :]

    def cores(self, name, items):
        k, span = self.span(name)
        slot_at, width = k % 2, SUMS[k][1]
        self.free(("core", slot_at))
        for slot, right, shift, wide in items:
            self.cs[slot_at, :, shift : shift + wide] = low(
                times_plain(self.perm[slot, 0:BLOCKS, :], right[...])
            )
        self.post(
            self.cs.at[slot_at, :, pl.ds(0, width)],
            self.cr.at[:, span],
            self.c_ss.at[k],
            self.c_rs.at[k],
            self.at.core_mate(),
            ("core", slot_at),
        )

    def over_x(self, name, items):
        f32 = jnp.float32
        k, whole = self.span(name)
        slot_at, width = k % 3, SUMS[k][1]
        self.free(("x", slot_at))
        self.came(self.cr.at[:, whole], self.c_ss.at[k], self.c_rs.at[k], self.at.core_mate())
        for slot, right, shift, wide in items:
            _, span = self.span(name, shift, wide)
            mine = times_plain(self.perm[slot, BLOCKS : BLOCKS + QUARTER, :], right[...])
            self.xs[slot_at, :, shift : shift + wide] = low(
                mine + self.cr[0:QUARTER, span].astype(f32)
            )
        self.post(
            self.xs.at[slot_at, :, pl.ds(0, width)],
            self.xr.at[:, whole],
            self.x_ss.at[k],
            self.x_rs.at[k],
            self.at.x_mate(),
            ("x", slot_at),
        )
        for slot, right, shift, wide in items:
            _, span = self.span(name, shift, wide)
            mine = times_plain(self.perm[slot, BLOCKS + QUARTER : 2 * BLOCKS, :], right[...])
            self.own[k % 4, :, shift : shift + wide] = mine + self.cr[QUARTER:BLOCKS, span].astype(f32)

    def along_z(self, name):
        k, span = self.span(name)
        self.came(self.xr.at[:, span], self.x_ss.at[k], self.x_rs.at[k], self.at.x_mate())
        own = self.own.at[k % 4, :, pl.ds(0, SUMS[k][1])]
        own[...] += self.xr[:, span].astype(jnp.float32)
        line = LineSum(
            self.at,
            own,
            self.zs.at[:, :, span],
            self.zr.at[:, :, span],
            self.z_ss.at[k],
            self.z_rs.at[k],
            SHARD,
            self.into(name),
        )
        line.begin()
        self.lines[name] = line

    def relay(self, name):
        self.lines[name].relay()

    def finish(self, name):
        self.lines[name].finish()

    def drain(self):
        for copy in self.last.values():
            copy.wait_send()
        for line in self.lines.values():
            line.drain()


class DecoderScatter(Mail):
    def __init__(self, place, one, two, out, bufs, sems):
        super().__init__()
        self.at, self.one, self.two, self.out = place, one, two, out
        self.cr, self.xs, self.xr, self.own, self.zs1, self.zr1, self.zs2, self.zr2 = bufs[:8]
        self.fin, self.ys, self.yr, self.whole, self.part = bufs[8:]
        (
            self.c_ss, self.c_rs, self.x_ss, self.x_rs, self.z1_ss, self.z1_rs,
            self.z2_ss, self.z2_rs, self.y_ss, self.y_rs, self.f_ss, self.f_rs,
        ) = sems
        self.lanes = pl.ds(pl.multiple_of(place.col * ONE_HALF, 128), ONE_HALF)

    def rows(self, s, x):
        return pl.ds(pl.multiple_of(((self.at.z + s) % 4 * 2 + x) * SHARD, 16), SHARD)

    def begin(self):
        at = self.at
        others = pl.ds(pl.multiple_of((1 - at.col) * ONE_HALF, 128), ONE_HALF)
        src = self.one.at[:, :, others]
        self.go(src, self.cr, self.c_ss, self.c_rs, at.core_mate())
        self.line_two = LineSum(
            at, self.two, self.zs2, self.zr2, self.z2_ss, self.z2_rs, 2 * SHARD,
            self.fin.at[:, pl.ds(ONE_HALF, TWO_HALF)],
        )
        self.line_two.begin()

    def sums(self, s, x):
        rows = self.rows(s, x)
        f32 = jnp.float32
        return self.one[:, rows, self.lanes].astype(f32) + self.cr[:, rows, :].astype(f32)

    def over_x(self):
        at = self.at
        self.came(self.cr, self.c_ss, self.c_rs, at.core_mate())
        for s in range(4):
            self.xs[s] = low(self.sums(s, 1 - at.x))
        self.go(self.xs, self.xr, self.x_ss, self.x_rs, at.x_mate())

    def along_z(self):
        at = self.at
        self.came(self.xr, self.x_ss, self.x_rs, at.x_mate())
        for s in range(4):
            total = self.sums(s, at.x) + self.xr[s].astype(jnp.float32)
            for r in range(2):
                first = (2 * s + r) * SHARD
                self.own[first : first + SHARD, :] = total[r]
        self.line_one = LineSum(
            at, self.own, self.zs1, self.zr1, self.z1_ss, self.z1_rs, 2 * SHARD,
            self.fin.at[:, pl.ds(0, ONE_HALF)],
        )
        self.line_one.begin()

    def over_rows(self):
        at = self.at
        self.line_one.finish()
        self.line_two.finish()
        rows = pl.ds(pl.multiple_of((1 - at.row) * SHARD, 8), SHARD)
        self.ys[...] = low(self.fin[rows, :])
        self.go(self.ys, self.yr, self.y_ss, self.y_rs, at.row_mate())

    def to_cores(self):
        at = self.at
        self.came(self.yr, self.y_ss, self.y_rs, at.row_mate())
        rows = pl.ds(pl.multiple_of(at.row * SHARD, 8), SHARD)
        self.whole[...] = self.fin[rows, :] + self.yr[...].astype(jnp.float32)
        theirs = pl.ds(pl.multiple_of((1 - at.col) * (SHARD // 2), 8), SHARD // 2)
        self.go(self.whole.at[theirs, :], self.part, self.f_ss, self.f_rs, at.core_mate())

    def finish(self):
        at = self.at
        width = ONE_HALF + TWO_HALF
        mine = pl.ds(pl.multiple_of(at.col * (SHARD // 2), 8), SHARD // 2)
        self.out[:, pl.ds(pl.multiple_of(at.col * width, 128), width)] = self.whole[mine, :]
        self.came(self.part, self.f_ss, self.f_rs, at.core_mate())
        self.out[:, pl.ds(pl.multiple_of((1 - at.col) * width, 128), width)] = self.part[...]

    def drain(self):
        super().drain()
        self.line_one.drain()
        self.line_two.drain()


class Everyone(Mail):
    def __init__(self, place, bufs, sems):
        super().__init__()
        self.at = place
        self.send, self.got, self.one, self.ones = bufs
        self.ss, self.rs, self.o_ss, self.o_rs = sems
        self.waits = []

    def first(self, enc, dec):
        self.send[0, 0:16, :] = enc
        self.send[0, 16:24, 0:DD] = dec
        self.send[0, 16:24, DD:D] = jnp.zeros((8, D - DD), jnp.float32)
        self.post(0)

    def post(self, i):
        at = self.at
        mates = ([at.core_mate()], [at.row_mate()], [at.x_mate()], [at.z_mate(s) for s in (1, 2, 3)])
        for j, mate in enumerate(mates[i]):
            self.go(
                self.send.at[i], self.got.at[i + j], self.ss.at[i + j], self.rs.at[i + j], mate
            )
        self.waits.append([(i + j, mate) for j, mate in enumerate(mates[i])])

    def stage(self, i):
        total = self.send[i - 1]
        for slot, mate in self.waits[i - 1]:
            self.came(self.got.at[slot], self.ss.at[slot], self.rs.at[slot], mate)
            total = total + self.got[slot]
        self.send[i] = total
        if i < 4:
            self.post(i)

    def total(self):
        return self.send[4]

    def number(self, value):
        at = self.at
        groups = (at.cube(), [at.z_mate(s) for s in (1, 2, 3)])
        total = jnp.zeros((8, 128), jnp.float32) + value
        first = 0
        for i, mates in enumerate(groups):
            self.one[i] = total
            for j, mate in enumerate(mates):
                slot = first + j
                self.go(
                    self.one.at[i], self.ones.at[slot], self.o_ss.at[slot], self.o_rs.at[slot], mate
                )
            for j, mate in enumerate(mates):
                slot = first + j
                self.came(self.ones.at[slot], self.o_ss.at[slot], self.o_rs.at[slot], mate)
                total = total + self.ones[slot]
            first += len(mates)
        return total[0:1, 0:1]


def encoder_attention_back(qkv_ref, d_out, out_ref):
    allowed = same_clip()
    halves = half_lanes()
    for p in range(3):
        spans = [slice(part * HALF_D + 128 * p, part * HALF_D + 128 * (p + 1)) for part in range(3)]
        q, k, v = (qkv_ref[:, span] for span in spans)
        d_pair = d_out[:, 128 * p : 128 * (p + 1)]
        found = []
        for h in range(2):
            one = jnp.where(halves[h], q, jnp.zeros_like(q))
            weights, total = encoder_scores(one, k, allowed)
            soft = weights / total
            d_one = jnp.where(halves[h], d_pair, jnp.zeros_like(d_pair))
            d_soft = times_trans(d_one, v)
            delta = jnp.sum(soft * d_soft, axis=-1, keepdims=True)
            d_scores = low(soft * (d_soft - delta))
            found.append(
                (
                    times_plain(d_scores, k) * SCALE,
                    trans_times(d_scores, q) * SCALE,
                    trans_times(low(soft), d_pair),
                )
            )
        for part in range(3):
            out_ref[:, spans[part]] = low(jnp.where(halves[0], found[0][part], found[1][part]))


def encoder_back_body(wide, *refs):
    f32 = jnp.float32
    gfeat_ref, x_in, qkv_in, o_in, h_ref, slope_ref, px_in, gain_ref, w_ref = refs[:9]
    refs = refs[9:]
    if wide:
        one_ref, two_ref, loss_ref, dvec_ref = refs[:4]
        refs = refs[4:]
    genc_ref, gemb_ref, gvec_ref = refs[:3]
    refs = refs[3:]
    if wide:
        gdec_ref, total_ref = refs[:2]
        refs = refs[2:]
    wa_s, wb_s, du_s, dqkv_s, feat_s, sent_s, got_s, h_s, slope_s = refs[:9]
    x_ref, qkv_ref, o_ref, px_ref, in_sem = refs[9:14]
    load_sem, f_ss, f_rs, y_ss, y_rs = refs[14:19]
    refs = refs[19:]
    arriving = [
        pltpu.make_async_copy(src, dst, in_sem.at[i])
        for i, (src, dst) in enumerate(
            ((x_in, x_ref), (qkv_in, qkv_ref), (o_in, o_ref), (px_in, px_ref))
        )
    ]
    arriving[0].start()
    place = Place()
    greet(place.mates(wide) + (place.cube()[2:3] + place.cube()[4:] if wide else []))
    swap = Swap(place, sent_s, got_s, y_ss, y_rs)
    swapped = remote(gfeat_ref, feat_s, f_ss, f_rs, place.row_mate())
    swapped.start()

    def into(name):
        if name == "emb":
            return gemb_ref
        start, width = {"at": (0, A_COLS), "up": (UP_AT, HID), "dn": (DN_AT, HID)}[name[:2]]
        return genc_ref.at[int(name[2]), :, pl.ds(start, width)]

    scatter = Scatter(place, refs[:9], refs[9:15], into) if wide else None
    dec = DecoderScatter(place, one_ref, two_ref, gdec_ref, refs[15:28], refs[28:40]) if wide else None
    everyone = Everyone(place, refs[40:44], refs[44:48]) if wide else None

    def load(layer, part):
        src, dst = (
            (w_ref.at[layer, :, pl.ds(0, A_COLS)], wa_s),
            (w_ref.at[layer, :, pl.ds(A_COLS, 2 * HID)], wb_s),
            (h_ref.at[layer], h_s),
            (slope_ref.at[layer], slope_s),
        )[part]
        return pltpu.make_async_copy(src, dst, load_sem.at[layer, part])

    load(1, 2).start()
    load(1, 3).start()
    load(1, 1).start()
    load(1, 0).start()
    for copy in arriving[1:]:
        copy.start()

    lefts = {}

    def factor(slot, left):
        lefts[slot] = left
        if wide:
            scatter.turn(slot, left)

    def emit(name, items):
        if wide:
            scatter.cores(name, items)
            return
        for slot, right, shift, width in items:
            value = low(trans_times(lefts[slot], right[...]))
            if name == "emb":
                gemb_ref[...] = value
                continue
            start = {"at": 0, "up": UP_AT, "dn": DN_AT}[name[:2]] + shift
            genc_ref[int(name[2]), :, start : start + width] = value

    def later(step, *args):
        if wide:
            getattr(scatter, step)(*args)

    def dec_step(step):
        if wide:
            getattr(dec, step)()

    dec_step("begin")
    swapped.wait_recv()
    dec_step("over_x")
    near, far = gfeat_ref[...].astype(f32), feat_s[...].astype(f32)
    first = place.row == 0
    grad = jnp.concatenate([jnp.where(first, near, far), jnp.where(first, far, near)], axis=0)
    gvec_ref[...] = jnp.zeros(gvec_ref.shape, f32)

    def note(row, grad_out, scaled):
        gvec_ref[row : row + 1, :] = column_sum(grad_out * scaled)
        gvec_ref[row + 1 : row + 2, :] = column_sum(grad_out)

    arriving[0].wait()
    scaled, inv = norm_rows(x_ref[2 * LAYERS])
    note(4 * LAYERS, grad, scaled)
    d_x = norm_rows_back(grad, scaled, inv, gain_ref[4 * LAYERS : 4 * LAYERS + 1, :])
    for layer in (1, 0):
        gains = gain_ref[4 * layer : 4 * layer + 4, :]
        dn, up, at = (f"{kind}{layer}" for kind in ("dn", "up", "at"))
        scaled2, inv2 = norm_rows(x_ref[2 * layer + 1])
        n2 = low(scaled2 * gains[2:3] + gains[3:4])
        d_low = low(d_x)
        factor(0, d_low)
        dn_items = [(0, h_s, 0, HID)]
        load(layer, 2).wait()
        emit(dn, dn_items)
        load(layer, 3).wait()
        load(layer, 1).wait()
        d_hidden = times_plain(d_low, wb_s[:, HID : 2 * HID])
        du_s[...] = low(d_hidden * slope_s[...])
        swap.start(2 * layer + 1, times_trans(du_s[...], wb_s[:, 0:HID]))
        later("over_x", dn, dn_items)
        factor(1, n2)
        up_items = [(1, du_s, 0, HID)]
        emit(up, up_items)
        later("over_x", up, up_items)
        if layer == 1:
            load(0, 2).start()
            load(0, 3).start()
            load(0, 1).start()
            if wide:
                dec.line_two.relay()
        else:
            later("along_z", "at1")
            later("relay", "up1")
        d_n2 = swap.total(2 * layer + 1)
        note(4 * layer + 2, d_n2, scaled2)
        d_x = d_x + norm_rows_back(d_n2, scaled2, inv2, gains[2:3])
        d_low = low(d_x)
        factor(2, d_low)
        load(layer, 0).wait()
        if layer == 1:
            for copy in arriving[1:]:
                copy.wait()
        d_att = low(times_plain(d_low, wa_s[:, QKV_W:A_COLS]))
        encoder_attention_back(qkv_ref.at[layer], d_att, dqkv_s)
        swap.start(2 * layer, times_trans(dqkv_s[...], wa_s[:, 0:QKV_W]))
        scaled1, inv1 = norm_rows(x_ref[2 * layer])
        factor(3, low(scaled1 * gains[0:1] + gains[1:2]))
        at_items = [(3, dqkv_s, 0, QKV_W), (2, o_ref.at[layer], QKV_W, HALF_D)]
        emit(at, at_items)
        if layer == 1:
            load(0, 0).start()
            dec_step("along_z")
        else:
            later("relay", "at1")
        later("along_z", dn)
        later("over_x", at, at_items)
        later("along_z", up)
        later("relay", dn)
        if layer == 1:
            if wide:
                dec.line_one.relay()
        d_n1 = swap.total(2 * layer)
        note(4 * layer, d_n1, scaled1)
        d_x = d_x + norm_rows_back(d_n1, scaled1, inv1, gains[0:1])
    factor(0, low(d_x))
    emb_items = [(0, px_ref, 0, D)]
    emit("emb", emb_items)
    later("relay", "up0")
    later("over_x", "emb", emb_items)
    if wide:
        lane = lane_ids((1, DD))
        dvec = jnp.where(row_ids((8, 1)) < 7, dvec_ref[...], 0.0)
        loss = jnp.where(lane == 0, loss_ref[0:1, 0:1], 0.0)
        dvec = dvec + jnp.where(row_ids((8, 1)) == 7, loss, 0.0)
        everyone.first(0.5 * gvec_ref[...], dvec)
        dec.over_rows()
        everyone.stage(1)
        scatter.along_z("at0")
        everyone.stage(2)
        dec.to_cores()
        scatter.along_z("emb")
        everyone.stage(3)
        scatter.relay("at0")
        dec.finish()
        scatter.relay("emb")
        everyone.stage(4)
        square = jnp.zeros((1, 1), f32)
        for name, _ in SUMS:
            scatter.finish(name)
            whole = into(name)[...]
            square = square + jnp.sum(whole * whole)
        square = square + jnp.sum(gdec_ref[...] * gdec_ref[...])
        square = everyone.number(square)
        total_ref[...] = everyone.total()
        total_ref[23:24, 0:128] += jnp.where(lane_ids((1, 128)) == 1, square, 0.0)
        scatter.drain()
        dec.drain()
        everyone.drain()
    swapped.wait_send()
    swap.drain()


def run_encoder_back(wide, *operands):
    bf, f32 = jnp.bfloat16, jnp.float32
    vmem = pl.BlockSpec(memory_space=pltpu.VMEM)
    dma = pltpu.SemaphoreType.DMA
    shape = jax.ShapeDtypeStruct
    rows, kind = (SHARD, f32) if wide else (D, bf)
    scratch = [
        pltpu.VMEM((D, A_COLS), bf),
        pltpu.VMEM((D, 2 * HID), bf),
        pltpu.VMEM((PAIR, HID), bf),
        pltpu.VMEM((PAIR, QKV_W), bf),
        pltpu.VMEM((128, D), bf),
        pltpu.VMEM((2, PAIR, D), bf),
        pltpu.VMEM((2 * LAYERS, PAIR, D), bf),
        pltpu.VMEM((PAIR, HID), bf),
        pltpu.VMEM((PAIR, HID), f32),
        pltpu.VMEM((2 * LAYERS + 1, PAIR, D), f32),
        pltpu.VMEM((LAYERS, PAIR, QKV_W), bf),
        pltpu.VMEM((LAYERS, PAIR, HALF_D), bf),
        pltpu.VMEM((PAIR, D), bf),
        dma((4,)),
        dma((LAYERS, 4)),
        dma,
        dma,
        dma((2 * LAYERS,)),
        dma((2 * LAYERS,)),
    ]
    outs = [
        shape((LAYERS, rows, ENC_COLS), kind),
        shape((rows, D), kind),
        shape((16, D), f32),
    ]
    anywhere = pl.BlockSpec(memory_space=pl.ANY)
    in_specs = [vmem] + [anywhere] * 6 + [vmem, anywhere]
    if wide:
        outs += [shape((SHARD // 2, PART_ONE + PART_TWO), f32), shape((24, D), f32)]
        in_specs += [vmem] * 4
        n = len(SUMS)
        both = ONE_HALF + TWO_HALF
        scratch += [
            pltpu.VMEM((4, D, PAIR), bf),
            pltpu.VMEM((2, D, PAIR), bf),
            pltpu.VMEM((2, BLOCKS, HID), bf),
            pltpu.VMEM((BLOCKS, SUM_COLS), bf),
            pltpu.VMEM((3, QUARTER, HID), bf),
            pltpu.VMEM((QUARTER, SUM_COLS), bf),
            pltpu.VMEM((3, SHARD, SUM_COLS), bf),
            pltpu.VMEM((4, SHARD, SUM_COLS), bf),
            pltpu.VMEM((4, QUARTER, HID), f32),
            dma((n,)),
            dma((n,)),
            dma((n,)),
            dma((n,)),
            dma((n, 4)),
            dma((n, 4)),
            pltpu.VMEM((2, DD, ONE_HALF), bf),
            pltpu.VMEM((4, 2, SHARD, ONE_HALF), bf),
            pltpu.VMEM((4, 2, SHARD, ONE_HALF), bf),
            pltpu.VMEM((8 * SHARD, ONE_HALF), f32),
            pltpu.VMEM((3, 2 * SHARD, ONE_HALF), bf),
            pltpu.VMEM((4, 2 * SHARD, ONE_HALF), bf),
            pltpu.VMEM((3, 2 * SHARD, TWO_HALF), bf),
            pltpu.VMEM((4, 2 * SHARD, TWO_HALF), bf),
            pltpu.VMEM((2 * SHARD, both), f32),
            pltpu.VMEM((SHARD, both), bf),
            pltpu.VMEM((SHARD, both), bf),
            pltpu.VMEM((SHARD, both), f32),
            pltpu.VMEM((SHARD // 2, both), f32),
            dma,
            dma,
            dma,
            dma,
            dma((4,)),
            dma((4,)),
            dma((4,)),
            dma((4,)),
            dma,
            dma,
            dma,
            dma,
            pltpu.VMEM((5, 24, D), f32),
            pltpu.VMEM((6, 24, D), f32),
            pltpu.VMEM((2, 8, 128), f32),
            pltpu.VMEM((10, 8, 128), f32),
            dma((6,)),
            dma((6,)),
            dma((10,)),
            dma((10,)),
        ]
    return pl.pallas_call(
        functools.partial(encoder_back_body, wide),
        out_shape=tuple(outs),
        in_specs=in_specs,
        out_specs=(vmem,) * len(outs),
        scratch_shapes=scratch,
        compiler_params=pltpu.CompilerParams(
            collective_id=2, has_side_effects=True, vmem_limit_bytes=63 * MIB
        ),
        cost_estimate=pl.CostEstimate(
            flops=20 * 10**9, bytes_accessed=60 * 10**6, transcendentals=10**6
        ),
        name="encoder_back",
    )(*operands)


def adam_at(refs, spot, grad, decay_rate, step_rate):
    master, first, second, master_out, first_out, second_out = refs
    new = adam_update(master[spot], first[spot], second[spot], grad, decay_rate, step_rate)
    master_out[spot], first_out[spot], second_out[spot] = new


def head_pieces(rows, heads):
    pieces = []
    for h in range(heads):
        for part in range(3):
            at = (part * heads + h) * HEAD
            pieces.append(rows[:, at : at + HEAD])
    pieces.append(rows[:, 3 * heads * HEAD :])
    return jnp.concatenate(pieces, axis=-1)


def update_body(*refs):
    f32 = jnp.float32
    total_ref = refs[0]
    grads = refs[1:4]
    states = [refs[4 + 3 * i : 7 + 3 * i] for i in range(5)]
    loss_ref, norm_ref = refs[19:21]
    outs = [refs[21 + 3 * i : 24 + 3 * i] for i in range(5)]
    total = total_ref[...]
    squares = jnp.sum(total[0:23, :] * total[0:23, :]) + jnp.sum(total[23:24, 1:2])
    norm = jnp.sqrt(jnp.zeros((1, 1), f32) + squares)
    factor = jnp.minimum(1.0, CLIP_MAX / (norm + 1e-06))
    step = pl.program_id(0)
    rows = grads[0].shape[1]

    @pl.loop(0, rows // 8)
    def _(i):
        spot = pl.ds(pl.multiple_of(i * 8, 8), 8)
        grad = head_pieces(grads[0][0, spot, :], HEADS // 2)
        adam_at(states[0] + outs[0], (0, 0, spot, slice(None)), grad * factor, DECAY, RATE)

    @pl.when(step == 0)
    def _():
        loss_ref[0, 0] = jnp.sum(total[23:24, 0:1])
        norm_ref[0, 0] = jnp.sum(norm)
        adam_at(states[1] + outs[1], (0,), grads[1][...] * factor, DECAY, RATE)

    @pl.when(step == 1)
    def _():
        both = ONE_HALF + TWO_HALF
        grad = grads[2][...]
        one = jnp.concatenate([grad[:, 0:ONE_HALF], grad[:, both : both + ONE_HALF]], axis=-1)
        two = jnp.concatenate([grad[:, ONE_HALF:both], grad[:, both + ONE_HALF :]], axis=-1)
        pieces = [one[:, 0:ED_AT], two[:, 0:192], two[:, UP_TWO:], one[:, ED_AT : ED_AT + DD]]
        grad = head_pieces(jnp.concatenate(pieces, axis=-1), DHEADS // 2)
        adam_at(states[2] + outs[2], (0,), grad * factor, DECAY, RATE)

    @pl.when(step == 2)
    def _():
        place = Place()
        own = shard_at(place.z, place.x, place.col)
        for kind, top, count, width in ((3, 0, 10, D), (4, 16, 7, DD)):
            share = width // N_SHARDS
            turned = pltpu.roll(total, (D - own * share) % D, 1)
            grad = turned[top : top + count, 0:share] * factor
            adam_at(states[kind] + outs[kind], (slice(None), slice(None)), grad, 0.0, VEC_RATE)


def run_update(total, grads, states):
    f32 = jnp.float32
    smem = pl.BlockSpec(memory_space=pltpu.SMEM)
    flat = [a for triple in states for a in triple]
    scalar = jax.ShapeDtypeStruct((1, 1), f32)
    outs = (scalar, scalar) + tuple(jax.ShapeDtypeStruct(a.shape, f32) for a in flat)
    rows = SHARD // 2

    def whole(array):
        return pl.BlockSpec(array.shape, lambda i: (0,) * array.ndim)

    enc = pl.BlockSpec((1, 1, rows, ENC_COLS), lambda i: (i // 2, 0, i % 2, 0))
    enc_grad = pl.BlockSpec((1, rows, ENC_COLS), lambda i: (i // 2, i % 2, 0))
    state_specs = [enc] * 3 + [whole(a) for a in flat[3:]]
    return pl.pallas_call(
        update_body,
        grid=(2 * LAYERS,),
        out_shape=outs,
        in_specs=[whole(total), enc_grad, whole(grads[1]), whole(grads[2])] + state_specs,
        out_specs=tuple([smem, smem] + state_specs),
        compiler_params=pltpu.CompilerParams(vmem_limit_bytes=60 * MIB),
        name="update",
    )(total, *grads, *flat)


def head_order(matrix, heads, width):
    lead = matrix.shape[:-1]
    cut = matrix[..., :width].reshape(lead + (heads, 3, HEAD))
    cut = jnp.swapaxes(cut, -3, -2).reshape(lead + (width,))
    return jnp.concatenate([cut, matrix[..., width:]], axis=-1)


def head_order_back(matrix, heads, width):
    lead = matrix.shape[:-1]
    cut = matrix[..., :width].reshape(lead + (3, heads, HEAD))
    cut = jnp.swapaxes(cut, -3, -2).reshape(lead + (width,))
    return jnp.concatenate([cut, matrix[..., width:]], axis=-1)


def sine_table(length, width):
    column = np.arange(width)
    freq = np.exp(-math.log(10000.0) * (2.0 * (column // 2)) / width)
    angle = np.arange(length)[:, None] * freq
    table = np.where(column % 2 == 0, np.sin(angle), np.cos(angle))
    return np.pad(table, ((0, ROWS - length), (0, 0))).astype(np.float32)


def frequency_rows(width):
    column = np.arange(width)
    freq = np.exp(-math.log(10000.0) * (2.0 * (column // 2)) / width)
    return np.broadcast_to(freq.astype(np.float32), (8, width))


def split_parts(matrices):
    gap = [(0, 0)] * (matrices.ndim - 1)
    one = jnp.concatenate([matrices[..., :ED_AT], matrices[..., 3072:]], axis=-1)
    one = jnp.pad(one, gap + [(0, PART_ONE - one.shape[-1])])
    out = jnp.pad(matrices[..., ED_AT:768], gap + [(0, UP_TWO - 192)])
    return one, jnp.concatenate([out, matrices[..., 768:3072]], axis=-1)


def join_parts(one, two):
    return jnp.concatenate(
        [one[..., :ED_AT], two[..., :192], two[..., UP_TWO:], one[..., ED_AT : ED_AT + DD]], axis=-1
    )


def gather_vectors(enc_vec, dec_vec, group):
    vectors = jnp.concatenate([enc_vec.reshape(-1), dec_vec.reshape(-1)])
    vectors = lax.all_gather(low(vectors), group, axis=0, tiled=False).astype(jnp.float32)
    cut = enc_vec.size
    enc_gains = jnp.swapaxes(vectors[:, :cut].reshape(-1, *enc_vec.shape), 0, 1).reshape(-1, D)
    dec_gains = jnp.swapaxes(vectors[:, cut:].reshape(-1, *dec_vec.shape), 0, 1).reshape(-1, DD)
    return (
        jnp.pad(enc_gains, ((0, 16 - enc_gains.shape[0]), (0, 0))),
        jnp.pad(dec_gains, ((0, 8 - dec_gains.shape[0]), (0, 0))),
    )


def update_plain(loss_part, dec_vec_grads, enc_vec_grads, grads, states):
    everyone = ("row", "clip", "col")
    n_enc, n_dec = states[3][0].shape[0], states[4][0].shape[0]
    enc_vec_total, dec_vec_total, loss_total, square = lax.psum(
        (
            0.5 * enc_vec_grads[:n_enc],
            dec_vec_grads[:n_dec],
            loss_part,
            sum(jnp.sum(g * g) for g in grads),
        ),
        everyone,
    )
    square = square + jnp.sum(enc_vec_total**2) + jnp.sum(dec_vec_total**2)
    grad_norm = jnp.sqrt(square)
    factor = jnp.minimum(1.0, CLIP_MAX / (grad_norm + 1e-06))
    shard = lax.axis_index("clip") * lax.axis_size("col") + lax.axis_index("col")
    own = []
    for total, state in ((enc_vec_total, states[3][0]), (dec_vec_total, states[4][0])):
        width = state.shape[1]
        own.append(lax.dynamic_slice_in_dim(total, shard * width, width, 1))
    decays = (DECAY, DECAY, DECAY, 0.0, 0.0)
    rates = (RATE, RATE, RATE, VEC_RATE, VEC_RATE)
    results = []
    for triple, grad, decay_rate, step_rate in zip(states, (*grads, *own), decays, rates):
        grad = grad.reshape(triple[0].shape)
        results.extend(adam_update(*triple, grad * factor, decay_rate, step_rate))
    return (loss_total, grad_norm, *results)


def local(
    patches,
    visible,
    masked,
    enc_layers,
    enc_first,
    enc_second,
    embed,
    embed_first,
    embed_second,
    dec_mats,
    dec_first,
    dec_second,
    enc_vec,
    enc_vec_first,
    enc_vec_second,
    dec_vec,
    dec_vec_first,
    dec_vec_second,
):
    f32 = jnp.float32
    group = ("clip", "col")
    everyone = ("row", "clip", "col")
    wide = lax.axis_size("clip") == 8 and lax.axis_size("col") == 2
    freq = jnp.asarray(frequency_rows(D))
    table = jnp.asarray(sine_table(TUBES, DD))
    if wide:
        feat, xs, qkv, att, hid, slope, px, padded, enc_gains, dec_gains, enc_full, one, two = (
            run_encoder(True, visible, patches, freq, embed, enc_layers, dec_mats, enc_vec, dec_vec)
        )
    else:
        embed_full = lax.all_gather(low(embed[0]), group, axis=0, tiled=True)
        enc_here = low(head_order(enc_layers[:, 0], HEADS // 2, QKV_W))
        enc_full = lax.all_gather(enc_here, group, axis=1, tiled=True)
        dec_here = low(head_order(dec_mats[0], DHEADS // 2, ED_AT))
        dec_full = lax.all_gather(dec_here, everyone, axis=0, tiled=True).reshape(2, DD, -1)
        enc_gains, dec_gains = gather_vectors(enc_vec, dec_vec, group)
        feat, xs, qkv, att, hid, slope, px, padded = run_encoder(
            False, visible, patches, freq, embed_full, enc_full, enc_gains
        )
        one, two = split_parts(dec_full)
    loss_block, grad_one, grad_two, dec_vec_grads, grad_feat = run_decoder(
        wide, visible, feat, padded, table, one, two, dec_gains
    )
    kept = (grad_feat, xs, qkv, att, hid, slope, px, enc_gains, enc_full)
    states = (
        (enc_layers, enc_first, enc_second),
        (embed, embed_first, embed_second),
        (dec_mats, dec_first, dec_second),
        (enc_vec, enc_vec_first, enc_vec_second),
        (dec_vec, dec_vec_first, dec_vec_second),
    )
    if wide:
        enc_total, embed_total, _, dec_total, total = run_encoder_back(
            True, *kept, grad_one, grad_two, loss_block, dec_vec_grads
        )
        grads = (enc_total, embed_total, dec_total)
        loss_total, grad_norm, *results = run_update(total, grads, states)
        return (loss_total[0, 0], grad_norm[0, 0], *results)
    dec_grads = join_parts(grad_one, grad_two)
    dec_total = lax.psum_scatter(
        dec_grads.reshape(-1, dec_grads.shape[-1]), everyone, scatter_dimension=0, tiled=True
    ).astype(f32)
    enc_total, embed_total, enc_vec_grads = run_encoder_back(False, *kept)
    enc_total = lax.psum_scatter(enc_total, group, scatter_dimension=1, tiled=True).astype(f32)
    embed_total = lax.psum_scatter(embed_total, group, scatter_dimension=0, tiled=True).astype(f32)
    grads = (
        head_order_back(enc_total, HEADS // 2, QKV_W),
        embed_total,
        head_order_back(dec_total, DHEADS // 2, ED_AT),
    )
    return update_plain(loss_block[0, 0], dec_vec_grads, enc_vec_grads, grads, states)


def solution(mesh):
    in_specs = (
        P(None, ("clip", "col"), None, "row"),
        P(None, ("clip", "col"), None),
        P(None, ("clip", "col"), None),
        P(None, "row", ("clip", "col"), None),
        P(None, "row", ("clip", "col"), None),
        P(None, "row", ("clip", "col"), None),
        P("row", ("clip", "col"), None),
        P("row", ("clip", "col"), None),
        P("row", ("clip", "col"), None),
        P("row", ("clip", "col"), None),
        P("row", ("clip", "col"), None),
        P("row", ("clip", "col"), None),
        P(None, ("clip", "col")),
        P(None, ("clip", "col")),
        P(None, ("clip", "col")),
        P(None, ("clip", "col")),
        P(None, ("clip", "col")),
        P(None, ("clip", "col")),
    )
    out_specs = (
        P(),
        P(),
        P(None, "row", ("clip", "col"), None),
        P(None, "row", ("clip", "col"), None),
        P(None, "row", ("clip", "col"), None),
        P("row", ("clip", "col"), None),
        P("row", ("clip", "col"), None),
        P("row", ("clip", "col"), None),
        P("row", ("clip", "col"), None),
        P("row", ("clip", "col"), None),
        P("row", ("clip", "col"), None),
        P(None, ("clip", "col")),
        P(None, ("clip", "col")),
        P(None, ("clip", "col")),
        P(None, ("clip", "col")),
        P(None, ("clip", "col")),
        P(None, ("clip", "col")),
    )
    return jax.shard_map(local, mesh=mesh, in_specs=in_specs, out_specs=out_specs, check_vma=False)
```

```python
import functools
import math

import jax
import jax.numpy as jnp
import numpy as np
from jax import lax
from jax.experimental import pallas as pl
from jax.experimental.pallas import tpu as pltpu
from jax.sharding import PartitionSpec as P

D = 768
HEADS = 12
HEAD = 64
FF = 3072
DD = 384
DHEADS = 6
DFF = 1536
PIX = 1536
TUBES = 1176
VIS = 118
LAYERS = 2
MICRO = 2
STEP = 10
MASKED = 1058


EPS_NORM = 1e-06
CLIP_MAX = 1.0
BETA_ONE = 0.9
BETA_TWO = 0.999
RATE = 0.06
VEC_RATE = 0.2
DECAY = 0.05
EPS_ADAM = 1e-08


def times_plain(left, right):
    return jnp.dot(left, right, preferred_element_type=jnp.float32)


def times_trans(left, right):
    return lax.dot_general(
        left, right, (((1,), (1,)), ((), ())), preferred_element_type=jnp.float32
    )


def trans_times(left, right):
    return lax.dot_general(
        left, right, (((0,), (0,)), ((), ())), preferred_element_type=jnp.float32
    )


def gelu_pair(values):
    cumul = 0.5 * (1.0 + lax.erf(values * 0.7071067811865476))
    density = jnp.exp(-0.5 * values * values) * 0.3989422804014327
    return (values * cumul, cumul + values * density)


def adam_update(master, first, second, grad_clip, decay_rate, step_rate):
    first_new = BETA_ONE * first + (1.0 - BETA_ONE) * grad_clip
    second_new = BETA_TWO * second + (1.0 - BETA_TWO) * grad_clip * grad_clip
    first_hat = first_new / (1.0 - BETA_ONE**STEP)
    second_hat = second_new / (1.0 - BETA_TWO**STEP)
    master_new = master - step_rate * (
        first_hat / (jnp.sqrt(second_hat) + EPS_ADAM) + decay_rate * master
    )
    return (master_new, first_new, second_new)


LOG2E = 1.4426950408889634
SCALE = HEAD ** (-0.5)
MIB = 1 << 20
MESH_IDS = pl.DeviceIdType.MESH
N_SHARDS = 16
SHARD = D // N_SHARDS
PART_ONE = 1024
PART_TWO = 2560
ONE_HALF, TWO_HALF = PART_ONE // 2, PART_TWO // 2
ED_AT = 3 * DD // 2
UP_TWO, DN_TWO, HD_TWO = 256, 1024, 1792


def low(values):
    return values.astype(jnp.bfloat16)


def lane_ids(shape):
    return lax.broadcasted_iota(jnp.int32, shape, len(shape) - 1)


def row_ids(shape):
    return lax.broadcasted_iota(jnp.int32, shape, 0)


def remote(src, dst, send_sem, recv_sem, device):
    return pltpu.make_async_remote_copy(
        src_ref=src,
        dst_ref=dst,
        send_sem=send_sem,
        recv_sem=recv_sem,
        device_id=device,
        device_id_type=MESH_IDS,
    )


class Place:
    def __init__(self):
        self.clip = lax.axis_index("clip")
        self.row = lax.axis_index("row")
        self.col = lax.axis_index("col")
        self.z = self.clip // 2
        self.x = self.clip % 2

    def z_mate(self, step):
        return (((self.z + step) % 4) * 2 + self.x, self.row, self.col)

    def x_mate(self):
        return (self.z * 2 + 1 - self.x, self.row, self.col)

    def core_mate(self):
        return (self.clip, self.row, 1 - self.col)

    def row_mate(self):
        return (self.clip, 1 - self.row, self.col)

    def mates(self, wide):
        near = [self.row_mate()]
        if wide:
            near += [self.core_mate(), self.x_mate()] + [self.z_mate(s) for s in (1, 2, 3)]
        return near

    def cube(self):
        found = []
        for i in range(1, 8):
            x = 1 - self.x if i & 1 else self.x
            row = 1 - self.row if i & 2 else self.row
            col = 1 - self.col if i & 4 else self.col
            found.append((self.z * 2 + x, row, col))
        return found


def shard_at(z, x, col):
    return (z * 2 + x) * 2 + col


def greet(mates):
    barrier = pltpu.get_barrier_semaphore()
    for mate in mates:
        pl.semaphore_signal(barrier, inc=1, device_id=mate, device_id_type=MESH_IDS)
    pl.semaphore_wait(barrier, len(mates))


class Mail:
    def __init__(self):
        self.sent = []

    def go(self, src, dst, ss, rs, device, only=None):
        copy = remote(src, dst, ss, rs, device)
        if only is None:
            copy.start()
        else:
            pl.when(only)(copy.start)
        self.sent.append((copy, only))

    def came(self, dst, ss, rs, device):
        remote(dst, dst, ss, rs, device).wait_recv()

    def drain(self):
        for copy, only in self.sent:
            if only is None:
                copy.wait_send()
            else:
                pl.when(only)(copy.wait_send)
        self.sent = []


class Gather(Mail):
    def __init__(self, place, own, spot, sems, over_x_first=None):
        super().__init__()
        self.at, self.own, self.spot, self.turned = place, own, spot, over_x_first
        self.z_ss, self.z_rs, self.x_ss, self.x_rs, self.c_ss, self.c_rs = sems

    def line(self, k, src, dst):
        for s, only in ((2, None), (1, self.at.z != 3), (3, self.at.z != 0)):
            ss, rs = self.z_ss.at[k, s - 1], self.z_rs.at[k, s - 1]
            self.go(src, dst, ss, rs, self.at.z_mate(s), only)

    def landed(self, k, s, spot):
        at = self.at
        self.came(spot, self.z_ss.at[k, s - 1], self.z_rs.at[k, s - 1], at.z_mate(s))
        if s == 2:
            for step, only in ((3, at.z == 1), (1, at.z == 2)):
                slot = (2 + step) % 4 - 1
                ss, rs = self.z_ss.at[k, 3], self.z_rs.at[k, slot]
                self.go(spot, spot, ss, rs, at.z_mate(step), only)

    def to_core(self, k, slot, spot):
        self.go(spot, spot, self.c_ss.at[k, slot], self.c_rs.at[k, slot], self.at.core_mate())

    def begin(self, k):
        at = self.at
        src, dst = self.own(k), self.spot(k, at.z, at.x, at.col)
        if k == self.turned:
            self.go(src, dst, self.x_ss.at[k, 0], self.x_rs.at[k, 0], at.x_mate())
        self.line(k, src, dst)
        if k != self.turned:
            self.go(src, dst, self.x_ss.at[k, 0], self.x_rs.at[k, 0], at.x_mate())
        self.go(src, dst, self.c_ss.at[k, 0], self.c_rs.at[k, 0], at.core_mate())

    def begin_lined(self, blocks):
        at = self.at
        for s in (0, 2, 1, 3):
            z = (at.z - s) % 4
            spot = self.spot(0, z, at.x, at.col)
            self.go(blocks.at[z], spot, self.x_ss.at[0, s], self.x_rs.at[0, s], at.x_mate())
            self.go(blocks.at[z], spot, self.c_ss.at[0, s], self.c_rs.at[0, s], at.core_mate())

    def begin_turned(self, extra):
        at, k = self.at, self.turned
        spot = self.spot(k, at.z, 1 - at.x, at.col)
        self.came(spot, self.x_ss.at[k, 0], self.x_rs.at[k, 0], at.x_mate())
        self.line(extra, spot, spot)
        self.to_core(k, 4, spot)

    def forward_turned(self, extra):
        at, k = self.at, self.turned
        for s in (2, 1, 3):
            for line, x, slot in ((k, at.x, s), (extra, 1 - at.x, 4 + s)):
                spot = self.spot(k, (at.z - s) % 4, x, at.col)
                self.landed(line, s, spot)
                self.to_core(k, slot, spot)

    def forward(self, k):
        for s in (2, 1, 3):
            self.one("forward", s, k)

    def across(self, k):
        for s in (0, 2, 1, 3):
            self.one("across", s, k)

    def one(self, step, s, k=0):
        at = self.at
        if step == "across":
            spot = self.spot(k, (at.z - s) % 4, 1 - at.x, at.col)
            self.came(spot, self.x_ss.at[k, s], self.x_rs.at[k, s], at.x_mate())
            self.to_core(k, 4 + s, spot)
            return
        spot = self.spot(k, (at.z - s) % 4, at.x, at.col)
        self.landed(k, s, spot)
        self.go(spot, spot, self.x_ss.at[k, s], self.x_rs.at[k, s], at.x_mate())
        self.to_core(k, s, spot)

    def finish(self, k):
        at = self.at
        for s in range(8):
            x = at.x if s < 4 else 1 - at.x
            spot = self.spot(k, (at.z - s % 4) % 4, x, 1 - at.col)
            self.came(spot, self.c_ss.at[k, s], self.c_rs.at[k, s], at.core_mate())


class LineSum(Mail):
    def __init__(self, place, own, sent, got, ss, rs, rows, into):
        super().__init__()
        self.at, self.own, self.out, self.got, self.ss, self.rs = place, own, sent, got, ss, rs
        self.rows, self.into = rows, into
        self.middle = jnp.logical_or(place.z == 1, place.z == 2)

    def block(self, s):
        return self.own[self.rows * s : self.rows * (s + 1), :]

    def begin(self):
        at = self.at
        self.into[...] = self.block(0)
        for s, end, step in ((1, 3, 3), (3, 0, 1)):
            self.out[s - 1] = low(self.block(s))
            src = self.out.at[s - 1]
            dst = self.got.at[s - 1]
            inner = at.z != end
            self.go(src, dst, self.ss.at[s - 1], self.rs.at[s - 1], at.z_mate(s), inner)
            other = self.got.at[3]
            self.go(src, other, self.ss.at[3], self.rs.at[3], at.z_mate(step), at.z == end)
        outer = jnp.logical_not(self.middle)

        @pl.when(outer)
        def _():
            self.out[1] = low(self.block(2))

        self.go(
            self.out.at[1], self.got.at[1], self.ss.at[1], self.rs.at[1], at.z_mate(2), outer
        )

    def relay(self):
        at = self.at

        @pl.when(self.middle)
        def _():
            self.came(self.got.at[3], self.ss.at[3], self.rs.at[3], at.z_mate(1))
            self.out[1] = low(self.block(2) + self.got[3].astype(jnp.float32))

        self.go(
            self.out.at[1], self.got.at[1], self.ss.at[1], self.rs.at[1], at.z_mate(2), self.middle
        )

    def finish(self):
        at = self.at

        def add(s):
            self.came(self.got.at[s - 1], self.ss.at[s - 1], self.rs.at[s - 1], at.z_mate(s))
            self.into[...] += self.got[s - 1].astype(jnp.float32)

        add(2)
        pl.when(at.z != 0)(lambda: add(1))
        pl.when(at.z != 3)(lambda: add(3))


class Swap:
    def __init__(self, place, sent, got, send_sems, recv_sems):
        self.at, self.sent, self.got = place, sent, got
        self.ss, self.rs = send_sems, recv_sems
        self.copies = {}

    def start(self, i, value):
        slot = i % self.sent.shape[0]
        for j in [j for j in self.copies if j % self.sent.shape[0] == slot]:
            self.copies.pop(j).wait_send()
        self.sent[slot] = low(value)
        copy = remote(
            self.sent.at[slot], self.got.at[i], self.ss.at[i], self.rs.at[i], self.at.row_mate()
        )
        copy.start()
        self.copies[i] = copy

    def total(self, i):
        self.copies[i].wait_recv()
        sent = self.sent[i % self.sent.shape[0]]
        return sent.astype(jnp.float32) + self.got[i].astype(jnp.float32)

    def drain(self):
        for copy in self.copies.values():
            copy.wait_send()


ROWS = 1216
LANES = 1280
STEP_ROWS = 608
N_STEPS = ROWS // STEP_ROWS
KEY_ROWS = 640


def norm_rows(rows):
    average = jnp.mean(rows, axis=-1, keepdims=True)
    centred = rows - average
    inv_dev = lax.rsqrt(jnp.mean(centred * centred, axis=-1, keepdims=True) + EPS_NORM)
    return centred * inv_dev, inv_dev


def norm_rows_back(grad_out, scaled, inv_dev, gain_row):
    inner = grad_out * gain_row
    return inv_dev * (
        inner
        - jnp.mean(inner, axis=-1, keepdims=True)
        - scaled * jnp.mean(inner * scaled, axis=-1, keepdims=True)
    )


def column_sum(values):
    return jnp.sum(values, axis=0, keepdims=True)


def decoder_body(wide, *refs):
    bf, f32 = jnp.bfloat16, jnp.float32
    seen_ref, feat_ref, padded_ref, table_ref, one_ref, two_in, vec_ref = refs[:7]
    loss_ref, gone_ref, gtwo_ref, gvec_ref, gfeat_ref = refs[7:12]
    z_s, n1_s, q_s, k_s, v_s, o_s, do_s, dx_s, dqkv_s, dqt_s, lse_s, delta_s = refs[12:24]
    lse_t, delta_t, wqkv_s, wo_s, y_s, gqkv_s, go_s, gup_s, gdn_s, ghd_s = refs[24:34]
    gy_s, gv_s, pixel_ref, seen_s, near_sem, far_ss, far_rs = refs[34:41]
    if wide:
        two_s, cr_s, xs_s, xr_s, c_ss, c_rs, x_ss, x_rs = refs[41:49]
        g_s = two_s
    else:
        two_s, g_s = two_in, gtwo_ref
    place = Place()
    greet(place.mates(wide))

    def chip_rows(s, x):
        return pl.ds(pl.multiple_of(((place.z + s) % 4 * 2 + x) * SHARD, 16), SHARD)

    own_lanes = pl.ds(pl.multiple_of(place.col * TWO_HALF, 128), TWO_HALF)
    other_lanes = pl.ds(pl.multiple_of((1 - place.col) * TWO_HALF, 128), TWO_HALF)
    if wide:

        def spot(k, z, x, col):
            rows = pl.ds(pl.multiple_of((z * 2 + x) * SHARD, 16), SHARD)
            return two_s.at[:, rows, pl.ds(pl.multiple_of(col * TWO_HALF, 128), TWO_HALF)]

        gather = Gather(place, lambda k: two_in, spot, refs[49:55])
        gather.begin_lined(two_in)
        for step in range(4):
            two_s[:, chip_rows(step, place.x), own_lanes] = two_in[(place.z + step) % 4]

    def tile(i):
        return pl.ds(pl.multiple_of(i * STEP_ROWS, STEP_ROWS), STEP_ROWS)

    def near(i):
        rows = tile(i)
        return pltpu.make_async_copy(
            padded_ref.at[place.row, rows, :], pixel_ref.at[place.row, rows, :], near_sem.at[i]
        )

    def far(i, half):
        rows = tile(i)
        return remote(
            padded_ref.at[1 - place.row, rows, :],
            pixel_ref.at[half, rows, :],
            far_ss.at[i],
            far_rs.at[i],
            place.row_mate(),
        )

    @pl.loop(0, N_STEPS)
    def _(i):
        near(i).start()
        far(i, place.row).start()

    half = 3 * HEAD
    up0, dn0, hd0, ed0 = UP_TWO, DN_TWO, HD_TWO, ED_AT
    vec = vec_ref[...]
    gain1, shift1, gain2, shift2, gain_f, shift_f, token = [vec[i : i + 1] for i in range(7)]

    for part in range(3):
        for r in range(2):
            wqkv_s[:, part * DD + r * half : part * DD + (r + 1) * half] = one_ref[
                r, :, part * half : (part + 1) * half
            ]
    for ref in (q_s, k_s, v_s, do_s):
        ref[ROWS:LANES, :] = jnp.zeros((LANES - ROWS, DD), bf)
    delta_s[ROWS:LANES, :] = jnp.zeros((LANES - ROWS, 128), f32)
    for ref in (gqkv_s, go_s, gup_s, gdn_s, ghd_s, gy_s, gv_s):
        ref[...] = jnp.zeros(ref.shape, f32)
    for r in range(2):
        y_s[:, r * DD : (r + 1) * DD] = low(
            times_trans(feat_ref[:, r * DD : (r + 1) * DD], one_ref[r, :, ed0 : ed0 + DD])
        )
    seen_s[...] = jnp.full(seen_s.shape, -1, jnp.int32)
    seen_s[0:1, 0:VIS] = seen_ref[place.row]
    seen = seen_s[0:1, :]

    def picks(i):
        ids = row_ids((STEP_ROWS, 128)) + i * STEP_ROWS
        hits = ids == seen
        taken = jnp.sum(hits.astype(f32), axis=-1, keepdims=True)
        valid = (row_ids((STEP_ROWS, 1)) + i * STEP_ROWS < TUBES).astype(f32)
        return hits.astype(bf), valid - taken

    @pl.loop(0, N_STEPS)
    def _(i):
        hits, hidden = picks(i)
        placed = times_plain(hits, y_s[...])
        z = placed[:, :DD] + placed[:, DD:] + table_ref[tile(i), :] + token * hidden
        z_s[tile(i), :] = z
        scaled, _ = norm_rows(z)
        n1 = low(scaled * gain1 + shift1)
        n1_s[tile(i), :] = n1
        q_s[tile(i), :] = low(times_plain(n1, wqkv_s[:, 0:DD]))
        k_s[tile(i), :] = low(times_plain(n1, wqkv_s[:, DD : 2 * DD]))
        v_s[tile(i), :] = low(times_plain(n1, wqkv_s[:, 2 * DD : 3 * DD]))

    first_half = lane_ids((1, 128)) < HEAD
    half_masks = [first_half, jnp.logical_not(first_half)]
    last_keys = lane_ids((1, 128)) < TUBES - (LANES - 128)
    ones = jnp.ones((LANES, 128), bf)
    lse_s[...] = jnp.zeros(lse_s.shape, f32)
    for p in range(3):
        lanes = slice(128 * p, 128 * (p + 1))

        @pl.loop(0, N_STEPS)
        def _(i):
            queries = q_s[tile(i), lanes]
            parts = []
            stat = lse_s[tile(i), :]
            for h in range(2):
                one = jnp.where(half_masks[h], queries, jnp.zeros_like(queries))
                scores = times_trans(one, k_s[:, lanes])
                tail = jnp.where(last_keys, scores[:, LANES - 128 :], -1e30)
                scores = jnp.concatenate([scores[:, : LANES - 128], tail], axis=-1)
                top = jnp.max(scores, axis=-1, keepdims=True) * (SCALE * LOG2E)
                weights = low(jnp.exp2(scores * (SCALE * LOG2E) - top))
                both = times_plain(weights, jnp.concatenate([v_s[:, lanes], ones], axis=-1))
                total = both[:, 128:129]
                parts.append(both[:, 0:128] / total)
                lse = top + jnp.log(total) * LOG2E
                stat = jnp.where(lane_ids((1, 128)) == 2 * p + h, lse, stat)
            lse_s[tile(i), :] = stat
            o_s[tile(i), lanes] = low(jnp.where(first_half, parts[0], parts[1]))

        if wide:
            for step in ((0,), (2,), (1, 3))[p]:
                gather.one("across", step)
    if wide:
        gather.finish(0)
    for r in range(2):
        wo_s[:, r * half : (r + 1) * half] = two_s[r, :, 0:half]
    lse_t[...] = lse_s[...].T

    @pl.loop(0, N_STEPS)
    def _(i):
        _, hidden = picks(i)
        near(i).wait()
        far(i, 1 - place.row).wait_recv()
        attended = o_s[tile(i), :]
        x1 = z_s[tile(i), :] + times_trans(attended, wo_s[...])
        scaled2, inv2 = norm_rows(x1)
        n2 = low(scaled2 * gain2 + shift2)
        x2 = x1
        acts, slopes, d_preds, d_us = [], [], [], []
        for r in range(2):
            u = times_plain(n2, two_s[r, :, up0 : up0 + 768])
            act, slope = gelu_pair(u)
            act = low(act)
            acts.append(act)
            slopes.append(slope)
            x2 = x2 + times_trans(act, two_s[r, :, dn0 : dn0 + 768])
        scaled_f, inv_f = norm_rows(x2)
        t = low(scaled_f * gain_f + shift_f)
        d_t = jnp.zeros((STEP_ROWS, DD), f32)
        for r in range(2):
            error = times_plain(t, two_s[r, :, hd0 : hd0 + 768]) - pixel_ref[r, tile(i), :].astype(
                f32
            )
            error = error * hidden
            gv_s[7:8, :] += column_sum(error * error)
            d_pred = low(error * (2.0 / PIX))
            d_preds.append(d_pred)
            d_t = d_t + times_trans(d_pred, two_s[r, :, hd0 : hd0 + 768])
        ghd_s[...] += trans_times(t, jnp.concatenate(d_preds, axis=-1))
        gv_s[4:5, 0:DD] += column_sum(d_t * scaled_f)
        gv_s[5:6, 0:DD] += column_sum(d_t)
        d_x2 = norm_rows_back(d_t, scaled_f, inv_f, gain_f)
        d_low = low(d_x2)
        d_n2 = jnp.zeros((STEP_ROWS, DD), f32)
        for r in range(2):
            d_u = low(times_plain(d_low, two_s[r, :, dn0 : dn0 + 768]) * slopes[r])
            d_us.append(d_u)
            d_n2 = d_n2 + times_trans(d_u, two_s[r, :, up0 : up0 + 768])
        gdn_s[...] += trans_times(d_low, jnp.concatenate(acts, axis=-1))
        gup_s[...] += trans_times(n2, jnp.concatenate(d_us, axis=-1))
        gv_s[2:3, 0:DD] += column_sum(d_n2 * scaled2)
        gv_s[3:4, 0:DD] += column_sum(d_n2)
        d_x1 = d_x2 + norm_rows_back(d_n2, scaled2, inv2, gain2)
        dx_s[tile(i), :] = d_x1
        d_low = low(d_x1)
        go_s[...] += trans_times(d_low, attended)
        d_o = low(times_plain(d_low, wo_s[...]))
        do_s[tile(i), :] = d_o
        both = d_o.astype(f32) * attended.astype(f32)
        stat = jnp.zeros((STEP_ROWS, 128), f32)
        for p in range(3):
            pair = both[:, 128 * p : 128 * (p + 1)]
            for h in range(2):
                one = jnp.sum(jnp.where(half_masks[h], pair, 0.0), axis=-1, keepdims=True)
                stat = jnp.where(lane_ids((1, 128)) == 2 * p + h, one, stat)
        delta_s[tile(i), :] = stat

    if wide:
        gather.drain()
    for r in range(2):
        g_s[r, :, 0:half] = low(go_s[:, r * half : (r + 1) * half])
        g_s[r, :, half:up0] = jnp.zeros((DD, up0 - half), bf)
        g_s[r, :, up0 : up0 + 768] = low(gup_s[:, r * 768 : (r + 1) * 768])
        g_s[r, :, dn0 : dn0 + 768] = low(gdn_s[:, r * 768 : (r + 1) * 768])
        g_s[r, :, hd0 : hd0 + 768] = low(ghd_s[:, r * 768 : (r + 1) * 768])
    if wide:
        to_core = remote(g_s.at[:, :, other_lanes], cr_s, c_ss, c_rs, place.core_mate())
        to_core.start()
        to_x = remote(xs_s, xr_s, x_ss, x_rs, place.x_mate())
    delta_t[...] = delta_s[...].T

    for p in range(3):
        lanes = slice(128 * p, 128 * (p + 1))
        dqt_s[...] = jnp.zeros(dqt_s.shape, f32)

        @pl.loop(0, LANES // KEY_ROWS)
        def _(j):
            rows = pl.ds(pl.multiple_of(j * KEY_ROWS, KEY_ROWS), KEY_ROWS)
            keys, values = k_s[rows, lanes], v_s[rows, lanes]
            bias = jnp.where(row_ids((KEY_ROWS, 1)) + j * KEY_ROWS < TUBES, 0.0, -1e30)
            d_keys, d_values = [], []
            for h in range(2):
                key_one = jnp.where(half_masks[h], keys, jnp.zeros_like(keys))
                value_one = jnp.where(half_masks[h], values, jnp.zeros_like(values))
                lse = lse_t[2 * p + h : 2 * p + h + 1, :]
                delta = delta_t[2 * p + h : 2 * p + h + 1, :]
                scores = times_trans(key_one, q_s[:, lanes])
                soft = jnp.exp2((scores * (SCALE * LOG2E) + bias) - lse)
                d_soft = times_trans(value_one, do_s[:, lanes])
                d_scores = low(soft * (d_soft - delta))
                d_values.append(times_plain(low(soft), do_s[:, lanes]))
                d_keys.append(times_plain(d_scores, q_s[:, lanes]))
                dqt_s[...] += trans_times(key_one, d_scores)
            k_out = slice(DD + 128 * p, DD + 128 * (p + 1))
            v_out = slice(2 * DD + 128 * p, 2 * DD + 128 * (p + 1))
            dqkv_s[rows, k_out] = low(jnp.where(first_half, d_keys[0], d_keys[1]) * SCALE)
            dqkv_s[rows, v_out] = low(jnp.where(first_half, d_values[0], d_values[1]))

        dqkv_s[:, lanes] = low(dqt_s[...].T * SCALE)
        if wide and p == 0:
            to_core.wait_recv()
            for s in range(4):
                rows = chip_rows(s, 1 - place.x)
                xs_s[s] = low(g_s[:, rows, own_lanes].astype(f32) + cr_s[:, rows, :].astype(f32))
            to_x.start()

    @pl.loop(0, N_STEPS)
    def _(i):
        hits, hidden = picks(i)
        d_qkv = dqkv_s[tile(i), :]
        gqkv_s[...] += trans_times(n1_s[tile(i), :], d_qkv)
        d_n1 = times_trans(d_qkv, wqkv_s[...])
        scaled1, inv1 = norm_rows(z_s[tile(i), :])
        gv_s[0:1, 0:DD] += column_sum(d_n1 * scaled1)
        gv_s[1:2, 0:DD] += column_sum(d_n1)
        d_z = dx_s[tile(i), :] + norm_rows_back(d_n1, scaled1, inv1, gain1)
        gv_s[6:7, 0:DD] += column_sum(d_z * hidden)
        gy_s[...] += trans_times(hits, low(d_z))

    d_y = low(gy_s[...])
    for r in range(2):
        gone_ref[r, :, ed0 : ed0 + DD] = low(trans_times(d_y, feat_ref[:, r * DD : (r + 1) * DD]))
        gone_ref[r, :, ed0 + DD : PART_ONE] = jnp.zeros((DD, PART_ONE - ed0 - DD), bf)
        gfeat_ref[:, r * DD : (r + 1) * DD] = low(times_plain(d_y, one_ref[r, :, ed0 : ed0 + DD]))
        for part in range(3):
            gone_ref[r, :, part * half : (part + 1) * half] = low(
                gqkv_s[:, part * DD + r * half : part * DD + (r + 1) * half]
            )
    if wide:
        to_x.wait_recv()
        for s in range(4):
            rows = chip_rows(s, place.x)
            total = g_s[:, rows, own_lanes].astype(f32) + cr_s[:, rows, :].astype(f32)
            total = total + xr_s[s].astype(f32)
            for r in range(2):
                at = (2 * s + r) * SHARD
                gtwo_ref[at : at + SHARD, :] = total[r]
        to_core.wait_send()
        to_x.wait_send()
    gvec_ref[...] = gv_s[:, 0:DD]

    @pl.loop(0, N_STEPS)
    def _(i):
        far(i, place.row).wait_send()

    loss_ref[...] = jnp.zeros((8, 128), f32) + jnp.sum(gv_s[7:8, :]) / PIX


def run_decoder(wide, *operands):
    bf, f32 = jnp.bfloat16, jnp.float32
    vmem = pl.BlockSpec(memory_space=pltpu.VMEM)
    dma = pltpu.SemaphoreType.DMA
    if wide:
        two = jax.ShapeDtypeStruct((8 * SHARD, TWO_HALF), f32)
    else:
        two = jax.ShapeDtypeStruct((2, DD, PART_TWO), bf)
    scratch = [
        pltpu.VMEM((ROWS, DD), f32),
        pltpu.VMEM((ROWS, DD), bf),
        pltpu.VMEM((LANES, DD), bf),
        pltpu.VMEM((LANES, DD), bf),
        pltpu.VMEM((LANES, DD), bf),
        pltpu.VMEM((ROWS, DD), bf),
        pltpu.VMEM((LANES, DD), bf),
        pltpu.VMEM((ROWS, DD), f32),
        pltpu.VMEM((LANES, 3 * DD), bf),
        pltpu.VMEM((128, LANES), f32),
        pltpu.VMEM((LANES, 128), f32),
        pltpu.VMEM((LANES, 128), f32),
        pltpu.VMEM((128, LANES), f32),
        pltpu.VMEM((128, LANES), f32),
        pltpu.VMEM((DD, 3 * DD), bf),
        pltpu.VMEM((DD, DD), bf),
        pltpu.VMEM((128, 2 * DD), bf),
        pltpu.VMEM((DD, 3 * DD), f32),
        pltpu.VMEM((DD, DD), f32),
        pltpu.VMEM((DD, DFF), f32),
        pltpu.VMEM((DD, DFF), f32),
        pltpu.VMEM((DD, DFF), f32),
        pltpu.VMEM((128, DD), f32),
        pltpu.VMEM((8, 768), f32),
        pltpu.VMEM((2, ROWS, PIX // 2), bf),
        pltpu.VMEM((8, 128), jnp.int32),
        dma((N_STEPS,)),
        dma((N_STEPS,)),
        dma((N_STEPS,)),
    ]
    if wide:
        scratch += [
            pltpu.VMEM((2, DD, PART_TWO), bf),
            pltpu.VMEM((2, DD, TWO_HALF), bf),
            pltpu.VMEM((4, 2, SHARD, TWO_HALF), bf),
            pltpu.VMEM((4, 2, SHARD, TWO_HALF), bf),
            dma,
            dma,
            dma,
            dma,
        ]
        scratch += [dma((1, 4)), dma((1, 3)), dma((1, 4)), dma((1, 4)), dma((1, 8)), dma((1, 8))]
    return pl.pallas_call(
        functools.partial(decoder_body, wide),
        out_shape=(
            jax.ShapeDtypeStruct((8, 128), f32),
            jax.ShapeDtypeStruct((2, DD, PART_ONE), bf),
            two,
            jax.ShapeDtypeStruct((8, DD), f32),
            jax.ShapeDtypeStruct((128, D), bf),
        ),
        in_specs=[vmem, vmem, pl.BlockSpec(memory_space=pl.ANY), vmem, vmem, vmem, vmem],
        out_specs=(vmem,) * 5,
        scratch_shapes=scratch,
        compiler_params=pltpu.CompilerParams(
            collective_id=4, has_side_effects=True, vmem_limit_bytes=63 * MIB
        ),
        cost_estimate=pl.CostEstimate(
            flops=30 * 10**9, bytes_accessed=20 * 10**6, transcendentals=20 * 10**6
        ),
        name="decoder",
    )(*operands)


PAIR = 256
HALF_D = D // 2
QKV_W = 3 * D // 2
HID = FF // 2
A_COLS = QKV_W + D // 2
ENC_COLS = A_COLS + 2 * HID
UP_AT, DN_AT = A_COLS, A_COLS + HID
EMB_ROWS = SHARD + 16
GATHERS = (
    (-1, 0, D),
    (0, 0, A_COLS),
    (0, UP_AT, HID),
    (0, DN_AT, HID),
    (1, 0, A_COLS),
    (1, UP_AT, HID),
    (1, DN_AT, HID),
    (-2, 0, PART_ONE),
)
PART_ONE_AT = len(GATHERS) - 1


def half_lanes():
    first = lane_ids((1, 128)) < HEAD
    return [first, jnp.logical_not(first)]


def same_clip():
    a, b = row_ids((PAIR, PAIR)), lane_ids((PAIR, PAIR))
    return jnp.logical_and(a // 128 == b // 128, b % 128 < VIS)


def encoder_scores(queries, keys, allowed):
    scores = jnp.where(allowed, times_trans(queries, keys), -1e30)
    top = jnp.max(scores, axis=-1, keepdims=True) * (SCALE * LOG2E)
    weights = jnp.exp2(scores * (SCALE * LOG2E) - top)
    return weights, jnp.sum(weights, axis=-1, keepdims=True)


def encoder_attention(qkv_ref, out_ref):
    allowed = same_clip()
    halves = half_lanes()
    for p in range(3):
        q = qkv_ref[:, 128 * p : 128 * (p + 1)]
        k = qkv_ref[:, HALF_D + 128 * p : HALF_D + 128 * (p + 1)]
        v = qkv_ref[:, 2 * HALF_D + 128 * p : 2 * HALF_D + 128 * (p + 1)]
        parts = []
        for h in range(2):
            one = jnp.where(halves[h], q, jnp.zeros_like(q))
            weights, total = encoder_scores(one, k, allowed)
            parts.append(times_plain(low(weights), v) / total)
        out_ref[:, 128 * p : 128 * (p + 1)] = low(jnp.where(halves[0], parts[0], parts[1]))


def pack_heads(dst, src, heads):
    for part in range(3):
        for h in range(heads):
            at = (part * heads + h) * HEAD
            dst[:, at : at + HEAD] = low(src[:, (3 * h + part) * HEAD : (3 * h + part + 1) * HEAD])


def encoder_body(wide, *refs):
    f32 = jnp.float32
    if wide:
        seen_ref, pixel_ref, freq_ref, emb_ref, enc_ref, dec_ref, evec_ref, dvec_ref = refs[:8]
        refs = refs[8:]
    else:
        seen_ref, pixel_ref, freq_ref, emb_full, w_s, gain_in = refs[:6]
        refs = refs[6:]
    feat_ref, *kept_out = refs[:7]
    padded_out = refs[7]
    refs = refs[8:]
    if wide:
        gain_ref, dgain_ref, w_out, one_out, two_out = refs[:5]
        emb_s, w_s, embc_s, emb_in, enc_in, small_s, one_s, two_s, block_s = refs[5:14]
        refs = refs[14:]
    sent_s, got_s, padded_s, seen_s, pad_sem, y_ss, y_rs = refs[:7]
    kept = refs[7:13]
    kept_sem = refs[13]
    refs = refs[14:]
    x_ref, qkv_ref, o_ref, h_ref, slope_ref, px_ref = kept
    leaving = []

    def leave(src, at=None):
        i = [ref is src for ref in kept].index(True)
        dst = kept_out[i]
        if at is not None:
            src, dst = src.at[at], dst.at[at]
        copy = pltpu.make_async_copy(src, dst, kept_sem.at[len(leaving)])
        copy.start()
        leaving.append(copy)

    place = Place()
    greet(place.mates(wide))
    swap = Swap(place, sent_s, got_s, y_ss, y_rs)
    if wide:

        def own_part(k):
            layer, start, width = GATHERS[k]
            if layer == -1:
                return emb_in
            if layer == -2:
                return spot(k, place.z, place.x, place.col)
            return enc_in.at[layer, :, pl.ds(start, width)]

        def spot(k, z, x, col):
            layer, start, width = GATHERS[k]
            if layer == -2:
                rows = pl.ds(pl.multiple_of((z * 2 + x) * SHARD, 16), SHARD)
                return one_s.at[:, rows, pl.ds(pl.multiple_of(col * ONE_HALF, 128), ONE_HALF)]
            rows = EMB_ROWS if layer < 0 else SHARD
            first = pl.multiple_of(shard_at(z, x, col) * rows, 16)
            if layer == -1:
                return emb_s.at[pl.ds(first, rows), :]
            return w_s.at[layer, pl.ds(first, rows), pl.ds(start, width)]

        gather = Gather(place, own_part, spot, refs[:6], over_x_first=PART_ONE_AT)
        extra = len(GATHERS)
        keep_sem, block_ss, block_rs, seed_ss, seed_rs = refs[6:11]
        emb_in[0:SHARD, :] = low(emb_ref[0])
        small_s[...] = jnp.zeros(small_s.shape, f32)
        small_s[0:10, 0:SHARD] = evec_ref[...]
        small_s[0:7, SHARD : SHARD + DD // N_SHARDS] = dvec_ref[...]
        emb_in[SHARD:EMB_ROWS, 0:128] = low(small_s[...])
        emb_in[SHARD:EMB_ROWS, 128:D] = jnp.zeros((EMB_ROWS - SHARD, D - 128), jnp.bfloat16)
        gather.begin(0)
        for layer in range(LAYERS):
            pack_heads(enc_in.at[layer], enc_ref.at[layer, 0], HEADS // 2)
            enc_in[layer, :, QKV_W:] = low(enc_ref[layer, 0, :, QKV_W:])
            if layer == 0:
                gather.begin(1)
                gather.begin(2)
                gather.begin(3)
        own = shard_at(place.z, place.x, place.col)
        emb_s[pl.ds(pl.multiple_of(own * EMB_ROWS, 16), EMB_ROWS), :] = emb_in[...]
        for layer in range(LAYERS):
            w_s[layer, pl.ds(pl.multiple_of(own * SHARD, 16), SHARD), :] = enc_in[layer]
        mine = pl.ds(pl.multiple_of(place.col * (SHARD // 2), 8), SHARD // 2)
        block_s[mine, :] = jnp.zeros((SHARD // 2, PART_ONE + PART_TWO), f32)
        shard = dec_ref[0]
        heads = DHEADS // 2
        for part in range(3):
            for h in range(heads):
                at = (3 * h + part) * HEAD
                to = (part * heads + h) * HEAD
                block_s[mine, to : to + HEAD] = shard[:, at : at + HEAD]
        block_s[mine, ED_AT : ED_AT + DD] = shard[:, 3072:3456]
        block_s[mine, PART_ONE : PART_ONE + 192] = shard[:, ED_AT:768]
        block_s[mine, PART_ONE + UP_TWO : PART_ONE + PART_TWO] = shard[:, 768:3072]
        spread = remote(
            block_s.at[mine, :], block_s.at[mine, :], block_ss, block_rs, place.core_mate()
        )
        spread.start()
        theirs = pl.ds(pl.multiple_of((1 - place.col) * (SHARD // 2), 8), SHARD // 2)
        half_one = spot(PART_ONE_AT, place.z, place.x, place.col)
        half_two = two_s.at[place.z]
        seeds = [
            remote(part.at[place.row], part.at[place.row], ss, rs, place.row_mate())
            for part, ss, rs in (
                (half_one, seed_ss.at[0], seed_rs.at[0]),
                (half_two, seed_ss.at[1], seed_rs.at[1]),
            )
        ]
        seeds_back = [
            remote(part.at[1 - place.row], part.at[1 - place.row], ss, rs, place.row_mate())
            for part, ss, rs in (
                (half_one, seed_ss.at[0], seed_rs.at[0]),
                (half_two, seed_ss.at[1], seed_rs.at[1]),
            )
        ]

    def step(name, k):
        if wide:
            getattr(gather, name)(k)

    odd = (lane_ids((1, D)) % 2).astype(f32) * (0.5 * math.pi)
    freq = freq_ref[0:1, :]
    places = []
    seen_s[...] = jnp.full(seen_s.shape, -1, jnp.int32)
    whole = TUBES // 16 * 16
    for m in range(MICRO):
        seen_s[m : m + 1, 0:VIS] = seen_ref[m]
        row = seen_s[m : m + 1, :]
        hits = (row_ids((TUBES, 128)) == row).astype(jnp.bfloat16)
        px_ref[128 * m : 128 * (m + 1), :] = low(trans_times(hits, pixel_ref[m, 0]))
        column = jnp.broadcast_to(row.astype(f32), (128, 128)).T[:, 0:1]
        places.append(jnp.sin(column * freq + odd))
        padded_s[m, 0:whole, :] = pixel_ref[m, 0, 0:whole, :]
        rest = pixel_ref[m, 0, whole:TUBES, :].astype(f32)
        rest = jnp.concatenate([rest, jnp.zeros((ROWS - TUBES, D), f32)], axis=0)
        padded_s[m, whole:ROWS, :] = low(rest)
    pad_copy = pltpu.make_async_copy(padded_s, padded_out, pad_sem)
    pad_copy.start()
    leave(px_ref)

    if wide:
        gather.forward(0)
        gather.forward(1)
        gather.begin(4)
        gather.across(0)
        gather.finish(0)
        for s in range(N_SHARDS):
            embc_s[SHARD * s : SHARD * (s + 1), :] = emb_s[EMB_ROWS * s : EMB_ROWS * s + SHARD, :]
            tail = emb_s[EMB_ROWS * s + SHARD : EMB_ROWS * (s + 1), 0:128].astype(f32)
            gain_ref[:, SHARD * s : SHARD * (s + 1)] = tail[:, 0:SHARD]
            dgain_ref[:, DD // 16 * s : DD // 16 * (s + 1)] = tail[0:8, SHARD : SHARD + DD // 16]
        emb_full, gain_in = embc_s, gain_ref
    swap.start(0, times_trans(px_ref[...], emb_full[...]))
    if wide:
        other_rows = block_s.at[theirs, :]
        remote(other_rows, other_rows, block_ss, block_rs, place.core_mate()).wait_recv()
        lanes = pl.ds(pl.multiple_of(place.col * ONE_HALF, 128), ONE_HALF)
        half_one.at[place.row][...] = low(block_s[:, lanes])
        lanes = pl.ds(pl.multiple_of(PART_ONE + place.col * TWO_HALF, 128), TWO_HALF)
        half_two.at[place.row][...] = low(block_s[:, lanes])
        for copy in seeds:
            copy.start()
    step("forward", 2)
    step("across", 1)
    x = swap.total(0) + jnp.concatenate(places, axis=0)
    for layer in range(LAYERS):
        gains = gain_in[4 * layer : 4 * layer + 4, :]
        x_ref[2 * layer] = x
        leave(x_ref, 2 * layer)
        scaled, _ = norm_rows(x)
        n1 = low(scaled * gains[0:1] + gains[1:2])
        first = 1 + 3 * layer
        step("finish", first)
        qkv_ref[layer] = low(times_plain(n1, w_s[layer, :, 0:QKV_W]))
        encoder_attention(qkv_ref.at[layer], o_ref.at[layer])
        if wide and layer == 1:
            gather.forward(6)
        swap.start(1 + 2 * layer, times_trans(o_ref[layer], w_s[layer, :, QKV_W:A_COLS]))
        if wide and layer == 0:
            gather.begin(5)
            gather.forward(3)
        elif wide:
            gather.begin_turned(extra)
            gather.line(extra + 1, half_two, half_two)
        step("across", first + 1)
        x = x + swap.total(1 + 2 * layer)
        x_ref[2 * layer + 1] = x
        leave(x_ref, 2 * layer + 1)
        leave(qkv_ref, layer)
        leave(o_ref, layer)
        scaled, _ = norm_rows(x)
        n2 = low(scaled * gains[2:3] + gains[3:4])
        step("finish", first + 1)
        act, slope = gelu_pair(times_plain(n2, w_s[layer, :, UP_AT:DN_AT]))
        act = low(act)
        h_ref[layer] = act
        slope_ref[layer] = slope
        leave(h_ref, layer)
        leave(slope_ref, layer)
        if layer == 0:
            step("begin", 6)
        step("across", first + 2)
        step("finish", first + 2)
        swap.start(2 + 2 * layer, times_trans(act, w_s[layer, :, DN_AT:ENC_COLS]))
        if wide:
            keep = pltpu.make_async_copy(w_s.at[layer], w_out.at[layer], keep_sem.at[layer])
            keep.start()
        if wide and layer == 0:
            gather.forward(4)
            for copy in seeds_back:
                copy.wait_recv()
            gather.begin(PART_ONE_AT)
            gather.across(4)
            gather.forward(5)
        elif wide:
            gather.forward_turned(extra)
        x = x + swap.total(2 + 2 * layer)
    x_ref[2 * LAYERS] = x
    leave(x_ref, 2 * LAYERS)
    scaled, _ = norm_rows(x)
    gains = gain_in[4 * LAYERS : 4 * LAYERS + 2, :]
    feat = low(scaled * gains[0:1] + gains[1:2])
    feat_ref[...] = jnp.where(place.row == 0, feat[0:128], feat[128:256])
    swap.drain()
    pad_copy.wait()
    for copy in leaving:
        copy.wait()
    if wide:
        gather.finish(PART_ONE_AT)
        for s in (2, 1, 3):
            gather.landed(extra + 1, s, two_s.at[(place.z - s) % 4])
        one_copy = pltpu.make_async_copy(one_s, one_out, keep_sem.at[LAYERS])
        one_copy.start()
        two_copy = pltpu.make_async_copy(two_s, two_out, keep_sem.at[LAYERS + 1])
        two_copy.start()
        spread.wait_send()
        for copy in seeds:
            copy.wait_send()
        gather.drain()
        one_copy.wait()
        two_copy.wait()
        for layer in range(LAYERS):
            pltpu.make_async_copy(w_s.at[layer], w_out.at[layer], keep_sem.at[layer]).wait()


def run_encoder(wide, *operands):
    bf, f32 = jnp.bfloat16, jnp.float32
    vmem = pl.BlockSpec(memory_space=pltpu.VMEM)
    dma = pltpu.SemaphoreType.DMA
    shape = jax.ShapeDtypeStruct
    n_swaps = 1 + 2 * LAYERS
    outs = [
        shape((128, D), bf),
        shape((2 * LAYERS + 1, PAIR, D), f32),
        shape((LAYERS, PAIR, QKV_W), bf),
        shape((LAYERS, PAIR, HALF_D), bf),
        shape((LAYERS, PAIR, HID), bf),
        shape((LAYERS, PAIR, HID), f32),
        shape((PAIR, D), bf),
        shape((MICRO, ROWS, D), bf),
    ]
    out_specs = [vmem] + [pl.BlockSpec(memory_space=pl.ANY)] * (len(outs) - 1)
    kept = [pltpu.VMEM(out.shape, out.dtype) for out in outs[1:7]]
    scratch = []
    if wide:
        anywhere = pl.BlockSpec(memory_space=pl.ANY)
        outs += [
            shape((16, D), f32),
            shape((8, DD), f32),
            shape((LAYERS, D, ENC_COLS), bf),
            shape((2, DD, PART_ONE), bf),
            shape((4, 2, SHARD, TWO_HALF), bf),
        ]
        out_specs += [vmem, vmem, anywhere, anywhere, anywhere]
        scratch += [
            pltpu.VMEM((N_SHARDS * EMB_ROWS, D), bf),
            pltpu.VMEM((LAYERS, D, ENC_COLS), bf),
            pltpu.VMEM((D, D), bf),
            pltpu.VMEM((EMB_ROWS, D), bf),
            pltpu.VMEM((LAYERS, SHARD, ENC_COLS), bf),
            pltpu.VMEM((16, 128), f32),
            pltpu.VMEM((2, DD, PART_ONE), bf),
            pltpu.VMEM((4, 2, SHARD, TWO_HALF), bf),
            pltpu.VMEM((SHARD, PART_ONE + PART_TWO), f32),
        ]
    scratch += [
        pltpu.VMEM((n_swaps, PAIR, D), bf),
        pltpu.VMEM((n_swaps, PAIR, D), bf),
        pltpu.VMEM((MICRO, ROWS, D), bf),
        pltpu.VMEM((8, 128), jnp.int32),
        dma,
        dma((n_swaps,)),
        dma((n_swaps,)),
        *kept,
        dma((2 + 6 * LAYERS,)),
    ]
    if wide:
        n = len(GATHERS)
        scratch += [dma((n + 2, 4)), dma((n + 2, 3)), dma((n, 4)), dma((n, 4)), dma((n, 8)), dma((n, 8))]
        scratch += [dma((LAYERS + 2,)), dma, dma, dma((2,)), dma((2,))]
    return pl.pallas_call(
        functools.partial(encoder_body, wide),
        out_shape=tuple(outs),
        in_specs=[vmem] * len(operands),
        out_specs=tuple(out_specs),
        scratch_shapes=scratch,
        compiler_params=pltpu.CompilerParams(
            collective_id=1, has_side_effects=True, vmem_limit_bytes=60 * MIB
        ),
        cost_estimate=pl.CostEstimate(
            flops=10 * 10**9, bytes_accessed=60 * 10**6, transcendentals=10**6
        ),
        name="encoder",
    )(*operands)


SUMS = (
    ("dn1", HID),
    ("up1", HID),
    ("at1", A_COLS),
    ("dn0", HID),
    ("up0", HID),
    ("at0", A_COLS),
    ("emb", D),
)
SUM_AT = {name: sum(w for _, w in SUMS[:i]) for i, (name, _) in enumerate(SUMS)}
SUM_COLS = sum(w for _, w in SUMS)
BLOCKS = N_SHARDS // 2 * SHARD
QUARTER = BLOCKS // 2


class Scatter(Mail):
    def __init__(self, place, bufs, sems, into):
        super().__init__()
        self.at, self.into = place, into
        self.perm, self.flip, self.cs, self.cr, self.xs, self.xr, self.zs, self.zr, self.own = bufs
        self.c_ss, self.c_rs, self.x_ss, self.x_rs, self.z_ss, self.z_rs = sems
        self.last = {}
        self.lines = {}

    def span(self, name, shift=0, width=None):
        k = [n for n, _ in SUMS].index(name)
        return k, pl.ds(SUM_AT[name] + shift, SUMS[k][1] if width is None else width)

    def post(self, src, dst, ss, rs, device, key):
        copy = remote(src, dst, ss, rs, device)
        copy.start()
        self.last[key] = copy

    def free(self, key):
        if key in self.last:
            self.last.pop(key).wait_send()

    def turn(self, slot, left):
        at = self.at
        flip = self.flip.at[slot % 2]
        flip[...] = left.T
        order = [
            (s, x, c) for c, x in ((1, 1), (1, 0), (0, 1), (0, 0)) for s in range(4)
        ]
        for i, (s, other_x, other_c) in enumerate(order):
            x = 1 - at.x if other_x else at.x
            c = 1 - at.col if other_c else at.col
            first = pl.multiple_of(shard_at((at.z + s) % 4, x, c) * SHARD, 16)
            self.perm[slot, SHARD * i : SHARD * (i + 1), :] = flip[pl.ds(first, SHARD), :]

    def cores(self, name, items):
        k, span = self.span(name)
        slot_at, width = k % 2, SUMS[k][1]
        self.free(("core", slot_at))
        for slot, right, shift, wide in items:
            self.cs[slot_at, :, shift : shift + wide] = low(
                times_plain(self.perm[slot, 0:BLOCKS, :], right[...])
            )
        self.post(
            self.cs.at[slot_at, :, pl.ds(0, width)],
            self.cr.at[:, span],
            self.c_ss.at[k],
            self.c_rs.at[k],
            self.at.core_mate(),
            ("core", slot_at),
        )

    def over_x(self, name, items):
        f32 = jnp.float32
        k, whole = self.span(name)
        slot_at, width = k % 3, SUMS[k][1]
        self.free(("x", slot_at))
        self.came(self.cr.at[:, whole], self.c_ss.at[k], self.c_rs.at[k], self.at.core_mate())
        for slot, right, shift, wide in items:
            _, span = self.span(name, shift, wide)
            mine = times_plain(self.perm[slot, BLOCKS : BLOCKS + QUARTER, :], right[...])
            self.xs[slot_at, :, shift : shift + wide] = low(
                mine + self.cr[0:QUARTER, span].astype(f32)
            )
        self.post(
            self.xs.at[slot_at, :, pl.ds(0, width)],
            self.xr.at[:, whole],
            self.x_ss.at[k],
            self.x_rs.at[k],
            self.at.x_mate(),
            ("x", slot_at),
        )
        for slot, right, shift, wide in items:
            _, span = self.span(name, shift, wide)
            mine = times_plain(self.perm[slot, BLOCKS + QUARTER : 2 * BLOCKS, :], right[...])
            self.own[k % 4, :, shift : shift + wide] = mine + self.cr[QUARTER:BLOCKS, span].astype(f32)

    def along_z(self, name):
        k, span = self.span(name)
        self.came(self.xr.at[:, span], self.x_ss.at[k], self.x_rs.at[k], self.at.x_mate())
        own = self.own.at[k % 4, :, pl.ds(0, SUMS[k][1])]
        own[...] += self.xr[:, span].astype(jnp.float32)
        line = LineSum(
            self.at,
            own,
            self.zs.at[:, :, span],
            self.zr.at[:, :, span],
            self.z_ss.at[k],
            self.z_rs.at[k],
            SHARD,
            self.into(name),
        )
        line.begin()
        self.lines[name] = line

    def relay(self, name):
        self.lines[name].relay()

    def finish(self, name):
        self.lines[name].finish()

    def drain(self):
        for copy in self.last.values():
            copy.wait_send()
        for line in self.lines.values():
            line.drain()


class DecoderScatter(Mail):
    def __init__(self, place, one, two, out, bufs, sems):
        super().__init__()
        self.at, self.one, self.two, self.out = place, one, two, out
        self.cr, self.xs, self.xr, self.own, self.zs1, self.zr1, self.zs2, self.zr2 = bufs[:8]
        self.fin, self.ys, self.yr, self.whole, self.part = bufs[8:]
        (
            self.c_ss, self.c_rs, self.x_ss, self.x_rs, self.z1_ss, self.z1_rs,
            self.z2_ss, self.z2_rs, self.y_ss, self.y_rs, self.f_ss, self.f_rs,
        ) = sems
        self.lanes = pl.ds(pl.multiple_of(place.col * ONE_HALF, 128), ONE_HALF)

    def rows(self, s, x):
        return pl.ds(pl.multiple_of(((self.at.z + s) % 4 * 2 + x) * SHARD, 16), SHARD)

    def begin(self):
        at = self.at
        others = pl.ds(pl.multiple_of((1 - at.col) * ONE_HALF, 128), ONE_HALF)
        src = self.one.at[:, :, others]
        self.go(src, self.cr, self.c_ss, self.c_rs, at.core_mate())
        self.line_two = LineSum(
            at, self.two, self.zs2, self.zr2, self.z2_ss, self.z2_rs, 2 * SHARD,
            self.fin.at[:, pl.ds(ONE_HALF, TWO_HALF)],
        )
        self.line_two.begin()

    def sums(self, s, x):
        rows = self.rows(s, x)
        f32 = jnp.float32
        return self.one[:, rows, self.lanes].astype(f32) + self.cr[:, rows, :].astype(f32)

    def over_x(self):
        at = self.at
        self.came(self.cr, self.c_ss, self.c_rs, at.core_mate())
        for s in range(4):
            self.xs[s] = low(self.sums(s, 1 - at.x))
        self.go(self.xs, self.xr, self.x_ss, self.x_rs, at.x_mate())

    def along_z(self):
        at = self.at
        self.came(self.xr, self.x_ss, self.x_rs, at.x_mate())
        for s in range(4):
            total = self.sums(s, at.x) + self.xr[s].astype(jnp.float32)
            for r in range(2):
                first = (2 * s + r) * SHARD
                self.own[first : first + SHARD, :] = total[r]
        self.line_one = LineSum(
            at, self.own, self.zs1, self.zr1, self.z1_ss, self.z1_rs, 2 * SHARD,
            self.fin.at[:, pl.ds(0, ONE_HALF)],
        )
        self.line_one.begin()

    def over_rows(self):
        at = self.at
        self.line_one.finish()
        self.line_two.finish()
        rows = pl.ds(pl.multiple_of((1 - at.row) * SHARD, 8), SHARD)
        self.ys[...] = low(self.fin[rows, :])
        self.go(self.ys, self.yr, self.y_ss, self.y_rs, at.row_mate())

    def to_cores(self):
        at = self.at
        self.came(self.yr, self.y_ss, self.y_rs, at.row_mate())
        rows = pl.ds(pl.multiple_of(at.row * SHARD, 8), SHARD)
        self.whole[...] = self.fin[rows, :] + self.yr[...].astype(jnp.float32)
        theirs = pl.ds(pl.multiple_of((1 - at.col) * (SHARD // 2), 8), SHARD // 2)
        self.go(self.whole.at[theirs, :], self.part, self.f_ss, self.f_rs, at.core_mate())

    def finish(self):
        at = self.at
        width = ONE_HALF + TWO_HALF
        mine = pl.ds(pl.multiple_of(at.col * (SHARD // 2), 8), SHARD // 2)
        self.out[:, pl.ds(pl.multiple_of(at.col * width, 128), width)] = self.whole[mine, :]
        self.came(self.part, self.f_ss, self.f_rs, at.core_mate())
        self.out[:, pl.ds(pl.multiple_of((1 - at.col) * width, 128), width)] = self.part[...]

    def drain(self):
        super().drain()
        self.line_one.drain()
        self.line_two.drain()


class Everyone(Mail):
    def __init__(self, place, bufs, sems):
        super().__init__()
        self.at = place
        self.send, self.got, self.one, self.ones = bufs
        self.ss, self.rs, self.o_ss, self.o_rs = sems
        self.waits = []

    def first(self, enc, dec):
        self.send[0, 0:16, :] = enc
        self.send[0, 16:24, 0:DD] = dec
        self.send[0, 16:24, DD:D] = jnp.zeros((8, D - DD), jnp.float32)
        self.post(0)

    def post(self, i):
        at = self.at
        mates = ([at.core_mate()], [at.row_mate()], [at.x_mate()], [at.z_mate(s) for s in (1, 2, 3)])
        for j, mate in enumerate(mates[i]):
            self.go(
                self.send.at[i], self.got.at[i + j], self.ss.at[i + j], self.rs.at[i + j], mate
            )
        self.waits.append([(i + j, mate) for j, mate in enumerate(mates[i])])

    def stage(self, i):
        total = self.send[i - 1]
        for slot, mate in self.waits[i - 1]:
            self.came(self.got.at[slot], self.ss.at[slot], self.rs.at[slot], mate)
            total = total + self.got[slot]
        self.send[i] = total
        if i < 4:
            self.post(i)

    def total(self):
        return self.send[4]

    def number(self, value):
        at = self.at
        groups = (at.cube(), [at.z_mate(s) for s in (1, 2, 3)])
        total = jnp.zeros((8, 128), jnp.float32) + value
        first = 0
        for i, mates in enumerate(groups):
            self.one[i] = total
            for j, mate in enumerate(mates):
                slot = first + j
                self.go(
                    self.one.at[i], self.ones.at[slot], self.o_ss.at[slot], self.o_rs.at[slot], mate
                )
            for j, mate in enumerate(mates):
                slot = first + j
                self.came(self.ones.at[slot], self.o_ss.at[slot], self.o_rs.at[slot], mate)
                total = total + self.ones[slot]
            first += len(mates)
        return total[0:1, 0:1]


def encoder_attention_back(qkv_ref, d_out, out_ref):
    allowed = same_clip()
    halves = half_lanes()
    for p in range(3):
        spans = [slice(part * HALF_D + 128 * p, part * HALF_D + 128 * (p + 1)) for part in range(3)]
        q, k, v = (qkv_ref[:, span] for span in spans)
        d_pair = d_out[:, 128 * p : 128 * (p + 1)]
        found = []
        for h in range(2):
            one = jnp.where(halves[h], q, jnp.zeros_like(q))
            weights, total = encoder_scores(one, k, allowed)
            soft = weights / total
            d_one = jnp.where(halves[h], d_pair, jnp.zeros_like(d_pair))
            d_soft = times_trans(d_one, v)
            delta = jnp.sum(soft * d_soft, axis=-1, keepdims=True)
            d_scores = low(soft * (d_soft - delta))
            found.append(
                (
                    times_plain(d_scores, k) * SCALE,
                    trans_times(d_scores, q) * SCALE,
                    trans_times(low(soft), d_pair),
                )
            )
        for part in range(3):
            out_ref[:, spans[part]] = low(jnp.where(halves[0], found[0][part], found[1][part]))


def encoder_back_body(wide, *refs):
    f32 = jnp.float32
    gfeat_ref, x_in, qkv_in, o_in, h_ref, slope_ref, px_in, gain_ref, w_ref = refs[:9]
    refs = refs[9:]
    if wide:
        one_ref, two_ref, loss_ref, dvec_ref = refs[:4]
        refs = refs[4:]
    genc_ref, gemb_ref, gvec_ref = refs[:3]
    refs = refs[3:]
    if wide:
        gdec_ref, total_ref = refs[:2]
        refs = refs[2:]
    wa_s, wb_s, du_s, dqkv_s, feat_s, sent_s, got_s, h_s, slope_s = refs[:9]
    x_ref, qkv_ref, o_ref, px_ref, in_sem = refs[9:14]
    load_sem, f_ss, f_rs, y_ss, y_rs = refs[14:19]
    refs = refs[19:]
    arriving = [
        pltpu.make_async_copy(src, dst, in_sem.at[i])
        for i, (src, dst) in enumerate(
            ((x_in, x_ref), (qkv_in, qkv_ref), (o_in, o_ref), (px_in, px_ref))
        )
    ]
    arriving[0].start()
    place = Place()
    greet(place.mates(wide) + (place.cube()[2:3] + place.cube()[4:] if wide else []))
    swap = Swap(place, sent_s, got_s, y_ss, y_rs)
    swapped = remote(gfeat_ref, feat_s, f_ss, f_rs, place.row_mate())
    swapped.start()

    def into(name):
        if name == "emb":
            return gemb_ref
        start, width = {"at": (0, A_COLS), "up": (UP_AT, HID), "dn": (DN_AT, HID)}[name[:2]]
        return genc_ref.at[int(name[2]), :, pl.ds(start, width)]

    scatter = Scatter(place, refs[:9], refs[9:15], into) if wide else None
    dec = DecoderScatter(place, one_ref, two_ref, gdec_ref, refs[15:28], refs[28:40]) if wide else None
    everyone = Everyone(place, refs[40:44], refs[44:48]) if wide else None

    def load(layer, part):
        src, dst = (
            (w_ref.at[layer, :, pl.ds(0, A_COLS)], wa_s),
            (w_ref.at[layer, :, pl.ds(A_COLS, 2 * HID)], wb_s),
            (h_ref.at[layer], h_s),
            (slope_ref.at[layer], slope_s),
        )[part]
        return pltpu.make_async_copy(src, dst, load_sem.at[layer, part])

    load(1, 2).start()
    load(1, 3).start()
    load(1, 1).start()
    load(1, 0).start()
    for copy in arriving[1:]:
        copy.start()

    lefts = {}

    def factor(slot, left):
        lefts[slot] = left
        if wide:
            scatter.turn(slot, left)

    def emit(name, items):
        if wide:
            scatter.cores(name, items)
            return
        for slot, right, shift, width in items:
            value = low(trans_times(lefts[slot], right[...]))
            if name == "emb":
                gemb_ref[...] = value
                continue
            start = {"at": 0, "up": UP_AT, "dn": DN_AT}[name[:2]] + shift
            genc_ref[int(name[2]), :, start : start + width] = value

    def later(step, *args):
        if wide:
            getattr(scatter, step)(*args)

    def dec_step(step):
        if wide:
            getattr(dec, step)()

    dec_step("begin")
    swapped.wait_recv()
    dec_step("over_x")
    near, far = gfeat_ref[...].astype(f32), feat_s[...].astype(f32)
    first = place.row == 0
    grad = jnp.concatenate([jnp.where(first, near, far), jnp.where(first, far, near)], axis=0)
    gvec_ref[...] = jnp.zeros(gvec_ref.shape, f32)

    def note(row, grad_out, scaled):
        gvec_ref[row : row + 1, :] = column_sum(grad_out * scaled)
        gvec_ref[row + 1 : row + 2, :] = column_sum(grad_out)

    arriving[0].wait()
    scaled, inv = norm_rows(x_ref[2 * LAYERS])
    note(4 * LAYERS, grad, scaled)
    d_x = norm_rows_back(grad, scaled, inv, gain_ref[4 * LAYERS : 4 * LAYERS + 1, :])
    for layer in (1, 0):
        gains = gain_ref[4 * layer : 4 * layer + 4, :]
        dn, up, at = (f"{kind}{layer}" for kind in ("dn", "up", "at"))
        scaled2, inv2 = norm_rows(x_ref[2 * layer + 1])
        n2 = low(scaled2 * gains[2:3] + gains[3:4])
        d_low = low(d_x)
        factor(0, d_low)
        dn_items = [(0, h_s, 0, HID)]
        load(layer, 2).wait()
        emit(dn, dn_items)
        load(layer, 3).wait()
        load(layer, 1).wait()
        d_hidden = times_plain(d_low, wb_s[:, HID : 2 * HID])
        du_s[...] = low(d_hidden * slope_s[...])
        swap.start(2 * layer + 1, times_trans(du_s[...], wb_s[:, 0:HID]))
        later("over_x", dn, dn_items)
        factor(1, n2)
        up_items = [(1, du_s, 0, HID)]
        emit(up, up_items)
        later("over_x", up, up_items)
        if layer == 1:
            load(0, 2).start()
            load(0, 3).start()
            load(0, 1).start()
            if wide:
                dec.line_two.relay()
        else:
            later("along_z", "at1")
            later("relay", "up1")
        d_n2 = swap.total(2 * layer + 1)
        note(4 * layer + 2, d_n2, scaled2)
        d_x = d_x + norm_rows_back(d_n2, scaled2, inv2, gains[2:3])
        d_low = low(d_x)
        factor(2, d_low)
        load(layer, 0).wait()
        if layer == 1:
            for copy in arriving[1:]:
                copy.wait()
        d_att = low(times_plain(d_low, wa_s[:, QKV_W:A_COLS]))
        encoder_attention_back(qkv_ref.at[layer], d_att, dqkv_s)
        swap.start(2 * layer, times_trans(dqkv_s[...], wa_s[:, 0:QKV_W]))
        scaled1, inv1 = norm_rows(x_ref[2 * layer])
        factor(3, low(scaled1 * gains[0:1] + gains[1:2]))
        at_items = [(3, dqkv_s, 0, QKV_W), (2, o_ref.at[layer], QKV_W, HALF_D)]
        emit(at, at_items)
        if layer == 1:
            load(0, 0).start()
            dec_step("along_z")
        else:
            later("relay", "at1")
        later("along_z", dn)
        later("over_x", at, at_items)
        later("along_z", up)
        later("relay", dn)
        if layer == 1:
            if wide:
                dec.line_one.relay()
        d_n1 = swap.total(2 * layer)
        note(4 * layer, d_n1, scaled1)
        d_x = d_x + norm_rows_back(d_n1, scaled1, inv1, gains[0:1])
    factor(0, low(d_x))
    emb_items = [(0, px_ref, 0, D)]
    emit("emb", emb_items)
    later("relay", "up0")
    later("over_x", "emb", emb_items)
    if wide:
        lane = lane_ids((1, DD))
        dvec = jnp.where(row_ids((8, 1)) < 7, dvec_ref[...], 0.0)
        loss = jnp.where(lane == 0, loss_ref[0:1, 0:1], 0.0)
        dvec = dvec + jnp.where(row_ids((8, 1)) == 7, loss, 0.0)
        everyone.first(0.5 * gvec_ref[...], dvec)
        dec.over_rows()
        everyone.stage(1)
        scatter.along_z("at0")
        everyone.stage(2)
        dec.to_cores()
        scatter.along_z("emb")
        everyone.stage(3)
        scatter.relay("at0")
        dec.finish()
        scatter.relay("emb")
        everyone.stage(4)
        square = jnp.zeros((1, 1), f32)
        for name, _ in SUMS:
            scatter.finish(name)
            whole = into(name)[...]
            square = square + jnp.sum(whole * whole)
        square = square + jnp.sum(gdec_ref[...] * gdec_ref[...])
        square = everyone.number(square)
        total_ref[...] = everyone.total()
        total_ref[23:24, 0:128] += jnp.where(lane_ids((1, 128)) == 1, square, 0.0)
        scatter.drain()
        dec.drain()
        everyone.drain()
    swapped.wait_send()
    swap.drain()


def run_encoder_back(wide, *operands):
    bf, f32 = jnp.bfloat16, jnp.float32
    vmem = pl.BlockSpec(memory_space=pltpu.VMEM)
    dma = pltpu.SemaphoreType.DMA
    shape = jax.ShapeDtypeStruct
    rows, kind = (SHARD, f32) if wide else (D, bf)
    scratch = [
        pltpu.VMEM((D, A_COLS), bf),
        pltpu.VMEM((D, 2 * HID), bf),
        pltpu.VMEM((PAIR, HID), bf),
        pltpu.VMEM((PAIR, QKV_W), bf),
        pltpu.VMEM((128, D), bf),
        pltpu.VMEM((2, PAIR, D), bf),
        pltpu.VMEM((2 * LAYERS, PAIR, D), bf),
        pltpu.VMEM((PAIR, HID), bf),
        pltpu.VMEM((PAIR, HID), f32),
        pltpu.VMEM((2 * LAYERS + 1, PAIR, D), f32),
        pltpu.VMEM((LAYERS, PAIR, QKV_W), bf),
        pltpu.VMEM((LAYERS, PAIR, HALF_D), bf),
        pltpu.VMEM((PAIR, D), bf),
        dma((4,)),
        dma((LAYERS, 4)),
        dma,
        dma,
        dma((2 * LAYERS,)),
        dma((2 * LAYERS,)),
    ]
    outs = [
        shape((LAYERS, rows, ENC_COLS), kind),
        shape((rows, D), kind),
        shape((16, D), f32),
    ]
    anywhere = pl.BlockSpec(memory_space=pl.ANY)
    in_specs = [vmem] + [anywhere] * 6 + [vmem, anywhere]
    if wide:
        outs += [shape((SHARD // 2, PART_ONE + PART_TWO), f32), shape((24, D), f32)]
        in_specs += [vmem] * 4
        n = len(SUMS)
        both = ONE_HALF + TWO_HALF
        scratch += [
            pltpu.VMEM((4, D, PAIR), bf),
            pltpu.VMEM((2, D, PAIR), bf),
            pltpu.VMEM((2, BLOCKS, HID), bf),
            pltpu.VMEM((BLOCKS, SUM_COLS), bf),
            pltpu.VMEM((3, QUARTER, HID), bf),
            pltpu.VMEM((QUARTER, SUM_COLS), bf),
            pltpu.VMEM((3, SHARD, SUM_COLS), bf),
            pltpu.VMEM((4, SHARD, SUM_COLS), bf),
            pltpu.VMEM((4, QUARTER, HID), f32),
            dma((n,)),
            dma((n,)),
            dma((n,)),
            dma((n,)),
            dma((n, 4)),
            dma((n, 4)),
            pltpu.VMEM((2, DD, ONE_HALF), bf),
            pltpu.VMEM((4, 2, SHARD, ONE_HALF), bf),
            pltpu.VMEM((4, 2, SHARD, ONE_HALF), bf),
            pltpu.VMEM((8 * SHARD, ONE_HALF), f32),
            pltpu.VMEM((3, 2 * SHARD, ONE_HALF), bf),
            pltpu.VMEM((4, 2 * SHARD, ONE_HALF), bf),
            pltpu.VMEM((3, 2 * SHARD, TWO_HALF), bf),
            pltpu.VMEM((4, 2 * SHARD, TWO_HALF), bf),
            pltpu.VMEM((2 * SHARD, both), f32),
            pltpu.VMEM((SHARD, both), bf),
            pltpu.VMEM((SHARD, both), bf),
            pltpu.VMEM((SHARD, both), f32),
            pltpu.VMEM((SHARD // 2, both), f32),
            dma,
            dma,
            dma,
            dma,
            dma((4,)),
            dma((4,)),
            dma((4,)),
            dma((4,)),
            dma,
            dma,
            dma,
            dma,
            pltpu.VMEM((5, 24, D), f32),
            pltpu.VMEM((6, 24, D), f32),
            pltpu.VMEM((2, 8, 128), f32),
            pltpu.VMEM((10, 8, 128), f32),
            dma((6,)),
            dma((6,)),
            dma((10,)),
            dma((10,)),
        ]
    return pl.pallas_call(
        functools.partial(encoder_back_body, wide),
        out_shape=tuple(outs),
        in_specs=in_specs,
        out_specs=(vmem,) * len(outs),
        scratch_shapes=scratch,
        compiler_params=pltpu.CompilerParams(
            collective_id=2, has_side_effects=True, vmem_limit_bytes=63 * MIB
        ),
        cost_estimate=pl.CostEstimate(
            flops=20 * 10**9, bytes_accessed=60 * 10**6, transcendentals=10**6
        ),
        name="encoder_back",
    )(*operands)


def adam_at(refs, spot, grad, decay_rate, step_rate):
    master, first, second, master_out, first_out, second_out = refs
    new = adam_update(master[spot], first[spot], second[spot], grad, decay_rate, step_rate)
    master_out[spot], first_out[spot], second_out[spot] = new


def head_pieces(rows, heads):
    pieces = []
    for h in range(heads):
        for part in range(3):
            at = (part * heads + h) * HEAD
            pieces.append(rows[:, at : at + HEAD])
    pieces.append(rows[:, 3 * heads * HEAD :])
    return jnp.concatenate(pieces, axis=-1)


def update_body(*refs):
    f32 = jnp.float32
    total_ref = refs[0]
    grads = refs[1:4]
    states = [refs[4 + 3 * i : 7 + 3 * i] for i in range(5)]
    loss_ref, norm_ref = refs[19:21]
    outs = [refs[21 + 3 * i : 24 + 3 * i] for i in range(5)]
    total = total_ref[...]
    squares = jnp.sum(total[0:23, :] * total[0:23, :]) + jnp.sum(total[23:24, 1:2])
    norm = jnp.sqrt(jnp.zeros((1, 1), f32) + squares)
    factor = jnp.minimum(1.0, CLIP_MAX / (norm + 1e-06))
    step = pl.program_id(0)
    rows = grads[0].shape[1]

    @pl.loop(0, rows // 8)
    def _(i):
        spot = pl.ds(pl.multiple_of(i * 8, 8), 8)
        grad = head_pieces(grads[0][0, spot, :], HEADS // 2)
        adam_at(states[0] + outs[0], (0, 0, spot, slice(None)), grad * factor, DECAY, RATE)

    @pl.when(step == 0)
    def _():
        loss_ref[0, 0] = jnp.sum(total[23:24, 0:1])
        norm_ref[0, 0] = jnp.sum(norm)
        adam_at(states[1] + outs[1], (0,), grads[1][...] * factor, DECAY, RATE)

    @pl.when(step == 1)
    def _():
        both = ONE_HALF + TWO_HALF
        grad = grads[2][...]
        one = jnp.concatenate([grad[:, 0:ONE_HALF], grad[:, both : both + ONE_HALF]], axis=-1)
        two = jnp.concatenate([grad[:, ONE_HALF:both], grad[:, both + ONE_HALF :]], axis=-1)
        pieces = [one[:, 0:ED_AT], two[:, 0:192], two[:, UP_TWO:], one[:, ED_AT : ED_AT + DD]]
        grad = head_pieces(jnp.concatenate(pieces, axis=-1), DHEADS // 2)
        adam_at(states[2] + outs[2], (0,), grad * factor, DECAY, RATE)

    @pl.when(step == 2)
    def _():
        place = Place()
        own = shard_at(place.z, place.x, place.col)
        for kind, top, count, width in ((3, 0, 10, D), (4, 16, 7, DD)):
            share = width // N_SHARDS
            turned = pltpu.roll(total, (D - own * share) % D, 1)
            grad = turned[top : top + count, 0:share] * factor
            adam_at(states[kind] + outs[kind], (slice(None), slice(None)), grad, 0.0, VEC_RATE)


def run_update(total, grads, states):
    f32 = jnp.float32
    smem = pl.BlockSpec(memory_space=pltpu.SMEM)
    flat = [a for triple in states for a in triple]
    scalar = jax.ShapeDtypeStruct((1, 1), f32)
    outs = (scalar, scalar) + tuple(jax.ShapeDtypeStruct(a.shape, f32) for a in flat)
    rows = SHARD // 2

    def whole(array):
        return pl.BlockSpec(array.shape, lambda i: (0,) * array.ndim)

    enc = pl.BlockSpec((1, 1, rows, ENC_COLS), lambda i: (i // 2, 0, i % 2, 0))
    enc_grad = pl.BlockSpec((1, rows, ENC_COLS), lambda i: (i // 2, i % 2, 0))
    state_specs = [enc] * 3 + [whole(a) for a in flat[3:]]
    return pl.pallas_call(
        update_body,
        grid=(2 * LAYERS,),
        out_shape=outs,
        in_specs=[whole(total), enc_grad, whole(grads[1]), whole(grads[2])] + state_specs,
        out_specs=tuple([smem, smem] + state_specs),
        compiler_params=pltpu.CompilerParams(vmem_limit_bytes=60 * MIB),
        name="update",
    )(total, *grads, *flat)


def head_order(matrix, heads, width):
    lead = matrix.shape[:-1]
    cut = matrix[..., :width].reshape(lead + (heads, 3, HEAD))
    cut = jnp.swapaxes(cut, -3, -2).reshape(lead + (width,))
    return jnp.concatenate([cut, matrix[..., width:]], axis=-1)


def head_order_back(matrix, heads, width):
    lead = matrix.shape[:-1]
    cut = matrix[..., :width].reshape(lead + (3, heads, HEAD))
    cut = jnp.swapaxes(cut, -3, -2).reshape(lead + (width,))
    return jnp.concatenate([cut, matrix[..., width:]], axis=-1)


def sine_table(length, width):
    column = np.arange(width)
    freq = np.exp(-math.log(10000.0) * (2.0 * (column // 2)) / width)
    angle = np.arange(length)[:, None] * freq
    table = np.where(column % 2 == 0, np.sin(angle), np.cos(angle))
    return np.pad(table, ((0, ROWS - length), (0, 0))).astype(np.float32)


def frequency_rows(width):
    column = np.arange(width)
    freq = np.exp(-math.log(10000.0) * (2.0 * (column // 2)) / width)
    return np.broadcast_to(freq.astype(np.float32), (8, width))


def split_parts(matrices):
    gap = [(0, 0)] * (matrices.ndim - 1)
    one = jnp.concatenate([matrices[..., :ED_AT], matrices[..., 3072:]], axis=-1)
    one = jnp.pad(one, gap + [(0, PART_ONE - one.shape[-1])])
    out = jnp.pad(matrices[..., ED_AT:768], gap + [(0, UP_TWO - 192)])
    return one, jnp.concatenate([out, matrices[..., 768:3072]], axis=-1)


def join_parts(one, two):
    return jnp.concatenate(
        [one[..., :ED_AT], two[..., :192], two[..., UP_TWO:], one[..., ED_AT : ED_AT + DD]], axis=-1
    )


def gather_vectors(enc_vec, dec_vec, group):
    vectors = jnp.concatenate([enc_vec.reshape(-1), dec_vec.reshape(-1)])
    vectors = lax.all_gather(low(vectors), group, axis=0, tiled=False).astype(jnp.float32)
    cut = enc_vec.size
    enc_gains = jnp.swapaxes(vectors[:, :cut].reshape(-1, *enc_vec.shape), 0, 1).reshape(-1, D)
    dec_gains = jnp.swapaxes(vectors[:, cut:].reshape(-1, *dec_vec.shape), 0, 1).reshape(-1, DD)
    return (
        jnp.pad(enc_gains, ((0, 16 - enc_gains.shape[0]), (0, 0))),
        jnp.pad(dec_gains, ((0, 8 - dec_gains.shape[0]), (0, 0))),
    )


def update_plain(loss_part, dec_vec_grads, enc_vec_grads, grads, states):
    everyone = ("row", "clip", "col")
    n_enc, n_dec = states[3][0].shape[0], states[4][0].shape[0]
    enc_vec_total, dec_vec_total, loss_total, square = lax.psum(
        (
            0.5 * enc_vec_grads[:n_enc],
            dec_vec_grads[:n_dec],
            loss_part,
            sum(jnp.sum(g * g) for g in grads),
        ),
        everyone,
    )
    square = square + jnp.sum(enc_vec_total**2) + jnp.sum(dec_vec_total**2)
    grad_norm = jnp.sqrt(square)
    factor = jnp.minimum(1.0, CLIP_MAX / (grad_norm + 1e-06))
    shard = lax.axis_index("clip") * lax.axis_size("col") + lax.axis_index("col")
    own = []
    for total, state in ((enc_vec_total, states[3][0]), (dec_vec_total, states[4][0])):
        width = state.shape[1]
        own.append(lax.dynamic_slice_in_dim(total, shard * width, width, 1))
    decays = (DECAY, DECAY, DECAY, 0.0, 0.0)
    rates = (RATE, RATE, RATE, VEC_RATE, VEC_RATE)
    results = []
    for triple, grad, decay_rate, step_rate in zip(states, (*grads, *own), decays, rates):
        grad = grad.reshape(triple[0].shape)
        results.extend(adam_update(*triple, grad * factor, decay_rate, step_rate))
    return (loss_total, grad_norm, *results)


def local(
    patches,
    visible,
    masked,
    enc_layers,
    enc_first,
    enc_second,
    embed,
    embed_first,
    embed_second,
    dec_mats,
    dec_first,
    dec_second,
    enc_vec,
    enc_vec_first,
    enc_vec_second,
    dec_vec,
    dec_vec_first,
    dec_vec_second,
):
    f32 = jnp.float32
    group = ("clip", "col")
    everyone = ("row", "clip", "col")
    wide = lax.axis_size("clip") == 8 and lax.axis_size("col") == 2
    freq = jnp.asarray(frequency_rows(D))
    table = jnp.asarray(sine_table(TUBES, DD))
    if wide:
        feat, xs, qkv, att, hid, slope, px, padded, enc_gains, dec_gains, enc_full, one, two = (
            run_encoder(True, visible, patches, freq, embed, enc_layers, dec_mats, enc_vec, dec_vec)
        )
    else:
        embed_full = lax.all_gather(low(embed[0]), group, axis=0, tiled=True)
        enc_here = low(head_order(enc_layers[:, 0], HEADS // 2, QKV_W))
        enc_full = lax.all_gather(enc_here, group, axis=1, tiled=True)
        dec_here = low(head_order(dec_mats[0], DHEADS // 2, ED_AT))
        dec_full = lax.all_gather(dec_here, everyone, axis=0, tiled=True).reshape(2, DD, -1)
        enc_gains, dec_gains = gather_vectors(enc_vec, dec_vec, group)
        feat, xs, qkv, att, hid, slope, px, padded = run_encoder(
            False, visible, patches, freq, embed_full, enc_full, enc_gains
        )
        one, two = split_parts(dec_full)
    loss_block, grad_one, grad_two, dec_vec_grads, grad_feat = run_decoder(
        wide, visible, feat, padded, table, one, two, dec_gains
    )
    kept = (grad_feat, xs, qkv, att, hid, slope, px, enc_gains, enc_full)
    states = (
        (enc_layers, enc_first, enc_second),
        (embed, embed_first, embed_second),
        (dec_mats, dec_first, dec_second),
        (enc_vec, enc_vec_first, enc_vec_second),
        (dec_vec, dec_vec_first, dec_vec_second),
    )
    if wide:
        enc_total, embed_total, _, dec_total, total = run_encoder_back(
            True, *kept, grad_one, grad_two, loss_block, dec_vec_grads
        )
        grads = (enc_total, embed_total, dec_total)
        loss_total, grad_norm, *results = run_update(total, grads, states)
        return (loss_total[0, 0], grad_norm[0, 0], *results)
    dec_grads = join_parts(grad_one, grad_two)
    dec_total = lax.psum_scatter(
        dec_grads.reshape(-1, dec_grads.shape[-1]).astype(f32),
        everyone,
        scatter_dimension=0,
        tiled=True,
    )
    enc_total, embed_total, enc_vec_grads = run_encoder_back(False, *kept)
    enc_total = lax.psum_scatter(enc_total.astype(f32), group, scatter_dimension=1, tiled=True)
    embed_total = lax.psum_scatter(embed_total.astype(f32), group, scatter_dimension=0, tiled=True)
    grads = (
        head_order_back(enc_total, HEADS // 2, QKV_W),
        embed_total,
        head_order_back(dec_total, DHEADS // 2, ED_AT),
    )
    return update_plain(loss_block[0, 0], dec_vec_grads, enc_vec_grads, grads, states)


def solution(mesh):
    in_specs = (
        P(None, ("clip", "col"), None, "row"),
        P(None, ("clip", "col"), None),
        P(None, ("clip", "col"), None),
        P(None, "row", ("clip", "col"), None),
        P(None, "row", ("clip", "col"), None),
        P(None, "row", ("clip", "col"), None),
        P("row", ("clip", "col"), None),
        P("row", ("clip", "col"), None),
        P("row", ("clip", "col"), None),
        P("row", ("clip", "col"), None),
        P("row", ("clip", "col"), None),
        P("row", ("clip", "col"), None),
        P(None, ("clip", "col")),
        P(None, ("clip", "col")),
        P(None, ("clip", "col")),
        P(None, ("clip", "col")),
        P(None, ("clip", "col")),
        P(None, ("clip", "col")),
    )
    out_specs = (
        P(),
        P(),
        P(None, "row", ("clip", "col"), None),
        P(None, "row", ("clip", "col"), None),
        P(None, "row", ("clip", "col"), None),
        P("row", ("clip", "col"), None),
        P("row", ("clip", "col"), None),
        P("row", ("clip", "col"), None),
        P("row", ("clip", "col"), None),
        P("row", ("clip", "col"), None),
        P("row", ("clip", "col"), None),
        P(None, ("clip", "col")),
        P(None, ("clip", "col")),
        P(None, ("clip", "col")),
        P(None, ("clip", "col")),
        P(None, ("clip", "col")),
        P(None, ("clip", "col")),
    )
    return jax.shard_map(local, mesh=mesh, in_specs=in_specs, out_specs=out_specs, check_vma=False)
```

```python
import functools
import math

import jax
import jax.numpy as jnp
import numpy as np
from jax import lax
from jax.experimental import pallas as pl
from jax.experimental.pallas import tpu as pltpu
from jax.sharding import PartitionSpec as P

D = 768
HEADS = 12
HEAD = 64
FF = 3072
DD = 384
DHEADS = 6
DFF = 1536
PIX = 1536
TUBES = 1176
VIS = 118
LAYERS = 2
MICRO = 2
STEP = 10
MASKED = 1058


EPS_NORM = 1e-06
CLIP_MAX = 1.0
BETA_ONE = 0.9
BETA_TWO = 0.999
RATE = 0.06
VEC_RATE = 0.2
DECAY = 0.05
EPS_ADAM = 1e-08


def times_plain(left, right):
    return jnp.dot(left, right, preferred_element_type=jnp.float32)


def times_trans(left, right):
    return lax.dot_general(
        left, right, (((1,), (1,)), ((), ())), preferred_element_type=jnp.float32
    )


def trans_times(left, right):
    return lax.dot_general(
        left, right, (((0,), (0,)), ((), ())), preferred_element_type=jnp.float32
    )


def gelu_pair(values):
    cumul = 0.5 * (1.0 + lax.erf(values * 0.7071067811865476))
    density = jnp.exp(-0.5 * values * values) * 0.3989422804014327
    return (values * cumul, cumul + values * density)


def adam_update(master, first, second, grad_clip, decay_rate, step_rate):
    first_new = BETA_ONE * first + (1.0 - BETA_ONE) * grad_clip
    second_new = BETA_TWO * second + (1.0 - BETA_TWO) * grad_clip * grad_clip
    first_hat = first_new / (1.0 - BETA_ONE**STEP)
    second_hat = second_new / (1.0 - BETA_TWO**STEP)
    master_new = master - step_rate * (
        first_hat / (jnp.sqrt(second_hat) + EPS_ADAM) + decay_rate * master
    )
    return (master_new, first_new, second_new)


LOG2E = 1.4426950408889634
SCALE = HEAD ** (-0.5)
MIB = 1 << 20
MESH_IDS = pl.DeviceIdType.MESH
N_SHARDS = 16
SHARD = D // N_SHARDS
PART_ONE = 1024
PART_TWO = 2560
ONE_HALF, TWO_HALF = PART_ONE // 2, PART_TWO // 2
ED_AT = 3 * DD // 2
UP_TWO, DN_TWO, HD_TWO = 256, 1024, 1792


def low(values):
    return values.astype(jnp.bfloat16)


def lane_ids(shape):
    return lax.broadcasted_iota(jnp.int32, shape, len(shape) - 1)


def row_ids(shape):
    return lax.broadcasted_iota(jnp.int32, shape, 0)


def remote(src, dst, send_sem, recv_sem, device):
    return pltpu.make_async_remote_copy(
        src_ref=src,
        dst_ref=dst,
        send_sem=send_sem,
        recv_sem=recv_sem,
        device_id=device,
        device_id_type=MESH_IDS,
    )


class Place:
    def __init__(self):
        self.clip = lax.axis_index("clip")
        self.row = lax.axis_index("row")
        self.col = lax.axis_index("col")
        self.z = self.clip // 2
        self.x = self.clip % 2

    def z_mate(self, step):
        return (((self.z + step) % 4) * 2 + self.x, self.row, self.col)

    def x_mate(self):
        return (self.z * 2 + 1 - self.x, self.row, self.col)

    def core_mate(self):
        return (self.clip, self.row, 1 - self.col)

    def row_mate(self):
        return (self.clip, 1 - self.row, self.col)

    def mates(self, wide):
        near = [self.row_mate()]
        if wide:
            near += [self.core_mate(), self.x_mate()] + [self.z_mate(s) for s in (1, 2, 3)]
        return near

    def cube(self):
        found = []
        for i in range(1, 8):
            x = 1 - self.x if i & 1 else self.x
            row = 1 - self.row if i & 2 else self.row
            col = 1 - self.col if i & 4 else self.col
            found.append((self.z * 2 + x, row, col))
        return found


def shard_at(z, x, col):
    return (z * 2 + x) * 2 + col


def greet(mates):
    barrier = pltpu.get_barrier_semaphore()
    for mate in mates:
        pl.semaphore_signal(barrier, inc=1, device_id=mate, device_id_type=MESH_IDS)
    pl.semaphore_wait(barrier, len(mates))


class Mail:
    def __init__(self):
        self.sent = []

    def go(self, src, dst, ss, rs, device, only=None):
        copy = remote(src, dst, ss, rs, device)
        if only is None:
            copy.start()
        else:
            pl.when(only)(copy.start)
        self.sent.append((copy, only))

    def came(self, dst, ss, rs, device):
        remote(dst, dst, ss, rs, device).wait_recv()

    def drain(self):
        for copy, only in self.sent:
            if only is None:
                copy.wait_send()
            else:
                pl.when(only)(copy.wait_send)
        self.sent = []


class Gather(Mail):
    def __init__(self, place, own, spot, sems, over_x_first=None):
        super().__init__()
        self.at, self.own, self.spot, self.turned = place, own, spot, over_x_first
        self.z_ss, self.z_rs, self.x_ss, self.x_rs, self.c_ss, self.c_rs = sems

    def line(self, k, src, dst):
        for s, only in ((2, None), (1, self.at.z != 3), (3, self.at.z != 0)):
            ss, rs = self.z_ss.at[k, s - 1], self.z_rs.at[k, s - 1]
            self.go(src, dst, ss, rs, self.at.z_mate(s), only)

    def landed(self, k, s, spot):
        at = self.at
        self.came(spot, self.z_ss.at[k, s - 1], self.z_rs.at[k, s - 1], at.z_mate(s))
        if s == 2:
            for step, only in ((3, at.z == 1), (1, at.z == 2)):
                slot = (2 + step) % 4 - 1
                ss, rs = self.z_ss.at[k, 3], self.z_rs.at[k, slot]
                self.go(spot, spot, ss, rs, at.z_mate(step), only)

    def to_core(self, k, slot, spot):
        self.go(spot, spot, self.c_ss.at[k, slot], self.c_rs.at[k, slot], self.at.core_mate())

    def begin(self, k):
        at = self.at
        src, dst = self.own(k), self.spot(k, at.z, at.x, at.col)
        if k == self.turned:
            self.go(src, dst, self.x_ss.at[k, 0], self.x_rs.at[k, 0], at.x_mate())
        self.line(k, src, dst)
        if k != self.turned:
            self.go(src, dst, self.x_ss.at[k, 0], self.x_rs.at[k, 0], at.x_mate())
        self.go(src, dst, self.c_ss.at[k, 0], self.c_rs.at[k, 0], at.core_mate())

    def begin_lined(self, blocks):
        at = self.at
        for s in (0, 2, 1, 3):
            z = (at.z - s) % 4
            spot = self.spot(0, z, at.x, at.col)
            self.go(blocks.at[z], spot, self.x_ss.at[0, s], self.x_rs.at[0, s], at.x_mate())
            self.go(blocks.at[z], spot, self.c_ss.at[0, s], self.c_rs.at[0, s], at.core_mate())

    def begin_turned(self, extra):
        at, k = self.at, self.turned
        spot = self.spot(k, at.z, 1 - at.x, at.col)
        self.came(spot, self.x_ss.at[k, 0], self.x_rs.at[k, 0], at.x_mate())
        self.line(extra, spot, spot)
        self.to_core(k, 4, spot)

    def forward_turned(self, extra):
        at, k = self.at, self.turned
        for s in (2, 1, 3):
            for line, x, slot in ((k, at.x, s), (extra, 1 - at.x, 4 + s)):
                spot = self.spot(k, (at.z - s) % 4, x, at.col)
                self.landed(line, s, spot)
                self.to_core(k, slot, spot)

    def forward(self, k):
        for s in (2, 1, 3):
            self.one("forward", s, k)

    def across(self, k):
        for s in (0, 2, 1, 3):
            self.one("across", s, k)

    def one(self, step, s, k=0):
        at = self.at
        if step == "across":
            spot = self.spot(k, (at.z - s) % 4, 1 - at.x, at.col)
            self.came(spot, self.x_ss.at[k, s], self.x_rs.at[k, s], at.x_mate())
            self.to_core(k, 4 + s, spot)
            return
        spot = self.spot(k, (at.z - s) % 4, at.x, at.col)
        self.landed(k, s, spot)
        self.go(spot, spot, self.x_ss.at[k, s], self.x_rs.at[k, s], at.x_mate())
        self.to_core(k, s, spot)

    def finish(self, k):
        at = self.at
        for s in range(8):
            x = at.x if s < 4 else 1 - at.x
            spot = self.spot(k, (at.z - s % 4) % 4, x, 1 - at.col)
            self.came(spot, self.c_ss.at[k, s], self.c_rs.at[k, s], at.core_mate())


class LineSum(Mail):
    def __init__(self, place, own, sent, got, ss, rs, rows, into):
        super().__init__()
        self.at, self.own, self.out, self.got, self.ss, self.rs = place, own, sent, got, ss, rs
        self.rows, self.into = rows, into
        self.middle = jnp.logical_or(place.z == 1, place.z == 2)

    def block(self, s):
        return self.own[self.rows * s : self.rows * (s + 1), :]

    def begin(self):
        at = self.at
        self.into[...] = self.block(0)
        for s, end, step in ((1, 3, 3), (3, 0, 1)):
            self.out[s - 1] = low(self.block(s))
            src = self.out.at[s - 1]
            dst = self.got.at[s - 1]
            inner = at.z != end
            self.go(src, dst, self.ss.at[s - 1], self.rs.at[s - 1], at.z_mate(s), inner)
            other = self.got.at[3]
            self.go(src, other, self.ss.at[3], self.rs.at[3], at.z_mate(step), at.z == end)
        outer = jnp.logical_not(self.middle)

        @pl.when(outer)
        def _():
            self.out[1] = low(self.block(2))

        self.go(
            self.out.at[1], self.got.at[1], self.ss.at[1], self.rs.at[1], at.z_mate(2), outer
        )

    def relay(self):
        at = self.at

        @pl.when(self.middle)
        def _():
            self.came(self.got.at[3], self.ss.at[3], self.rs.at[3], at.z_mate(1))
            self.out[1] = low(self.block(2) + self.got[3].astype(jnp.float32))

        self.go(
            self.out.at[1], self.got.at[1], self.ss.at[1], self.rs.at[1], at.z_mate(2), self.middle
        )

    def finish(self):
        at = self.at

        def add(s):
            self.came(self.got.at[s - 1], self.ss.at[s - 1], self.rs.at[s - 1], at.z_mate(s))
            self.into[...] += self.got[s - 1].astype(jnp.float32)

        add(2)
        pl.when(at.z != 0)(lambda: add(1))
        pl.when(at.z != 3)(lambda: add(3))


class Swap:
    def __init__(self, place, sent, got, send_sems, recv_sems):
        self.at, self.sent, self.got = place, sent, got
        self.ss, self.rs = send_sems, recv_sems
        self.copies = {}

    def start(self, i, value):
        slot = i % self.sent.shape[0]
        for j in [j for j in self.copies if j % self.sent.shape[0] == slot]:
            self.copies.pop(j).wait_send()
        self.sent[slot] = low(value)
        copy = remote(
            self.sent.at[slot], self.got.at[i], self.ss.at[i], self.rs.at[i], self.at.row_mate()
        )
        copy.start()
        self.copies[i] = copy

    def total(self, i):
        self.copies[i].wait_recv()
        sent = self.sent[i % self.sent.shape[0]]
        return sent.astype(jnp.float32) + self.got[i].astype(jnp.float32)

    def drain(self):
        for copy in self.copies.values():
            copy.wait_send()


ROWS = 1216
LANES = 1280
STEP_ROWS = 608
N_STEPS = ROWS // STEP_ROWS
KEY_ROWS = 640


def norm_rows(rows):
    average = jnp.mean(rows, axis=-1, keepdims=True)
    centred = rows - average
    inv_dev = lax.rsqrt(jnp.mean(centred * centred, axis=-1, keepdims=True) + EPS_NORM)
    return centred * inv_dev, inv_dev


def norm_rows_back(grad_out, scaled, inv_dev, gain_row):
    inner = grad_out * gain_row
    return inv_dev * (
        inner
        - jnp.mean(inner, axis=-1, keepdims=True)
        - scaled * jnp.mean(inner * scaled, axis=-1, keepdims=True)
    )


def column_sum(values):
    return jnp.sum(values, axis=0, keepdims=True)


def decoder_body(wide, *refs):
    bf, f32 = jnp.bfloat16, jnp.float32
    seen_ref, feat_ref, padded_ref, table_ref, one_ref, two_in, vec_ref = refs[:7]
    loss_ref, gone_ref, gtwo_ref, gvec_ref, gfeat_ref = refs[7:12]
    z_s, n1_s, q_s, k_s, v_s, o_s, do_s, dx_s, dqkv_s, dqt_s, lse_s, delta_s = refs[12:24]
    lse_t, delta_t, wqkv_s, wo_s, y_s, gqkv_s, go_s, gup_s, gdn_s, ghd_s = refs[24:34]
    gy_s, gv_s, pixel_ref, seen_s, near_sem, far_ss, far_rs = refs[34:41]
    if wide:
        two_s, cr_s, xs_s, xr_s, c_ss, c_rs, x_ss, x_rs = refs[41:49]
        g_s = two_s
    else:
        two_s, g_s = two_in, gtwo_ref
    place = Place()
    greet(place.mates(wide))

    def chip_rows(s, x):
        return pl.ds(pl.multiple_of(((place.z + s) % 4 * 2 + x) * SHARD, 16), SHARD)

    own_lanes = pl.ds(pl.multiple_of(place.col * TWO_HALF, 128), TWO_HALF)
    other_lanes = pl.ds(pl.multiple_of((1 - place.col) * TWO_HALF, 128), TWO_HALF)
    if wide:

        def spot(k, z, x, col):
            rows = pl.ds(pl.multiple_of((z * 2 + x) * SHARD, 16), SHARD)
            return two_s.at[:, rows, pl.ds(pl.multiple_of(col * TWO_HALF, 128), TWO_HALF)]

        gather = Gather(place, lambda k: two_in, spot, refs[49:55])
        gather.begin_lined(two_in)
        for step in range(4):
            two_s[:, chip_rows(step, place.x), own_lanes] = two_in[(place.z + step) % 4]

    def tile(i):
        return pl.ds(pl.multiple_of(i * STEP_ROWS, STEP_ROWS), STEP_ROWS)

    def near(i):
        rows = tile(i)
        return pltpu.make_async_copy(
            padded_ref.at[place.row, rows, :], pixel_ref.at[place.row, rows, :], near_sem.at[i]
        )

    def far(i, half):
        rows = tile(i)
        return remote(
            padded_ref.at[1 - place.row, rows, :],
            pixel_ref.at[half, rows, :],
            far_ss.at[i],
            far_rs.at[i],
            place.row_mate(),
        )

    @pl.loop(0, N_STEPS)
    def _(i):
        near(i).start()
        far(i, place.row).start()

    half = 3 * HEAD
    up0, dn0, hd0, ed0 = UP_TWO, DN_TWO, HD_TWO, ED_AT
    vec = vec_ref[...]
    gain1, shift1, gain2, shift2, gain_f, shift_f, token = [vec[i : i + 1] for i in range(7)]

    for part in range(3):
        for r in range(2):
            wqkv_s[:, part * DD + r * half : part * DD + (r + 1) * half] = one_ref[
                r, :, part * half : (part + 1) * half
            ]
    for ref in (q_s, k_s, v_s, do_s):
        ref[ROWS:LANES, :] = jnp.zeros((LANES - ROWS, DD), bf)
    delta_s[ROWS:LANES, :] = jnp.zeros((LANES - ROWS, 128), f32)
    for ref in (gqkv_s, go_s, gup_s, gdn_s, ghd_s, gy_s, gv_s):
        ref[...] = jnp.zeros(ref.shape, f32)
    for r in range(2):
        y_s[:, r * DD : (r + 1) * DD] = low(
            times_trans(feat_ref[:, r * DD : (r + 1) * DD], one_ref[r, :, ed0 : ed0 + DD])
        )
    seen_s[...] = jnp.full(seen_s.shape, -1, jnp.int32)
    seen_s[0:1, 0:VIS] = seen_ref[place.row]
    seen = seen_s[0:1, :]

    def picks(i):
        ids = row_ids((STEP_ROWS, 128)) + i * STEP_ROWS
        hits = ids == seen
        taken = jnp.sum(hits.astype(f32), axis=-1, keepdims=True)
        valid = (row_ids((STEP_ROWS, 1)) + i * STEP_ROWS < TUBES).astype(f32)
        return hits.astype(bf), valid - taken

    @pl.loop(0, N_STEPS)
    def _(i):
        hits, hidden = picks(i)
        placed = times_plain(hits, y_s[...])
        z = placed[:, :DD] + placed[:, DD:] + table_ref[tile(i), :] + token * hidden
        z_s[tile(i), :] = z
        scaled, _ = norm_rows(z)
        n1 = low(scaled * gain1 + shift1)
        n1_s[tile(i), :] = n1
        q_s[tile(i), :] = low(times_plain(n1, wqkv_s[:, 0:DD]))
        k_s[tile(i), :] = low(times_plain(n1, wqkv_s[:, DD : 2 * DD]))
        v_s[tile(i), :] = low(times_plain(n1, wqkv_s[:, 2 * DD : 3 * DD]))

    first_half = lane_ids((1, 128)) < HEAD
    half_masks = [first_half, jnp.logical_not(first_half)]
    last_keys = lane_ids((1, 128)) < TUBES - (LANES - 128)
    ones = jnp.ones((LANES, 128), bf)
    lse_s[...] = jnp.zeros(lse_s.shape, f32)
    for p in range(3):
        lanes = slice(128 * p, 128 * (p + 1))

        @pl.loop(0, N_STEPS)
        def _(i):
            queries = q_s[tile(i), lanes]
            parts = []
            stat = lse_s[tile(i), :]
            for h in range(2):
                one = jnp.where(half_masks[h], queries, jnp.zeros_like(queries))
                scores = times_trans(one, k_s[:, lanes])
                tail = jnp.where(last_keys, scores[:, LANES - 128 :], -1e30)
                scores = jnp.concatenate([scores[:, : LANES - 128], tail], axis=-1)
                top = jnp.max(scores, axis=-1, keepdims=True) * (SCALE * LOG2E)
                weights = low(jnp.exp2(scores * (SCALE * LOG2E) - top))
                both = times_plain(weights, jnp.concatenate([v_s[:, lanes], ones], axis=-1))
                total = both[:, 128:129]
                parts.append(both[:, 0:128] / total)
                lse = top + jnp.log(total) * LOG2E
                stat = jnp.where(lane_ids((1, 128)) == 2 * p + h, lse, stat)
            lse_s[tile(i), :] = stat
            o_s[tile(i), lanes] = low(jnp.where(first_half, parts[0], parts[1]))

        if wide:
            for step in ((0,), (2,), (1, 3))[p]:
                gather.one("across", step)
    if wide:
        gather.finish(0)
    for r in range(2):
        wo_s[:, r * half : (r + 1) * half] = two_s[r, :, 0:half]
    lse_t[...] = lse_s[...].T

    @pl.loop(0, N_STEPS)
    def _(i):
        _, hidden = picks(i)
        near(i).wait()
        far(i, 1 - place.row).wait_recv()
        attended = o_s[tile(i), :]
        x1 = z_s[tile(i), :] + times_trans(attended, wo_s[...])
        scaled2, inv2 = norm_rows(x1)
        n2 = low(scaled2 * gain2 + shift2)
        x2 = x1
        acts, slopes, d_preds, d_us = [], [], [], []
        for r in range(2):
            u = times_plain(n2, two_s[r, :, up0 : up0 + 768])
            act, slope = gelu_pair(u)
            act = low(act)
            acts.append(act)
            slopes.append(slope)
            x2 = x2 + times_trans(act, two_s[r, :, dn0 : dn0 + 768])
        scaled_f, inv_f = norm_rows(x2)
        t = low(scaled_f * gain_f + shift_f)
        d_t = jnp.zeros((STEP_ROWS, DD), f32)
        for r in range(2):
            error = times_plain(t, two_s[r, :, hd0 : hd0 + 768]) - pixel_ref[r, tile(i), :].astype(
                f32
            )
            error = error * hidden
            gv_s[7:8, :] += column_sum(error * error)
            d_pred = low(error * (2.0 / PIX))
            d_preds.append(d_pred)
            d_t = d_t + times_trans(d_pred, two_s[r, :, hd0 : hd0 + 768])
        ghd_s[...] += trans_times(t, jnp.concatenate(d_preds, axis=-1))
        gv_s[4:5, 0:DD] += column_sum(d_t * scaled_f)
        gv_s[5:6, 0:DD] += column_sum(d_t)
        d_x2 = norm_rows_back(d_t, scaled_f, inv_f, gain_f)
        d_low = low(d_x2)
        d_n2 = jnp.zeros((STEP_ROWS, DD), f32)
        for r in range(2):
            d_u = low(times_plain(d_low, two_s[r, :, dn0 : dn0 + 768]) * slopes[r])
            d_us.append(d_u)
            d_n2 = d_n2 + times_trans(d_u, two_s[r, :, up0 : up0 + 768])
        gdn_s[...] += trans_times(d_low, jnp.concatenate(acts, axis=-1))
        gup_s[...] += trans_times(n2, jnp.concatenate(d_us, axis=-1))
        gv_s[2:3, 0:DD] += column_sum(d_n2 * scaled2)
        gv_s[3:4, 0:DD] += column_sum(d_n2)
        d_x1 = d_x2 + norm_rows_back(d_n2, scaled2, inv2, gain2)
        dx_s[tile(i), :] = d_x1
        d_low = low(d_x1)
        go_s[...] += trans_times(d_low, attended)
        d_o = low(times_plain(d_low, wo_s[...]))
        do_s[tile(i), :] = d_o
        both = d_o.astype(f32) * attended.astype(f32)
        stat = jnp.zeros((STEP_ROWS, 128), f32)
        for p in range(3):
            pair = both[:, 128 * p : 128 * (p + 1)]
            for h in range(2):
                one = jnp.sum(jnp.where(half_masks[h], pair, 0.0), axis=-1, keepdims=True)
                stat = jnp.where(lane_ids((1, 128)) == 2 * p + h, one, stat)
        delta_s[tile(i), :] = stat

    if wide:
        gather.drain()
    for r in range(2):
        g_s[r, :, 0:half] = low(go_s[:, r * half : (r + 1) * half])
        g_s[r, :, half:up0] = jnp.zeros((DD, up0 - half), bf)
        g_s[r, :, up0 : up0 + 768] = low(gup_s[:, r * 768 : (r + 1) * 768])
        g_s[r, :, dn0 : dn0 + 768] = low(gdn_s[:, r * 768 : (r + 1) * 768])
        g_s[r, :, hd0 : hd0 + 768] = low(ghd_s[:, r * 768 : (r + 1) * 768])
    if wide:
        to_core = remote(g_s.at[:, :, other_lanes], cr_s, c_ss, c_rs, place.core_mate())
        to_core.start()
        to_x = remote(xs_s, xr_s, x_ss, x_rs, place.x_mate())
    delta_t[...] = delta_s[...].T

    for p in range(3):
        lanes = slice(128 * p, 128 * (p + 1))
        dqt_s[...] = jnp.zeros(dqt_s.shape, f32)

        @pl.loop(0, LANES // KEY_ROWS)
        def _(j):
            rows = pl.ds(pl.multiple_of(j * KEY_ROWS, KEY_ROWS), KEY_ROWS)
            keys, values = k_s[rows, lanes], v_s[rows, lanes]
            bias = jnp.where(row_ids((KEY_ROWS, 1)) + j * KEY_ROWS < TUBES, 0.0, -1e30)
            d_keys, d_values = [], []
            for h in range(2):
                key_one = jnp.where(half_masks[h], keys, jnp.zeros_like(keys))
                value_one = jnp.where(half_masks[h], values, jnp.zeros_like(values))
                lse = lse_t[2 * p + h : 2 * p + h + 1, :]
                delta = delta_t[2 * p + h : 2 * p + h + 1, :]
                scores = times_trans(key_one, q_s[:, lanes])
                soft = jnp.exp2((scores * (SCALE * LOG2E) + bias) - lse)
                d_soft = times_trans(value_one, do_s[:, lanes])
                d_scores = low(soft * (d_soft - delta))
                d_values.append(times_plain(low(soft), do_s[:, lanes]))
                d_keys.append(times_plain(d_scores, q_s[:, lanes]))
                dqt_s[...] += trans_times(key_one, d_scores)
            k_out = slice(DD + 128 * p, DD + 128 * (p + 1))
            v_out = slice(2 * DD + 128 * p, 2 * DD + 128 * (p + 1))
            dqkv_s[rows, k_out] = low(jnp.where(first_half, d_keys[0], d_keys[1]) * SCALE)
            dqkv_s[rows, v_out] = low(jnp.where(first_half, d_values[0], d_values[1]))

        dqkv_s[:, lanes] = low(dqt_s[...].T * SCALE)
        if wide and p == 0:
            to_core.wait_recv()
            for s in range(4):
                rows = chip_rows(s, 1 - place.x)
                xs_s[s] = low(g_s[:, rows, own_lanes].astype(f32) + cr_s[:, rows, :].astype(f32))
            to_x.start()

    @pl.loop(0, N_STEPS)
    def _(i):
        hits, hidden = picks(i)
        d_qkv = dqkv_s[tile(i), :]
        gqkv_s[...] += trans_times(n1_s[tile(i), :], d_qkv)
        d_n1 = times_trans(d_qkv, wqkv_s[...])
        scaled1, inv1 = norm_rows(z_s[tile(i), :])
        gv_s[0:1, 0:DD] += column_sum(d_n1 * scaled1)
        gv_s[1:2, 0:DD] += column_sum(d_n1)
        d_z = dx_s[tile(i), :] + norm_rows_back(d_n1, scaled1, inv1, gain1)
        gv_s[6:7, 0:DD] += column_sum(d_z * hidden)
        gy_s[...] += trans_times(hits, low(d_z))

    d_y = low(gy_s[...])
    for r in range(2):
        gone_ref[r, :, ed0 : ed0 + DD] = low(trans_times(d_y, feat_ref[:, r * DD : (r + 1) * DD]))
        gone_ref[r, :, ed0 + DD : PART_ONE] = jnp.zeros((DD, PART_ONE - ed0 - DD), bf)
        gfeat_ref[:, r * DD : (r + 1) * DD] = low(times_plain(d_y, one_ref[r, :, ed0 : ed0 + DD]))
        for part in range(3):
            gone_ref[r, :, part * half : (part + 1) * half] = low(
                gqkv_s[:, part * DD + r * half : part * DD + (r + 1) * half]
            )
    if wide:
        to_x.wait_recv()
        for s in range(4):
            rows = chip_rows(s, place.x)
            total = g_s[:, rows, own_lanes].astype(f32) + cr_s[:, rows, :].astype(f32)
            total = total + xr_s[s].astype(f32)
            for r in range(2):
                at = (2 * s + r) * SHARD
                gtwo_ref[at : at + SHARD, :] = total[r]
        to_core.wait_send()
        to_x.wait_send()
    gvec_ref[...] = gv_s[:, 0:DD]

    @pl.loop(0, N_STEPS)
    def _(i):
        far(i, place.row).wait_send()

    loss_ref[...] = jnp.zeros((8, 128), f32) + jnp.sum(gv_s[7:8, :]) / PIX


def run_decoder(wide, *operands):
    bf, f32 = jnp.bfloat16, jnp.float32
    vmem = pl.BlockSpec(memory_space=pltpu.VMEM)
    dma = pltpu.SemaphoreType.DMA
    if wide:
        two = jax.ShapeDtypeStruct((8 * SHARD, TWO_HALF), f32)
    else:
        two = jax.ShapeDtypeStruct((2, DD, PART_TWO), bf)
    scratch = [
        pltpu.VMEM((ROWS, DD), f32),
        pltpu.VMEM((ROWS, DD), bf),
        pltpu.VMEM((LANES, DD), bf),
        pltpu.VMEM((LANES, DD), bf),
        pltpu.VMEM((LANES, DD), bf),
        pltpu.VMEM((ROWS, DD), bf),
        pltpu.VMEM((LANES, DD), bf),
        pltpu.VMEM((ROWS, DD), f32),
        pltpu.VMEM((LANES, 3 * DD), bf),
        pltpu.VMEM((128, LANES), f32),
        pltpu.VMEM((LANES, 128), f32),
        pltpu.VMEM((LANES, 128), f32),
        pltpu.VMEM((128, LANES), f32),
        pltpu.VMEM((128, LANES), f32),
        pltpu.VMEM((DD, 3 * DD), bf),
        pltpu.VMEM((DD, DD), bf),
        pltpu.VMEM((128, 2 * DD), bf),
        pltpu.VMEM((DD, 3 * DD), f32),
        pltpu.VMEM((DD, DD), f32),
        pltpu.VMEM((DD, DFF), f32),
        pltpu.VMEM((DD, DFF), f32),
        pltpu.VMEM((DD, DFF), f32),
        pltpu.VMEM((128, DD), f32),
        pltpu.VMEM((8, 768), f32),
        pltpu.VMEM((2, ROWS, PIX // 2), bf),
        pltpu.VMEM((8, 128), jnp.int32),
        dma((N_STEPS,)),
        dma((N_STEPS,)),
        dma((N_STEPS,)),
    ]
    if wide:
        scratch += [
            pltpu.VMEM((2, DD, PART_TWO), bf),
            pltpu.VMEM((2, DD, TWO_HALF), bf),
            pltpu.VMEM((4, 2, SHARD, TWO_HALF), bf),
            pltpu.VMEM((4, 2, SHARD, TWO_HALF), bf),
            dma,
            dma,
            dma,
            dma,
        ]
        scratch += [dma((1, 4)), dma((1, 3)), dma((1, 4)), dma((1, 4)), dma((1, 8)), dma((1, 8))]
    return pl.pallas_call(
        functools.partial(decoder_body, wide),
        out_shape=(
            jax.ShapeDtypeStruct((8, 128), f32),
            jax.ShapeDtypeStruct((2, DD, PART_ONE), bf),
            two,
            jax.ShapeDtypeStruct((8, DD), f32),
            jax.ShapeDtypeStruct((128, D), bf),
        ),
        in_specs=[vmem, vmem, pl.BlockSpec(memory_space=pl.ANY), vmem, vmem, vmem, vmem],
        out_specs=(vmem,) * 5,
        scratch_shapes=scratch,
        compiler_params=pltpu.CompilerParams(
            collective_id=4, has_side_effects=True, vmem_limit_bytes=63 * MIB
        ),
        cost_estimate=pl.CostEstimate(
            flops=30 * 10**9, bytes_accessed=20 * 10**6, transcendentals=20 * 10**6
        ),
        name="decoder",
    )(*operands)


PAIR = 256
HALF_D = D // 2
QKV_W = 3 * D // 2
HID = FF // 2
A_COLS = QKV_W + D // 2
ENC_COLS = A_COLS + 2 * HID
UP_AT, DN_AT = A_COLS, A_COLS + HID
EMB_ROWS = SHARD + 16
GATHERS = (
    (-1, 0, D),
    (0, 0, A_COLS),
    (0, UP_AT, HID),
    (0, DN_AT, HID),
    (1, 0, A_COLS),
    (1, UP_AT, HID),
    (1, DN_AT, HID),
    (-2, 0, PART_ONE),
)
PART_ONE_AT = len(GATHERS) - 1


def half_lanes():
    first = lane_ids((1, 128)) < HEAD
    return [first, jnp.logical_not(first)]


def same_clip():
    a, b = row_ids((PAIR, PAIR)), lane_ids((PAIR, PAIR))
    return jnp.logical_and(a // 128 == b // 128, b % 128 < VIS)


def encoder_scores(queries, keys, allowed):
    scores = jnp.where(allowed, times_trans(queries, keys), -1e30)
    top = jnp.max(scores, axis=-1, keepdims=True) * (SCALE * LOG2E)
    weights = jnp.exp2(scores * (SCALE * LOG2E) - top)
    return weights, jnp.sum(weights, axis=-1, keepdims=True)


def encoder_attention(qkv_ref, out_ref):
    allowed = same_clip()
    halves = half_lanes()
    for p in range(3):
        q = qkv_ref[:, 128 * p : 128 * (p + 1)]
        k = qkv_ref[:, HALF_D + 128 * p : HALF_D + 128 * (p + 1)]
        v = qkv_ref[:, 2 * HALF_D + 128 * p : 2 * HALF_D + 128 * (p + 1)]
        parts = []
        for h in range(2):
            one = jnp.where(halves[h], q, jnp.zeros_like(q))
            weights, total = encoder_scores(one, k, allowed)
            parts.append(times_plain(low(weights), v) / total)
        out_ref[:, 128 * p : 128 * (p + 1)] = low(jnp.where(halves[0], parts[0], parts[1]))


def pack_heads(dst, src, heads):
    for part in range(3):
        for h in range(heads):
            at = (part * heads + h) * HEAD
            dst[:, at : at + HEAD] = low(src[:, (3 * h + part) * HEAD : (3 * h + part + 1) * HEAD])


def encoder_body(wide, *refs):
    f32 = jnp.float32
    if wide:
        seen_ref, pixel_ref, freq_ref, emb_ref, enc_ref, dec_ref, evec_ref, dvec_ref = refs[:8]
        refs = refs[8:]
    else:
        seen_ref, pixel_ref, freq_ref, emb_full, w_s, gain_in = refs[:6]
        refs = refs[6:]
    feat_ref, *kept_out = refs[:7]
    padded_out = refs[7]
    refs = refs[8:]
    if wide:
        gain_ref, dgain_ref, w_out, one_out, two_out = refs[:5]
        emb_s, w_s, embc_s, emb_in, enc_in, small_s, one_s, two_s, block_s = refs[5:14]
        refs = refs[14:]
    sent_s, got_s, padded_s, seen_s, pad_sem, y_ss, y_rs = refs[:7]
    kept = refs[7:13]
    kept_sem = refs[13]
    refs = refs[14:]
    x_ref, qkv_ref, o_ref, h_ref, slope_ref, px_ref = kept
    leaving = []

    def leave(src, at=None):
        i = [ref is src for ref in kept].index(True)
        dst = kept_out[i]
        if at is not None:
            src, dst = src.at[at], dst.at[at]
        copy = pltpu.make_async_copy(src, dst, kept_sem.at[len(leaving)])
        copy.start()
        leaving.append(copy)

    place = Place()
    greet(place.mates(wide))
    swap = Swap(place, sent_s, got_s, y_ss, y_rs)
    if wide:

        def own_part(k):
            layer, start, width = GATHERS[k]
            if layer == -1:
                return emb_in
            if layer == -2:
                return spot(k, place.z, place.x, place.col)
            return enc_in.at[layer, :, pl.ds(start, width)]

        def spot(k, z, x, col):
            layer, start, width = GATHERS[k]
            if layer == -2:
                rows = pl.ds(pl.multiple_of((z * 2 + x) * SHARD, 16), SHARD)
                return one_s.at[:, rows, pl.ds(pl.multiple_of(col * ONE_HALF, 128), ONE_HALF)]
            rows = EMB_ROWS if layer < 0 else SHARD
            first = pl.multiple_of(shard_at(z, x, col) * rows, 16)
            if layer == -1:
                return emb_s.at[pl.ds(first, rows), :]
            return w_s.at[layer, pl.ds(first, rows), pl.ds(start, width)]

        gather = Gather(place, own_part, spot, refs[:6], over_x_first=PART_ONE_AT)
        extra = len(GATHERS)
        keep_sem, block_ss, block_rs, seed_ss, seed_rs = refs[6:11]
        emb_in[0:SHARD, :] = low(emb_ref[0])
        small_s[...] = jnp.zeros(small_s.shape, f32)
        small_s[0:10, 0:SHARD] = evec_ref[...]
        small_s[0:7, SHARD : SHARD + DD // N_SHARDS] = dvec_ref[...]
        emb_in[SHARD:EMB_ROWS, 0:128] = low(small_s[...])
        emb_in[SHARD:EMB_ROWS, 128:D] = jnp.zeros((EMB_ROWS - SHARD, D - 128), jnp.bfloat16)
        gather.begin(0)
        for layer in range(LAYERS):
            pack_heads(enc_in.at[layer], enc_ref.at[layer, 0], HEADS // 2)
            enc_in[layer, :, QKV_W:] = low(enc_ref[layer, 0, :, QKV_W:])
            if layer == 0:
                gather.begin(1)
                gather.begin(2)
                gather.begin(3)
        own = shard_at(place.z, place.x, place.col)
        emb_s[pl.ds(pl.multiple_of(own * EMB_ROWS, 16), EMB_ROWS), :] = emb_in[...]
        for layer in range(LAYERS):
            w_s[layer, pl.ds(pl.multiple_of(own * SHARD, 16), SHARD), :] = enc_in[layer]
        mine = pl.ds(pl.multiple_of(place.col * (SHARD // 2), 8), SHARD // 2)
        block_s[mine, :] = jnp.zeros((SHARD // 2, PART_ONE + PART_TWO), f32)
        shard = dec_ref[0]
        heads = DHEADS // 2
        for part in range(3):
            for h in range(heads):
                at = (3 * h + part) * HEAD
                to = (part * heads + h) * HEAD
                block_s[mine, to : to + HEAD] = shard[:, at : at + HEAD]
        block_s[mine, ED_AT : ED_AT + DD] = shard[:, 3072:3456]
        block_s[mine, PART_ONE : PART_ONE + 192] = shard[:, ED_AT:768]
        block_s[mine, PART_ONE + UP_TWO : PART_ONE + PART_TWO] = shard[:, 768:3072]
        spread = remote(
            block_s.at[mine, :], block_s.at[mine, :], block_ss, block_rs, place.core_mate()
        )
        spread.start()
        theirs = pl.ds(pl.multiple_of((1 - place.col) * (SHARD // 2), 8), SHARD // 2)
        half_one = spot(PART_ONE_AT, place.z, place.x, place.col)
        half_two = two_s.at[place.z]
        seeds = [
            remote(part.at[place.row], part.at[place.row], ss, rs, place.row_mate())
            for part, ss, rs in (
                (half_one, seed_ss.at[0], seed_rs.at[0]),
                (half_two, seed_ss.at[1], seed_rs.at[1]),
            )
        ]
        seeds_back = [
            remote(part.at[1 - place.row], part.at[1 - place.row], ss, rs, place.row_mate())
            for part, ss, rs in (
                (half_one, seed_ss.at[0], seed_rs.at[0]),
                (half_two, seed_ss.at[1], seed_rs.at[1]),
            )
        ]

    def step(name, k):
        if wide:
            getattr(gather, name)(k)

    odd = (lane_ids((1, D)) % 2).astype(f32) * (0.5 * math.pi)
    freq = freq_ref[0:1, :]
    places = []
    seen_s[...] = jnp.full(seen_s.shape, -1, jnp.int32)
    whole = TUBES // 16 * 16
    for m in range(MICRO):
        seen_s[m : m + 1, 0:VIS] = seen_ref[m]
        row = seen_s[m : m + 1, :]
        hits = (row_ids((TUBES, 128)) == row).astype(jnp.bfloat16)
        px_ref[128 * m : 128 * (m + 1), :] = low(trans_times(hits, pixel_ref[m, 0]))
        column = jnp.broadcast_to(row.astype(f32), (128, 128)).T[:, 0:1]
        places.append(jnp.sin(column * freq + odd))
        padded_s[m, 0:whole, :] = pixel_ref[m, 0, 0:whole, :]
        rest = pixel_ref[m, 0, whole:TUBES, :].astype(f32)
        rest = jnp.concatenate([rest, jnp.zeros((ROWS - TUBES, D), f32)], axis=0)
        padded_s[m, whole:ROWS, :] = low(rest)
    pad_copy = pltpu.make_async_copy(padded_s, padded_out, pad_sem)
    pad_copy.start()
    leave(px_ref)

    if wide:
        gather.forward(0)
        gather.forward(1)
        gather.begin(4)
        gather.across(0)
        gather.finish(0)
        for s in range(N_SHARDS):
            embc_s[SHARD * s : SHARD * (s + 1), :] = emb_s[EMB_ROWS * s : EMB_ROWS * s + SHARD, :]
            tail = emb_s[EMB_ROWS * s + SHARD : EMB_ROWS * (s + 1), 0:128].astype(f32)
            gain_ref[:, SHARD * s : SHARD * (s + 1)] = tail[:, 0:SHARD]
            dgain_ref[:, DD // 16 * s : DD // 16 * (s + 1)] = tail[0:8, SHARD : SHARD + DD // 16]
        emb_full, gain_in = embc_s, gain_ref
    swap.start(0, times_trans(px_ref[...], emb_full[...]))
    if wide:
        other_rows = block_s.at[theirs, :]
        remote(other_rows, other_rows, block_ss, block_rs, place.core_mate()).wait_recv()
        lanes = pl.ds(pl.multiple_of(place.col * ONE_HALF, 128), ONE_HALF)
        half_one.at[place.row][...] = low(block_s[:, lanes])
        lanes = pl.ds(pl.multiple_of(PART_ONE + place.col * TWO_HALF, 128), TWO_HALF)
        half_two.at[place.row][...] = low(block_s[:, lanes])
        for copy in seeds:
            copy.start()
    step("forward", 2)
    step("across", 1)
    x = swap.total(0) + jnp.concatenate(places, axis=0)
    for layer in range(LAYERS):
        gains = gain_in[4 * layer : 4 * layer + 4, :]
        x_ref[2 * layer] = x
        leave(x_ref, 2 * layer)
        scaled, _ = norm_rows(x)
        n1 = low(scaled * gains[0:1] + gains[1:2])
        first = 1 + 3 * layer
        step("finish", first)
        qkv_ref[layer] = low(times_plain(n1, w_s[layer, :, 0:QKV_W]))
        encoder_attention(qkv_ref.at[layer], o_ref.at[layer])
        if wide and layer == 1:
            gather.forward(6)
        swap.start(1 + 2 * layer, times_trans(o_ref[layer], w_s[layer, :, QKV_W:A_COLS]))
        if wide and layer == 0:
            gather.begin(5)
            gather.forward(3)
        elif wide:
            gather.begin_turned(extra)
            gather.line(extra + 1, half_two, half_two)
        step("across", first + 1)
        x = x + swap.total(1 + 2 * layer)
        x_ref[2 * layer + 1] = x
        leave(x_ref, 2 * layer + 1)
        leave(qkv_ref, layer)
        leave(o_ref, layer)
        scaled, _ = norm_rows(x)
        n2 = low(scaled * gains[2:3] + gains[3:4])
        step("finish", first + 1)
        act, slope = gelu_pair(times_plain(n2, w_s[layer, :, UP_AT:DN_AT]))
        act = low(act)
        h_ref[layer] = act
        slope_ref[layer] = slope
        leave(h_ref, layer)
        leave(slope_ref, layer)
        if layer == 0:
            step("begin", 6)
        step("across", first + 2)
        step("finish", first + 2)
        swap.start(2 + 2 * layer, times_trans(act, w_s[layer, :, DN_AT:ENC_COLS]))
        if wide:
            keep = pltpu.make_async_copy(w_s.at[layer], w_out.at[layer], keep_sem.at[layer])
            keep.start()
        if wide and layer == 0:
            gather.forward(4)
            for copy in seeds_back:
                copy.wait_recv()
            gather.begin(PART_ONE_AT)
            gather.across(4)
            gather.forward(5)
        elif wide:
            gather.forward_turned(extra)
        x = x + swap.total(2 + 2 * layer)
    x_ref[2 * LAYERS] = x
    leave(x_ref, 2 * LAYERS)
    scaled, _ = norm_rows(x)
    gains = gain_in[4 * LAYERS : 4 * LAYERS + 2, :]
    feat = low(scaled * gains[0:1] + gains[1:2])
    feat_ref[...] = jnp.where(place.row == 0, feat[0:128], feat[128:256])
    swap.drain()
    pad_copy.wait()
    for copy in leaving:
        copy.wait()
    if wide:
        gather.finish(PART_ONE_AT)
        for s in (2, 1, 3):
            gather.landed(extra + 1, s, two_s.at[(place.z - s) % 4])
        one_copy = pltpu.make_async_copy(one_s, one_out, keep_sem.at[LAYERS])
        one_copy.start()
        two_copy = pltpu.make_async_copy(two_s, two_out, keep_sem.at[LAYERS + 1])
        two_copy.start()
        spread.wait_send()
        for copy in seeds:
            copy.wait_send()
        gather.drain()
        one_copy.wait()
        two_copy.wait()
        for layer in range(LAYERS):
            pltpu.make_async_copy(w_s.at[layer], w_out.at[layer], keep_sem.at[layer]).wait()


def run_encoder(wide, *operands):
    bf, f32 = jnp.bfloat16, jnp.float32
    vmem = pl.BlockSpec(memory_space=pltpu.VMEM)
    dma = pltpu.SemaphoreType.DMA
    shape = jax.ShapeDtypeStruct
    n_swaps = 1 + 2 * LAYERS
    outs = [
        shape((128, D), bf),
        shape((2 * LAYERS + 1, PAIR, D), f32),
        shape((LAYERS, PAIR, QKV_W), bf),
        shape((LAYERS, PAIR, HALF_D), bf),
        shape((LAYERS, PAIR, HID), bf),
        shape((LAYERS, PAIR, HID), f32),
        shape((PAIR, D), bf),
        shape((MICRO, ROWS, D), bf),
    ]
    out_specs = [vmem] + [pl.BlockSpec(memory_space=pl.ANY)] * (len(outs) - 1)
    kept = [pltpu.VMEM(out.shape, out.dtype) for out in outs[1:7]]
    scratch = []
    if wide:
        anywhere = pl.BlockSpec(memory_space=pl.ANY)
        outs += [
            shape((16, D), f32),
            shape((8, DD), f32),
            shape((LAYERS, D, ENC_COLS), bf),
            shape((2, DD, PART_ONE), bf),
            shape((4, 2, SHARD, TWO_HALF), bf),
        ]
        out_specs += [vmem, vmem, anywhere, anywhere, anywhere]
        scratch += [
            pltpu.VMEM((N_SHARDS * EMB_ROWS, D), bf),
            pltpu.VMEM((LAYERS, D, ENC_COLS), bf),
            pltpu.VMEM((D, D), bf),
            pltpu.VMEM((EMB_ROWS, D), bf),
            pltpu.VMEM((LAYERS, SHARD, ENC_COLS), bf),
            pltpu.VMEM((16, 128), f32),
            pltpu.VMEM((2, DD, PART_ONE), bf),
            pltpu.VMEM((4, 2, SHARD, TWO_HALF), bf),
            pltpu.VMEM((SHARD, PART_ONE + PART_TWO), f32),
        ]
    scratch += [
        pltpu.VMEM((n_swaps, PAIR, D), bf),
        pltpu.VMEM((n_swaps, PAIR, D), bf),
        pltpu.VMEM((MICRO, ROWS, D), bf),
        pltpu.VMEM((8, 128), jnp.int32),
        dma,
        dma((n_swaps,)),
        dma((n_swaps,)),
        *kept,
        dma((2 + 6 * LAYERS,)),
    ]
    if wide:
        n = len(GATHERS)
        scratch += [dma((n + 2, 4)), dma((n + 2, 3)), dma((n, 4)), dma((n, 4)), dma((n, 8)), dma((n, 8))]
        scratch += [dma((LAYERS + 2,)), dma, dma, dma((2,)), dma((2,))]
    return pl.pallas_call(
        functools.partial(encoder_body, wide),
        out_shape=tuple(outs),
        in_specs=[vmem] * len(operands),
        out_specs=tuple(out_specs),
        scratch_shapes=scratch,
        compiler_params=pltpu.CompilerParams(
            collective_id=1, has_side_effects=True, vmem_limit_bytes=60 * MIB
        ),
        cost_estimate=pl.CostEstimate(
            flops=10 * 10**9, bytes_accessed=60 * 10**6, transcendentals=10**6
        ),
        name="encoder",
    )(*operands)


SUMS = (
    ("dn1", HID),
    ("up1", HID),
    ("at1", A_COLS),
    ("dn0", HID),
    ("up0", HID),
    ("at0", A_COLS),
    ("emb", D),
)
SUM_AT = {name: sum(w for _, w in SUMS[:i]) for i, (name, _) in enumerate(SUMS)}
SUM_COLS = sum(w for _, w in SUMS)
BLOCKS = N_SHARDS // 2 * SHARD
QUARTER = BLOCKS // 2


class Scatter(Mail):
    def __init__(self, place, bufs, sems, into):
        super().__init__()
        self.at, self.into = place, into
        self.perm, self.flip, self.cs, self.cr, self.xs, self.xr, self.zs, self.zr, self.own = bufs
        self.c_ss, self.c_rs, self.x_ss, self.x_rs, self.z_ss, self.z_rs = sems
        self.last = {}
        self.lines = {}

    def span(self, name, shift=0, width=None):
        k = [n for n, _ in SUMS].index(name)
        return k, pl.ds(SUM_AT[name] + shift, SUMS[k][1] if width is None else width)

    def post(self, src, dst, ss, rs, device, key):
        copy = remote(src, dst, ss, rs, device)
        copy.start()
        self.last[key] = copy

    def free(self, key):
        if key in self.last:
            self.last.pop(key).wait_send()

    def turn(self, slot, left):
        at = self.at
        flip = self.flip.at[slot % 2]
        flip[...] = left.T
        order = [
            (s, x, c) for c, x in ((1, 1), (1, 0), (0, 1), (0, 0)) for s in range(4)
        ]
        for i, (s, other_x, other_c) in enumerate(order):
            x = 1 - at.x if other_x else at.x
            c = 1 - at.col if other_c else at.col
            first = pl.multiple_of(shard_at((at.z + s) % 4, x, c) * SHARD, 16)
            self.perm[slot, SHARD * i : SHARD * (i + 1), :] = flip[pl.ds(first, SHARD), :]

    def cores(self, name, items):
        k, span = self.span(name)
        slot_at, width = k % 2, SUMS[k][1]
        self.free(("core", slot_at))
        for slot, right, shift, wide in items:
            self.cs[slot_at, :, shift : shift + wide] = low(
                times_plain(self.perm[slot, 0:BLOCKS, :], right[...])
            )
        self.post(
            self.cs.at[slot_at, :, pl.ds(0, width)],
            self.cr.at[:, span],
            self.c_ss.at[k],
            self.c_rs.at[k],
            self.at.core_mate(),
            ("core", slot_at),
        )

    def over_x(self, name, items):
        f32 = jnp.float32
        k, whole = self.span(name)
        slot_at, width = k % 3, SUMS[k][1]
        self.free(("x", slot_at))
        self.came(self.cr.at[:, whole], self.c_ss.at[k], self.c_rs.at[k], self.at.core_mate())
        for slot, right, shift, wide in items:
            _, span = self.span(name, shift, wide)
            mine = times_plain(self.perm[slot, BLOCKS : BLOCKS + QUARTER, :], right[...])
            self.xs[slot_at, :, shift : shift + wide] = low(
                mine + self.cr[0:QUARTER, span].astype(f32)
            )
        self.post(
            self.xs.at[slot_at, :, pl.ds(0, width)],
            self.xr.at[:, whole],
            self.x_ss.at[k],
            self.x_rs.at[k],
            self.at.x_mate(),
            ("x", slot_at),
        )
        for slot, right, shift, wide in items:
            _, span = self.span(name, shift, wide)
            mine = times_plain(self.perm[slot, BLOCKS + QUARTER : 2 * BLOCKS, :], right[...])
            self.own[k % 4, :, shift : shift + wide] = mine + self.cr[QUARTER:BLOCKS, span].astype(f32)

    def along_z(self, name):
        k, span = self.span(name)
        self.came(self.xr.at[:, span], self.x_ss.at[k], self.x_rs.at[k], self.at.x_mate())
        own = self.own.at[k % 4, :, pl.ds(0, SUMS[k][1])]
        own[...] += self.xr[:, span].astype(jnp.float32)
        line = LineSum(
            self.at,
            own,
            self.zs.at[:, :, span],
            self.zr.at[:, :, span],
            self.z_ss.at[k],
            self.z_rs.at[k],
            SHARD,
            self.into(name),
        )
        line.begin()
        self.lines[name] = line

    def relay(self, name):
        self.lines[name].relay()

    def finish(self, name):
        self.lines[name].finish()

    def drain(self):
        for copy in self.last.values():
            copy.wait_send()
        for line in self.lines.values():
            line.drain()


class DecoderScatter(Mail):
    def __init__(self, place, one, two, out, bufs, sems):
        super().__init__()
        self.at, self.one, self.two, self.out = place, one, two, out
        self.cr, self.xs, self.xr, self.own, self.zs1, self.zr1, self.zs2, self.zr2 = bufs[:8]
        self.fin, self.ys, self.yr, self.whole, self.part = bufs[8:]
        (
            self.c_ss, self.c_rs, self.x_ss, self.x_rs, self.z1_ss, self.z1_rs,
            self.z2_ss, self.z2_rs, self.y_ss, self.y_rs, self.f_ss, self.f_rs,
        ) = sems
        self.lanes = pl.ds(pl.multiple_of(place.col * ONE_HALF, 128), ONE_HALF)

    def rows(self, s, x):
        return pl.ds(pl.multiple_of(((self.at.z + s) % 4 * 2 + x) * SHARD, 16), SHARD)

    def begin(self):
        at = self.at
        others = pl.ds(pl.multiple_of((1 - at.col) * ONE_HALF, 128), ONE_HALF)
        src = self.one.at[:, :, others]
        self.go(src, self.cr, self.c_ss, self.c_rs, at.core_mate())
        self.line_two = LineSum(
            at, self.two, self.zs2, self.zr2, self.z2_ss, self.z2_rs, 2 * SHARD,
            self.fin.at[:, pl.ds(ONE_HALF, TWO_HALF)],
        )
        self.line_two.begin()

    def sums(self, s, x):
        rows = self.rows(s, x)
        f32 = jnp.float32
        return self.one[:, rows, self.lanes].astype(f32) + self.cr[:, rows, :].astype(f32)

    def over_x(self):
        at = self.at
        self.came(self.cr, self.c_ss, self.c_rs, at.core_mate())
        for s in range(4):
            self.xs[s] = low(self.sums(s, 1 - at.x))
        self.go(self.xs, self.xr, self.x_ss, self.x_rs, at.x_mate())

    def along_z(self):
        at = self.at
        self.came(self.xr, self.x_ss, self.x_rs, at.x_mate())
        for s in range(4):
            total = self.sums(s, at.x) + self.xr[s].astype(jnp.float32)
            for r in range(2):
                first = (2 * s + r) * SHARD
                self.own[first : first + SHARD, :] = total[r]
        self.line_one = LineSum(
            at, self.own, self.zs1, self.zr1, self.z1_ss, self.z1_rs, 2 * SHARD,
            self.fin.at[:, pl.ds(0, ONE_HALF)],
        )
        self.line_one.begin()

    def over_rows(self):
        at = self.at
        self.line_one.finish()
        self.line_two.finish()
        rows = pl.ds(pl.multiple_of((1 - at.row) * SHARD, 8), SHARD)
        self.ys[...] = low(self.fin[rows, :])
        self.go(self.ys, self.yr, self.y_ss, self.y_rs, at.row_mate())

    def to_cores(self):
        at = self.at
        self.came(self.yr, self.y_ss, self.y_rs, at.row_mate())
        rows = pl.ds(pl.multiple_of(at.row * SHARD, 8), SHARD)
        self.whole[...] = self.fin[rows, :] + self.yr[...].astype(jnp.float32)
        theirs = pl.ds(pl.multiple_of((1 - at.col) * (SHARD // 2), 8), SHARD // 2)
        self.go(self.whole.at[theirs, :], self.part, self.f_ss, self.f_rs, at.core_mate())

    def finish(self):
        at = self.at
        width = ONE_HALF + TWO_HALF
        mine = pl.ds(pl.multiple_of(at.col * (SHARD // 2), 8), SHARD // 2)
        self.out[:, pl.ds(pl.multiple_of(at.col * width, 128), width)] = self.whole[mine, :]
        self.came(self.part, self.f_ss, self.f_rs, at.core_mate())
        self.out[:, pl.ds(pl.multiple_of((1 - at.col) * width, 128), width)] = self.part[...]

    def drain(self):
        super().drain()
        self.line_one.drain()
        self.line_two.drain()


class Everyone(Mail):
    def __init__(self, place, bufs, sems):
        super().__init__()
        self.at = place
        self.send, self.got, self.one, self.ones = bufs
        self.ss, self.rs, self.o_ss, self.o_rs = sems
        self.waits = []

    def first(self, enc, dec):
        self.send[0, 0:16, :] = enc
        self.send[0, 16:24, 0:DD] = dec
        self.send[0, 16:24, DD:D] = jnp.zeros((8, D - DD), jnp.float32)
        self.post(0)

    def post(self, i):
        at = self.at
        mates = ([at.core_mate()], [at.row_mate()], [at.x_mate()], [at.z_mate(s) for s in (1, 2, 3)])
        for j, mate in enumerate(mates[i]):
            self.go(
                self.send.at[i], self.got.at[i + j], self.ss.at[i + j], self.rs.at[i + j], mate
            )
        self.waits.append([(i + j, mate) for j, mate in enumerate(mates[i])])

    def stage(self, i):
        total = self.send[i - 1]
        for slot, mate in self.waits[i - 1]:
            self.came(self.got.at[slot], self.ss.at[slot], self.rs.at[slot], mate)
            total = total + self.got[slot]
        self.send[i] = total
        if i < 4:
            self.post(i)

    def total(self):
        return self.send[4]

    def number(self, value):
        at = self.at
        groups = (at.cube(), [at.z_mate(s) for s in (1, 2, 3)])
        total = jnp.zeros((8, 128), jnp.float32) + value
        first = 0
        for i, mates in enumerate(groups):
            self.one[i] = total
            for j, mate in enumerate(mates):
                slot = first + j
                self.go(
                    self.one.at[i], self.ones.at[slot], self.o_ss.at[slot], self.o_rs.at[slot], mate
                )
            for j, mate in enumerate(mates):
                slot = first + j
                self.came(self.ones.at[slot], self.o_ss.at[slot], self.o_rs.at[slot], mate)
                total = total + self.ones[slot]
            first += len(mates)
        return total[0:1, 0:1]


def encoder_attention_back(qkv_ref, d_out, out_ref):
    allowed = same_clip()
    halves = half_lanes()
    for p in range(3):
        spans = [slice(part * HALF_D + 128 * p, part * HALF_D + 128 * (p + 1)) for part in range(3)]
        q, k, v = (qkv_ref[:, span] for span in spans)
        d_pair = d_out[:, 128 * p : 128 * (p + 1)]
        found = []
        for h in range(2):
            one = jnp.where(halves[h], q, jnp.zeros_like(q))
            weights, total = encoder_scores(one, k, allowed)
            soft = weights / total
            d_one = jnp.where(halves[h], d_pair, jnp.zeros_like(d_pair))
            d_soft = times_trans(d_one, v)
            delta = jnp.sum(soft * d_soft, axis=-1, keepdims=True)
            d_scores = low(soft * (d_soft - delta))
            found.append(
                (
                    times_plain(d_scores, k) * SCALE,
                    trans_times(d_scores, q) * SCALE,
                    trans_times(low(soft), d_pair),
                )
            )
        for part in range(3):
            out_ref[:, spans[part]] = low(jnp.where(halves[0], found[0][part], found[1][part]))


def encoder_back_body(wide, *refs):
    f32 = jnp.float32
    gfeat_ref, x_in, qkv_in, o_in, h_ref, slope_ref, px_in, gain_ref, w_ref = refs[:9]
    refs = refs[9:]
    if wide:
        one_ref, two_ref, loss_ref, dvec_ref = refs[:4]
        refs = refs[4:]
    genc_ref, gemb_ref, gvec_ref = refs[:3]
    refs = refs[3:]
    if wide:
        gdec_ref, total_ref = refs[:2]
        refs = refs[2:]
    wa_s, wb_s, du_s, dqkv_s, feat_s, sent_s, got_s, h_s, slope_s = refs[:9]
    x_ref, qkv_ref, o_ref, px_ref, in_sem = refs[9:14]
    load_sem, f_ss, f_rs, y_ss, y_rs = refs[14:19]
    refs = refs[19:]
    arriving = [
        pltpu.make_async_copy(src, dst, in_sem.at[i])
        for i, (src, dst) in enumerate(
            ((x_in, x_ref), (qkv_in, qkv_ref), (o_in, o_ref), (px_in, px_ref))
        )
    ]
    arriving[0].start()
    place = Place()
    greet(place.mates(wide) + (place.cube()[2:3] + place.cube()[4:] if wide else []))
    swap = Swap(place, sent_s, got_s, y_ss, y_rs)
    swapped = remote(gfeat_ref, feat_s, f_ss, f_rs, place.row_mate())
    swapped.start()

    def into(name):
        if name == "emb":
            return gemb_ref
        start, width = {"at": (0, A_COLS), "up": (UP_AT, HID), "dn": (DN_AT, HID)}[name[:2]]
        return genc_ref.at[int(name[2]), :, pl.ds(start, width)]

    scatter = Scatter(place, refs[:9], refs[9:15], into) if wide else None
    dec = DecoderScatter(place, one_ref, two_ref, gdec_ref, refs[15:28], refs[28:40]) if wide else None
    everyone = Everyone(place, refs[40:44], refs[44:48]) if wide else None

    def load(layer, part):
        src, dst = (
            (w_ref.at[layer, :, pl.ds(0, A_COLS)], wa_s),
            (w_ref.at[layer, :, pl.ds(A_COLS, 2 * HID)], wb_s),
            (h_ref.at[layer], h_s),
            (slope_ref.at[layer], slope_s),
        )[part]
        return pltpu.make_async_copy(src, dst, load_sem.at[layer, part])

    load(1, 2).start()
    load(1, 3).start()
    load(1, 1).start()
    load(1, 0).start()
    for copy in arriving[1:]:
        copy.start()

    lefts = {}

    def factor(slot, left):
        lefts[slot] = left
        if wide:
            scatter.turn(slot, left)

    def emit(name, items):
        if wide:
            scatter.cores(name, items)
            return
        for slot, right, shift, width in items:
            value = low(trans_times(lefts[slot], right[...]))
            if name == "emb":
                gemb_ref[...] = value
                continue
            start = {"at": 0, "up": UP_AT, "dn": DN_AT}[name[:2]] + shift
            genc_ref[int(name[2]), :, start : start + width] = value

    def later(step, *args):
        if wide:
            getattr(scatter, step)(*args)

    def dec_step(step):
        if wide:
            getattr(dec, step)()

    dec_step("begin")
    dec_step("over_x")
    swapped.wait_recv()
    near, far = gfeat_ref[...].astype(f32), feat_s[...].astype(f32)
    first = place.row == 0
    grad = jnp.concatenate([jnp.where(first, near, far), jnp.where(first, far, near)], axis=0)
    gvec_ref[...] = jnp.zeros(gvec_ref.shape, f32)

    def note(row, grad_out, scaled):
        gvec_ref[row : row + 1, :] = column_sum(grad_out * scaled)
        gvec_ref[row + 1 : row + 2, :] = column_sum(grad_out)

    arriving[0].wait()
    scaled, inv = norm_rows(x_ref[2 * LAYERS])
    note(4 * LAYERS, grad, scaled)
    d_x = norm_rows_back(grad, scaled, inv, gain_ref[4 * LAYERS : 4 * LAYERS + 1, :])
    for layer in (1, 0):
        gains = gain_ref[4 * layer : 4 * layer + 4, :]
        dn, up, at = (f"{kind}{layer}" for kind in ("dn", "up", "at"))
        scaled2, inv2 = norm_rows(x_ref[2 * layer + 1])
        n2 = low(scaled2 * gains[2:3] + gains[3:4])
        d_low = low(d_x)
        factor(0, d_low)
        dn_items = [(0, h_s, 0, HID)]
        load(layer, 2).wait()
        emit(dn, dn_items)
        load(layer, 3).wait()
        load(layer, 1).wait()
        d_hidden = times_plain(d_low, wb_s[:, HID : 2 * HID])
        du_s[...] = low(d_hidden * slope_s[...])
        swap.start(2 * layer + 1, times_trans(du_s[...], wb_s[:, 0:HID]))
        later("over_x", dn, dn_items)
        factor(1, n2)
        up_items = [(1, du_s, 0, HID)]
        emit(up, up_items)
        later("over_x", up, up_items)
        if layer == 1:
            load(0, 2).start()
            load(0, 3).start()
            load(0, 1).start()
            if wide:
                dec.line_two.relay()
        else:
            later("along_z", "at1")
            later("relay", "up1")
        d_n2 = swap.total(2 * layer + 1)
        note(4 * layer + 2, d_n2, scaled2)
        d_x = d_x + norm_rows_back(d_n2, scaled2, inv2, gains[2:3])
        d_low = low(d_x)
        factor(2, d_low)
        load(layer, 0).wait()
        if layer == 1:
            for copy in arriving[1:]:
                copy.wait()
        d_att = low(times_plain(d_low, wa_s[:, QKV_W:A_COLS]))
        encoder_attention_back(qkv_ref.at[layer], d_att, dqkv_s)
        swap.start(2 * layer, times_trans(dqkv_s[...], wa_s[:, 0:QKV_W]))
        scaled1, inv1 = norm_rows(x_ref[2 * layer])
        factor(3, low(scaled1 * gains[0:1] + gains[1:2]))
        at_items = [(3, dqkv_s, 0, QKV_W), (2, o_ref.at[layer], QKV_W, HALF_D)]
        emit(at, at_items)
        if layer == 1:
            load(0, 0).start()
            dec_step("along_z")
        else:
            later("relay", "at1")
        later("along_z", dn)
        later("over_x", at, at_items)
        later("along_z", up)
        later("relay", dn)
        if layer == 1:
            if wide:
                dec.line_one.relay()
        d_n1 = swap.total(2 * layer)
        note(4 * layer, d_n1, scaled1)
        d_x = d_x + norm_rows_back(d_n1, scaled1, inv1, gains[0:1])
    factor(0, low(d_x))
    emb_items = [(0, px_ref, 0, D)]
    emit("emb", emb_items)
    later("over_x", "emb", emb_items)
    later("relay", "up0")
    if wide:
        lane = lane_ids((1, DD))
        dvec = jnp.where(row_ids((8, 1)) < 7, dvec_ref[...], 0.0)
        loss = jnp.where(lane == 0, loss_ref[0:1, 0:1], 0.0)
        dvec = dvec + jnp.where(row_ids((8, 1)) == 7, loss, 0.0)
        everyone.first(0.5 * gvec_ref[...], dvec)
        dec.over_rows()
        everyone.stage(1)
        scatter.along_z("at0")
        everyone.stage(2)
        dec.to_cores()
        scatter.along_z("emb")
        everyone.stage(3)
        scatter.relay("at0")
        dec.finish()
        scatter.relay("emb")
        everyone.stage(4)
        square = jnp.zeros((1, 1), f32)
        for name, _ in SUMS:
            scatter.finish(name)
            whole = into(name)[...]
            square = square + jnp.sum(whole * whole)
        square = square + jnp.sum(gdec_ref[...] * gdec_ref[...])
        square = everyone.number(square)
        total_ref[...] = everyone.total()
        total_ref[23:24, 0:128] += jnp.where(lane_ids((1, 128)) == 1, square, 0.0)
        scatter.drain()
        dec.drain()
        everyone.drain()
    swapped.wait_send()
    swap.drain()


def run_encoder_back(wide, *operands):
    bf, f32 = jnp.bfloat16, jnp.float32
    vmem = pl.BlockSpec(memory_space=pltpu.VMEM)
    dma = pltpu.SemaphoreType.DMA
    shape = jax.ShapeDtypeStruct
    rows, kind = (SHARD, f32) if wide else (D, bf)
    scratch = [
        pltpu.VMEM((D, A_COLS), bf),
        pltpu.VMEM((D, 2 * HID), bf),
        pltpu.VMEM((PAIR, HID), bf),
        pltpu.VMEM((PAIR, QKV_W), bf),
        pltpu.VMEM((128, D), bf),
        pltpu.VMEM((2, PAIR, D), bf),
        pltpu.VMEM((2 * LAYERS, PAIR, D), bf),
        pltpu.VMEM((PAIR, HID), bf),
        pltpu.VMEM((PAIR, HID), f32),
        pltpu.VMEM((2 * LAYERS + 1, PAIR, D), f32),
        pltpu.VMEM((LAYERS, PAIR, QKV_W), bf),
        pltpu.VMEM((LAYERS, PAIR, HALF_D), bf),
        pltpu.VMEM((PAIR, D), bf),
        dma((4,)),
        dma((LAYERS, 4)),
        dma,
        dma,
        dma((2 * LAYERS,)),
        dma((2 * LAYERS,)),
    ]
    outs = [
        shape((LAYERS, rows, ENC_COLS), kind),
        shape((rows, D), kind),
        shape((16, D), f32),
    ]
    anywhere = pl.BlockSpec(memory_space=pl.ANY)
    in_specs = [vmem] + [anywhere] * 6 + [vmem, anywhere]
    if wide:
        outs += [shape((SHARD // 2, PART_ONE + PART_TWO), f32), shape((24, D), f32)]
        in_specs += [vmem] * 4
        n = len(SUMS)
        both = ONE_HALF + TWO_HALF
        scratch += [
            pltpu.VMEM((4, D, PAIR), bf),
            pltpu.VMEM((2, D, PAIR), bf),
            pltpu.VMEM((2, BLOCKS, HID), bf),
            pltpu.VMEM((BLOCKS, SUM_COLS), bf),
            pltpu.VMEM((3, QUARTER, HID), bf),
            pltpu.VMEM((QUARTER, SUM_COLS), bf),
            pltpu.VMEM((3, SHARD, SUM_COLS), bf),
            pltpu.VMEM((4, SHARD, SUM_COLS), bf),
            pltpu.VMEM((4, QUARTER, HID), f32),
            dma((n,)),
            dma((n,)),
            dma((n,)),
            dma((n,)),
            dma((n, 4)),
            dma((n, 4)),
            pltpu.VMEM((2, DD, ONE_HALF), bf),
            pltpu.VMEM((4, 2, SHARD, ONE_HALF), bf),
            pltpu.VMEM((4, 2, SHARD, ONE_HALF), bf),
            pltpu.VMEM((8 * SHARD, ONE_HALF), f32),
            pltpu.VMEM((3, 2 * SHARD, ONE_HALF), bf),
            pltpu.VMEM((4, 2 * SHARD, ONE_HALF), bf),
            pltpu.VMEM((3, 2 * SHARD, TWO_HALF), bf),
            pltpu.VMEM((4, 2 * SHARD, TWO_HALF), bf),
            pltpu.VMEM((2 * SHARD, both), f32),
            pltpu.VMEM((SHARD, both), bf),
            pltpu.VMEM((SHARD, both), bf),
            pltpu.VMEM((SHARD, both), f32),
            pltpu.VMEM((SHARD // 2, both), f32),
            dma,
            dma,
            dma,
            dma,
            dma((4,)),
            dma((4,)),
            dma((4,)),
            dma((4,)),
            dma,
            dma,
            dma,
            dma,
            pltpu.VMEM((5, 24, D), f32),
            pltpu.VMEM((6, 24, D), f32),
            pltpu.VMEM((2, 8, 128), f32),
            pltpu.VMEM((10, 8, 128), f32),
            dma((6,)),
            dma((6,)),
            dma((10,)),
            dma((10,)),
        ]
    return pl.pallas_call(
        functools.partial(encoder_back_body, wide),
        out_shape=tuple(outs),
        in_specs=in_specs,
        out_specs=(vmem,) * len(outs),
        scratch_shapes=scratch,
        compiler_params=pltpu.CompilerParams(
            collective_id=2, has_side_effects=True, vmem_limit_bytes=63 * MIB
        ),
        cost_estimate=pl.CostEstimate(
            flops=20 * 10**9, bytes_accessed=60 * 10**6, transcendentals=10**6
        ),
        name="encoder_back",
    )(*operands)


def adam_at(refs, spot, grad, decay_rate, step_rate):
    master, first, second, master_out, first_out, second_out = refs
    new = adam_update(master[spot], first[spot], second[spot], grad, decay_rate, step_rate)
    master_out[spot], first_out[spot], second_out[spot] = new


def head_pieces(rows, heads):
    pieces = []
    for h in range(heads):
        for part in range(3):
            at = (part * heads + h) * HEAD
            pieces.append(rows[:, at : at + HEAD])
    pieces.append(rows[:, 3 * heads * HEAD :])
    return jnp.concatenate(pieces, axis=-1)


def update_body(*refs):
    f32 = jnp.float32
    total_ref = refs[0]
    grads = refs[1:4]
    states = [refs[4 + 3 * i : 7 + 3 * i] for i in range(5)]
    loss_ref, norm_ref = refs[19:21]
    outs = [refs[21 + 3 * i : 24 + 3 * i] for i in range(5)]
    total = total_ref[...]
    squares = jnp.sum(total[0:23, :] * total[0:23, :]) + jnp.sum(total[23:24, 1:2])
    norm = jnp.sqrt(jnp.zeros((1, 1), f32) + squares)
    factor = jnp.minimum(1.0, CLIP_MAX / (norm + 1e-06))
    step = pl.program_id(0)
    rows = grads[0].shape[1]

    @pl.loop(0, rows // 8)
    def _(i):
        spot = pl.ds(pl.multiple_of(i * 8, 8), 8)
        grad = head_pieces(grads[0][0, spot, :], HEADS // 2)
        adam_at(states[0] + outs[0], (0, 0, spot, slice(None)), grad * factor, DECAY, RATE)

    @pl.when(step == 0)
    def _():
        loss_ref[0, 0] = jnp.sum(total[23:24, 0:1])
        norm_ref[0, 0] = jnp.sum(norm)
        adam_at(states[1] + outs[1], (0,), grads[1][...] * factor, DECAY, RATE)

    @pl.when(step == 1)
    def _():
        both = ONE_HALF + TWO_HALF
        grad = grads[2][...]
        one = jnp.concatenate([grad[:, 0:ONE_HALF], grad[:, both : both + ONE_HALF]], axis=-1)
        two = jnp.concatenate([grad[:, ONE_HALF:both], grad[:, both + ONE_HALF :]], axis=-1)
        pieces = [one[:, 0:ED_AT], two[:, 0:192], two[:, UP_TWO:], one[:, ED_AT : ED_AT + DD]]
        grad = head_pieces(jnp.concatenate(pieces, axis=-1), DHEADS // 2)
        adam_at(states[2] + outs[2], (0,), grad * factor, DECAY, RATE)

    @pl.when(step == 2)
    def _():
        place = Place()
        own = shard_at(place.z, place.x, place.col)
        for kind, top, count, width in ((3, 0, 10, D), (4, 16, 7, DD)):
            share = width // N_SHARDS
            turned = pltpu.roll(total, (D - own * share) % D, 1)
            grad = turned[top : top + count, 0:share] * factor
            adam_at(states[kind] + outs[kind], (slice(None), slice(None)), grad, 0.0, VEC_RATE)


def run_update(total, grads, states):
    f32 = jnp.float32
    smem = pl.BlockSpec(memory_space=pltpu.SMEM)
    flat = [a for triple in states for a in triple]
    scalar = jax.ShapeDtypeStruct((1, 1), f32)
    outs = (scalar, scalar) + tuple(jax.ShapeDtypeStruct(a.shape, f32) for a in flat)
    rows = SHARD // 2

    def whole(array):
        return pl.BlockSpec(array.shape, lambda i: (0,) * array.ndim)

    enc = pl.BlockSpec((1, 1, rows, ENC_COLS), lambda i: (i // 2, 0, i % 2, 0))
    enc_grad = pl.BlockSpec((1, rows, ENC_COLS), lambda i: (i // 2, i % 2, 0))
    state_specs = [enc] * 3 + [whole(a) for a in flat[3:]]
    return pl.pallas_call(
        update_body,
        grid=(2 * LAYERS,),
        out_shape=outs,
        in_specs=[whole(total), enc_grad, whole(grads[1]), whole(grads[2])] + state_specs,
        out_specs=tuple([smem, smem] + state_specs),
        compiler_params=pltpu.CompilerParams(vmem_limit_bytes=60 * MIB),
        name="update",
    )(total, *grads, *flat)


def head_order(matrix, heads, width):
    lead = matrix.shape[:-1]
    cut = matrix[..., :width].reshape(lead + (heads, 3, HEAD))
    cut = jnp.swapaxes(cut, -3, -2).reshape(lead + (width,))
    return jnp.concatenate([cut, matrix[..., width:]], axis=-1)


def head_order_back(matrix, heads, width):
    lead = matrix.shape[:-1]
    cut = matrix[..., :width].reshape(lead + (3, heads, HEAD))
    cut = jnp.swapaxes(cut, -3, -2).reshape(lead + (width,))
    return jnp.concatenate([cut, matrix[..., width:]], axis=-1)


def sine_table(length, width):
    column = np.arange(width)
    freq = np.exp(-math.log(10000.0) * (2.0 * (column // 2)) / width)
    angle = np.arange(length)[:, None] * freq
    table = np.where(column % 2 == 0, np.sin(angle), np.cos(angle))
    return np.pad(table, ((0, ROWS - length), (0, 0))).astype(np.float32)


def frequency_rows(width):
    column = np.arange(width)
    freq = np.exp(-math.log(10000.0) * (2.0 * (column // 2)) / width)
    return np.broadcast_to(freq.astype(np.float32), (8, width))


def split_parts(matrices):
    gap = [(0, 0)] * (matrices.ndim - 1)
    one = jnp.concatenate([matrices[..., :ED_AT], matrices[..., 3072:]], axis=-1)
    one = jnp.pad(one, gap + [(0, PART_ONE - one.shape[-1])])
    out = jnp.pad(matrices[..., ED_AT:768], gap + [(0, UP_TWO - 192)])
    return one, jnp.concatenate([out, matrices[..., 768:3072]], axis=-1)


def join_parts(one, two):
    return jnp.concatenate(
        [one[..., :ED_AT], two[..., :192], two[..., UP_TWO:], one[..., ED_AT : ED_AT + DD]], axis=-1
    )


def gather_vectors(enc_vec, dec_vec, group):
    vectors = jnp.concatenate([enc_vec.reshape(-1), dec_vec.reshape(-1)])
    vectors = lax.all_gather(low(vectors), group, axis=0, tiled=False).astype(jnp.float32)
    cut = enc_vec.size
    enc_gains = jnp.swapaxes(vectors[:, :cut].reshape(-1, *enc_vec.shape), 0, 1).reshape(-1, D)
    dec_gains = jnp.swapaxes(vectors[:, cut:].reshape(-1, *dec_vec.shape), 0, 1).reshape(-1, DD)
    return (
        jnp.pad(enc_gains, ((0, 16 - enc_gains.shape[0]), (0, 0))),
        jnp.pad(dec_gains, ((0, 8 - dec_gains.shape[0]), (0, 0))),
    )


def update_plain(loss_part, dec_vec_grads, enc_vec_grads, grads, states):
    everyone = ("row", "clip", "col")
    n_enc, n_dec = states[3][0].shape[0], states[4][0].shape[0]
    enc_vec_total, dec_vec_total, loss_total, square = lax.psum(
        (
            0.5 * enc_vec_grads[:n_enc],
            dec_vec_grads[:n_dec],
            loss_part,
            sum(jnp.sum(g * g) for g in grads),
        ),
        everyone,
    )
    square = square + jnp.sum(enc_vec_total**2) + jnp.sum(dec_vec_total**2)
    grad_norm = jnp.sqrt(square)
    factor = jnp.minimum(1.0, CLIP_MAX / (grad_norm + 1e-06))
    shard = lax.axis_index("clip") * lax.axis_size("col") + lax.axis_index("col")
    own = []
    for total, state in ((enc_vec_total, states[3][0]), (dec_vec_total, states[4][0])):
        width = state.shape[1]
        own.append(lax.dynamic_slice_in_dim(total, shard * width, width, 1))
    decays = (DECAY, DECAY, DECAY, 0.0, 0.0)
    rates = (RATE, RATE, RATE, VEC_RATE, VEC_RATE)
    results = []
    for triple, grad, decay_rate, step_rate in zip(states, (*grads, *own), decays, rates):
        grad = grad.reshape(triple[0].shape)
        results.extend(adam_update(*triple, grad * factor, decay_rate, step_rate))
    return (loss_total, grad_norm, *results)


def local(
    patches,
    visible,
    masked,
    enc_layers,
    enc_first,
    enc_second,
    embed,
    embed_first,
    embed_second,
    dec_mats,
    dec_first,
    dec_second,
    enc_vec,
    enc_vec_first,
    enc_vec_second,
    dec_vec,
    dec_vec_first,
    dec_vec_second,
):
    f32 = jnp.float32
    group = ("clip", "col")
    everyone = ("row", "clip", "col")
    wide = lax.axis_size("clip") == 8 and lax.axis_size("col") == 2
    freq = jnp.asarray(frequency_rows(D))
    table = jnp.asarray(sine_table(TUBES, DD))
    if wide:
        feat, xs, qkv, att, hid, slope, px, padded, enc_gains, dec_gains, enc_full, one, two = (
            run_encoder(True, visible, patches, freq, embed, enc_layers, dec_mats, enc_vec, dec_vec)
        )
    else:
        embed_full = lax.all_gather(low(embed[0]), group, axis=0, tiled=True)
        enc_here = low(head_order(enc_layers[:, 0], HEADS // 2, QKV_W))
        enc_full = lax.all_gather(enc_here, group, axis=1, tiled=True)
        dec_here = low(head_order(dec_mats[0], DHEADS // 2, ED_AT))
        dec_full = lax.all_gather(dec_here, everyone, axis=0, tiled=True).reshape(2, DD, -1)
        enc_gains, dec_gains = gather_vectors(enc_vec, dec_vec, group)
        feat, xs, qkv, att, hid, slope, px, padded = run_encoder(
            False, visible, patches, freq, embed_full, enc_full, enc_gains
        )
        one, two = split_parts(dec_full)
    loss_block, grad_one, grad_two, dec_vec_grads, grad_feat = run_decoder(
        wide, visible, feat, padded, table, one, two, dec_gains
    )
    kept = (grad_feat, xs, qkv, att, hid, slope, px, enc_gains, enc_full)
    states = (
        (enc_layers, enc_first, enc_second),
        (embed, embed_first, embed_second),
        (dec_mats, dec_first, dec_second),
        (enc_vec, enc_vec_first, enc_vec_second),
        (dec_vec, dec_vec_first, dec_vec_second),
    )
    if wide:
        enc_total, embed_total, _, dec_total, total = run_encoder_back(
            True, *kept, grad_one, grad_two, loss_block, dec_vec_grads
        )
        grads = (enc_total, embed_total, dec_total)
        loss_total, grad_norm, *results = run_update(total, grads, states)
        return (loss_total[0, 0], grad_norm[0, 0], *results)
    dec_grads = join_parts(grad_one, grad_two)
    dec_total = lax.psum_scatter(
        dec_grads.reshape(-1, dec_grads.shape[-1]).astype(f32),
        everyone,
        scatter_dimension=0,
        tiled=True,
    )
    enc_total, embed_total, enc_vec_grads = run_encoder_back(False, *kept)
    enc_total = lax.psum_scatter(enc_total.astype(f32), group, scatter_dimension=1, tiled=True)
    embed_total = lax.psum_scatter(embed_total.astype(f32), group, scatter_dimension=0, tiled=True)
    grads = (
        head_order_back(enc_total, HEADS // 2, QKV_W),
        embed_total,
        head_order_back(dec_total, DHEADS // 2, ED_AT),
    )
    return update_plain(loss_block[0, 0], dec_vec_grads, enc_vec_grads, grads, states)


def solution(mesh):
    in_specs = (
        P(None, ("clip", "col"), None, "row"),
        P(None, ("clip", "col"), None),
        P(None, ("clip", "col"), None),
        P(None, "row", ("clip", "col"), None),
        P(None, "row", ("clip", "col"), None),
        P(None, "row", ("clip", "col"), None),
        P("row", ("clip", "col"), None),
        P("row", ("clip", "col"), None),
        P("row", ("clip", "col"), None),
        P("row", ("clip", "col"), None),
        P("row", ("clip", "col"), None),
        P("row", ("clip", "col"), None),
        P(None, ("clip", "col")),
        P(None, ("clip", "col")),
        P(None, ("clip", "col")),
        P(None, ("clip", "col")),
        P(None, ("clip", "col")),
        P(None, ("clip", "col")),
    )
    out_specs = (
        P(),
        P(),
        P(None, "row", ("clip", "col"), None),
        P(None, "row", ("clip", "col"), None),
        P(None, "row", ("clip", "col"), None),
        P("row", ("clip", "col"), None),
        P("row", ("clip", "col"), None),
        P("row", ("clip", "col"), None),
        P("row", ("clip", "col"), None),
        P("row", ("clip", "col"), None),
        P("row", ("clip", "col"), None),
        P(None, ("clip", "col")),
        P(None, ("clip", "col")),
        P(None, ("clip", "col")),
        P(None, ("clip", "col")),
        P(None, ("clip", "col")),
        P(None, ("clip", "col")),
    )
    return jax.shard_map(local, mesh=mesh, in_specs=in_specs, out_specs=out_specs, check_vma=False)
```
